32 devices in a mesh: seq: 8 (over z, core), dp: 4 (over y, x).
Axes of the slice: x: 2, y: 2, z: 4, core: 2. Of those that a mesh axis runs over, the one named last changes fastest.
Arguments:
- tokens: bfloat16 [4, 1024, 1024], P('dp', 'seq'), may hold values from -6 to 6
- cotangent: bfloat16 [4, 1024, 1024], P('dp', 'seq'), may hold values from -6 to 6
- doc_lengths: int32 [4, 4], P('dp'), may hold values from 1 to 960, 1024 in all within a row
- decay_exponent: int32 [1536], replicated, may hold values from 4 to 19
- branch_weight: bfloat16 [1024, 1536], P(('seq', 'dp')), may hold values from -0.1875 to 0.1875
- input_weight: bfloat16 [1024, 1536], P(('seq', 'dp')), may hold values from -0.1875 to 0.1875
- decay_weight: bfloat16 [1536, 1536], P(('seq', 'dp')), may hold values from -0.15625 to 0.15625
- inject_weight: bfloat16 [1536, 1536], P(('seq', 'dp')), may hold values from -0.15625 to 0.15625
- output_weight: bfloat16 [1536, 1024], P(('seq', 'dp')), may hold values from -0.15625 to 0.15625
- mlp_gate: bfloat16 [1024, 3072], P(('seq', 'dp')), may hold values from -0.1875 to 0.1875
- mlp_up: bfloat16 [1024, 3072], P(('seq', 'dp')), may hold values from -0.1875 to 0.1875
- mlp_down: bfloat16 [3072, 1024], P(('seq', 'dp')), may hold values from -0.109375 to 0.109375
- first_gain: bfloat16 [1024], P(('seq', 'dp')), may hold values from 0.5 to 1.5
- second_gain: bfloat16 [1024], P(('seq', 'dp')), may hold values from 0.5 to 1.5
- conv_taps: bfloat16 [1536, 4], P(('seq', 'dp')), may hold values from -3 to 3
- conv_bias: bfloat16 [1536], P(('seq', 'dp')), may hold values from -3 to 3
- decay_bias: bfloat16 [1536], P(('seq', 'dp')), may hold values from -4 to 4
- inject_bias: bfloat16 [1536], P(('seq', 'dp')), may hold values from -4 to 4
Outputs:
- activations: bfloat16 [4, 1024, 1024], P('dp', 'seq')
- d_tokens: float32 [4, 1024, 1024], P('dp', 'seq')
- grad_branch_weight: float32 [1024, 1536], P(('seq', 'dp'))
- grad_input_weight: float32 [1024, 1536], P(('seq', 'dp'))
- grad_decay_weight: float32 [1536, 1536], P(('seq', 'dp'))
- grad_inject_weight: float32 [1536, 1536], P(('seq', 'dp'))
- grad_output_weight: float32 [1536, 1024], P(('seq', 'dp'))
- grad_mlp_gate: float32 [1024, 3072], P(('seq', 'dp'))
- grad_mlp_up: float32 [1024, 3072], P(('seq', 'dp'))
- grad_mlp_down: float32 [3072, 1024], P(('seq', 'dp'))
- grad_first_gain: float32 [1024], P(('seq', 'dp'))
- grad_second_gain: float32 [1024], P(('seq', 'dp'))
- grad_conv_taps: float32 [1536, 4], P(('seq', 'dp'))
- grad_conv_bias: float32 [1536], P(('seq', 'dp'))
- grad_decay_bias: float32 [1536], P(('seq', 'dp'))
- grad_inject_bias: float32 [1536], P(('seq', 'dp'))
The draws below stay inside these ranges and needn't reach their ends.
Inputs may be any that keep to these rules, and one draw needn't show every extreme that they name: `doc_lengths`: each row sums to 1024; in each row the longest document has exactly 960 tokens.
All inputs are finite; a program needn't handle non-finite values.
Results may differ from the reference program's by a relative error of at most 0.018.
Values may be sent and summed in bfloat16 or wider, within the bound.
A program may use at most 256 MiB of HBM per device.

```python
import math
import jax
import jax.numpy as jnp
import numpy as np
from jax import lax

D = 1024
WIDTH = 1536
FF = 3072
TOK_DEV = 128
SEGS = 4
GROUPS = 4
GROUP_TOK = 1024


def set_ends(drawn, stream_key, low, largest):
    spot = [jax.random.randint(jax.random.fold_in(stream_key, axis), (), 0, length) for axis, length in enumerate(drawn.shape)]
    widest = drawn.shape.index(max(drawn.shape))
    beside = spot[:widest] + [(spot[widest] + 1) % drawn.shape[widest]] + spot[widest + 1:]
    return drawn.at[tuple(spot)].set(low).at[tuple(beside)].set(largest)


def levels(stream_key, dims, shards, least, high):
    loudness, own = 1.0, jax.random.fold_in(stream_key, 6)
    for position, parts in shards:
        heights = jnp.exp(jax.random.uniform(jax.random.fold_in(own, position), (parts,), jnp.float32, least / len(shards), high / len(shards)))
        loudness = loudness * jnp.repeat(heights, dims[position] // parts).reshape([-1 if axis == position else 1 for axis in range(len(dims))])
    return loudness


def profile(amount, total, bound, lean):
    portions = [(1 << 20) // math.isqrt(rank ** lean) + 1 for rank in range(2, amount + 1)]
    surplus, holding = total - bound - (amount - 1), [1] * (amount - 1)
    while surplus > 0:
        free = [i for i in range(amount - 1) if holding[i] < bound]
        pool, left = sum([portions[i] for i in free]), surplus
        for i in free:
            extra = min(bound - holding[i], max(1, left * portions[i] // pool), surplus)
            holding[i] = holding[i] + extra
            surplus = surplus - extra
    return np.array([bound] + holding)


def ragged_sizes(stream_key, count, total, limit, skew):
    if count == 2:
        one = jax.random.randint(stream_key, (), max(1, total - limit), min(limit, total - 1) + 1)
        return jnp.stack([one, total - one])
    sizes = jnp.asarray(profile(count, total, limit, skew), jnp.int32)
    pairs = (count - 1) // 2
    source_of, receiver = sizes[1:1 + 2 * pairs:2], sizes[2:2 + 2 * pairs:2]
    margin = jnp.minimum(source_of - 1, limit - receiver)
    passed = jax.random.randint(jax.random.fold_in(stream_key, 1), (pairs,), 0, 1 << 20) % (margin + 1)
    sizes = sizes.at[1:1 + 2 * pairs:2].set(source_of - passed).at[2:2 + 2 * pairs:2].set(receiver + passed)
    return sizes[jax.random.permutation(jax.random.fold_in(stream_key, 2), count)]


def bell_draw(stream_key, dims, spread, most, split=(), kind=jnp.bfloat16):
    level = levels(stream_key, dims, split, -0.22, 0.18) if split else 1.0
    values = jax.random.normal(stream_key, dims, jnp.float32) * spread * level
    return jnp.minimum(jnp.maximum(values, -most), most).astype(kind)


def setup_inputs(seed: int = 0) -> dict:
    key_list = jax.random.split(jax.random.key(seed), 19)
    return {
        "tokens": bell_draw(key_list[0], (GROUPS, GROUP_TOK, D), 1.0, 6.0, ((0, 4), (1, 8))),
        "cotangent": bell_draw(key_list[1], (GROUPS, GROUP_TOK, D), 1.0, 6.0, ((0, 4), (1, 8))),
        "doc_lengths": jax.vmap(lambda own: ragged_sizes(own, SEGS, GROUP_TOK, GROUP_TOK - TOK_DEV // 2, 2))(jax.random.split(key_list[2], GROUPS)).reshape((GROUPS, SEGS)).astype(jnp.int32),
        "decay_exponent": set_ends(jax.random.randint(key_list[3], (WIDTH,), 4, 20), jax.random.fold_in(key_list[3], 1), 4, 19).astype(jnp.int32),
        "branch_weight": bell_draw(key_list[4], (D, WIDTH), D ** -0.5, 0.1875, ((0, 32),)),
        "input_weight": bell_draw(key_list[5], (D, WIDTH), D ** -0.5, 0.1875, ((0, 32),)),
        "decay_weight": bell_draw(key_list[6], (WIDTH, WIDTH), WIDTH ** -0.5, 0.15625, ((0, 32),)),
        "inject_weight": bell_draw(key_list[7], (WIDTH, WIDTH), WIDTH ** -0.5, 0.15625, ((0, 32),)),
        "output_weight": bell_draw(key_list[8], (WIDTH, D), WIDTH ** -0.5, 0.15625, ((0, 32),)),
        "mlp_gate": bell_draw(key_list[9], (D, FF), D ** -0.5, 0.1875, ((0, 32),)),
        "mlp_up": bell_draw(key_list[10], (D, FF), D ** -0.5, 0.1875, ((0, 32),)),
        "mlp_down": bell_draw(key_list[11], (FF, D), FF ** -0.5, 0.109375, ((0, 32),)),
        "first_gain": jnp.clip(1.0 + 0.1 * jax.random.normal(key_list[12], (D,), jnp.float32), 0.5, 1.5).astype(jnp.bfloat16),
        "second_gain": jnp.clip(1.0 + 0.1 * jax.random.normal(key_list[13], (D,), jnp.float32), 0.5, 1.5).astype(jnp.bfloat16),
        "conv_taps": bell_draw(key_list[14], (WIDTH, 4), 0.5, 3.0, ((0, 32),)),
        "conv_bias": bell_draw(key_list[15], (WIDTH,), 0.5, 3.0, ((0, 32),)),
        "decay_bias": bell_draw(key_list[16], (WIDTH,), 1.0, 4.0, ((0, 32),)),
        "inject_bias": bell_draw(key_list[17], (WIDTH,), 1.0, 4.0, ((0, 32),)),
    }


@jax.custom_vjp
def low(v):
    return lax.optimization_barrier(v.astype(jnp.bfloat16)).astype(jnp.float32)

@jax.custom_vjp
def low_back(v):
    return v

def low_keep(v):
    return (low(v), None)

def low_pass(kept, grad):
    return (grad,)

def back_keep(v):
    return (v, None)

def back_low(kept, grad):
    return (low(grad),)
low.defvjp(low_keep, low_pass)
low_back.defvjp(back_keep, back_low)
eps_norm = 1e-06
floor_gap = 1e-05
rate_scale = 8.0

def matmul(left, right):
    return jnp.dot(left, right, precision=lax.Precision.HIGHEST)

def normed(values, gain):
    return values * lax.rsqrt(lax.optimization_barrier(jnp.mean(values * values, axis=-1, keepdims=True)) + eps_norm) * gain

def combine(early, late):
    return (early[0] * late[0], late[0] * early[1] + late[1])

def row_layer(x, lengths, params, scale):
    branch_w, input_w, decay_w, inject_w, output_w, gate_w, up_w, down_w, gain_one, gain_two, taps, conv_b, decay_b, inject_b = params
    count = x.shape[0]
    width = input_w.shape[1]
    pos = jnp.arange(count, dtype=jnp.int32)
    ends = jnp.cumsum(lengths).astype(jnp.int32)
    starts = (ends - lengths).astype(jnp.int32)
    seg = lax.optimization_barrier(jnp.sum((ends[None, :] <= pos[:, None]).astype(jnp.int32), axis=1)).astype(jnp.int32)
    first = jnp.any(starts[None, :] == pos[:, None], axis=1)[:, None]
    n_one = low(normed(x, gain_one))
    gate_pre = low_back(matmul(n_one, branch_w))
    gated = jax.nn.gelu(gate_pre)
    u_val = low(low_back(matmul(n_one, input_w)))
    conv = conv_b + taps[:, 0] * u_val
    for k in range(1, 4):
        shifted = jnp.concatenate([jnp.zeros((k, width), jnp.float32), u_val[:-k]], 0)
        seg_prev = jnp.concatenate([jnp.full((k,), -1, jnp.int32), seg[:-k]], 0)
        same = (seg_prev == seg)[:, None]
        conv = conv + jnp.where(same, taps[:, k] * shifted, 0.0)
    conv_out = low(conv)
    pre_decay = low_back(matmul(conv_out, decay_w) + decay_b)
    pre_inject = low_back(matmul(conv_out, inject_w) + inject_b)
    rgate = jax.nn.sigmoid(pre_decay)
    igate = jax.nn.sigmoid(pre_inject)
    log_a = -rate_scale * rgate * scale
    gap = -jnp.expm1(2.0 * log_a)
    mult = jnp.where(first, 1.0, jnp.sqrt(jnp.maximum(gap, floor_gap)))
    decay = jnp.where(first, 0.0, jnp.exp(log_a))
    drive = mult * igate * conv_out
    _, state = lax.associative_scan(combine, (decay, drive), axis=0)
    mixed = low(state * gated)
    x_one = x + low_back(matmul(mixed, output_w))
    n_two = low(normed(x_one, gain_two))
    p_one = low_back(matmul(n_two, gate_w))
    p_two = low_back(matmul(n_two, up_w))
    hidden = low(jax.nn.gelu(p_one) * p_two)
    return x_one + matmul(hidden, down_w)

def reference(tokens, cotangent, doc_lengths, decay_exponent, branch_weight, input_weight, decay_weight, inject_weight, output_weight, mlp_gate, mlp_up, mlp_down, first_gain, second_gain, conv_taps, conv_bias, decay_bias, inject_bias):
    scale = jnp.exp2(-decay_exponent.astype(jnp.float32))
    params = tuple((p.astype(jnp.float32) for p in (branch_weight, input_weight, decay_weight, inject_weight, output_weight, mlp_gate, mlp_up, mlp_down, first_gain, second_gain, conv_taps, conv_bias, decay_bias, inject_bias)))

    def forward(x_all, weights):

        def one_row(pair):
            return row_layer(pair[0], pair[1], weights, scale)
        return lax.map(jax.checkpoint(one_row), (x_all, doc_lengths))
    x_all = tokens.astype(jnp.float32)
    result, pull = jax.vjp(forward, x_all, params)
    d_tokens, grads = pull(cotangent.astype(jnp.float32))
    return (result.astype(jnp.bfloat16), d_tokens, grads[0], grads[1], grads[2], grads[3], grads[4], grads[5], grads[6], grads[7], grads[8], grads[9], grads[10], grads[11], grads[12], grads[13])
```

```python
import itertools
import math
from functools import partial
from types import SimpleNamespace

import jax
import jax.numpy as jnp
from jax import lax
from jax.experimental import pallas as pl
from jax.experimental.pallas import tpu as pltpu
from jax.sharding import Mesh, PartitionSpec as P

f32, bf16 = jnp.float32, jnp.bfloat16
MESH = pl.DeviceIdType.MESH
AXES = ("zh", "zl", "c", "yh", "yl", "xh", "xl")
RING = 4
PLANE = 4
SHARES = RING * 2 * PLANE
SEMS = 512

eps_norm = 1e-06
floor_gap = 1e-05
rate_scale = 8.0
gelu_root = math.sqrt(2.0 / math.pi)
gelu_cube = 0.044715


def dot(left, right):
    return jnp.dot(left, right, preferred_element_type=f32)


def dot_nt(left, right):
    return lax.dot_general(left, right, (((1,), (1,)), ((), ())), preferred_element_type=f32)


def dot_tn(left, right):
    return lax.dot_general(left, right, (((0,), (0,)), ((), ())), preferred_element_type=f32)


def gelu_parts(v):
    t = jnp.tanh(gelu_root * (v + gelu_cube * v * v * v))
    half = 0.5 * (1.0 + t)
    slope = half + 0.5 * v * (1.0 - t * t) * gelu_root * (1.0 + 3.0 * gelu_cube * v * v)
    return v * half, slope


def minus_expm1(y):
    poly = jnp.full_like(y, 1.0 / 8.0)
    poly = 1.0 + y * poly
    for k in (7, 6, 5, 4, 3, 2):
        poly = 1.0 + y * poly * (1.0 / k)
    return jnp.where(y > -0.35, -y * poly, 1.0 - jnp.exp(y))


def inverse_rms(v):
    return lax.rsqrt(jnp.mean(v * v, axis=-1, keepdims=True) + eps_norm)


def loop(total, step, body):
    def run(j, _):
        body(pl.multiple_of(j * step, step))
        return 0

    lax.fori_loop(0, total // step, run, 0)


def layer(dims, *refs):
    T, D, W, F, CW, CF = dims.T, dims.D, dims.W, dims.F, dims.CW, dims.CF
    RD, RW, RF, NL = dims.RD, dims.RW, dims.RF, dims.NL
    M = PLANE * T
    r = SimpleNamespace(**dict(zip(dims.names, refs, strict=True)))

    zh, zl, c = lax.axis_index("zh"), lax.axis_index("zl"), lax.axis_index("c")
    yl, xl = lax.axis_index("yl"), lax.axis_index("xl")
    p = yl * 2 + xl
    px, py, pd = yl * 2 + (1 - xl), (1 - yl) * 2 + xl, (1 - yl) * 2 + (1 - xl)
    to_x, to_y, to_d = {"xl": 1 - xl}, {"yl": 1 - yl}, {"yl": 1 - yl, "xl": 1 - xl}
    plane_peers = ((px, to_x), (py, to_y), (pd, to_d))
    to_core = {"c": 1 - c}
    flat_z = zh * NL + zl
    places = RING * NL * 2
    pos = flat_z * 2 + c

    def place(at):
        return {"zh": at // (2 * NL), "zl": (at // 2) % NL, "c": at % 2}

    count = itertools.count()

    def new(n=1):
        first = next(count)
        for _ in range(n - 1):
            next(count)
        assert first + n <= SEMS
        return first

    sent = []

    def push(src, dst, dev, rsem, pred=None):
        i = new()

        def make():
            return pltpu.make_async_remote_copy(
                src, dst, r.ss.at[i], r.rs.at[rsem], device_id=dev, device_id_type=MESH
            )

        if pred is None:
            make().start()
        else:
            pl.when(pred)(lambda: make().start())
        entry = (make, pred)
        sent.append(entry)
        return entry

    def settle(*entries):
        for entry in entries:
            make, pred = entry
            if pred is None:
                make().wait_send()
            else:
                pl.when(pred)(lambda make=make: make().wait_send())
            sent.remove(entry)

    def arrived(dst, rsem, pred=None):
        def wait():
            pltpu.make_async_remote_copy(
                dst, dst, r.ss.at[0], r.rs.at[rsem], device_id=to_core, device_id_type=MESH
            ).wait_recv()

        if pred is None:
            wait()
        else:
            pl.when(pred)(wait)

    def keep_local(src, dst, rsem):
        pltpu.make_async_copy(src, dst, r.rs.at[rsem]).start()

    new()

    def ds(start, size, unit):
        return pl.ds(pl.multiple_of(start, unit), size)

    class Gather:
        def __init__(self, buf):
            self.buf, half = buf, buf.shape[1] // 2
            self.h0, self.h1 = pl.ds(0, half), pl.ds(half, half)
            self.rx0, self.rx1, self.ry0, self.ry1, self.rd0, self.rd1 = (new() for _ in range(6))
            self.out = []

        def start(self):
            b = self.buf
            own0, own1 = b.at[p, self.h0], b.at[p, self.h1]
            self.out.append(push(own0, own0, to_x, self.rx0))
            self.out.append(push(own1, own1, to_y, self.ry1))
            self.out.append(push(own1, own1, to_x, self.rx1))
            self.out.append(push(own0, own0, to_y, self.ry0))

        def mid(self):
            b = self.buf
            got0, got1 = b.at[px, self.h0], b.at[py, self.h1]
            arrived(got0, self.rx0)
            self.out.append(push(got0, got0, to_y, self.rd0))
            arrived(got1, self.ry1)
            self.out.append(push(got1, got1, to_x, self.rd1))

        def wait_x(self):
            arrived(self.buf.at[px, self.h1], self.rx1)

        def wait_y(self):
            arrived(self.buf.at[py, self.h0], self.ry0)

        def wait_d(self):
            arrived(self.buf.at[pd, self.h0], self.rd0)
            arrived(self.buf.at[pd, self.h1], self.rd1)

        def end(self):
            self.wait_x()
            self.wait_y()
            self.wait_d()
            settle(*self.out)

    class Scatter:
        def __init__(self, buf, recv):
            self.buf, self.recv = buf, recv
            self.half = buf.shape[1] // 2
            self.h0, self.h1 = pl.ds(0, self.half), pl.ds(self.half, self.half)
            self.sems = [new() for _ in range(6)]
            self.out = []

        def start(self):
            b, v, s = self.buf, self.recv, self.sems
            self.out.append(push(b.at[pd, self.h0], v.at[0], to_x, s[0]))
            self.out.append(push(b.at[pd, self.h1], v.at[1], to_y, s[1]))
            self.out.append(push(b.at[px, self.h0], v.at[2], to_x, s[2]))
            self.out.append(push(b.at[py, self.h1], v.at[3], to_y, s[3]))

        def mid(self):
            b, v, s = self.buf, self.recv, self.sems
            arrived(v.at[0], s[0])
            step = 16

            def add0(o):
                b[py, pl.ds(o, step)] = (b[py, pl.ds(o, step)].astype(f32) + v[0, pl.ds(o, step)].astype(f32)).astype(bf16)

            loop(self.half, step, add0)
            self.out.append(push(b.at[py, self.h0], v.at[4], to_y, s[4]))
            arrived(v.at[1], s[1])

            def add1(o):
                q = pl.ds(pl.multiple_of(self.half + o, step), step)
                b[px, q] = (b[px, q].astype(f32) + v[1, pl.ds(o, step)].astype(f32)).astype(bf16)

            loop(self.half, step, add1)
            self.out.append(push(b.at[px, self.h1], v.at[5], to_x, s[5]))

        def end(self):
            for k in (2, 3, 4, 5):
                arrived(self.recv.at[k], self.sems[k])
            settle(*self.out)

        def total(self, half, o, step):
            b, v = self.buf, self.recv
            own = b[p, pl.ds(pl.multiple_of(half * self.half + o, step), step)].astype(f32)
            q = pl.ds(o, step)
            return own + v[2 + half, q].astype(f32) + v[4 + half, q].astype(f32)

        def each(self, step, body):
            for half in (0, 1):
                loop(self.half, step, lambda o: body(pl.multiple_of(half * self.half + o, step), self.total(half, o, step)))

    def z_send(src, block, rz):
        out = []
        for s in (1, 2):
            out.append(push(src, block(zh), {"zh": zh + s}, rz + zh, zh + s < RING))
            out.append(push(src, block(zh), {"zh": zh - s}, rz + zh, zh - s >= 0))
        return out

    def z_forward(block, rz):
        last = RING - 1
        arrived(block(0), rz, zh == last - 1)
        one = push(block(0), block(0), {"zh": zh + 1}, rz, zh == last - 1)
        arrived(block(last), rz + last, zh == 1)
        two = push(block(last), block(last), {"zh": zh - 1}, rz + last, zh == 1)
        return [one, two]

    def z_wait(block, rz):
        last = RING - 1
        arrived(block(0), rz, (zh == 1) | (zh == last))
        arrived(block(1), rz + 1, zh != 1)
        arrived(block(2), rz + 2, zh != 2)
        arrived(block(last), rz + last, (zh == 0) | (zh == last - 1))

    class ZSum:
        def __init__(self, block, slot, add):
            self.block, self.slot, self.add = block, slot, add
            self.sems = new(4)
            self.out = []

        def send(self):
            b, v, s = self.block, self.slot, self.sems
            last = RING - 1
            o = self.out
            o.append(push(b(last), v(1), {"zh": zh + 1}, s + 1, zh == 0))
            o.append(push(b(0), v(3), {"zh": zh - 1}, s + 3, zh == last))
            o.append(push(b(zh + 2), v(1), {"zh": zh + 2}, s + 1, zh == 0))
            o.append(push(b(zh - 2), v(3), {"zh": zh - 2}, s + 3, zh == last))
            o.append(push(b(zh + 1), v(0), {"zh": zh + 1}, s + 0, zh < last))
            o.append(push(b(zh - 1), v(2), {"zh": zh - 1}, s + 2, zh > 0))

        def forward(self):
            b, v, s = self.block, self.slot, self.sems
            last = RING - 1

            def up():
                arrived(v(1), s + 1)
                self.add(last, 1)

            def down():
                arrived(v(3), s + 3)
                self.add(0, 3)

            pl.when(zh == 1)(up)
            self.out.append(push(b(last), v(1), {"zh": zh + 2}, s + 1, zh == 1))
            pl.when(zh == last - 1)(down)
            self.out.append(push(b(0), v(3), {"zh": zh - 2}, s + 3, zh == last - 1))

        def end(self):
            v, s = self.slot, self.sems
            arrived(v(0), s, zh >= 1)
            arrived(v(1), s + 1, zh >= 2)
            arrived(v(2), s + 2, zh <= 2)
            arrived(v(3), s + 3, zh <= 1)
            settle(*self.out)

        def total(self, own, parts):
            for part, pred in zip(parts, (zh >= 1, zh >= 2, zh <= 2, zh <= 1), strict=True):
                own = own + jnp.where(pred, part.astype(f32), 0.0)
            return own

    class Columns:
        def __init__(self, sources, w, R, C):
            self.sources, self.w, self.R, self.C = sources, w, R, C
            self.ra, self.rz, self.rc = new(), new(4), new()
            self.out = []

        def spread(self):
            R, C = self.R, self.C
            for i, src in enumerate(self.sources):
                dst = self.w.at[zh, c, ds(p * R, R, 16), pl.ds(i * C, C)]
                for k, dev in plane_peers:
                    self.out.append(push(src.at[:, ds(k * C, C, 128)], dst, dev, self.ra))
                keep_local(src.at[:, ds(p * C, C, 128)], dst, self.ra)

        def block(self, z):
            return self.w.at[z, c]

        def z_send(self):
            arrived(self.w.at[zh, c], self.ra)
            self.out += z_send(self.block(zh), self.block, self.rz)

        def z_forward(self):
            self.out += z_forward(self.block, self.rz)

        def z_wait(self):
            z_wait(self.block, self.rz)
            half = self.w.at[:, c]
            self.out.append(push(half, half, to_core, self.rc))

        def end(self):
            arrived(self.w.at[:, 1 - c], self.rc)
            settle(*self.out)

    class Rows:
        def __init__(self, src, w, stage, R):
            self.src, self.w, self.stage, self.R = src, w, stage, R
            self.rl, self.rz, self.rp, self.rc = new(), new(4), new(), new()
            self.out = []

        def block(self, z):
            return self.stage.at[z]

        def z_send(self):
            keep_local(self.src, self.block(zh), self.rl)
            self.out += z_send(self.src, self.block, self.rz)

        def z_forward(self):
            self.out += z_forward(self.block, self.rz)

        def z_wait(self):
            R = self.R
            pltpu.make_async_copy(self.src, self.block(zh), r.rs.at[self.rl]).wait()
            z_wait(self.block, self.rz)
            dst = self.w.at[ds((c * PLANE + p) * R, R, 16)]
            for k, dev in plane_peers:
                self.out.append(push(self.stage.at[k], dst, dev, self.rp))
            keep_local(self.stage.at[p], dst, self.rp)

        def plane_wait(self):
            H = PLANE * self.R
            half = self.w.at[ds(c * H, H, 16)]
            arrived(half, self.rp)
            self.out.append(push(half, half, to_core, self.rc))

        def end(self):
            H = PLANE * self.R
            arrived(self.w.at[ds((1 - c) * H, H, 16)], self.rc)
            settle(*self.out)

    class ColumnsGrad:
        def __init__(self, g, other, slots, land, R, lane0, lanes, outs):
            self.g, self.other, self.slots, self.land = g, other, slots, land
            self.R, self.lanes, self.outs = R, pl.ds(lane0, lanes), outs
            self.rc, self.rl = new(), new()
            self.zsum = ZSum(
                lambda z: g.at[z, c, :, self.lanes], lambda k: slots.at[k, :, self.lanes], self.add_slot
            )

        def add_slot(self, z, k):
            g, q = self.g, self.lanes

            def add(o):
                s = pl.ds(o, 16)
                g[z, c, s, q] = (g[z, c, s, q].astype(f32) + self.slots[k, s, q].astype(f32)).astype(bf16)

            loop(PLANE * self.R, 16, add)

        def core_send(self):
            self.pushed = push(
                self.g.at[:, 1 - c, :, self.lanes], self.other.at[:, :, self.lanes], to_core, self.rc
            )

        def z_send(self):
            g, q = self.g, self.lanes
            arrived(self.other.at[:, :, q], self.rc)
            for z in range(RING):

                def add(o):
                    s = pl.ds(o, 16)
                    g[z, c, s, q] = (g[z, c, s, q].astype(f32) + self.other[z, s, q].astype(f32)).astype(bf16)

                loop(PLANE * self.R, 16, add)
            self.zsum.send()

        def z_forward(self):
            self.zsum.forward()

        def plane_send(self):
            g, q, R = self.g, self.lanes, self.R
            self.zsum.end()

            def add(o):
                s = pl.ds(o, 16)
                parts = [self.slots[k, s, q] for k in range(4)]
                g[zh, c, s, q] = self.zsum.total(g[zh, c, s, q].astype(f32), parts).astype(bf16)

            loop(PLANE * R, 16, add)
            dst = self.land.at[p, :, q]
            self.out = [self.pushed]
            for k, dev in plane_peers:
                self.out.append(push(g.at[zh, c, ds(k * R, R, 16), q], dst, dev, self.rl))
            keep_local(g.at[zh, c, ds(p * R, R, 16), q], dst, self.rl)

        def end(self):
            arrived(self.land.at[:, :, self.lanes], self.rl)
            settle(*self.out)
            for lane0, C, out in self.outs:
                for k in range(PLANE):
                    out[:, k * C : (k + 1) * C] = self.land[k, :, lane0 : lane0 + C].astype(f32)

    class RowsGrad:
        def __init__(self, g, other, stage, slots, R, out):
            self.g, self.other, self.stage, self.slots, self.R, self.result = g, other, stage, slots, R, out
            self.rc, self.rl = new(), new()
            self.zsum = ZSum(lambda z: stage.at[z], lambda k: slots.at[k], self.add_slot)

        def add_slot(self, z, k):
            g = self.stage

            def add(o):
                s = pl.ds(o, 16)
                g[z, s] = (g[z, s].astype(f32) + self.slots[k, s].astype(f32)).astype(bf16)

            loop(self.R, 16, add)

        def core_send(self):
            H = PLANE * self.R
            self.out = [push(self.g.at[ds((1 - c) * H, H, 16)], self.other, to_core, self.rc)]

        def plane_send(self):
            R, H, g = self.R, PLANE * self.R, self.g
            arrived(self.other, self.rc)

            def add(o):
                s = ds(c * H + o, 16, 16)
                g[s] = (g[s].astype(f32) + self.other[pl.ds(o, 16)].astype(f32)).astype(bf16)

            loop(H, 16, add)
            dst = self.stage.at[p]
            for k, dev in plane_peers:
                self.out.append(push(g.at[ds(c * H + k * R, R, 16)], dst, dev, self.rl))
            keep_local(g.at[ds(c * H + p * R, R, 16)], dst, self.rl)

        def z_send(self):
            arrived(self.stage, self.rl)
            self.zsum.send()

        def z_forward(self):
            self.zsum.forward()

        def end(self):
            self.zsum.end()
            settle(*self.out)

            def add(o):
                s = pl.ds(o, 16)
                self.result[s] = self.zsum.total(self.stage[zh, s].astype(f32), [self.slots[k, s] for k in range(4)])

            loop(self.R, 16, add)

    class Carry:
        def __init__(self, buf, later):
            self.buf, self.later = buf, later
            self.sems = new(places)
            self.out = []

        def send(self):
            own = self.buf.at[pos]
            order = range(places) if self.later else reversed(range(places))
            for at in order:
                pred = (pos < at) if self.later else (pos > at)
                self.out.append(push(own, own, place(at), self.sems + pos, pred))

        def fold(self, into):
            into[...] = jnp.zeros_like(into)
            order = range(places) if self.later else reversed(range(places))
            for at in order:
                pred = (pos > at) if self.later else (pos < at)

                def take(at=at):
                    arrived(self.buf.at[at], self.sems + at)
                    part = self.buf[at]
                    into[0:PLANE] = part[0:PLANE] * into[0:PLANE] + part[PLANE : 2 * PLANE]

                pl.when(pred)(take)
            settle(*self.out)

    barrier = pltpu.get_barrier_semaphore()
    for _, dev in plane_peers:
        pl.semaphore_signal(barrier, 1, device_id=dev, device_id_type=MESH)
    for at in range(places):

        @pl.when(pos != at)
        def _(at=at):
            pl.semaphore_signal(barrier, 1, device_id=place(at), device_id_type=MESH)

    pl.semaphore_wait(barrier, len(plane_peers) + places - 1)

    in_branch = Columns((r.input_weight, r.branch_weight), r.w_ib, RD, CW)
    dec_inj = Columns((r.decay_weight, r.inject_weight), r.w_di, RW, CW)
    gate_up = Columns((r.mlp_gate, r.mlp_up), r.w_gu, RD, CF)
    output = Rows(r.output_weight, r.w_o, r.st_o, RW)
    down = Rows(r.mlp_down, r.w_dn, r.st_dn, RF)
    ag_one, ag_conv, ag_two = Gather(r.n_one), Gather(r.conv), Gather(r.n_two)
    ag_cot, ag_out = Gather(r.cot_all), Gather(r.d_out)

    in_branch.spread()
    output.z_send()

    def norm_one(o):
        s = pl.ds(o, 16)
        v = r.tokens[s].astype(f32)
        r.n_one[p, s] = (v * inverse_rms(v) * r.gains[0:1]).astype(bf16)

    loop(T, 16, norm_one)
    ag_one.start()
    dec_inj.spread()
    gate_up.spread()
    r.cot_all[p] = r.cotangent[...]
    in_branch.z_send()
    ag_one.mid()
    ag_cot.start()
    dec_inj.z_send()
    gate_up.z_send()
    down.z_send()
    output.z_forward()
    in_branch.z_forward()
    in_branch.z_wait()
    ag_one.end()
    in_branch.end()

    n_one = r.n_one[...].reshape(M, D)
    r.pair[:, 0 : 2 * CW] = dot(n_one, r.w_ib[...].reshape(D, 2 * CW))
    for k in range(PLANE):
        r.u[k, 8 : 8 + T] = r.pair[k * T : (k + 1) * T, 0:CW].astype(bf16).astype(f32)
    halo_f = new()
    after, before = flat_z + c, flat_z - (1 - c)
    to_next = {"zh": after // NL, "zl": after % NL, "c": 1 - c}
    to_prev = {"zh": before // NL, "zl": before % NL, "c": 1 - c}
    sent_f = push(r.u.at[:, pl.ds(T, 8)], r.u.at[:, pl.ds(0, 8)], to_next, halo_f, pos < places - 1)

    def gates_one(o):
        s = pl.ds(o, 16)
        r.gated[s], r.slope[s] = gelu_parts(r.pair[s, CW : 2 * CW])

    loop(M, 16, gates_one)

    @pl.when(pos == 0)
    def _():
        r.u[:, 0:8] = jnp.zeros((PLANE, 8, CW), f32)

    arrived(r.u.at[:, pl.ds(0, 8)], halo_f, pos > 0)
    settle(sent_f)

    for k in range(PLANE):

        def convolve(o, k=k):
            ext = r.u[k, pl.ds(o, 24)]
            rows = ds(k * T + o, 16, 16)
            keep = r.masks[rows]
            total = r.chan[4:5] + r.chan[0:1] * ext[8:24]
            for j in range(1, 4):
                total = total + jnp.where(keep[:, j : j + 1] > 0.5, r.chan[j : j + 1] * ext[8 - j : 24 - j], 0.0)
            r.conv[p, rows] = total.astype(bf16)

        loop(T, 16, convolve)
    ag_conv.start()
    ag_cot.mid()
    dec_inj.z_forward()
    ag_conv.mid()
    output.z_wait()
    dec_inj.z_wait()
    output.plane_wait()
    dec_inj.end()

    def pre(q):
        return dot(r.conv[q], r.w_di[q].reshape(W // RING, 2 * CW))

    r.pair[:, 0 : 2 * CW] = pre(p)
    for q, wait in ((px, ag_conv.wait_x), (py, ag_conv.wait_y), (pd, ag_conv.wait_d)):
        wait()
        r.pair[:, 0 : 2 * CW] += pre(q)
    settle(*ag_conv.out)

    def decay_terms(s, rg):
        log_a = -rate_scale * rg * r.chan[7:8]
        gap = minus_expm1(2.0 * log_a)
        first = r.masks[s][:, 0:1] > 0.5
        return log_a, gap, jnp.where(first, 1.0, jnp.sqrt(jnp.maximum(gap, floor_gap))), first

    def gates_two(o):
        s = pl.ds(o, 16)
        rg = jax.nn.sigmoid(r.pair[s, 0:CW] + r.chan[5:6])
        ig = jax.nn.sigmoid(r.pair[s, CW : 2 * CW] + r.chan[6:7])
        log_a, _, mult, first = decay_terms(s, rg)
        r.rgate[s], r.igate[s] = rg, ig
        r.decay[s] = jnp.where(first, 0.0, jnp.exp(log_a))
        r.work[s] = mult * ig * r.conv[p, s].astype(f32)

    loop(M, 16, gates_two)
    row = lax.broadcasted_iota(jnp.int32, (8, CW), 0)

    def scan_forward(j, carry):
        out = []
        for k in range(PLANE):
            s = ds(k * T + j * 8, 8, 8)
            a, b = r.decay[s], r.work[s]
            for n in (1, 2, 4):
                a_b = jnp.where(row >= n, pltpu.roll(a, n, 0), 1.0)
                b_b = jnp.where(row >= n, pltpu.roll(b, n, 0), 0.0)
                a, b = a * a_b, a * b_b + b
            total, prod = b + a * carry[2 * k], a * carry[2 * k + 1]
            r.state[k, ds(8 + j * 8, 8, 8)] = total
            r.cum[s] = prod
            out += [total[7:8], prod[7:8]]
        return tuple(out)

    zero, one = jnp.zeros((1, CW), f32), jnp.ones((1, CW), f32)
    ends = lax.fori_loop(0, T // 8, scan_forward, (zero, one) * PLANE)
    carry_f = Carry(r.carry_f, True)
    for k in range(PLANE):
        r.carry_f[pos, k : k + 1] = ends[2 * k + 1]
        r.carry_f[pos, PLANE + k : PLANE + k + 1] = ends[2 * k]
        r.ends[k : k + 1] = ends[2 * k + 1]
    carry_f.send()
    output.end()
    carry_f.fold(r.into)

    for k in range(PLANE):
        into = r.into[k : k + 1]
        r.state[k, 0:8] = jnp.broadcast_to(into, (8, CW))

        def mix(o, k=k, into=into):
            s, t = ds(k * T + o, 16, 16), ds(8 + o, 16, 8)
            state = r.state[k, t] + r.cum[s] * into
            r.state[k, t] = state
            r.mixed[s] = (state * r.gated[s]).astype(bf16)

        loop(T, 16, mix)

    step = 256

    def out_part(o):
        q = pl.ds(o, step)
        r.part[:, :, q] = dot(r.mixed[...], r.w_o[:, q]).astype(bf16).reshape(PLANE, T, step)

    loop(D, step, out_part)
    rs_one = Scatter(r.part, r.got_one)
    rs_one.start()
    ag_cot.end()
    gate_up.z_forward()
    rs_one.mid()
    rs_one.end()

    def norm_two(o, summed):
        s = pl.ds(o, 16)
        v = r.tokens[s].astype(f32) + summed
        r.x_one[s] = v
        r.n_two[p, s] = (v * inverse_rms(v) * r.gains[1:2]).astype(bf16)

    rs_one.each(16, norm_two)
    ag_two.start()
    gate_up.z_wait()
    down.z_forward()
    ag_two.mid()
    gate_up.end()
    ag_two.end()

    def mlp_in(o):
        q = pl.ds(o, step)
        r.pair[:, q] = dot(r.n_two[...].reshape(M, D), r.w_gu[:, :, :, q].reshape(D, step))

    loop(2 * CF, step, mlp_in)
    down.z_wait()

    def gates_mlp(o):
        s = pl.ds(o, 16)
        value, slope = gelu_parts(r.pair[s, 0:CF])
        up = r.pair[s, CF : 2 * CF]
        r.hidden[s] = (value * up).astype(bf16)
        r.pair[s, 0:CF] = slope * up
        r.pair[s, CF : 2 * CF] = value

    loop(M, 16, gates_mlp)
    down.plane_wait()
    down.end()

    for k in range(CF // step):
        q = pl.ds(k * step, step)
        back = dot_nt(r.cot_all[...].reshape(M, D), r.w_dn[q])
        r.d_pair[:, k * step : (k + 1) * step] = (back * r.pair[:, k * step : (k + 1) * step]).astype(bf16)
        r.d_pair[:, CF + k * step : CF + (k + 1) * step] = (
            back * r.pair[:, CF + k * step : CF + (k + 1) * step]
        ).astype(bf16)
    chunk = PLANE * RD * 2

    def d_two_part(z, _):
        q = ds(z * chunk, chunk, chunk)
        r.part[:, :, q] = (
            dot_nt(r.d_pair[...], r.w_gu[z].reshape(chunk, 2 * CF)).astype(bf16).reshape(PLANE, T, chunk)
        )
        return 0

    lax.fori_loop(0, RING, d_two_part, 0)
    rs_two = Scatter(r.part, r.got_two)
    rs_two.start()

    def act_part(o):
        q = pl.ds(o, step)
        r.part_act[:, :, q] = dot(r.hidden[...], r.w_dn[:, q]).astype(bf16).reshape(PLANE, T, step)

    loop(D, step, act_part)
    rs_act = Scatter(r.part_act, r.got_act)
    rs_act.start()

    def grad_down(o):
        q = pl.ds(o, step)
        r.w_dn[q] = dot_tn(r.hidden[:, q], r.cot_all[...].reshape(M, D)).astype(bf16)

    loop(CF, step, grad_down)
    g_down = RowsGrad(r.w_dn, r.h_dn, r.sg_dn, r.z_dn, RF, r.grad_mlp_down)
    g_down.core_send()
    rs_two.mid()
    g_down.plane_send()

    def grad_gate_up(z, _):
        q = ds(z * chunk, chunk, chunk)
        value = dot_tn(r.n_two[:, :, q].reshape(M, chunk), r.d_pair[...])
        r.w_gu[z] = value.astype(bf16).reshape(2, chunk // 2, 2 * CF)
        return 0

    lax.fori_loop(0, RING, grad_gate_up, 0)
    g_gu = ColumnsGrad(
        r.w_gu, r.h_gu, r.z_gu, r.l_gu, RD, 0, 2 * CF, ((0, CF, r.grad_mlp_gate), (CF, CF, r.grad_mlp_up))
    )
    g_gu.core_send()
    rs_two.end()
    r.ggain[...] = jnp.zeros_like(r.ggain)
    r.gchan[...] = jnp.zeros_like(r.gchan)

    def norm_two_back(o, d_two):
        s = pl.ds(o, 16)
        v = r.x_one[s]
        rs = inverse_rms(v)
        z = v * rs
        dz = d_two * r.gains[1:2]
        r.ggain[1:2] += jnp.sum(d_two * z, axis=0, keepdims=True)
        d_one = r.cotangent[s].astype(f32) + rs * (dz - z * jnp.mean(dz * z, axis=-1, keepdims=True))
        r.d_one[s] = d_one
        r.d_out[p, s] = d_one.astype(bf16)

    rs_two.each(16, norm_two_back)
    ag_out.start()
    g_down.z_send()
    rs_act.mid()
    g_gu.z_send()
    ag_out.mid()
    g_down.z_forward()
    rs_act.end()

    def finish_act(o, summed):
        s = pl.ds(o, 16)
        r.activations[s] = (r.x_one[s] + summed).astype(bf16)

    rs_act.each(16, finish_act)
    ag_out.end()

    r.work[...] = dot_nt(r.d_out[...].reshape(M, D), r.w_o[...])
    for k in range(PLANE):

        def split(o, k=k):
            s = ds(k * T + o, 16, 16)
            d_mixed = r.work[s]
            r.d_gu[s, CW : 2 * CW] = (d_mixed * r.state[k, ds(8 + o, 16, 8)] * r.slope[s]).astype(bf16)
            r.work[s] = d_mixed * r.gated[s]

        loop(T, 16, split)

    def scan_backward(i, carry):
        j = T // 8 - 1 - i
        out = []
        for k in range(PLANE):
            s = ds(k * T + j * 8, 8, 8)
            decay, b = r.decay[s], r.work[s]
            a = jnp.where(row < 7, pltpu.roll(decay, 7, 0), carry[3 * k + 2])
            for n in (1, 2, 4):
                a_b = jnp.where(row < 8 - n, pltpu.roll(a, 8 - n, 0), 1.0)
                b_b = jnp.where(row < 8 - n, pltpu.roll(b, 8 - n, 0), 0.0)
                a, b = a * a_b, a * b_b + b
            total, prod = b + a * carry[3 * k], a * carry[3 * k + 1]
            r.work[s], r.cum[s] = total, prod
            out += [total[0:1], prod[0:1], decay[0:1]]
        return tuple(out)

    heads = lax.fori_loop(0, T // 8, scan_backward, (zero, one, one) * PLANE)
    carry_b = Carry(r.carry_b, False)
    for k in range(PLANE):
        r.carry_b[pos, k : k + 1] = r.ends[k : k + 1]
        r.carry_b[pos, PLANE + k : PLANE + k + 1] = heads[3 * k] * heads[3 * k + 2]
    carry_b.send()

    def grad_out(o):
        q = pl.ds(o, 128)
        r.w_o[q] = dot_tn(r.mixed[:, q], r.d_out[...].reshape(M, D)).astype(bf16)

    loop(CW, 128, grad_out)
    g_out = RowsGrad(r.w_o, r.h_o, r.sg_o, r.z_o, RW, r.grad_output_weight)
    g_out.core_send()
    carry_b.fold(r.into)

    for k in range(PLANE):
        into = r.into[k : k + 1]

        def back(o, k=k, into=into):
            s = ds(k * T + o, 16, 16)
            adjoint = r.work[s] + r.cum[s] * into
            previous = r.state[k, pl.ds(o, 24)][7:23]
            rg, ig, decay, conv = r.rgate[s], r.igate[s], r.decay[s], r.conv[p, s].astype(f32)
            _, gap, mult, first = decay_terms(s, rg)
            d_mult = jnp.where(first, 0.0, adjoint * ig * conv)
            d_log = adjoint * previous * decay - jnp.where(
                gap > floor_gap, (1.0 - gap) * d_mult / mult, 0.0
            )
            d_decay = (-rate_scale * r.chan[7:8] * d_log * rg * (1.0 - rg)).astype(bf16)
            d_inject = (adjoint * mult * conv * ig * (1.0 - ig)).astype(bf16)
            r.d_pre[s, 0:CW] = d_decay
            r.d_pre[s, CW : 2 * CW] = d_inject
            r.gchan[5:6] += jnp.sum(d_decay.astype(f32), axis=0, keepdims=True)
            r.gchan[6:7] += jnp.sum(d_inject.astype(f32), axis=0, keepdims=True)
            r.d_conv[k, pl.ds(o, 16)] = adjoint * mult * ig

        loop(T, 16, back)

    def conv_part(q, _):
        r.part_conv[q] = dot_nt(r.d_pre[...], r.w_di[q].reshape(W // RING, 2 * CW)).astype(bf16)
        return 0

    lax.fori_loop(0, RING, conv_part, 0)
    rs_conv = Scatter(r.part_conv, r.got_conv)
    rs_conv.start()
    g_gu.z_forward()
    g_out.plane_send()

    def grad_dec_inj(q, _):
        value = dot_tn(r.conv[q], r.d_pre[...])
        r.w_di[q] = value.astype(bf16).reshape(2, W // SHARES * PLANE, 2 * CW)
        return 0

    lax.fori_loop(0, RING, grad_dec_inj, 0)
    g_di = ColumnsGrad(
        r.w_di, r.h_di, r.z_di, r.l_di, RW, 0, 2 * CW, ((0, CW, r.grad_decay_weight), (CW, CW, r.grad_inject_weight))
    )
    g_di.core_send()
    rs_conv.mid()

    def d_branch_part(z, _):
        q = ds(z * chunk, chunk, chunk)
        r.part[:, :, q] = (
            dot_nt(r.d_gu[:, CW : 2 * CW], r.w_ib[z, :, :, CW : 2 * CW].reshape(chunk, CW))
            .astype(bf16)
            .reshape(PLANE, T, chunk)
        )
        value = dot_tn(r.n_one[:, :, q].reshape(M, chunk), r.d_gu[:, CW : 2 * CW])
        r.w_ib[z, :, :, CW : 2 * CW] = value.astype(bf16).reshape(2, chunk // 2, CW)
        return 0

    lax.fori_loop(0, RING, d_branch_part, 0)
    g_branch = ColumnsGrad(r.w_ib, r.h_ib, r.z_ib, r.l_ib, RD, CW, CW, ((CW, CW, r.grad_branch_weight),))
    g_branch.core_send()
    g_out.z_send()
    g_di.z_send()
    g_branch.z_send()
    rs_conv.end()

    for half in (0, 1):
        rows = M // 2

        def add_conv(o, half=half):
            for k in (2 * half, 2 * half + 1):
                at = (k - 2 * half) * T + o
                r.d_conv[k, pl.ds(o, 16)] += rs_conv.total(half, pl.multiple_of(at, 16), 16)

        loop(T, 16, add_conv)
    halo_b = new()
    sent_b = push(r.d_conv.at[:, pl.ds(0, 8)], r.d_conv.at[:, pl.ds(T, 8)], to_prev, halo_b, pos > 0)
    for k in range(PLANE):

        def taps_back(o, k=k):
            ext = r.u[k, pl.ds(o, 24)]
            keep = r.masks[ds(k * T + o, 16, 16)]
            dc = r.d_conv[k, pl.ds(o, 16)]
            r.gchan[4:5] += jnp.sum(dc, axis=0, keepdims=True)
            r.gchan[0:1] += jnp.sum(dc * ext[8:24], axis=0, keepdims=True)
            for j in range(1, 4):
                term = jnp.where(keep[:, j : j + 1] > 0.5, dc * ext[8 - j : 24 - j], 0.0)
                r.gchan[j : j + 1] += jnp.sum(term, axis=0, keepdims=True)

        loop(T, 16, taps_back)

    @pl.when(pos == places - 1)
    def _():
        r.d_conv[:, T : T + 8] = jnp.zeros((PLANE, 8, CW), f32)

    arrived(r.d_conv.at[:, pl.ds(T, 8)], halo_b, pos < places - 1)
    settle(sent_b)
    for k in range(PLANE):

        def conv_back(o, k=k):
            ext = r.d_conv[k, pl.ds(o, 24)]
            rows = ds(k * T + o, 16, 16)
            keep = r.masks[rows]
            total = r.chan[0:1] * ext[0:16]
            for j in range(1, 4):
                total = total + jnp.where(keep[:, 3 + j : 4 + j] > 0.5, r.chan[j : j + 1] * ext[j : 16 + j], 0.0)
            r.d_gu[rows, 0:CW] = total.astype(bf16)

        loop(T, 16, conv_back)

    def d_input_part(z, _):
        q = ds(z * chunk, chunk, chunk)
        value = dot_nt(r.d_gu[:, 0:CW], r.w_ib[z, :, :, 0:CW].reshape(chunk, CW)).reshape(PLANE, T, chunk)
        r.part[:, :, q] = (r.part[:, :, q].astype(f32) + value).astype(bf16)
        return 0

    lax.fori_loop(0, RING, d_input_part, 0)
    rs_three = Scatter(r.part, r.got_three)
    rs_three.start()

    def grad_input(z, _):
        q = ds(z * chunk, chunk, chunk)
        value = dot_tn(r.n_one[:, :, q].reshape(M, chunk), r.d_gu[:, 0:CW])
        r.w_ib[z, :, :, 0:CW] = value.astype(bf16).reshape(2, chunk // 2, CW)
        return 0

    lax.fori_loop(0, RING, grad_input, 0)
    g_input = ColumnsGrad(r.w_ib, r.h_ib, r.z_ib, r.l_ib, RD, 0, CW, ((0, CW, r.grad_input_weight),))
    g_input.core_send()
    rs_three.mid()
    g_input.z_send()
    g_down.end()
    g_out.z_forward()
    g_di.z_forward()
    g_branch.z_forward()
    g_gu.plane_send()
    g_input.z_forward()
    rs_three.end()

    def norm_one_back(o, d_n):
        s = pl.ds(o, 16)
        v = r.tokens[s].astype(f32)
        rs = inverse_rms(v)
        z = v * rs
        dz = d_n * r.gains[0:1]
        r.ggain[0:1] += jnp.sum(d_n * z, axis=0, keepdims=True)
        r.d_tokens[s] = r.d_one[s] + rs * (dz - z * jnp.mean(dz * z, axis=-1, keepdims=True))

    rs_three.each(16, norm_one_back)
    g_out.end()
    g_di.plane_send()
    g_branch.plane_send()
    g_gu.end()
    g_input.plane_send()
    g_di.end()
    g_branch.end()
    g_input.end()
    assert not sent


WEIGHTS = (
    "branch_weight",
    "input_weight",
    "decay_weight",
    "inject_weight",
    "output_weight",
    "mlp_gate",
    "mlp_up",
    "mlp_down",
)


def run_layer(NL, tokens, cotangent, gains, chan, masks, weights):
    T, D = tokens.shape
    W, F = weights["branch_weight"].shape[1], weights["mlp_gate"].shape[1]
    CW, CF = W // PLANE, F // PLANE
    RD, RW, RF = D // SHARES, W // SHARES, F // SHARES
    M, places = PLANE * T, RING * NL * 2
    vmem, hbm = pl.BlockSpec(memory_space=pltpu.VMEM), pl.BlockSpec(memory_space=pl.ANY)
    ins = ["tokens", "cotangent", "gains", "chan", "masks", *WEIGHTS]
    outs = {
        "activations": ((T, D), bf16),
        "d_tokens": ((T, D), f32),
        **{"grad_" + name: (weights[name].shape, f32) for name in WEIGHTS},
        "ggain": ((8, D), f32),
        "gchan": ((8, CW), f32),
    }
    outs = {name if name[:5] != "grad_" else name: spec for name, spec in outs.items()}
    scratch = {
        "w_ib": ((RING, 2, PLANE * RD, 2 * CW), bf16),
        "w_di": ((RING, 2, PLANE * RW, 2 * CW), bf16),
        "w_gu": ((RING, 2, PLANE * RD, 2 * CF), bf16),
        "w_o": ((CW, D), bf16),
        "w_dn": ((CF, D), bf16),
        "st_o": ((RING, RW, D), bf16),
        "st_dn": ((RING, RF, D), bf16),
        "h_ib": ((RING, PLANE * RD, 2 * CW), bf16),
        "h_di": ((RING, PLANE * RW, 2 * CW), bf16),
        "h_gu": ((RING, PLANE * RD, 2 * CF), bf16),
        "h_o": ((CW // 2, D), bf16),
        "h_dn": ((CF // 2, D), bf16),
        "z_ib": ((4, PLANE * RD, 2 * CW), bf16),
        "z_di": ((4, PLANE * RW, 2 * CW), bf16),
        "z_gu": ((4, PLANE * RD, 2 * CF), bf16),
        "z_o": ((4, RW, D), bf16),
        "z_dn": ((4, RF, D), bf16),
        "l_ib": ((PLANE, RD, 2 * CW), bf16),
        "l_di": ((PLANE, RW, 2 * CW), bf16),
        "l_gu": ((PLANE, RD, 2 * CF), bf16),
        "sg_o": ((RING, RW, D), bf16),
        "sg_dn": ((RING, RF, D), bf16),
        "n_one": ((PLANE, T, D), bf16),
        "n_two": ((PLANE, T, D), bf16),
        "cot_all": ((PLANE, T, D), bf16),
        "d_out": ((PLANE, T, D), bf16),
        "conv": ((PLANE, M, CW), bf16),
        "part": ((PLANE, T, D), bf16),
        "part_act": ((PLANE, T, D), bf16),
        "part_conv": ((PLANE, M, CW), bf16),
        "got_one": ((6, T // 2, D), bf16),
        "got_two": ((6, T // 2, D), bf16),
        "got_three": ((6, T // 2, D), bf16),
        "got_act": ((6, T // 2, D), bf16),
        "got_conv": ((6, M // 2, CW), bf16),
        "mixed": ((M, CW), bf16),
        "hidden": ((M, CF), bf16),
        "d_pair": ((M, 2 * CF), bf16),
        "d_gu": ((M, 2 * CW), bf16),
        "d_pre": ((M, 2 * CW), bf16),
        "pair": ((M, 2 * CF), f32),
        "u": ((PLANE, T + 8, CW), f32),
        "state": ((PLANE, T + 8, CW), f32),
        "d_conv": ((PLANE, T + 8, CW), f32),
        **{name: ((M, CW), f32) for name in ("gated", "slope", "rgate", "igate", "decay", "work", "cum")},
        "x_one": ((T, D), f32),
        "d_one": ((T, D), f32),
        "carry_f": ((places, 2 * PLANE, CW), f32),
        "carry_b": ((places, 2 * PLANE, CW), f32),
        "into": ((8, CW), f32),
        "ends": ((8, CW), f32),
    }
    dims = SimpleNamespace(
        T=T, D=D, W=W, F=F, CW=CW, CF=CF, RD=RD, RW=RW, RF=RF, NL=NL, names=[*ins, *outs, *scratch, "ss", "rs"]
    )
    flops = 3 * 2 * M * (D * 2 * CW + W * 2 * CW + CW * D + 3 * D * CF)
    results = pl.pallas_call(
        partial(layer, dims),
        out_shape=[jax.ShapeDtypeStruct(shape, kind) for shape, kind in outs.values()],
        in_specs=[vmem] * 5 + [hbm] * len(WEIGHTS),
        out_specs=[vmem] * len(outs),
        scratch_shapes=[pltpu.VMEM(shape, kind) for shape, kind in scratch.values()]
        + [pltpu.SemaphoreType.DMA((SEMS,)), pltpu.SemaphoreType.DMA((SEMS,))],
        compiler_params=pltpu.CompilerParams(
            collective_id=0, has_side_effects=True, vmem_limit_bytes=62 * 2**20
        ),
        cost_estimate=pl.CostEstimate(flops=flops, bytes_accessed=8 * 2**20, transcendentals=M * CW * 16),
        name="griffin_layer",
    )(tokens, cotangent, gains, chan, masks, *[weights[name] for name in WEIGHTS])
    return dict(zip(outs, results, strict=True))


def local(
    sizes,
    tokens,
    cotangent,
    doc_lengths,
    decay_exponent,
    branch_weight,
    input_weight,
    decay_weight,
    inject_weight,
    output_weight,
    mlp_gate,
    mlp_up,
    mlp_down,
    first_gain,
    second_gain,
    conv_taps,
    conv_bias,
    decay_bias,
    inject_bias,
):
    devices = math.prod(sizes.values())
    width = branch_weight.shape[1]
    own_d, own_w = first_gain.shape[0], conv_bias.shape[0]
    NL = sizes["zl"]
    at = {name: lax.axis_index(name) for name in AXES}
    T = tokens.shape[1]

    small = jnp.concatenate(
        [
            jnp.stack([first_gain, second_gain]).reshape(-1),
            jnp.concatenate([conv_taps.T, jnp.stack([conv_bias, decay_bias, inject_bias])]).reshape(-1),
        ]
    ).astype(f32)
    small = jnp.concatenate([small, doc_lengths[0].astype(f32)])
    small = lax.all_gather(small, AXES)
    gains = small[:, : 2 * own_d].reshape(devices, 2, own_d).transpose(1, 0, 2).reshape(2, -1)
    chan = small[:, 2 * own_d : 2 * own_d + 7 * own_w].reshape(devices, 7, own_w).transpose(1, 0, 2).reshape(7, -1)
    scale = jnp.exp2(-decay_exponent.astype(f32))
    chan = jnp.concatenate([chan, scale[None]])
    mine = at["yl"] * 2 + at["xl"]
    chan = lax.dynamic_slice_in_dim(chan, mine * (width // PLANE), width // PLANE, 1)
    lengths = small[:, 2 * own_d + 7 * own_w :].astype(jnp.int32)
    across = sizes["xh"] * 2
    rows = (at["yh"] * 2 + jnp.arange(PLANE) // 2) * across + at["xh"] * 2 + jnp.arange(PLANE) % 2
    lengths = lengths[rows]

    ends = jnp.cumsum(lengths, axis=1)
    starts = ends - lengths
    index = (at["zh"] * NL + at["zl"]) * 2 + at["c"]
    count = T * RING * NL * 2
    where = index * T - 3 + jnp.arange(T + 6, dtype=jnp.int32)
    seg = jnp.sum((ends[:, None, :] <= where[None, :, None]).astype(jnp.int32), axis=2)
    seg = jnp.where((where < 0) | (where >= count), -1, seg)
    here = seg[:, 3 : 3 + T]
    first = jnp.any(starts[:, None, :] == where[None, 3 : 3 + T, None], axis=2)
    masks = [first]
    masks += [seg[:, 3 - k : 3 - k + T] == here for k in (1, 2, 3)]
    masks += [seg[:, 3 + k : 3 + k + T] == here for k in (1, 2, 3)]
    masks += [first]
    masks = jnp.stack(masks, axis=-1).astype(f32).reshape(PLANE * T, 8)

    weights = dict(
        zip(
            WEIGHTS,
            (branch_weight, input_weight, decay_weight, inject_weight, output_weight, mlp_gate, mlp_up, mlp_down),
            strict=True,
        )
    )
    groups = devices // SHARES
    if groups > 1:
        share = (at["zh"] * 2 + at["c"]) * PLANE + mine
        for name, value in weights.items():
            whole = lax.all_gather(value, AXES, axis=0, tiled=True)
            weights[name] = lax.dynamic_slice_in_dim(whole, share * (whole.shape[0] // SHARES), whole.shape[0] // SHARES)
    pad = jnp.zeros((6, gains.shape[1]), f32)
    got = run_layer(NL, tokens[0], cotangent[0], jnp.concatenate([gains, pad]), chan, masks, weights)
    grads = {name: got["grad_" + name] for name in WEIGHTS}
    if groups > 1:
        for name, value in grads.items():
            whole = jnp.zeros((value.shape[0] * SHARES, value.shape[1]), bf16)
            whole = lax.dynamic_update_slice_in_dim(whole, value.astype(bf16), share * value.shape[0], 0)
            grads[name] = lax.psum_scatter(whole, AXES, scatter_dimension=0, tiled=True).astype(f32)

    gain_grads = got["ggain"][:2].reshape(2, devices, own_d).transpose(1, 0, 2).reshape(devices, -1)
    chan_grads = jnp.zeros((7, width), f32)
    chan_grads = lax.dynamic_update_slice_in_dim(chan_grads, got["gchan"][:7], mine * (width // PLANE), 1)
    chan_grads = chan_grads.reshape(7, devices, own_w).transpose(1, 0, 2).reshape(devices, -1)
    sums = lax.psum_scatter(jnp.concatenate([gain_grads, chan_grads], 1), AXES, scatter_dimension=0, tiled=True)[0]
    gain_sum = sums[: 2 * own_d].reshape(2, own_d)
    chan_sum = sums[2 * own_d :].reshape(7, own_w)
    return (
        got["activations"][None],
        got["d_tokens"][None],
        *[grads[name] for name in WEIGHTS],
        gain_sum[0],
        gain_sum[1],
        chan_sum[:4].T,
        chan_sum[4],
        chan_sum[5],
        chan_sum[6],
    )


def solution(mesh):
    seq, dp = mesh.shape["seq"], mesh.shape["dp"]
    across = 1 << ((dp.bit_length() - 1) // 2)
    sizes = dict(zip(AXES, (RING, seq // (2 * RING), 2, dp // across // 2, 2, across // 2, 2), strict=True))
    split = Mesh(mesh.devices.reshape(tuple(sizes.values())), AXES)
    along_seq, along_dp = AXES[:3], AXES[3:]
    rows = P(along_dp, along_seq, None)
    in_specs = (rows, rows, P(along_dp, None), P(), *[P(AXES, None)] * 8, P(AXES), P(AXES), P(AXES, None), *[P(AXES)] * 3)
    out_specs = (rows, rows, *[P(AXES, None)] * 8, P(AXES), P(AXES), P(AXES, None), *[P(AXES)] * 3)
    return jax.shard_map(partial(local, sizes), mesh=split, in_specs=in_specs, out_specs=out_specs, check_vma=False)
```

```python
import itertools
import math
from functools import partial
from types import SimpleNamespace

import jax
import jax.numpy as jnp
from jax import lax
from jax.experimental import pallas as pl
from jax.experimental.pallas import tpu as pltpu
from jax.sharding import Mesh, PartitionSpec as P

f32, bf16 = jnp.float32, jnp.bfloat16
MESH = pl.DeviceIdType.MESH
AXES = ("zh", "zl", "c", "yh", "yl", "xh", "xl")
RING = 4
PLANE = 4
SHARES = RING * 2 * PLANE
SEMS = 640

eps_norm = 1e-06
floor_gap = 1e-05
rate_scale = 8.0
gelu_root = math.sqrt(2.0 / math.pi)
gelu_cube = 0.044715


def dot(left, right):
    return jnp.dot(left, right, preferred_element_type=f32)


def dot_nt(left, right):
    return lax.dot_general(left, right, (((1,), (1,)), ((), ())), preferred_element_type=f32)


def dot_tn(left, right):
    return lax.dot_general(left, right, (((0,), (0,)), ((), ())), preferred_element_type=f32)


def gelu_parts(v):
    t = jnp.tanh(gelu_root * (v + gelu_cube * v * v * v))
    half = 0.5 * (1.0 + t)
    slope = half + 0.5 * v * (1.0 - t * t) * gelu_root * (1.0 + 3.0 * gelu_cube * v * v)
    return v * half, slope


def minus_expm1(y):
    poly = jnp.full_like(y, 1.0 / 8.0)
    poly = 1.0 + y * poly
    for k in (7, 6, 5, 4, 3, 2):
        poly = 1.0 + y * poly * (1.0 / k)
    return jnp.where(y > -0.35, -y * poly, 1.0 - jnp.exp(y))


def inverse_rms(v):
    return lax.rsqrt(jnp.mean(v * v, axis=-1, keepdims=True) + eps_norm)


def loop(total, step, body):
    def run(j, _):
        body(pl.multiple_of(j * step, step))
        return 0

    lax.fori_loop(0, total // step, run, 0)


def layer(dims, *refs):
    T, D, W, F, CW, CF = dims.T, dims.D, dims.W, dims.F, dims.CW, dims.CF
    RD, RW, RF, NL = dims.RD, dims.RW, dims.RF, dims.NL
    M = PLANE * T
    r = SimpleNamespace(**dict(zip(dims.names, refs, strict=True)))

    zh, zl, c = lax.axis_index("zh"), lax.axis_index("zl"), lax.axis_index("c")
    yl, xl = lax.axis_index("yl"), lax.axis_index("xl")
    p = yl * 2 + xl
    px, py, pd = yl * 2 + (1 - xl), (1 - yl) * 2 + xl, (1 - yl) * 2 + (1 - xl)
    to_x, to_y, to_d = {"xl": 1 - xl}, {"yl": 1 - yl}, {"yl": 1 - yl, "xl": 1 - xl}
    plane_peers = ((px, to_x), (py, to_y), (pd, to_d))
    to_core = {"c": 1 - c}
    flat_z = zh * NL + zl
    places = RING * NL * 2
    pos = flat_z * 2 + c

    def place(at):
        return {"zh": at // (2 * NL), "zl": (at // 2) % NL, "c": at % 2}

    count = itertools.count()

    def new(n=1):
        first = next(count)
        for _ in range(n - 1):
            next(count)
        assert first + n <= SEMS
        return first

    sent = []

    def push(src, dst, dev, rsem, pred=None):
        i = new()

        def make():
            return pltpu.make_async_remote_copy(
                src, dst, r.ss.at[i], r.rs.at[rsem], device_id=dev, device_id_type=MESH
            )

        if pred is None:
            make().start()
        else:
            pl.when(pred)(lambda: make().start())
        entry = (make, pred)
        sent.append(entry)
        return entry

    def settle(*entries):
        for entry in entries:
            make, pred = entry
            if pred is None:
                make().wait_send()
            else:
                pl.when(pred)(lambda make=make: make().wait_send())
            sent.remove(entry)

    def arrived(dst, rsem, pred=None):
        def wait():
            pltpu.make_async_remote_copy(
                dst, dst, r.ss.at[0], r.rs.at[rsem], device_id=to_core, device_id_type=MESH
            ).wait_recv()

        if pred is None:
            wait()
        else:
            pl.when(pred)(wait)

    def keep_local(src, dst, rsem):
        pltpu.make_async_copy(src, dst, r.rs.at[rsem]).start()

    new()

    def ds(start, size, unit):
        return pl.ds(pl.multiple_of(start, unit), size)

    class Gather:
        def __init__(self, buf):
            self.buf, half = buf, buf.shape[1] // 2
            self.h0, self.h1 = pl.ds(0, half), pl.ds(half, half)
            self.rx0, self.rx1, self.ry0, self.ry1, self.rd0, self.rd1 = (new() for _ in range(6))
            self.out = []

        def start(self):
            b = self.buf
            own0, own1 = b.at[p, self.h0], b.at[p, self.h1]
            self.out.append(push(own0, own0, to_x, self.rx0))
            self.out.append(push(own1, own1, to_y, self.ry1))
            self.out.append(push(own1, own1, to_x, self.rx1))
            self.out.append(push(own0, own0, to_y, self.ry0))

        def mid(self):
            b = self.buf
            got0, got1 = b.at[px, self.h0], b.at[py, self.h1]
            arrived(got0, self.rx0)
            self.out.append(push(got0, got0, to_y, self.rd0))
            arrived(got1, self.ry1)
            self.out.append(push(got1, got1, to_x, self.rd1))

        def wait_x(self):
            arrived(self.buf.at[px, self.h1], self.rx1)

        def wait_y(self):
            arrived(self.buf.at[py, self.h0], self.ry0)

        def wait_d(self):
            arrived(self.buf.at[pd, self.h0], self.rd0)
            arrived(self.buf.at[pd, self.h1], self.rd1)

        def end(self):
            self.wait_x()
            self.wait_y()
            self.wait_d()
            settle(*self.out)

    class Scatter:
        def __init__(self, buf, recv):
            self.buf, self.recv = buf, recv
            self.half = buf.shape[1] // 2
            self.h0, self.h1 = pl.ds(0, self.half), pl.ds(self.half, self.half)
            self.sems = [new() for _ in range(6)]
            self.out = []

        def start(self):
            b, v, s = self.buf, self.recv, self.sems
            self.out.append(push(b.at[pd, self.h0], v.at[0], to_x, s[0]))
            self.out.append(push(b.at[pd, self.h1], v.at[1], to_y, s[1]))
            self.out.append(push(b.at[px, self.h0], v.at[2], to_x, s[2]))
            self.out.append(push(b.at[py, self.h1], v.at[3], to_y, s[3]))

        def mid(self):
            b, v, s = self.buf, self.recv, self.sems
            arrived(v.at[0], s[0])
            step = 16

            def add0(o):
                b[py, pl.ds(o, step)] = (b[py, pl.ds(o, step)].astype(f32) + v[0, pl.ds(o, step)].astype(f32)).astype(bf16)

            loop(self.half, step, add0)
            self.out.append(push(b.at[py, self.h0], v.at[4], to_y, s[4]))
            arrived(v.at[1], s[1])

            def add1(o):
                q = pl.ds(pl.multiple_of(self.half + o, step), step)
                b[px, q] = (b[px, q].astype(f32) + v[1, pl.ds(o, step)].astype(f32)).astype(bf16)

            loop(self.half, step, add1)
            self.out.append(push(b.at[px, self.h1], v.at[5], to_x, s[5]))

        def end(self):
            for k in (2, 3, 4, 5):
                arrived(self.recv.at[k], self.sems[k])
            settle(*self.out)

        def total(self, half, o, step):
            b, v = self.buf, self.recv
            own = b[p, pl.ds(pl.multiple_of(half * self.half + o, step), step)].astype(f32)
            q = pl.ds(o, step)
            return own + v[2 + half, q].astype(f32) + v[4 + half, q].astype(f32)

        def each(self, step, body):
            for half in (0, 1):
                loop(self.half, step, lambda o: body(pl.multiple_of(half * self.half + o, step), self.total(half, o, step)))

    def z_send(src, block, rz):
        out = []
        for s in (1, 2):
            out.append(push(src, block(zh), {"zh": zh + s}, rz + zh, zh + s < RING))
            out.append(push(src, block(zh), {"zh": zh - s}, rz + zh, zh - s >= 0))
        return out

    def z_forward(block, rz):
        last = RING - 1
        arrived(block(0), rz, zh == last - 1)
        one = push(block(0), block(0), {"zh": zh + 1}, rz, zh == last - 1)
        arrived(block(last), rz + last, zh == 1)
        two = push(block(last), block(last), {"zh": zh - 1}, rz + last, zh == 1)
        return [one, two]

    def z_wait(block, rz):
        last = RING - 1
        arrived(block(0), rz, (zh == 1) | (zh == last))
        arrived(block(1), rz + 1, zh != 1)
        arrived(block(2), rz + 2, zh != 2)
        arrived(block(last), rz + last, (zh == 0) | (zh == last - 1))

    class ZSum:
        def __init__(self, block, slot, add):
            self.block, self.slot, self.add = block, slot, add
            self.sems = new(4)
            self.out = []

        def send(self):
            b, v, s = self.block, self.slot, self.sems
            last = RING - 1
            o = self.out
            o.append(push(b(last), v(1), {"zh": zh + 1}, s + 1, zh == 0))
            o.append(push(b(0), v(3), {"zh": zh - 1}, s + 3, zh == last))
            o.append(push(b(zh + 2), v(1), {"zh": zh + 2}, s + 1, zh == 0))
            o.append(push(b(zh - 2), v(3), {"zh": zh - 2}, s + 3, zh == last))
            o.append(push(b(zh + 1), v(0), {"zh": zh + 1}, s + 0, zh < last))
            o.append(push(b(zh - 1), v(2), {"zh": zh - 1}, s + 2, zh > 0))

        def forward(self):
            b, v, s = self.block, self.slot, self.sems
            last = RING - 1

            def up():
                arrived(v(1), s + 1)
                self.add(last, 1)

            def down():
                arrived(v(3), s + 3)
                self.add(0, 3)

            pl.when(zh == 1)(up)
            self.out.append(push(b(last), v(1), {"zh": zh + 2}, s + 1, zh == 1))
            pl.when(zh == last - 1)(down)
            self.out.append(push(b(0), v(3), {"zh": zh - 2}, s + 3, zh == last - 1))

        def end(self):
            v, s = self.slot, self.sems
            arrived(v(0), s, zh >= 1)
            arrived(v(1), s + 1, zh >= 2)
            arrived(v(2), s + 2, zh <= 2)
            arrived(v(3), s + 3, zh <= 1)
            settle(*self.out)

        def total(self, own, parts):
            for part, pred in zip(parts, (zh >= 1, zh >= 2, zh <= 2, zh <= 1), strict=True):
                own = own + jnp.where(pred, part.astype(f32), 0.0)
            return own

    class Column:
        def __init__(self, src, w, R, C, lane0):
            self.src, self.w, self.R, self.C, self.lanes = src, w, R, C, pl.ds(lane0, C)
            self.ra, self.rz, self.rc = new(), new(4), new()
            self.out = []

        def spread(self):
            R, C, src = self.R, self.C, self.src
            dst = self.w.at[zh, c, ds(p * R, R, 16), self.lanes]
            for k, dev in plane_peers:
                self.out.append(push(src.at[:, ds(k * C, C, 128)], dst, dev, self.ra))
            keep_local(src.at[:, ds(p * C, C, 128)], dst, self.ra)

        def block(self, z):
            return self.w.at[z, c, :, self.lanes]

        def z_send(self):
            arrived(self.block(zh), self.ra)
            self.out += z_send(self.block(zh), self.block, self.rz)

        def z_forward(self):
            self.out += z_forward(self.block, self.rz)

        def z_wait(self):
            z_wait(self.block, self.rz)
            half = self.w.at[:, c, :, self.lanes]
            self.out.append(push(half, half, to_core, self.rc))

        def end(self):
            arrived(self.w.at[:, 1 - c, :, self.lanes], self.rc)
            settle(*self.out)

    class Rows:
        def __init__(self, src, w, stage, R):
            self.src, self.w, self.stage, self.R = src, w, stage, R
            self.rl, self.rz, self.rp, self.rc = new(), new(4), new(), new()
            self.out = []

        def block(self, z):
            return self.stage.at[z]

        def z_send(self):
            keep_local(self.src, self.block(zh), self.rl)
            self.out += z_send(self.src, self.block, self.rz)

        def z_forward(self):
            self.out += z_forward(self.block, self.rz)

        def z_wait(self):
            R = self.R
            pltpu.make_async_copy(self.src, self.block(zh), r.rs.at[self.rl]).wait()
            z_wait(self.block, self.rz)
            dst = self.w.at[ds((c * PLANE + p) * R, R, 16)]
            for k, dev in plane_peers:
                self.out.append(push(self.stage.at[k], dst, dev, self.rp))
            keep_local(self.stage.at[p], dst, self.rp)

        def plane_wait(self):
            H = PLANE * self.R
            half = self.w.at[ds(c * H, H, 16)]
            arrived(half, self.rp)
            self.out.append(push(half, half, to_core, self.rc))

        def end(self):
            H = PLANE * self.R
            arrived(self.w.at[ds((1 - c) * H, H, 16)], self.rc)
            settle(*self.out)

    class ColumnsGrad:
        def __init__(self, g, other, slots, land, R, lane0, lanes, outs):
            self.g, self.other, self.slots, self.land = g, other, slots, land
            self.R, self.lanes, self.outs = R, pl.ds(lane0, lanes), outs
            self.rc, self.rl = new(), new()
            self.zsum = ZSum(
                lambda z: g.at[z, c, :, self.lanes], lambda k: slots.at[k, :, self.lanes], self.add_slot
            )

        def add_slot(self, z, k):
            g, q = self.g, self.lanes

            def add(o):
                s = pl.ds(o, 16)
                g[z, c, s, q] = (g[z, c, s, q].astype(f32) + self.slots[k, s, q].astype(f32)).astype(bf16)

            loop(PLANE * self.R, 16, add)

        def core_send(self):
            self.pushed = push(
                self.g.at[:, 1 - c, :, self.lanes], self.other.at[:, :, self.lanes], to_core, self.rc
            )

        def z_send(self):
            g, q = self.g, self.lanes
            arrived(self.other.at[:, :, q], self.rc)
            for z in range(RING):

                def add(o):
                    s = pl.ds(o, 16)
                    g[z, c, s, q] = (g[z, c, s, q].astype(f32) + self.other[z, s, q].astype(f32)).astype(bf16)

                loop(PLANE * self.R, 16, add)
            self.zsum.send()

        def z_forward(self):
            self.zsum.forward()

        def plane_send(self):
            g, q, R = self.g, self.lanes, self.R
            self.zsum.end()

            def add(o):
                s = pl.ds(o, 16)
                parts = [self.slots[k, s, q] for k in range(4)]
                g[zh, c, s, q] = self.zsum.total(g[zh, c, s, q].astype(f32), parts).astype(bf16)

            loop(PLANE * R, 16, add)
            dst = self.land.at[p, :, q]
            self.out = [self.pushed]
            for k, dev in plane_peers:
                self.out.append(push(g.at[zh, c, ds(k * R, R, 16), q], dst, dev, self.rl))
            keep_local(g.at[zh, c, ds(p * R, R, 16), q], dst, self.rl)

        def end(self):
            arrived(self.land.at[:, :, self.lanes], self.rl)
            settle(*self.out)
            for lane0, C, out in self.outs:
                for k in range(PLANE):
                    out[:, k * C : (k + 1) * C] = self.land[k, :, lane0 : lane0 + C].astype(f32)

    class RowsGrad:
        def __init__(self, g, other, stage, slots, R, out):
            self.g, self.other, self.stage, self.slots, self.R, self.result = g, other, stage, slots, R, out
            self.rc, self.rl = new(), new()
            self.zsum = ZSum(lambda z: stage.at[z], lambda k: slots.at[k], self.add_slot)

        def add_slot(self, z, k):
            g = self.stage

            def add(o):
                s = pl.ds(o, 16)
                g[z, s] = (g[z, s].astype(f32) + self.slots[k, s].astype(f32)).astype(bf16)

            loop(self.R, 16, add)

        def core_send(self):
            H = PLANE * self.R
            self.out = [push(self.g.at[ds((1 - c) * H, H, 16)], self.other, to_core, self.rc)]

        def plane_send(self):
            R, H, g = self.R, PLANE * self.R, self.g
            arrived(self.other, self.rc)

            def add(o):
                s = ds(c * H + o, 16, 16)
                g[s] = (g[s].astype(f32) + self.other[pl.ds(o, 16)].astype(f32)).astype(bf16)

            loop(H, 16, add)
            dst = self.stage.at[p]
            for k, dev in plane_peers:
                self.out.append(push(g.at[ds(c * H + k * R, R, 16)], dst, dev, self.rl))
            keep_local(g.at[ds(c * H + p * R, R, 16)], dst, self.rl)

        def z_send(self):
            arrived(self.stage, self.rl)
            self.zsum.send()

        def z_forward(self):
            self.zsum.forward()

        def end(self):
            self.zsum.end()
            settle(*self.out)

            def add(o):
                s = pl.ds(o, 16)
                self.result[s] = self.zsum.total(self.stage[zh, s].astype(f32), [self.slots[k, s] for k in range(4)])

            loop(self.R, 16, add)

    class Carry:
        def __init__(self, buf, later):
            self.buf, self.later = buf, later
            self.sems = new(places)
            self.out = []

        def send(self):
            own = self.buf.at[pos]
            order = range(places) if self.later else reversed(range(places))
            for at in order:
                pred = (pos < at) if self.later else (pos > at)
                self.out.append(push(own, own, place(at), self.sems + pos, pred))

        def fold(self, into):
            into[...] = jnp.zeros_like(into)
            order = range(places) if self.later else reversed(range(places))
            for at in order:
                pred = (pos > at) if self.later else (pos < at)

                def take(at=at):
                    arrived(self.buf.at[at], self.sems + at)
                    part = self.buf[at]
                    into[0:PLANE] = part[0:PLANE] * into[0:PLANE] + part[PLANE : 2 * PLANE]

                pl.when(pred)(take)
            settle(*self.out)

    GL = PLANE * RD
    ring = zh * 2 + c
    home = {"yl": zh // 2, "xl": zh % 2}

    def ring_place(at):
        return {"zh": at // 2, "c": at % 2}

    class Small:
        def __init__(self):
            self.rk, self.rc, self.rg, self.ra = new(), new(), new(2 * RING), new(2)
            self.out = []

        def one(self):
            row = r.pack.at[:, pl.ds(0, GL + T)]
            for _, dev in plane_peers:
                self.out.append(push(row, r.pk.at[p], dev, self.rk))
            keep_local(row, r.pk.at[p], self.rk)
            chan = r.pack.at[:, pl.ds(GL + T, CW)]
            self.out.append(push(chan, r.pc.at[p], home, self.rc, p != zh))
            pl.when(p == zh)(lambda: keep_local(chan, r.pc.at[p], self.rc))

        def two(self):
            arrived(r.pk, self.rk)
            r.g_all[ring] = (r.pk[0, :, 0:GL] + r.pk[1, :, 0:GL]) + (r.pk[2, :, 0:GL] + r.pk[3, :, 0:GL])

            def chan():
                arrived(r.pc, self.rc)
                r.c_all[c] = (r.pc[0] + r.pc[1]) + (r.pc[2] + r.pc[3])

            pl.when(p == zh)(chan)
            for at in range(2 * RING):
                own = r.g_all.at[ring]
                self.out.append(push(own, own, ring_place(at), self.rg + ring, ring != at))
            for at in range(2 * RING):
                own = r.c_all.at[c]
                self.out.append(push(own, own, ring_place(at), self.ra + c, (p == zh) & (ring != at)))

        def three(self):
            for at in range(2 * RING):
                arrived(r.g_all.at[at], self.rg + at, ring != at)
            for at in range(2):
                arrived(r.c_all.at[at], self.ra + at, (p != zh) | (c != at))
            for at in range(2 * RING):
                r.gains[:, at * GL : (at + 1) * GL] = r.g_all[at]
            r.chan[...] = r.c_all[0] + r.c_all[1]
            r.chan[7:8] = r.scale[pl.ds(p, 1)]
            lane = lax.broadcasted_iota(jnp.int32, (8, 128), 0)
            for k in range(PLANE):
                rows = r.pk[k, :, GL : GL + T]
                for j in range(7):
                    r.masks[j, k * T : (k + 1) * T] = dot_tn(rows, (lane == j).astype(f32))
            settle(*self.out)

    class SmallGrad:
        def __init__(self):
            self.rg, self.rc, self.rp, self.ro = new(2 * RING), new(2 * RING), new(PLANE), new()
            self.out = []

        def chan_one(self):
            for cc in (0, 1):
                self.out.append(
                    push(r.gchan, r.gc.at[ring], {"zh": p, "c": cc}, self.rc + ring, (zh != p) | (c != cc))
                )

        def chan_two(self):
            def total():
                r.gc[ring] = r.gchan[...]
                value = r.gchan[...]
                for at in range(2 * RING):
                    arrived(r.gc.at[at], self.rc + at, ring != at)
                value = r.gc[0]
                for at in range(1, 2 * RING):
                    value = value + r.gc[at]
                r.chan_out[...] = value

            pl.when(p == zh)(total)
            for _, dev in plane_peers:
                self.out.append(push(r.chan_out, r.chan_out, dev, self.ro, p == zh))

        def gain_one(self):
            for at in range(2 * RING):
                src = r.ggain.at[:, pl.ds(at * GL, GL)]
                self.out.append(push(src, r.gg.at[ring], ring_place(at), self.rg + ring, ring != at))

        def gain_two(self):
            r.gg[ring] = r.ggain[:, ds(ring * GL, GL, 128)]
            for at in range(2 * RING):
                arrived(r.gg.at[at], self.rg + at, ring != at)
            value = r.gg[0]
            for at in range(1, 2 * RING):
                value = value + r.gg[at]
            r.gp[p] = value
            for _, dev in plane_peers:
                self.out.append(push(r.gp.at[p], r.gp.at[p], dev, self.rp + p))

        def end(self):
            for k, _ in plane_peers:
                arrived(r.gp.at[k], self.rp + k)
            r.gain_out[...] = (r.gp[0] + r.gp[1]) + (r.gp[2] + r.gp[3])
            arrived(r.chan_out, self.ro, p != zh)
            settle(*self.out)

    barrier = pltpu.get_barrier_semaphore()
    for _, dev in plane_peers:
        pl.semaphore_signal(barrier, 1, device_id=dev, device_id_type=MESH)
    for at in range(places):

        @pl.when(pos != at)
        def _(at=at):
            pl.semaphore_signal(barrier, 1, device_id=place(at), device_id_type=MESH)

    pl.semaphore_wait(barrier, len(plane_peers) + places - 1)

    w_i, w_b = Column(r.input_weight, r.w_ib, RD, CW, 0), Column(r.branch_weight, r.w_ib, RD, CW, CW)
    w_d, w_j = Column(r.decay_weight, r.w_di, RW, CW, 0), Column(r.inject_weight, r.w_di, RW, CW, CW)
    w_g, w_u = Column(r.mlp_gate, r.w_gu, RD, CF, 0), Column(r.mlp_up, r.w_gu, RD, CF, CF)
    w_o, w_dn = Rows(r.output_weight, r.w_o, r.st_o, RW), Rows(r.mlp_down, r.w_dn, r.st_dn, RF)
    ag_x, ag_conv, ag_two = Gather(r.x_all), Gather(r.conv), Gather(r.n_two)
    ag_cot, ag_out = Gather(r.cot_all), Gather(r.d_out)
    small, small_grad = Small(), SmallGrad()
    after, before = flat_z + c, flat_z - (1 - c)
    to_next = {"zh": after // NL, "zl": after % NL, "c": 1 - c}
    to_prev = {"zh": before // NL, "zl": before % NL, "c": 1 - c}
    step = 256
    chunk = PLANE * RD * 2

    small.one()
    halo_x = new()
    sent_x = push(r.tokens.at[pl.ds(T - 16, 16)], r.x_halo.at[p], to_next, halo_x, pos < places - 1)
    w_i.spread()
    w_o.z_send()
    r.x_all[p] = r.tokens[...]
    r.cot_all[p] = r.cotangent[...]
    ag_x.start()
    w_d.spread()
    w_j.spread()
    w_i.z_send()
    small.two()

    @pl.when(pos == 0)
    def _():
        r.x_halo[p] = jnp.zeros((16, D), bf16)

    arrived(r.x_halo.at[p], halo_x, pos > 0)
    halo_p = new(PLANE)
    sent_p = [push(r.x_halo.at[p], r.x_halo.at[p], dev, halo_p + p) for _, dev in plane_peers]
    ag_x.mid()
    w_b.spread()
    small.three()

    def norm_block(k):
        def norm_one(o):
            s = pl.ds(o, 32)
            v = r.x_all[k, s].astype(f32)
            r.n_one[k, s] = (v * inverse_rms(v) * r.gains[0:1]).astype(bf16)

        loop(T, 32, norm_one)

    norm_block(p)
    w_d.z_send()
    w_o.z_forward()
    ag_x.wait_x()
    norm_block(px)
    ag_x.wait_y()
    norm_block(py)
    for k, _ in plane_peers:
        arrived(r.x_halo.at[k], halo_p + k)
    v = r.x_halo[...].reshape(PLANE * 16, D).astype(f32)
    r.n_halo[...] = (v * inverse_rms(v) * r.gains[0:1]).astype(bf16).reshape(PLANE, 16, D)
    ag_x.wait_d()
    norm_block(pd)
    settle(*ag_x.out, sent_x, *sent_p)
    w_g.spread()
    w_u.spread()
    w_i.z_forward()
    w_i.z_wait()
    w_o.z_wait()
    w_j.z_send()
    w_i.end()

    def weight_ib(lanes):
        return r.w_ib[:, :, :, lanes].reshape(D, CW)

    lanes_a, lanes_b = pl.ds(0, CW), pl.ds(CW, CW)
    halo = dot(r.n_halo[...].reshape(PLANE * 16, D), weight_ib(lanes_a)).astype(bf16).astype(f32)
    body = dot(r.n_one[...].reshape(M, D), weight_ib(lanes_a)).astype(bf16).astype(f32)
    for k in range(PLANE):
        r.u[k, 0:8] = halo[k * 16 + 8 : (k + 1) * 16]
        r.u[k, 8 : 8 + T] = body[k * T : (k + 1) * T]

    def wide(j, rows):
        return jnp.concatenate([r.masks[j, rows]] * (CW // 128), axis=1) > 0.5

    def convolve(o):
        for k in range(PLANE):
            ext = r.u[k, pl.ds(o, 24)]
            rows = ds(k * T + o, 16, 16)
            total = r.chan[4:5] + r.chan[0:1] * ext[8:24]
            for j in range(1, 4):
                total = total + jnp.where(wide(j, rows), r.chan[j : j + 1] * ext[8 - j : 24 - j], 0.0)
            r.conv[p, rows] = total.astype(bf16)

    loop(T, 16, convolve)
    ag_conv.start()
    w_o.plane_wait()
    w_d.z_forward()
    w_d.z_wait()
    w_b.z_send()
    ag_conv.mid()
    w_d.end()

    def pre(q, lanes):
        return dot(r.conv[q], r.w_di[q, :, :, lanes].reshape(W // RING, CW))

    r.pair[:, 0:CW] = pre(p, lanes_a)
    for q, wait in ((px, ag_conv.wait_x), (py, ag_conv.wait_y), (pd, ag_conv.wait_d)):
        wait()
        r.pair[:, 0:CW] += pre(q, lanes_a)
    settle(*ag_conv.out)
    ag_cot.start()
    w_j.z_forward()
    w_j.z_wait()
    w_g.z_send()
    w_j.end()
    r.pair[:, CW : 2 * CW] = pre(0, lanes_b)
    for q in range(1, PLANE):
        r.pair[:, CW : 2 * CW] += pre(q, lanes_b)

    def decay_terms(s, rg):
        log_a = -rate_scale * rg * r.chan[7:8]
        gap = minus_expm1(2.0 * log_a)
        first = wide(0, s)
        return log_a, gap, jnp.where(first, 1.0, jnp.sqrt(jnp.maximum(gap, floor_gap))), first

    def gates_two(o):
        s = pl.ds(o, 16)
        rg = jax.nn.sigmoid(r.pair[s, 0:CW] + r.chan[5:6])
        ig = jax.nn.sigmoid(r.pair[s, CW : 2 * CW] + r.chan[6:7])
        log_a, _, mult, first = decay_terms(s, rg)
        r.rgate[s], r.igate[s] = rg, ig
        r.decay[s] = jnp.where(first, 0.0, jnp.exp(log_a))
        r.work[s] = mult * ig * r.conv[p, s].astype(f32)

    loop(M, 16, gates_two)
    row = lax.broadcasted_iota(jnp.int32, (8, CW), 0)

    def scan_forward(j, carry):
        out = []
        for k in range(PLANE):
            s = ds(k * T + j * 8, 8, 8)
            a, b = r.decay[s], r.work[s]
            for n in (1, 2, 4):
                a_b = jnp.where(row >= n, pltpu.roll(a, n, 0), 1.0)
                b_b = jnp.where(row >= n, pltpu.roll(b, n, 0), 0.0)
                a, b = a * a_b, a * b_b + b
            total, prod = b + a * carry[2 * k], a * carry[2 * k + 1]
            r.state[k, ds(8 + j * 8, 8, 8)] = total
            r.cum[s] = prod
            out += [total[7:8], prod[7:8]]
        return tuple(out)

    zero, one = jnp.zeros((1, CW), f32), jnp.ones((1, CW), f32)
    ends = lax.fori_loop(0, T // 8, scan_forward, (zero, one) * PLANE)
    carry_f = Carry(r.carry_f, True)
    for k in range(PLANE):
        r.carry_f[pos, k : k + 1] = ends[2 * k + 1]
        r.carry_f[pos, PLANE + k : PLANE + k + 1] = ends[2 * k]
        r.ends[k : k + 1] = ends[2 * k + 1]
    carry_f.send()
    ag_cot.mid()
    w_b.z_forward()
    w_b.z_wait()
    w_b.end()
    r.work[...] = dot(r.n_one[...].reshape(M, D), weight_ib(lanes_b))

    def gates_one(o):
        s = pl.ds(o, 16)
        r.gated[s], r.slope[s] = gelu_parts(r.work[s])

    loop(M, 16, gates_one)
    w_o.end()
    carry_f.fold(r.into)
    for k in range(PLANE):
        r.state[k, 0:8] = jnp.broadcast_to(r.into[k : k + 1], (8, CW))

    def mix(o):
        for k in range(PLANE):
            s, t = ds(k * T + o, 16, 16), ds(8 + o, 16, 8)
            state = r.state[k, t] + r.cum[s] * r.into[k : k + 1]
            r.state[k, t] = state
            r.mixed[s] = (state * r.gated[s]).astype(bf16)

    loop(T, 16, mix)

    def out_part(o):
        q = pl.ds(o, step)
        r.part[:, :, q] = dot(r.mixed[...], r.w_o[:, q]).astype(bf16).reshape(PLANE, T, step)

    loop(D, step, out_part)
    rs_one = Scatter(r.part, r.got_one)
    rs_one.start()
    w_u.z_send()
    ag_cot.end()
    rs_one.mid()
    w_g.z_forward()
    rs_one.end()

    def norm_two(o, summed):
        s = pl.ds(o, 16)
        v = r.tokens[s].astype(f32) + summed
        r.x_one[s] = v
        r.n_two[p, s] = (v * inverse_rms(v) * r.gains[1:2]).astype(bf16)

    rs_one.each(16, norm_two)
    ag_two.start()
    w_g.z_wait()
    w_dn.z_send()
    ag_two.mid()
    w_g.end()
    w_u.z_forward()
    ag_two.end()

    def mlp_in(o):
        q = pl.ds(o, step)
        r.pair[:, q] = dot(r.n_two[...].reshape(M, D), r.w_gu[:, :, :, q].reshape(D, step))

    loop(CF, step, mlp_in)
    w_u.z_wait()
    w_u.end()
    loop(CF, step, lambda o: mlp_in(pl.multiple_of(CF + o, step)))

    def gates_mlp(o):
        s = pl.ds(o, 16)
        value, slope = gelu_parts(r.pair[s, 0:CF])
        up = r.pair[s, CF : 2 * CF]
        r.hidden[s] = (value * up).astype(bf16)
        r.pair[s, 0:CF] = slope * up
        r.pair[s, CF : 2 * CF] = value

    loop(M, 16, gates_mlp)

    def grad_down(o):
        q = pl.ds(o, step)
        r.g_dn[q] = dot_tn(r.hidden[:, q], r.cot_all[...].reshape(M, D)).astype(bf16)

    loop(CF, step, grad_down)
    g_dn = RowsGrad(r.g_dn, r.h_dn, r.sg_dn, r.z_dn, RF, r.grad_mlp_down)
    g_dn.core_send()
    w_dn.z_forward()
    g_dn.plane_send()
    w_dn.z_wait()
    g_dn.z_send()
    w_dn.plane_wait()
    w_dn.end()

    for k in range(CF // step):
        q = pl.ds(k * step, step)
        back = dot_nt(r.cot_all[...].reshape(M, D), r.w_dn[q])
        r.d_pair[:, k * step : (k + 1) * step] = (back * r.pair[:, k * step : (k + 1) * step]).astype(bf16)
        r.d_pair[:, CF + k * step : CF + (k + 1) * step] = (
            back * r.pair[:, CF + k * step : CF + (k + 1) * step]
        ).astype(bf16)

    def d_two_part(z, _):
        q = ds(z * chunk, chunk, chunk)
        r.part[:, :, q] = (
            dot_nt(r.d_pair[...], r.w_gu[z].reshape(chunk, 2 * CF)).astype(bf16).reshape(PLANE, T, chunk)
        )
        return 0

    lax.fori_loop(0, RING, d_two_part, 0)
    rs_two = Scatter(r.part, r.got_two)
    rs_two.start()

    def grad_gate_up(lane0):
        lanes = pl.ds(lane0, CF)

        def run(z, _):
            q = ds(z * chunk, chunk, chunk)
            value = dot_tn(r.n_two[:, :, q].reshape(M, chunk), r.d_pair[:, lanes])
            r.w_gu[z, :, :, lanes] = value.astype(bf16).reshape(2, chunk // 2, CF)
            return 0

        lax.fori_loop(0, RING, run, 0)

    grad_gate_up(0)
    g_g = ColumnsGrad(r.w_gu, r.h_gu, r.z_gu, r.l_gu, RD, 0, CF, ((0, CF, r.grad_mlp_gate),))
    g_g.core_send()
    rs_two.mid()
    grad_gate_up(CF)
    g_u = ColumnsGrad(r.w_gu, r.h_gu, r.z_gu, r.l_gu, RD, CF, CF, ((CF, CF, r.grad_mlp_up),))
    g_u.core_send()
    g_dn.z_forward()
    g_g.z_send()

    def act_part(o):
        q = pl.ds(o, step)
        r.part_act[:, :, q] = dot(r.hidden[...], r.w_dn[:, q]).astype(bf16).reshape(PLANE, T, step)

    loop(D, step, act_part)
    r.ggain[...] = jnp.zeros_like(r.ggain)
    r.gchan[...] = jnp.zeros_like(r.gchan)
    rs_two.end()

    def norm_two_back(o, d_two):
        s = pl.ds(o, 16)
        v = r.x_one[s]
        rs = inverse_rms(v)
        z = v * rs
        dz = d_two * r.gains[1:2]
        r.ggain[1:2] += jnp.sum(d_two * z, axis=0, keepdims=True)
        d_one = r.cotangent[s].astype(f32) + rs * (dz - z * jnp.mean(dz * z, axis=-1, keepdims=True))
        r.d_one[s] = d_one
        r.d_out[p, s] = d_one.astype(bf16)

    rs_two.each(16, norm_two_back)
    ag_out.start()
    g_dn.end()
    g_u.z_send()
    ag_out.mid()
    g_g.z_forward()
    ag_out.end()
    rs_act = Scatter(r.part_act, r.got_act)
    rs_act.start()

    r.work[...] = dot_nt(r.d_out[...].reshape(M, D), r.w_o[...])

    def split(o):
        for k in range(PLANE):
            s = ds(k * T + o, 16, 16)
            d_mixed = r.work[s]
            r.d_gu[s, CW : 2 * CW] = (d_mixed * r.state[k, ds(8 + o, 16, 8)] * r.slope[s]).astype(bf16)
            r.work[s] = d_mixed * r.gated[s]

    loop(T, 16, split)

    def scan_backward(i, carry):
        j = T // 8 - 1 - i
        out = []
        for k in range(PLANE):
            s = ds(k * T + j * 8, 8, 8)
            decay, b = r.decay[s], r.work[s]
            a = jnp.where(row < 7, pltpu.roll(decay, 7, 0), carry[3 * k + 2])
            for n in (1, 2, 4):
                a_b = jnp.where(row < 8 - n, pltpu.roll(a, 8 - n, 0), 1.0)
                b_b = jnp.where(row < 8 - n, pltpu.roll(b, 8 - n, 0), 0.0)
                a, b = a * a_b, a * b_b + b
            total, prod = b + a * carry[3 * k], a * carry[3 * k + 1]
            r.work[s], r.cum[s] = total, prod
            out += [total[0:1], prod[0:1], decay[0:1]]
        return tuple(out)

    heads = lax.fori_loop(0, T // 8, scan_backward, (zero, one, one) * PLANE)
    carry_b = Carry(r.carry_b, False)
    for k in range(PLANE):
        r.carry_b[pos, k : k + 1] = r.ends[k : k + 1]
        r.carry_b[pos, PLANE + k : PLANE + k + 1] = heads[3 * k] * heads[3 * k + 2]
    carry_b.send()

    def grad_out(o):
        q = pl.ds(o, 128)
        r.w_o[q] = dot_tn(r.mixed[:, q], r.d_out[...].reshape(M, D)).astype(bf16)

    loop(CW, 128, grad_out)
    g_o = RowsGrad(r.w_o, r.h_o, r.sg_o, r.z_o, RW, r.grad_output_weight)
    g_o.core_send()
    rs_act.mid()

    def d_branch_part(z, _):
        q = ds(z * chunk, chunk, chunk)
        r.part[:, :, q] = (
            dot_nt(r.d_gu[:, lanes_b], r.w_ib[z, :, :, lanes_b].reshape(chunk, CW))
            .astype(bf16)
            .reshape(PLANE, T, chunk)
        )
        value = dot_tn(r.n_one[:, :, q].reshape(M, chunk), r.d_gu[:, lanes_b])
        r.w_ib[z, :, :, lanes_b] = value.astype(bf16).reshape(2, chunk // 2, CW)
        return 0

    lax.fori_loop(0, RING, d_branch_part, 0)
    g_b = ColumnsGrad(r.w_ib, r.h_ib, r.z_ib, r.l_ib, RD, CW, CW, ((CW, CW, r.grad_branch_weight),))
    g_b.core_send()
    g_g.plane_send()
    carry_b.fold(r.into)

    def back(o):
        sums = [jnp.zeros((1, CW), f32)] * 2
        for k in range(PLANE):
            s = ds(k * T + o, 16, 16)
            adjoint = r.work[s] + r.cum[s] * r.into[k : k + 1]
            previous = r.state[k, pl.ds(o, 24)][7:23]
            rg, ig, decay, conv = r.rgate[s], r.igate[s], r.decay[s], r.conv[p, s].astype(f32)
            _, gap, mult, first = decay_terms(s, rg)
            d_mult = jnp.where(first, 0.0, adjoint * ig * conv)
            d_log = adjoint * previous * decay - jnp.where(gap > floor_gap, (1.0 - gap) * d_mult / mult, 0.0)
            d_decay = (-rate_scale * r.chan[7:8] * d_log * rg * (1.0 - rg)).astype(bf16)
            d_inject = (adjoint * mult * conv * ig * (1.0 - ig)).astype(bf16)
            r.d_pre[s, 0:CW] = d_decay
            r.d_pre[s, CW : 2 * CW] = d_inject
            sums[0] = sums[0] + jnp.sum(d_decay.astype(f32), axis=0, keepdims=True)
            sums[1] = sums[1] + jnp.sum(d_inject.astype(f32), axis=0, keepdims=True)
            r.d_conv[k, pl.ds(o, 16)] = adjoint * mult * ig
        r.gchan[5:6] += sums[0]
        r.gchan[6:7] += sums[1]

    loop(T, 16, back)

    def conv_part(q, _):
        r.part_conv[q] = dot_nt(r.d_pre[...], r.w_di[q].reshape(W // RING, 2 * CW)).astype(bf16)
        return 0

    lax.fori_loop(0, RING, conv_part, 0)
    rs_act.end()
    rs_conv = Scatter(r.part_conv, r.got_conv)
    rs_conv.start()

    def finish_act(o, summed):
        s = pl.ds(o, 16)
        r.activations[s] = (r.x_one[s] + summed).astype(bf16)

    rs_act.each(16, finish_act)
    g_u.z_forward()
    g_b.z_send()

    def grad_dec_inj(lanes):
        def run(q, _):
            value = dot_tn(r.conv[q], r.d_pre[:, lanes])
            r.w_di[q, :, :, lanes] = value.astype(bf16).reshape(2, W // SHARES * PLANE, CW)
            return 0

        lax.fori_loop(0, RING, run, 0)

    grad_dec_inj(lanes_a)
    g_d = ColumnsGrad(r.w_di, r.h_di, r.z_di, r.l_di, RW, 0, CW, ((0, CW, r.grad_decay_weight),))
    g_d.core_send()
    g_o.plane_send()
    rs_conv.mid()
    grad_dec_inj(lanes_b)
    g_j = ColumnsGrad(r.w_di, r.h_di, r.z_di, r.l_di, RW, CW, CW, ((CW, CW, r.grad_inject_weight),))
    g_j.core_send()
    g_u.plane_send()
    g_o.z_send()
    g_b.z_forward()
    g_d.z_send()
    rs_conv.end()

    for half in (0, 1):

        def add_conv(o, half=half):
            for k in (2 * half, 2 * half + 1):
                at = (k - 2 * half) * T + o
                r.d_conv[k, pl.ds(o, 16)] += rs_conv.total(half, pl.multiple_of(at, 16), 16)

        loop(T, 16, add_conv)
    halo_b = new()
    sent_b = push(r.d_conv.at[:, pl.ds(0, 8)], r.d_conv.at[:, pl.ds(T, 8)], to_prev, halo_b, pos > 0)

    def taps_back(o):
        sums = [jnp.zeros((1, CW), f32)] * 5
        for k in range(PLANE):
            ext = r.u[k, pl.ds(o, 24)]
            rows = ds(k * T + o, 16, 16)
            dc = r.d_conv[k, pl.ds(o, 16)]
            sums[4] = sums[4] + jnp.sum(dc, axis=0, keepdims=True)
            sums[0] = sums[0] + jnp.sum(dc * ext[8:24], axis=0, keepdims=True)
            for j in range(1, 4):
                term = jnp.where(wide(j, rows), dc * ext[8 - j : 24 - j], 0.0)
                sums[j] = sums[j] + jnp.sum(term, axis=0, keepdims=True)
        for j in range(5):
            r.gchan[j : j + 1] += sums[j]

    loop(T, 16, taps_back)
    small_grad.chan_one()

    @pl.when(pos == places - 1)
    def _():
        r.d_conv[:, T : T + 8] = jnp.zeros((PLANE, 8, CW), f32)

    arrived(r.d_conv.at[:, pl.ds(T, 8)], halo_b, pos < places - 1)
    settle(sent_b)

    def conv_back(o):
        for k in range(PLANE):
            ext = r.d_conv[k, pl.ds(o, 24)]
            rows = ds(k * T + o, 16, 16)
            total = r.chan[0:1] * ext[0:16]
            for j in range(1, 4):
                total = total + jnp.where(wide(3 + j, rows), r.chan[j : j + 1] * ext[j : 16 + j], 0.0)
            r.d_gu[rows, 0:CW] = total.astype(bf16)

    loop(T, 16, conv_back)

    def d_input_part(z, _):
        q = ds(z * chunk, chunk, chunk)
        value = dot_nt(r.d_gu[:, lanes_a], r.w_ib[z, :, :, lanes_a].reshape(chunk, CW)).reshape(PLANE, T, chunk)
        r.part[:, :, q] = (r.part[:, :, q].astype(f32) + value).astype(bf16)
        return 0

    lax.fori_loop(0, RING, d_input_part, 0)
    rs_three = Scatter(r.part, r.got_three)
    rs_three.start()

    def grad_input(z, _):
        q = ds(z * chunk, chunk, chunk)
        value = dot_tn(r.n_one[:, :, q].reshape(M, chunk), r.d_gu[:, lanes_a])
        r.w_ib[z, :, :, lanes_a] = value.astype(bf16).reshape(2, chunk // 2, CW)
        return 0

    lax.fori_loop(0, RING, grad_input, 0)
    g_i = ColumnsGrad(r.w_ib, r.h_ib, r.z_ib, r.l_ib, RD, 0, CW, ((0, CW, r.grad_input_weight),))
    g_i.core_send()
    g_o.z_forward()
    g_b.plane_send()
    g_d.z_forward()
    rs_three.mid()
    small_grad.chan_two()
    g_j.z_send()
    g_i.z_send()
    g_o.end()
    g_g.end()
    g_u.end()
    rs_three.end()

    def norm_one_back(o, d_n):
        s = pl.ds(o, 16)
        v = r.tokens[s].astype(f32)
        rs = inverse_rms(v)
        z = v * rs
        dz = d_n * r.gains[0:1]
        r.ggain[0:1] += jnp.sum(d_n * z, axis=0, keepdims=True)
        r.d_tokens[s] = r.d_one[s] + rs * (dz - z * jnp.mean(dz * z, axis=-1, keepdims=True))

    rs_three.each(16, norm_one_back)
    small_grad.gain_one()
    g_d.plane_send()
    g_j.z_forward()
    g_i.z_forward()
    small_grad.gain_two()
    g_b.end()
    g_j.plane_send()
    g_i.plane_send()
    g_d.end()
    small_grad.end()
    g_j.end()
    g_i.end()
    assert not sent


WEIGHTS = (
    "branch_weight",
    "input_weight",
    "decay_weight",
    "inject_weight",
    "output_weight",
    "mlp_gate",
    "mlp_up",
    "mlp_down",
)


def run_layer(NL, tokens, cotangent, pack, scale, weights):
    T, D = tokens.shape
    W, F = weights["branch_weight"].shape[1], weights["mlp_gate"].shape[1]
    CW, CF = W // PLANE, F // PLANE
    RD, RW, RF = D // SHARES, W // SHARES, F // SHARES
    GL, M, places = PLANE * RD, PLANE * T, RING * NL * 2
    vmem, hbm = pl.BlockSpec(memory_space=pltpu.VMEM), pl.BlockSpec(memory_space=pl.ANY)
    ins = ["tokens", "cotangent", "pack", "scale", *WEIGHTS]
    outs = {
        "activations": ((T, D), bf16),
        "d_tokens": ((T, D), f32),
        **{"grad_" + name: (weights[name].shape, f32) for name in WEIGHTS},
        "gain_out": ((8, GL), f32),
        "chan_out": ((8, CW), f32),
    }
    scratch = {
        "w_ib": ((RING, 2, PLANE * RD, 2 * CW), bf16),
        "w_di": ((RING, 2, PLANE * RW, 2 * CW), bf16),
        "w_gu": ((RING, 2, PLANE * RD, 2 * CF), bf16),
        "w_o": ((CW, D), bf16),
        "w_dn": ((CF, D), bf16),
        "st_o": ((RING, RW, D), bf16),
        "st_dn": ((RING, RF, D), bf16),
        "h_ib": ((RING, PLANE * RD, 2 * CW), bf16),
        "h_di": ((RING, PLANE * RW, 2 * CW), bf16),
        "h_gu": ((RING, PLANE * RD, 2 * CF), bf16),
        "h_o": ((CW // 2, D), bf16),
        "h_dn": ((CF // 2, D), bf16),
        "z_ib": ((4, PLANE * RD, 2 * CW), bf16),
        "z_di": ((4, PLANE * RW, 2 * CW), bf16),
        "z_gu": ((4, PLANE * RD, 2 * CF), bf16),
        "z_o": ((4, RW, D), bf16),
        "z_dn": ((4, RF, D), bf16),
        "l_ib": ((PLANE, RD, 2 * CW), bf16),
        "l_di": ((PLANE, RW, 2 * CW), bf16),
        "l_gu": ((PLANE, RD, 2 * CF), bf16),
        "sg_o": ((RING, RW, D), bf16),
        "sg_dn": ((RING, RF, D), bf16),
        "n_one": ((PLANE, T, D), bf16),
        "n_two": ((PLANE, T, D), bf16),
        "cot_all": ((PLANE, T, D), bf16),
        "d_out": ((PLANE, T, D), bf16),
        "conv": ((PLANE, M, CW), bf16),
        "part": ((PLANE, T, D), bf16),
        "part_act": ((PLANE, T, D), bf16),
        "part_conv": ((PLANE, M, CW), bf16),
        "got_one": ((6, T // 2, D), bf16),
        "got_two": ((6, T // 2, D), bf16),
        "got_three": ((6, T // 2, D), bf16),
        "got_act": ((6, T // 2, D), bf16),
        "got_conv": ((6, M // 2, CW), bf16),
        "mixed": ((M, CW), bf16),
        "hidden": ((M, CF), bf16),
        "d_pair": ((M, 2 * CF), bf16),
        "d_gu": ((M, 2 * CW), bf16),
        "d_pre": ((M, 2 * CW), bf16),
        "pair": ((M, 2 * CF), f32),
        "u": ((PLANE, T + 8, CW), f32),
        "state": ((PLANE, T + 8, CW), f32),
        "d_conv": ((PLANE, T + 8, CW), f32),
        **{name: ((M, CW), f32) for name in ("gated", "slope", "rgate", "igate", "decay", "work", "cum")},
        "x_one": ((T, D), f32),
        "d_one": ((T, D), f32),
        "carry_f": ((places, 2 * PLANE, CW), f32),
        "carry_b": ((places, 2 * PLANE, CW), f32),
        "into": ((8, CW), f32),
        "x_all": ((PLANE, T, D), bf16),
        "x_halo": ((PLANE, 16, D), bf16),
        "n_halo": ((PLANE, 16, D), bf16),
        "g_dn": ((CF, D), bf16),
        "masks": ((7, M, 128), f32),
        "pk": ((PLANE, 8, GL + T), f32),
        "pc": ((PLANE, 8, CW), f32),
        "g_all": ((2 * RING, 8, GL), f32),
        "c_all": ((2, 8, CW), f32),
        "gains": ((8, D), f32),
        "chan": ((8, CW), f32),
        "ggain": ((8, D), f32),
        "gchan": ((8, CW), f32),
        "gg": ((2 * RING, 8, GL), f32),
        "gp": ((PLANE, 8, GL), f32),
        "gc": ((2 * RING, 8, CW), f32),
        "ends": ((8, CW), f32),
    }
    dims = SimpleNamespace(
        T=T, D=D, W=W, F=F, CW=CW, CF=CF, RD=RD, RW=RW, RF=RF, NL=NL, names=[*ins, *outs, *scratch, "ss", "rs"]
    )
    flops = 3 * 2 * M * (D * 2 * CW + W * 2 * CW + CW * D + 3 * D * CF)
    results = pl.pallas_call(
        partial(layer, dims),
        out_shape=[jax.ShapeDtypeStruct(shape, kind) for shape, kind in outs.values()],
        in_specs=[vmem] * 4 + [hbm] * len(WEIGHTS),
        out_specs=[vmem] * len(outs),
        scratch_shapes=[pltpu.VMEM(shape, kind) for shape, kind in scratch.values()]
        + [pltpu.SemaphoreType.DMA((SEMS,)), pltpu.SemaphoreType.DMA((SEMS,))],
        compiler_params=pltpu.CompilerParams(
            collective_id=0, has_side_effects=True, vmem_limit_bytes=62 * 2**20
        ),
        cost_estimate=pl.CostEstimate(flops=flops, bytes_accessed=8 * 2**20, transcendentals=M * CW * 16),
        name="griffin_layer",
    )(tokens, cotangent, pack, scale, *[weights[name] for name in WEIGHTS])
    return dict(zip(outs, results, strict=True))


def local(
    sizes,
    tokens,
    cotangent,
    doc_lengths,
    decay_exponent,
    branch_weight,
    input_weight,
    decay_weight,
    inject_weight,
    output_weight,
    mlp_gate,
    mlp_up,
    mlp_down,
    first_gain,
    second_gain,
    conv_taps,
    conv_bias,
    decay_bias,
    inject_bias,
):
    devices = math.prod(sizes.values())
    width = branch_weight.shape[1]
    NL = sizes["zl"]
    at = {name: lax.axis_index(name) for name in AXES}
    T = tokens.shape[1]

    mine = at["yl"] * 2 + at["xl"]
    ring = at["zh"] * 2 + at["c"]
    share = ring * PLANE + mine
    groups = devices // SHARES

    def pooled(value, axis=0):
        if groups == 1:
            return value
        whole = lax.all_gather(value, AXES, axis=axis, tiled=True)
        size = whole.shape[axis] // SHARES
        return lax.dynamic_slice_in_dim(whole, share * size, size, axis)

    gains = pooled(jnp.stack([first_gain, second_gain]).astype(f32), 1)
    chan = pooled(jnp.concatenate([conv_taps.T, jnp.stack([conv_bias, decay_bias, inject_bias])]).astype(f32), 1)
    RD, RW = gains.shape[1], chan.shape[1]
    gain_pack = lax.dynamic_update_slice(jnp.zeros((8, PLANE * RD), f32), gains, (0, mine * RD))
    chan_pack = lax.dynamic_update_slice(
        jnp.zeros((8, 2 * PLANE * RW), f32), chan, (0, (at["c"] * PLANE + mine) * RW)
    )
    scale = jnp.exp2(-decay_exponent.astype(f32)).reshape(PLANE, width // PLANE)
    scale = jnp.concatenate([scale, scale])

    lengths = doc_lengths[0]
    ends = jnp.cumsum(lengths)
    starts = ends - lengths
    index = (at["zh"] * NL + at["zl"]) * 2 + at["c"]
    count = T * RING * NL * 2
    where = index * T - 3 + jnp.arange(T + 6, dtype=jnp.int32)
    seg = jnp.sum((ends[:, None] <= where[None, :]).astype(jnp.int32), axis=0)
    seg = jnp.where((where < 0) | (where >= count), -1, seg)
    here = seg[3 : 3 + T]
    first = jnp.any(starts[:, None] == where[None, 3 : 3 + T], axis=0)
    masks = [first]
    masks += [seg[3 - k : 3 - k + T] == here for k in (1, 2, 3)]
    masks += [seg[3 + k : 3 + k + T] == here for k in (1, 2, 3)]
    masks = jnp.stack([*masks, first]).astype(f32)
    pack = jnp.concatenate([gain_pack, masks, chan_pack], axis=1)

    weights = dict(
        zip(
            WEIGHTS,
            (branch_weight, input_weight, decay_weight, inject_weight, output_weight, mlp_gate, mlp_up, mlp_down),
            strict=True,
        )
    )
    weights = {name: pooled(value) for name, value in weights.items()}
    got = run_layer(NL, tokens[0], cotangent[0], pack, scale, weights)

    def returned(value, axis=0):
        if groups == 1:
            return value
        shape = list(value.shape)
        size = shape[axis]
        shape[axis] = size * SHARES
        whole = lax.dynamic_update_slice_in_dim(jnp.zeros(shape, bf16), value.astype(bf16), share * size, axis)
        return lax.psum_scatter(whole, AXES, scatter_dimension=axis, tiled=True).astype(f32)

    grads = [returned(got["grad_" + name]) for name in WEIGHTS]
    gain_sum = returned(lax.dynamic_slice_in_dim(got["gain_out"], mine * RD, RD, 1)[:2], 1)
    chan_sum = lax.dynamic_slice_in_dim(got["chan_out"], (at["c"] * PLANE + mine) * RW, RW, 1)
    chan_sum = returned(chan_sum[:7], 1)
    return (
        got["activations"][None],
        got["d_tokens"][None],
        *grads,
        gain_sum[0],
        gain_sum[1],
        chan_sum[:4].T,
        chan_sum[4],
        chan_sum[5],
        chan_sum[6],
    )


def solution(mesh):
    seq, dp = mesh.shape["seq"], mesh.shape["dp"]
    across = 1 << ((dp.bit_length() - 1) // 2)
    sizes = dict(zip(AXES, (RING, seq // (2 * RING), 2, dp // across // 2, 2, across // 2, 2), strict=True))
    split = Mesh(mesh.devices.reshape(tuple(sizes.values())), AXES)
    along_seq, along_dp = AXES[:3], AXES[3:]
    rows = P(along_dp, along_seq, None)
    in_specs = (rows, rows, P(along_dp, None), P(), *[P(AXES, None)] * 8, P(AXES), P(AXES), P(AXES, None), *[P(AXES)] * 3)
    out_specs = (rows, rows, *[P(AXES, None)] * 8, P(AXES), P(AXES), P(AXES, None), *[P(AXES)] * 3)
    return jax.shard_map(partial(local, sizes), mesh=split, in_specs=in_specs, out_specs=out_specs, check_vma=False)
```

```python
import itertools
import math
from functools import partial
from types import SimpleNamespace

import jax
import jax.numpy as jnp
from jax import lax
from jax.experimental import pallas as pl
from jax.experimental.pallas import tpu as pltpu
from jax.sharding import Mesh, PartitionSpec as P

f32, bf16 = jnp.float32, jnp.bfloat16
MESH = pl.DeviceIdType.MESH
AXES = ("zh", "zl", "c", "yh", "yl", "xh", "xl")
RING = 4
PLANE = 4
SHARES = RING * 2 * PLANE
SENDS = 72
RECEIVES = 181

eps_norm = 1e-06
floor_gap = 1e-05
rate_scale = 8.0
gelu_root = math.sqrt(2.0 / math.pi)
gelu_cube = 0.044715


def dot(left, right):
    return jnp.dot(left, right, preferred_element_type=f32)


def dot_nt(left, right):
    return lax.dot_general(left, right, (((1,), (1,)), ((), ())), preferred_element_type=f32)


def dot_tn(left, right):
    return lax.dot_general(left, right, (((0,), (0,)), ((), ())), preferred_element_type=f32)


def gelu_parts(v):
    t = jnp.tanh(gelu_root * (v + gelu_cube * v * v * v))
    half = 0.5 * (1.0 + t)
    slope = half + 0.5 * v * (1.0 - t * t) * gelu_root * (1.0 + 3.0 * gelu_cube * v * v)
    return v * half, slope


def minus_expm1(y):
    poly = jnp.full_like(y, 1.0 / 8.0)
    poly = 1.0 + y * poly
    for k in (7, 6, 5, 4, 3, 2):
        poly = 1.0 + y * poly * (1.0 / k)
    return jnp.where(y > -0.35, -y * poly, 1.0 - jnp.exp(y))


def inverse_rms(v):
    return lax.rsqrt(jnp.mean(v * v, axis=-1, keepdims=True) + eps_norm)


def loop(total, step, body):
    def run(j, _):
        body(pl.multiple_of(j * step, step))
        return 0

    lax.fori_loop(0, total // step, run, 0)


def layer(dims, *refs):
    T, D, W, F, CW, CF = dims.T, dims.D, dims.W, dims.F, dims.CW, dims.CF
    RD, RW, RF, NL = dims.RD, dims.RW, dims.RF, dims.NL
    M = PLANE * T
    r = SimpleNamespace(**dict(zip(dims.names, refs, strict=True)))

    zh, zl, c = lax.axis_index("zh"), lax.axis_index("zl"), lax.axis_index("c")
    yl, xl = lax.axis_index("yl"), lax.axis_index("xl")
    p = yl * 2 + xl
    px, py, pd = yl * 2 + (1 - xl), (1 - yl) * 2 + xl, (1 - yl) * 2 + (1 - xl)
    to_x, to_y, to_d = {"xl": 1 - xl}, {"yl": 1 - yl}, {"yl": 1 - yl, "xl": 1 - xl}
    plane_peers = ((px, to_x), (py, to_y), (pd, to_d))
    to_core = {"c": 1 - c}
    flat_z = zh * NL + zl
    places = RING * NL * 2
    pos = flat_z * 2 + c

    def place(at):
        return {"zh": at // (2 * NL), "zl": (at // 2) % NL, "c": at % 2}

    count = itertools.count()

    def new(n=1):
        first = next(count)
        for _ in range(n - 1):
            next(count)
        assert first + n <= dims.receives
        return first

    spare = list(range(SENDS))
    sent = []

    def push(src, dst, dev, rsem, pred=None):
        i = spare.pop(0)

        def make():
            return pltpu.make_async_remote_copy(
                src, dst, r.ss.at[i], r.rs.at[rsem], device_id=dev, device_id_type=MESH
            )

        if pred is None:
            make().start()
        else:
            pl.when(pred)(lambda: make().start())
        entry = (make, pred, i)
        sent.append(entry)
        return entry

    def settle(*entries):
        for entry in entries:
            make, pred, i = entry
            if pred is None:
                make().wait_send()
            else:
                pl.when(pred)(lambda make=make: make().wait_send())
            sent.remove(entry)
            spare.append(i)

    def arrived(dst, rsem, pred=None):
        def wait():
            pltpu.make_async_remote_copy(
                dst, dst, r.ss.at[0], r.rs.at[rsem], device_id=to_core, device_id_type=MESH
            ).wait_recv()

        if pred is None:
            wait()
        else:
            pl.when(pred)(wait)

    def keep_local(src, dst, rsem):
        pltpu.make_async_copy(src, dst, r.rs.at[rsem]).start()

    def local_wait(src, dst, rsem):
        pltpu.make_async_copy(src, dst, r.rs.at[rsem]).wait()

    results = []

    def deliver(src, dst):
        sem = new()
        keep_local(src, dst, sem)
        results.append((src, dst, sem))

    def ds(start, size, unit):
        return pl.ds(pl.multiple_of(start, unit), size)

    class Gather:
        def __init__(self, buf):
            self.buf, half = buf, buf.shape[1] // 2
            self.h0, self.h1 = pl.ds(0, half), pl.ds(half, half)
            self.rx0, self.rx1, self.ry0, self.ry1, self.rd = (new() for _ in range(5))
            self.out = []

        def start(self):
            b = self.buf
            own0, own1 = b.at[p, self.h0], b.at[p, self.h1]
            self.out.append(push(own0, own0, to_x, self.rx0))
            self.out.append(push(own1, own1, to_y, self.ry1))
            self.out.append(push(own1, own1, to_x, self.rx1))
            self.out.append(push(own0, own0, to_y, self.ry0))

        def mid(self):
            b = self.buf
            got0, got1 = b.at[px, self.h0], b.at[py, self.h1]
            arrived(got0, self.rx0)
            self.out.append(push(got0, got0, to_y, self.rd))
            arrived(got1, self.ry1)
            self.out.append(push(got1, got1, to_x, self.rd))

        def wait_x(self):
            arrived(self.buf.at[px, self.h1], self.rx1)

        def wait_y(self):
            arrived(self.buf.at[py, self.h0], self.ry0)

        def wait_d(self):
            arrived(self.buf.at[pd], self.rd)

        def end(self):
            self.wait_x()
            self.wait_y()
            self.wait_d()
            settle(*self.out)

    class Scatter:
        def __init__(self, buf, recv):
            self.buf, self.recv = buf, recv
            self.half = buf.shape[1] // 2
            self.h0, self.h1 = pl.ds(0, self.half), pl.ds(self.half, self.half)
            self.sems = [new(), new(), *[new()] * 4]
            self.out = []

        def start(self):
            b, v, s = self.buf, self.recv, self.sems
            self.out.append(push(b.at[pd, self.h0], v.at[0], to_x, s[0]))
            self.out.append(push(b.at[pd, self.h1], v.at[1], to_y, s[1]))
            self.out.append(push(b.at[px, self.h0], v.at[2], to_x, s[2]))
            self.out.append(push(b.at[py, self.h1], v.at[3], to_y, s[3]))

        def mid(self):
            b, v, s = self.buf, self.recv, self.sems
            arrived(v.at[0], s[0])
            step = 16

            def add0(o):
                b[py, pl.ds(o, step)] = (b[py, pl.ds(o, step)].astype(f32) + v[0, pl.ds(o, step)].astype(f32)).astype(bf16)

            loop(self.half, step, add0)
            self.out.append(push(b.at[py, self.h0], v.at[4], to_y, s[4]))
            arrived(v.at[1], s[1])

            def add1(o):
                q = pl.ds(pl.multiple_of(self.half + o, step), step)
                b[px, q] = (b[px, q].astype(f32) + v[1, pl.ds(o, step)].astype(f32)).astype(bf16)

            loop(self.half, step, add1)
            self.out.append(push(b.at[px, self.h1], v.at[5], to_x, s[5]))

        def end(self):
            arrived(self.recv.at[pl.ds(2, 4)], self.sems[2])
            settle(*self.out)

        def total(self, half, o, step):
            b, v = self.buf, self.recv
            own = b[p, pl.ds(pl.multiple_of(half * self.half + o, step), step)].astype(f32)
            q = pl.ds(o, step)
            return own + v[2 + half, q].astype(f32) + v[4 + half, q].astype(f32)

        def each(self, step, body):
            for half in (0, 1):
                loop(self.half, step, lambda o: body(pl.multiple_of(half * self.half + o, step), self.total(half, o, step)))

    def z_send(src, block, rz):
        out = []
        for s in (2, 1):
            out.append(push(src, block(zh), {"zh": zh + s}, rz + zh, zh + s < RING))
            out.append(push(src, block(zh), {"zh": zh - s}, rz + zh, zh - s >= 0))
        return out

    def z_forward(block, rz):
        last = RING - 1
        arrived(block(0), rz, zh == last - 1)
        one = push(block(0), block(0), {"zh": zh + 1}, rz, zh == last - 1)
        arrived(block(last), rz + last, zh == 1)
        two = push(block(last), block(last), {"zh": zh - 1}, rz + last, zh == 1)
        return [one, two]

    def z_wait(block, rz):
        last = RING - 1
        arrived(block(0), rz, (zh == 1) | (zh == last))
        arrived(block(1), rz + 1, zh != 1)
        arrived(block(2), rz + 2, zh != 2)
        arrived(block(last), rz + last, (zh == 0) | (zh == last - 1))

    class ZSum:
        def __init__(self, block, slot, add):
            self.block, self.slot, self.add = block, slot, add
            self.sems = new(4)
            self.out = []

        def send(self):
            b, v, s = self.block, self.slot, self.sems
            last = RING - 1
            o = self.out
            o.append(push(b(last), v(1), {"zh": zh + 1}, s + 1, zh == 0))
            o.append(push(b(0), v(3), {"zh": zh - 1}, s + 3, zh == last))
            o.append(push(b(zh + 2), v(1), {"zh": zh + 2}, s + 1, zh == 0))
            o.append(push(b(zh - 2), v(3), {"zh": zh - 2}, s + 3, zh == last))
            o.append(push(b(zh + 1), v(0), {"zh": zh + 1}, s + 0, zh < last))
            o.append(push(b(zh - 1), v(2), {"zh": zh - 1}, s + 2, zh > 0))

        def forward(self):
            b, v, s = self.block, self.slot, self.sems
            last = RING - 1

            def up():
                arrived(v(1), s + 1)
                self.add(last, 1)

            def down():
                arrived(v(3), s + 3)
                self.add(0, 3)

            pl.when(zh == 1)(up)
            self.out.append(push(b(last), v(1), {"zh": zh + 2}, s + 1, zh == 1))
            pl.when(zh == last - 1)(down)
            self.out.append(push(b(0), v(3), {"zh": zh - 2}, s + 3, zh == last - 1))

        def end(self):
            v, s = self.slot, self.sems
            arrived(v(0), s, zh >= 1)
            arrived(v(1), s + 1, zh >= 2)
            arrived(v(2), s + 2, zh <= 2)
            arrived(v(3), s + 3, zh <= 1)
            settle(*self.out)

        def total(self, own, parts):
            for part, pred in zip(parts, (zh >= 1, zh >= 2, zh <= 2, zh <= 1), strict=True):
                own = own + jnp.where(pred, part.astype(f32), 0.0)
            return own

    class Column:
        def __init__(self, src, w, R, C, lane0):
            self.src, self.w, self.R, self.C, self.lanes = src, w, R, C, pl.ds(lane0, C)
            self.ra, self.rz, self.rc = new(), new(4), new()
            self.out = []

        def spread(self):
            R, C, src = self.R, self.C, self.src
            dst = self.w.at[zh, c, ds(p * R, R, 16), self.lanes]
            for k, dev in plane_peers:
                self.out.append(push(src.at[:, ds(k * C, C, 128)], dst, dev, self.ra))
            keep_local(src.at[:, ds(p * C, C, 128)], dst, self.ra)

        def block(self, z):
            return self.w.at[z, c, :, self.lanes]

        def z_send(self):
            arrived(self.block(zh), self.ra)
            self.out += z_send(self.block(zh), self.block, self.rz)

        def z_forward(self):
            self.out += z_forward(self.block, self.rz)

        def z_wait(self):
            z_wait(self.block, self.rz)
            half = self.w.at[:, c, :, self.lanes]
            self.out.append(push(half, half, to_core, self.rc))

        def end(self):
            arrived(self.w.at[:, 1 - c, :, self.lanes], self.rc)
            settle(*self.out)

    class Rows:
        def __init__(self, src, w, stage, R):
            self.src, self.w, self.stage, self.R = src, w, stage, R
            self.rz, self.rp, self.rc = new(4), new(), new()
            self.out = []

        def block(self, z):
            return self.stage.at[z]

        def z_send(self):
            self.out += z_send(self.src, self.block, self.rz)

        def z_forward(self):
            self.out += z_forward(self.block, self.rz)

        def hand(self, src, k, pred):
            R = self.R
            dst = self.w.at[ds((c * PLANE + p) * R, R, 16)]
            self.out.append(push(src, dst, {"yl": k // 2, "xl": k % 2}, self.rp, pred & (k != p)))
            pl.when(pred & (k == p))(lambda: keep_local(src, dst, self.rp))

        def hand_from(self, k, pred, waited=False):
            if not waited:
                arrived(self.block(k), self.rz + k, pred)
            self.hand(self.block(k), k, pred)

        def near(self):
            self.hand(self.src, zh, zh >= 0)
            self.hand_from(zh - 1, zh >= 1)
            self.hand_from(zh + 1, zh <= RING - 2)

        def far(self):
            last = RING - 1
            self.hand_from(zh - 2, (zh >= 2) & (zh != last - 1))
            self.hand_from(zh - 2, zh == last - 1, True)
            self.hand_from(zh + 2, (zh <= last - 2) & (zh != 1))
            self.hand_from(zh + 2, zh == 1, True)
            self.hand_from(0, zh == last)
            self.hand_from(last, zh == 0)

        def plane_wait(self):
            H = PLANE * self.R
            half = self.w.at[ds(c * H, H, 16)]
            arrived(half, self.rp)
            self.out.append(push(half, half, to_core, self.rc))

        def end(self):
            H = PLANE * self.R
            arrived(self.w.at[ds((1 - c) * H, H, 16)], self.rc)
            settle(*self.out)

    class ColumnsGrad:
        def __init__(self, g, other, slots, land, R, lane0, lanes, result):
            self.g, self.other, self.slots, self.land = g, other, slots, land
            self.R, self.lanes, self.result = R, pl.ds(lane0, lanes), result
            self.rc, self.rl = new(), new()
            self.zsum = ZSum(
                lambda z: g.at[z, c, :, self.lanes], lambda k: slots.at[k, :, self.lanes], self.add_slot
            )

        def add_slot(self, z, k):
            g, q = self.g, self.lanes

            def add(o):
                s = pl.ds(o, 16)
                g[z, c, s, q] = (g[z, c, s, q].astype(f32) + self.slots[k, s, q].astype(f32)).astype(bf16)

            loop(PLANE * self.R, 16, add)

        def core_send(self):
            self.pushed = push(
                self.g.at[:, 1 - c, :, self.lanes], self.other.at[:, :, self.lanes], to_core, self.rc
            )

        def z_send(self):
            g, q = self.g, self.lanes
            arrived(self.other.at[:, :, q], self.rc)
            for z in range(RING):

                def add(o):
                    s = pl.ds(o, 16)
                    g[z, c, s, q] = (g[z, c, s, q].astype(f32) + self.other[z, s, q].astype(f32)).astype(bf16)

                loop(PLANE * self.R, 16, add)
            self.zsum.send()

        def z_forward(self):
            self.zsum.forward()

        def plane_send(self):
            g, q, R = self.g, self.lanes, self.R
            self.zsum.end()

            def add(o):
                s = pl.ds(o, 16)
                parts = [self.slots[k, s, q] for k in range(4)]
                g[zh, c, s, q] = self.zsum.total(g[zh, c, s, q].astype(f32), parts).astype(bf16)

            loop(PLANE * R, 16, add)
            dst = self.land.at[p, :, q]
            self.out = [self.pushed]
            for k, dev in plane_peers:
                self.out.append(push(g.at[zh, c, ds(k * R, R, 16), q], dst, dev, self.rl))
            keep_local(g.at[zh, c, ds(p * R, R, 16), q], dst, self.rl)

        def end(self):
            arrived(self.land.at[:, :, self.lanes], self.rl)
            settle(*self.out)
            deliver(self.land.at[:, :, self.lanes], self.result.at[:, :, self.lanes])

    class RowsGrad:
        def __init__(self, g, other, stage, slots, R, total, result):
            self.g, self.other, self.stage, self.slots, self.R = g, other, stage, slots, R
            self.sum, self.result = total, result
            self.rc, self.rl = new(), new()
            self.zsum = ZSum(lambda z: stage.at[z], lambda k: slots.at[k], self.add_slot)

        def add_slot(self, z, k):
            g = self.stage

            def add(o):
                s = pl.ds(o, 16)
                g[z, s] = (g[z, s].astype(f32) + self.slots[k, s].astype(f32)).astype(bf16)

            loop(self.R, 16, add)

        def core_send(self):
            H = PLANE * self.R
            self.out = [push(self.g.at[ds((1 - c) * H, H, 16)], self.other, to_core, self.rc)]

        def plane_send(self):
            R, H, g = self.R, PLANE * self.R, self.g
            arrived(self.other, self.rc)

            def add(o):
                s = ds(c * H + o, 16, 16)
                g[s] = (g[s].astype(f32) + self.other[pl.ds(o, 16)].astype(f32)).astype(bf16)

            loop(H, 16, add)
            dst = self.stage.at[p]
            for k, dev in plane_peers:
                self.out.append(push(g.at[ds(c * H + k * R, R, 16)], dst, dev, self.rl))
            keep_local(g.at[ds(c * H + p * R, R, 16)], dst, self.rl)

        def z_send(self):
            arrived(self.stage, self.rl)
            self.zsum.send()

        def z_forward(self):
            self.zsum.forward()

        def end(self):
            self.zsum.end()
            settle(*self.out)

            def add(o):
                s = pl.ds(o, 16)
                self.sum[s] = self.zsum.total(self.stage[zh, s].astype(f32), [self.slots[k, s] for k in range(4)])

            loop(self.R, 16, add)
            deliver(self.sum, self.result)

    class Carry:
        def __init__(self, own, sib, buf, later):
            self.own, self.sib, self.buf, self.later = own, sib, buf, later
            self.rc, self.rz = new(), new(RING * NL)
            self.out = []

        def order(self):
            return range(RING * NL) if self.later else reversed(range(RING * NL))

        def send_core(self):
            self.out.append(push(self.own, self.sib, to_core, self.rc))

        def send(self):
            arrived(self.sib, self.rc)
            own, sib = self.own[...], self.sib[...]
            near = (c == 0) if self.later else (c == 1)
            head, tail = jnp.where(near, own, sib), jnp.where(near, sib, own)
            self.buf[flat_z, 0:PLANE] = tail[0:PLANE] * head[0:PLANE]
            self.buf[flat_z, PLANE : 2 * PLANE] = (
                tail[0:PLANE] * head[PLANE : 2 * PLANE] + tail[PLANE : 2 * PLANE]
            )
            part = self.buf.at[flat_z]
            for at in self.order():
                pred = (flat_z < at) if self.later else (flat_z > at)
                self.out.append(push(part, part, {"zh": at // NL, "zl": at % NL}, self.rz + flat_z, pred))

        def fold(self, into):
            into[...] = jnp.zeros_like(into)

            def take(part):
                into[0:PLANE] = part[0:PLANE] * into[0:PLANE] + part[PLANE : 2 * PLANE]

            for at in self.order():
                pred = (flat_z > at) if self.later else (flat_z < at)

                def chip(at=at):
                    arrived(self.buf.at[at], self.rz + at)
                    take(self.buf[at])

                pl.when(pred)(chip)
            pl.when((c == 1) if self.later else (c == 0))(lambda: take(self.sib[...]))
            settle(*self.out)

    GL = PLANE * RD
    ring = zh * 2 + c
    home = {"yl": zh // 2, "xl": zh % 2}

    def ring_place(at):
        return {"zh": at // 2, "c": at % 2}

    class Small:
        def __init__(self):
            self.rr, self.rk = new(), new()
            self.out = []

        def one(self):
            for at in range(2 * RING):
                self.out.append(push(r.pack, r.pr.at[ring], ring_place(at), self.rr, ring != at))
            keep_local(r.pack, r.pr.at[ring], self.rr)

        def two(self):
            arrived(r.pr, self.rr)
            for _, dev in plane_peers:
                self.out.append(push(r.pr, r.pp.at[p], dev, self.rk))
            keep_local(r.pr, r.pp.at[p], self.rk)

        def three(self):
            arrived(r.pp, self.rk)
            from_row = lax.broadcasted_iota(jnp.int32, (128, GL), 0)
            to_lane = lax.broadcasted_iota(jnp.int32, (128, GL), 1)
            whole = jnp.zeros((2 * RING * 16, GL), f32)
            for k in range(PLANE):
                move = ((to_lane == from_row + k * RD) & (from_row < RD)).astype(bf16)
                whole = whole + dot(r.pp[k].reshape(2 * RING * 16, 128), move)
            for at in range(2 * RING):
                r.gains[0:2, at * GL : (at + 1) * GL] = whole[at * 16 : at * 16 + 2]
            from_row = lax.broadcasted_iota(jnp.int32, (128, CW), 0)
            to_lane = lax.broadcasted_iota(jnp.int32, (128, CW), 1)
            whole = jnp.zeros((16, CW), f32)
            for k in range(PLANE):
                for cc in (0, 1):
                    move = ((to_lane == from_row + (cc * PLANE + k) * RW) & (from_row < RW)).astype(bf16)
                    whole = whole + dot(r.pp[k, 2 * p + cc], move)
            r.chan[...] = whole[2:10]
            rate = r.pack[...].astype(f32)
            for k in range(CW // 128):
                r.chan[7:8, k * 128 : (k + 1) * 128] = jnp.exp2(-rate[11 + k : 12 + k])

        def four(self):
            where = lax.broadcasted_iota(jnp.int32, (T, 128), 0).astype(f32) + (pos * T).astype(f32)
            for k in range(PLANE):
                part = r.pp[k, 0].astype(f32)
                starts, ends = [], []
                total = jnp.zeros((1, 1), f32)
                for j in range(dims.SEGS):
                    starts.append(total)
                    total = total + part[9:10, j : j + 1] * 256.0 + part[10:11, j : j + 1]
                    ends.append(total)

                def seg(shift):
                    at = where + float(shift)
                    value = jnp.zeros((T, 128), f32)
                    for end in ends:
                        value = value + jnp.where(at >= end, 1.0, 0.0)
                    return jnp.where((at < 0.0) | (at >= float(T * places)), -1.0, value)

                here = seg(0)
                rows = pl.ds(k * T, T)
                first = jnp.zeros((T, 128), f32)
                for start in starts:
                    first = jnp.where(where == start, 1.0, first)
                r.masks[0, rows] = first
                for j in (1, 2, 3):
                    r.masks[j, rows] = jnp.where(seg(-j) == here, 1.0, 0.0)
                    r.masks[3 + j, rows] = jnp.where(seg(j) == here, 1.0, 0.0)
            settle(*self.out)

    class SmallGrad:
        def __init__(self):
            self.rg, self.rc, self.rp, self.ro = new(2 * RING), new(2 * RING), new(PLANE), new()
            self.out = []

        def chan_one(self):
            for cc in (0, 1):
                self.out.append(
                    push(r.gchan, r.gc.at[ring], {"zh": p, "c": cc}, self.rc + ring, (zh != p) | (c != cc))
                )

        def chan_two(self):
            def total():
                r.gc[ring] = r.gchan[...]
                value = r.gchan[...]
                for at in range(2 * RING):
                    arrived(r.gc.at[at], self.rc + at, ring != at)
                value = r.gc[0]
                for at in range(1, 2 * RING):
                    value = value + r.gc[at]
                r.chan_sum[...] = value

            pl.when(p == zh)(total)
            for _, dev in plane_peers:
                self.out.append(push(r.chan_sum, r.chan_sum, dev, self.ro, p == zh))

        def gain_one(self):
            for at in range(2 * RING):
                src = r.ggain.at[:, pl.ds(at * GL, GL)]
                self.out.append(push(src, r.gg.at[ring], ring_place(at), self.rg + ring, ring != at))

        def gain_two(self):
            r.gg[ring] = r.ggain[:, ds(ring * GL, GL, 128)]
            for at in range(2 * RING):
                arrived(r.gg.at[at], self.rg + at, ring != at)
            value = r.gg[0]
            for at in range(1, 2 * RING):
                value = value + r.gg[at]
            r.gp[p] = value
            for _, dev in plane_peers:
                self.out.append(push(r.gp.at[p], r.gp.at[p], dev, self.rp + p))

        def end(self):
            for k, _ in plane_peers:
                arrived(r.gp.at[k], self.rp + k)
            gains = (r.gp[0] + r.gp[1]) + (r.gp[2] + r.gp[3])
            from_lane = lax.broadcasted_iota(jnp.int32, (GL, 128), 0)
            to_lane = lax.broadcasted_iota(jnp.int32, (GL, 128), 1)
            move = (from_lane == to_lane + p * RD).astype(f32)
            r.small_sum[0:8] = jnp.dot(gains, move, precision=lax.Precision.HIGHEST)
            arrived(r.chan_sum, self.ro, p != zh)
            from_lane = lax.broadcasted_iota(jnp.int32, (CW, 128), 0)
            to_lane = lax.broadcasted_iota(jnp.int32, (CW, 128), 1)
            move = (from_lane == to_lane + (c * PLANE + p) * RW).astype(f32)
            r.small_sum[8:16] = jnp.dot(r.chan_sum[...], move, precision=lax.Precision.HIGHEST)
            deliver(r.small_sum, r.small_out)
            settle(*self.out)

    barrier = pltpu.get_barrier_semaphore()
    for _, dev in plane_peers:
        pl.semaphore_signal(barrier, 1, device_id=dev, device_id_type=MESH)
    for at in range(places):

        @pl.when(pos != at)
        def _(at=at):
            pl.semaphore_signal(barrier, 1, device_id=place(at), device_id_type=MESH)

    first_loads = [
        (src, dst, new())
        for src, dst in (
            (r.pack_in, r.pack),
            (r.tokens, r.x_all.at[p]),
            (r.cotangent, r.cot_all.at[p]),
        )
    ]
    for load in first_loads:
        keep_local(*load)

    w_i, w_b = Column(r.input_weight, r.w_ib, RD, CW, 0), Column(r.branch_weight, r.w_ib, RD, CW, CW)
    w_d, w_j = Column(r.decay_weight, r.w_di, RW, CW, 0), Column(r.inject_weight, r.w_di, RW, CW, CW)
    w_g, w_u = Column(r.mlp_gate, r.w_gu, RD, CF, 0), Column(r.mlp_up, r.w_gu, RD, CF, CF)
    w_o, w_dn = Rows(r.output_weight, r.w_o, r.st_o, RW), Rows(r.mlp_down, r.w_dn, r.st_dn, RF)
    ag_x, ag_conv, ag_two = Gather(r.x_all), Gather(r.conv), Gather(r.n_two)
    ag_cot, ag_out = Gather(r.cot_all), Gather(r.d_out)
    small, small_grad = Small(), SmallGrad()
    after, before = flat_z + c, flat_z - (1 - c)
    to_next = {"zh": after // NL, "zl": after % NL, "c": 1 - c}
    to_prev = {"zh": before // NL, "zl": before % NL, "c": 1 - c}
    step = 256
    chunk = PLANE * RD * 2

    pl.semaphore_wait(barrier, len(plane_peers) + places - 1)
    local_wait(*first_loads[0])
    small.one()
    w_i.spread()
    local_wait(*first_loads[1])
    ag_x.start()
    halo_x = new()
    sent_x = push(r.x_all.at[p, pl.ds(T - 16, 16)], r.x_halo.at[p], to_next, halo_x, pos < places - 1)
    w_o.z_send()
    small.two()
    w_i.z_send()
    w_d.spread()

    @pl.when(pos == 0)
    def _():
        r.x_halo[p] = jnp.zeros((16, D), bf16)

    arrived(r.x_halo.at[p], halo_x, pos > 0)
    halo_p = new(PLANE)
    sent_p = [push(r.x_halo.at[p], r.x_halo.at[p], dev, halo_p + p) for _, dev in plane_peers]
    ag_x.mid()
    w_j.spread()
    w_b.spread()
    local_wait(*first_loads[2])
    small.three()

    def norm_block(k):
        def norm_one(o):
            s = pl.ds(o, 32)
            v = r.x_all[k, s].astype(f32)
            r.n_one[k, s] = (v * inverse_rms(v) * r.gains[0:1]).astype(bf16)

        loop(T, 32, norm_one)

    norm_block(p)
    w_o.z_forward()
    w_d.z_send()
    ag_x.wait_x()
    norm_block(px)
    ag_x.wait_y()
    norm_block(py)
    w_i.z_forward()
    small.four()
    for k, _ in plane_peers:
        arrived(r.x_halo.at[k], halo_p + k)
    v = r.x_halo[...].reshape(PLANE * 16, D).astype(f32)
    r.n_halo[...] = (v * inverse_rms(v) * r.gains[0:1]).astype(bf16).reshape(PLANE, 16, D)
    ag_x.wait_d()
    norm_block(pd)
    settle(*ag_x.out, sent_x, *sent_p)
    w_i.z_wait()
    w_g.spread()
    w_i.end()

    def weight_ib(lanes):
        return r.w_ib[:, :, :, lanes].reshape(D, CW)

    lanes_a, lanes_b = pl.ds(0, CW), pl.ds(CW, CW)
    halo = dot(r.n_halo[...].reshape(PLANE * 16, D), weight_ib(lanes_a)).astype(bf16).astype(f32)
    body = dot(r.n_one[...].reshape(M, D), weight_ib(lanes_a)).astype(bf16).astype(f32)
    for k in range(PLANE):
        r.u[k, 0:8] = halo[k * 16 + 8 : (k + 1) * 16]
        r.u[k, 8 : 8 + T] = body[k * T : (k + 1) * T]

    def wide(j, rows):
        return jnp.concatenate([r.masks[j, rows]] * (CW // 128), axis=1) > 0.5

    def convolve(o):
        for k in range(PLANE):
            ext = r.u[k, pl.ds(o, 24)]
            rows = ds(k * T + o, 16, 16)
            total = r.chan[4:5] + r.chan[0:1] * ext[8:24]
            for j in range(1, 4):
                total = total + jnp.where(wide(j, rows), r.chan[j : j + 1] * ext[8 - j : 24 - j], 0.0)
            r.conv[p, rows] = total.astype(bf16)

    loop(T, 16, convolve)
    ag_conv.start()
    w_d.z_forward()
    w_j.z_send()
    ag_conv.mid()
    w_d.z_wait()
    w_b.z_send()
    w_d.end()

    def pre(q, lanes):
        return dot(r.conv[q], r.w_di[q, :, :, lanes].reshape(W // RING, CW))

    r.pair[:, 0:CW] = pre(p, lanes_a)
    ag_conv.wait_x()
    r.pair[:, 0:CW] += pre(px, lanes_a)
    ag_conv.wait_y()
    r.pair[:, 0:CW] += pre(py, lanes_a)
    w_j.z_forward()
    w_g.z_send()
    ag_conv.wait_d()
    r.pair[:, 0:CW] += pre(pd, lanes_a)
    settle(*ag_conv.out)
    w_u.spread()
    w_o.near()
    w_o.far()
    w_j.z_wait()
    ag_cot.start()
    w_j.end()
    r.pair[:, CW : 2 * CW] = pre(0, lanes_b)
    for q in range(1, PLANE):
        r.pair[:, CW : 2 * CW] += pre(q, lanes_b)

    def decay_terms(s, rg):
        log_a = -rate_scale * rg * r.chan[7:8]
        gap = minus_expm1(2.0 * log_a)
        first = wide(0, s)
        return log_a, gap, jnp.where(first, 1.0, jnp.sqrt(jnp.maximum(gap, floor_gap))), first

    def gates_two(o):
        s = pl.ds(o, 16)
        rg = jax.nn.sigmoid(r.pair[s, 0:CW] + r.chan[5:6])
        ig = jax.nn.sigmoid(r.pair[s, CW : 2 * CW] + r.chan[6:7])
        log_a, _, mult, first = decay_terms(s, rg)
        r.rgate[s], r.igate[s] = rg, ig
        r.decay[s] = jnp.where(first, 0.0, jnp.exp(log_a))
        r.work[s] = mult * ig * r.conv[p, s].astype(f32)

    loop(M, 16, gates_two)
    row = lax.broadcasted_iota(jnp.int32, (8, CW), 0)

    def scan_forward(j, carry):
        out = []
        for k in range(PLANE):
            s = ds(k * T + j * 8, 8, 8)
            a, b = r.decay[s], r.work[s]
            for n in (1, 2, 4):
                a_b = jnp.where(row >= n, pltpu.roll(a, n, 0), 1.0)
                b_b = jnp.where(row >= n, pltpu.roll(b, n, 0), 0.0)
                a, b = a * a_b, a * b_b + b
            total, prod = b + a * carry[2 * k], a * carry[2 * k + 1]
            r.state[k, ds(8 + j * 8, 8, 8)] = total
            r.cum[s] = prod
            out += [total[7:8], prod[7:8]]
        return tuple(out)

    zero, one = jnp.zeros((1, CW), f32), jnp.ones((1, CW), f32)
    ends = lax.fori_loop(0, T // 8, scan_forward, (zero, one) * PLANE)
    carry_f = Carry(r.own_f, r.sib_f, r.carry_f, True)
    for k in range(PLANE):
        r.own_f[k : k + 1] = ends[2 * k + 1]
        r.own_f[PLANE + k : PLANE + k + 1] = ends[2 * k]
    carry_f.send_core()
    w_b.z_forward()
    w_b.z_wait()
    carry_f.send()
    w_o.plane_wait()
    ag_cot.mid()
    w_b.end()
    r.work[...] = dot(r.n_one[...].reshape(M, D), weight_ib(lanes_b))

    def gates_one(o):
        s = pl.ds(o, 16)
        r.gated[s], r.slope[s] = gelu_parts(r.work[s])

    loop(M, 16, gates_one)
    w_o.end()
    carry_f.fold(r.into)
    for k in range(PLANE):
        r.state[k, 0:8] = jnp.broadcast_to(r.into[k : k + 1], (8, CW))

    def mix(o):
        for k in range(PLANE):
            s, t = ds(k * T + o, 16, 16), ds(8 + o, 16, 8)
            state = r.state[k, t] + r.cum[s] * r.into[k : k + 1]
            r.state[k, t] = state
            r.mixed[s] = (state * r.gated[s]).astype(bf16)

    loop(T, 16, mix)

    def out_part(o):
        q = pl.ds(o, step)
        r.part[:, :, q] = dot(r.mixed[...], r.w_o[:, q]).astype(bf16).reshape(PLANE, T, step)

    loop(D, step, out_part)
    rs_one = Scatter(r.part, r.got_one)
    rs_one.start()
    w_g.z_forward()
    w_u.z_send()
    ag_cot.end()
    rs_one.mid()
    rs_one.end()

    def norm_two(o, summed):
        s = pl.ds(o, 16)
        v = r.x_all[p, s].astype(f32) + summed
        r.x_one[s] = v
        r.n_two[p, s] = (v * inverse_rms(v) * r.gains[1:2]).astype(bf16)

    rs_one.each(16, norm_two)
    ag_two.start()
    w_g.z_wait()
    w_dn.z_send()
    ag_two.mid()
    w_u.z_forward()
    w_g.end()
    ag_two.end()

    def mlp_in(o):
        q = pl.ds(o, step)
        r.pair[:, q] = dot(r.n_two[...].reshape(M, D), r.w_gu[:, :, :, q].reshape(D, step))

    loop(CF, step, mlp_in)
    w_u.z_wait()
    w_u.end()
    loop(CF, step, lambda o: mlp_in(pl.multiple_of(CF + o, step)))

    def gates_mlp(o):
        s = pl.ds(o, 16)
        value, slope = gelu_parts(r.pair[s, 0:CF])
        up = r.pair[s, CF : 2 * CF]
        r.hidden[s] = (value * up).astype(bf16)
        r.pair[s, 0:CF] = slope * up
        r.pair[s, CF : 2 * CF] = value

    loop(M, 16, gates_mlp)
    w_dn.near()

    def grad_down(o):
        q = pl.ds(o, step)
        r.g_dn[q] = dot_tn(r.hidden[:, q], r.cot_all[...].reshape(M, D)).astype(bf16)

    loop(CF, step, grad_down)
    g_dn = RowsGrad(r.g_dn, r.h_dn, r.sg_dn, r.z_dn, RF, r.t_dn, r.grad_mlp_down)
    g_dn.core_send()
    w_dn.z_forward()
    w_dn.far()
    w_dn.plane_wait()
    g_dn.plane_send()
    w_dn.end()

    for k in range(CF // step):
        q = pl.ds(k * step, step)
        back = dot_nt(r.cot_all[...].reshape(M, D), r.w_dn[q])
        r.d_pair[:, k * step : (k + 1) * step] = (back * r.pair[:, k * step : (k + 1) * step]).astype(bf16)
        r.d_pair[:, CF + k * step : CF + (k + 1) * step] = (
            back * r.pair[:, CF + k * step : CF + (k + 1) * step]
        ).astype(bf16)

    def d_two_part(z, _):
        q = ds(z * chunk, chunk, chunk)
        r.part[:, :, q] = (
            dot_nt(r.d_pair[...], r.w_gu[z].reshape(chunk, 2 * CF)).astype(bf16).reshape(PLANE, T, chunk)
        )
        return 0

    lax.fori_loop(0, RING, d_two_part, 0)
    rs_two = Scatter(r.part, r.got_two)
    rs_two.start()

    def grad_gate_up(lane0):
        lanes = pl.ds(lane0, CF)

        def run(z, _):
            q = ds(z * chunk, chunk, chunk)
            value = dot_tn(r.n_two[:, :, q].reshape(M, chunk), r.d_pair[:, lanes])
            r.w_gu[z, :, :, lanes] = value.astype(bf16).reshape(2, chunk // 2, CF)
            return 0

        lax.fori_loop(0, RING, run, 0)

    grad_gate_up(0)
    g_g = ColumnsGrad(r.w_gu, r.h_gu, r.z_gu, r.l_gu, RD, 0, CF, r.grads_gu)
    g_g.core_send()
    rs_two.mid()
    grad_gate_up(CF)
    g_u = ColumnsGrad(r.w_gu, r.h_gu, r.z_gu, r.l_gu, RD, CF, CF, r.grads_gu)
    g_u.core_send()
    g_dn.z_send()
    g_g.z_send()

    def act_part(o):
        q = pl.ds(o, step)
        r.part_act[:, :, q] = dot(r.hidden[...], r.w_dn[:, q]).astype(bf16).reshape(PLANE, T, step)

    loop(D, step, act_part)
    r.ggain[...] = jnp.zeros_like(r.ggain)
    r.gchan[...] = jnp.zeros_like(r.gchan)
    rs_two.end()

    def norm_two_back(o, d_two):
        s = pl.ds(o, 16)
        v = r.x_one[s]
        rs = inverse_rms(v)
        z = v * rs
        dz = d_two * r.gains[1:2]
        r.ggain[1:2] += jnp.sum(d_two * z, axis=0, keepdims=True)
        d_one = r.cot_all[p, s].astype(f32) + rs * (dz - z * jnp.mean(dz * z, axis=-1, keepdims=True))
        r.d_one[s] = d_one
        r.d_out[p, s] = d_one.astype(bf16)

    rs_two.each(16, norm_two_back)
    ag_out.start()
    g_u.z_send()
    ag_out.mid()
    g_dn.z_forward()
    ag_out.end()
    rs_act = Scatter(r.part_act, r.got_act)
    rs_act.start()

    r.work[...] = dot_nt(r.d_out[...].reshape(M, D), r.w_o[...])

    def split(o):
        for k in range(PLANE):
            s = ds(k * T + o, 16, 16)
            d_mixed = r.work[s]
            r.d_gu[s, CW : 2 * CW] = (d_mixed * r.state[k, ds(8 + o, 16, 8)] * r.slope[s]).astype(bf16)
            r.work[s] = d_mixed * r.gated[s]

    loop(T, 16, split)

    def scan_backward(i, carry):
        j = T // 8 - 1 - i
        out = []
        for k in range(PLANE):
            s = ds(k * T + j * 8, 8, 8)
            decay, b = r.decay[s], r.work[s]
            a = jnp.where(row < 7, pltpu.roll(decay, 7, 0), carry[3 * k + 2])
            for n in (1, 2, 4):
                a_b = jnp.where(row < 8 - n, pltpu.roll(a, 8 - n, 0), 1.0)
                b_b = jnp.where(row < 8 - n, pltpu.roll(b, 8 - n, 0), 0.0)
                a, b = a * a_b, a * b_b + b
            total, prod = b + a * carry[3 * k], a * carry[3 * k + 1]
            r.work[s], r.cum[s] = total, prod
            out += [total[0:1], prod[0:1], decay[0:1]]
        return tuple(out)

    heads = lax.fori_loop(0, T // 8, scan_backward, (zero, one, one) * PLANE)
    carry_b = Carry(r.own_b, r.sib_b, r.carry_b, False)
    for k in range(PLANE):
        r.own_b[k : k + 1] = r.own_f[k : k + 1]
        r.own_b[PLANE + k : PLANE + k + 1] = heads[3 * k] * heads[3 * k + 2]
    carry_b.send_core()

    def grad_out(o):
        q = pl.ds(o, 128)
        r.w_o[q] = dot_tn(r.mixed[:, q], r.d_out[...].reshape(M, D)).astype(bf16)

    loop(CW, 128, grad_out)
    g_o = RowsGrad(r.w_o, r.h_o, r.sg_o, r.z_o, RW, r.t_o, r.grad_output_weight)
    g_o.core_send()
    carry_b.send()
    rs_act.mid()

    def d_branch_part(z, _):
        q = ds(z * chunk, chunk, chunk)
        r.part[:, :, q] = (
            dot_nt(r.d_gu[:, lanes_b], r.w_ib[z, :, :, lanes_b].reshape(chunk, CW))
            .astype(bf16)
            .reshape(PLANE, T, chunk)
        )
        value = dot_tn(r.n_one[:, :, q].reshape(M, chunk), r.d_gu[:, lanes_b])
        r.w_ib[z, :, :, lanes_b] = value.astype(bf16).reshape(2, chunk // 2, CW)
        return 0

    lax.fori_loop(0, RING, d_branch_part, 0)
    g_b = ColumnsGrad(r.w_ib, r.h_ib, r.z_ib, r.l_ib, RD, CW, CW, r.grads_ib)
    g_b.core_send()
    g_o.plane_send()
    g_b.z_send()
    g_g.z_forward()
    carry_b.fold(r.into)

    def back(o):
        sums = [jnp.zeros((1, CW), f32)] * 2
        for k in range(PLANE):
            s = ds(k * T + o, 16, 16)
            adjoint = r.work[s] + r.cum[s] * r.into[k : k + 1]
            previous = r.state[k, pl.ds(o, 24)][7:23]
            rg, ig, decay, conv = r.rgate[s], r.igate[s], r.decay[s], r.conv[p, s].astype(f32)
            _, gap, mult, first = decay_terms(s, rg)
            d_mult = jnp.where(first, 0.0, adjoint * ig * conv)
            d_log = adjoint * previous * decay - jnp.where(gap > floor_gap, (1.0 - gap) * d_mult / mult, 0.0)
            d_decay = (-rate_scale * r.chan[7:8] * d_log * rg * (1.0 - rg)).astype(bf16)
            d_inject = (adjoint * mult * conv * ig * (1.0 - ig)).astype(bf16)
            r.d_pre[s, 0:CW] = d_decay
            r.d_pre[s, CW : 2 * CW] = d_inject
            sums[0] = sums[0] + jnp.sum(d_decay.astype(f32), axis=0, keepdims=True)
            sums[1] = sums[1] + jnp.sum(d_inject.astype(f32), axis=0, keepdims=True)
            r.d_conv[k, pl.ds(o, 16)] = adjoint * mult * ig
        r.gchan[5:6] += sums[0]
        r.gchan[6:7] += sums[1]

    loop(T, 16, back)

    def conv_part(q, _):
        r.part_conv[q] = dot_nt(r.d_pre[...], r.w_di[q].reshape(W // RING, 2 * CW)).astype(bf16)
        return 0

    lax.fori_loop(0, RING, conv_part, 0)
    rs_act.end()
    rs_conv = Scatter(r.part_conv, r.got_conv)
    rs_conv.start()

    def finish_act(o, summed):
        s = pl.ds(o, 16)
        r.act[s] = (r.x_one[s] + summed).astype(bf16)

    rs_act.each(16, finish_act)
    deliver(r.act, r.activations)
    g_o.z_send()
    g_u.z_forward()
    g_dn.end()

    def grad_dec_inj(lanes):
        def run(q, _):
            value = dot_tn(r.conv[q], r.d_pre[:, lanes])
            r.w_di[q, :, :, lanes] = value.astype(bf16).reshape(2, W // SHARES * PLANE, CW)
            return 0

        lax.fori_loop(0, RING, run, 0)

    grad_dec_inj(lanes_a)
    g_d = ColumnsGrad(r.w_di, r.h_di, r.z_di, r.l_di, RW, 0, CW, r.grads_di)
    g_d.core_send()
    rs_conv.mid()
    grad_dec_inj(lanes_b)
    g_j = ColumnsGrad(r.w_di, r.h_di, r.z_di, r.l_di, RW, CW, CW, r.grads_di)
    g_j.core_send()
    g_d.z_send()
    g_b.z_forward()
    g_g.plane_send()
    rs_conv.end()

    for half in (0, 1):

        def add_conv(o, half=half):
            for k in (2 * half, 2 * half + 1):
                at = (k - 2 * half) * T + o
                r.d_conv[k, pl.ds(o, 16)] += rs_conv.total(half, pl.multiple_of(at, 16), 16)

        loop(T, 16, add_conv)
    halo_b = new()
    for k in range(PLANE):
        r.halo_out[4 * k : 4 * k + 4] = r.d_conv[k, 0:4]
    sent_b = push(r.halo_out, r.halo_in, to_prev, halo_b, pos > 0)
    g_j.z_send()

    def taps_back(o):
        sums = [jnp.zeros((1, CW), f32)] * 5
        for k in range(PLANE):
            ext = r.u[k, pl.ds(o, 24)]
            rows = ds(k * T + o, 16, 16)
            dc = r.d_conv[k, pl.ds(o, 16)]
            sums[4] = sums[4] + jnp.sum(dc, axis=0, keepdims=True)
            sums[0] = sums[0] + jnp.sum(dc * ext[8:24], axis=0, keepdims=True)
            for j in range(1, 4):
                term = jnp.where(wide(j, rows), dc * ext[8 - j : 24 - j], 0.0)
                sums[j] = sums[j] + jnp.sum(term, axis=0, keepdims=True)
        for j in range(5):
            r.gchan[j : j + 1] += sums[j]

    loop(T, 16, taps_back)
    small_grad.chan_one()

    @pl.when(pos == places - 1)
    def _():
        r.halo_in[...] = jnp.zeros((16, CW), f32)

    arrived(r.halo_in, halo_b, pos < places - 1)
    for k in range(PLANE):
        r.d_conv[k, T : T + 8] = jnp.concatenate([r.halo_in[4 * k : 4 * k + 4], jnp.zeros((4, CW), f32)], axis=0)

    def conv_back(o):
        for k in range(PLANE):
            ext = r.d_conv[k, pl.ds(o, 24)]
            rows = ds(k * T + o, 16, 16)
            total = r.chan[0:1] * ext[0:16]
            for j in range(1, 4):
                total = total + jnp.where(wide(3 + j, rows), r.chan[j : j + 1] * ext[j : 16 + j], 0.0)
            r.d_gu[rows, 0:CW] = total.astype(bf16)

    loop(T, 16, conv_back)

    def d_input_part(z, _):
        q = ds(z * chunk, chunk, chunk)
        value = dot_nt(r.d_gu[:, lanes_a], r.w_ib[z, :, :, lanes_a].reshape(chunk, CW)).reshape(PLANE, T, chunk)
        r.part[:, :, q] = (r.part[:, :, q].astype(f32) + value).astype(bf16)
        return 0

    lax.fori_loop(0, RING, d_input_part, 0)
    rs_three = Scatter(r.part, r.got_three)
    rs_three.start()

    def grad_input(z, _):
        q = ds(z * chunk, chunk, chunk)
        value = dot_tn(r.n_one[:, :, q].reshape(M, chunk), r.d_gu[:, lanes_a])
        r.w_ib[z, :, :, lanes_a] = value.astype(bf16).reshape(2, chunk // 2, CW)
        return 0

    lax.fori_loop(0, RING, grad_input, 0)
    g_i = ColumnsGrad(r.w_ib, r.h_ib, r.z_ib, r.l_ib, RD, 0, CW, r.grads_ib)
    g_i.core_send()
    rs_three.mid()
    g_o.z_forward()
    g_i.z_send()
    g_u.plane_send()
    g_d.z_forward()
    g_b.plane_send()
    small_grad.chan_two()
    rs_three.end()

    def norm_one_back(o, d_n):
        s = pl.ds(o, 16)
        v = r.x_all[p, s].astype(f32)
        rs = inverse_rms(v)
        z = v * rs
        dz = d_n * r.gains[0:1]
        r.ggain[0:1] += jnp.sum(d_n * z, axis=0, keepdims=True)
        r.d_x[s] = r.d_one[s] + rs * (dz - z * jnp.mean(dz * z, axis=-1, keepdims=True))

    rs_three.each(16, norm_one_back)
    deliver(r.d_x, r.d_tokens)
    small_grad.gain_one()
    settle(sent_b)
    g_j.z_forward()
    g_i.z_forward()
    g_g.end()
    g_u.end()
    g_d.plane_send()
    g_o.end()
    small_grad.gain_two()
    g_b.end()
    g_j.plane_send()
    g_i.plane_send()
    g_d.end()
    small_grad.end()
    g_j.end()
    g_i.end()
    assert not sent
    for result in results:
        local_wait(*result)


WEIGHTS = (
    "branch_weight",
    "input_weight",
    "decay_weight",
    "inject_weight",
    "output_weight",
    "mlp_gate",
    "mlp_up",
    "mlp_down",
)


def run_layer(NL, SEGS, tokens, cotangent, pack, weights):
    T, D = tokens.shape
    W, F = weights["branch_weight"].shape[1], weights["mlp_gate"].shape[1]
    CW, CF = W // PLANE, F // PLANE
    RD, RW, RF = D // SHARES, W // SHARES, F // SHARES
    GL, M, places = PLANE * RD, PLANE * T, RING * NL * 2
    hbm = pl.BlockSpec(memory_space=pl.ANY)
    ins = ["tokens", "cotangent", "pack_in", *WEIGHTS]
    outs = {
        "activations": ((T, D), bf16),
        "d_tokens": ((T, D), f32),
        "grads_ib": ((PLANE, RD, 2 * CW), bf16),
        "grads_di": ((PLANE, RW, 2 * CW), bf16),
        "grads_gu": ((PLANE, RD, 2 * CF), bf16),
        "grad_output_weight": ((RW, D), f32),
        "grad_mlp_down": ((RF, D), f32),
        "small_out": ((16, 128), f32),
    }
    scratch = {
        "w_ib": ((RING, 2, PLANE * RD, 2 * CW), bf16),
        "w_di": ((RING, 2, PLANE * RW, 2 * CW), bf16),
        "w_gu": ((RING, 2, PLANE * RD, 2 * CF), bf16),
        "w_o": ((CW, D), bf16),
        "w_dn": ((CF, D), bf16),
        "st_o": ((RING, RW, D), bf16),
        "st_dn": ((RING, RF, D), bf16),
        "h_ib": ((RING, PLANE * RD, 2 * CW), bf16),
        "h_di": ((RING, PLANE * RW, 2 * CW), bf16),
        "h_gu": ((RING, PLANE * RD, 2 * CF), bf16),
        "h_o": ((CW // 2, D), bf16),
        "h_dn": ((CF // 2, D), bf16),
        "z_ib": ((4, PLANE * RD, 2 * CW), bf16),
        "z_di": ((4, PLANE * RW, 2 * CW), bf16),
        "z_gu": ((4, PLANE * RD, 2 * CF), bf16),
        "z_o": ((4, RW, D), bf16),
        "z_dn": ((4, RF, D), bf16),
        "l_ib": ((PLANE, RD, 2 * CW), bf16),
        "l_di": ((PLANE, RW, 2 * CW), bf16),
        "l_gu": ((PLANE, RD, 2 * CF), bf16),
        "sg_o": ((RING, RW, D), bf16),
        "sg_dn": ((RING, RF, D), bf16),
        "n_one": ((PLANE, T, D), bf16),
        "n_two": ((PLANE, T, D), bf16),
        "cot_all": ((PLANE, T, D), bf16),
        "d_out": ((PLANE, T, D), bf16),
        "conv": ((PLANE, M, CW), bf16),
        "part": ((PLANE, T, D), bf16),
        "part_act": ((PLANE, T, D), bf16),
        "part_conv": ((PLANE, M, CW), bf16),
        "got_one": ((6, T // 2, D), bf16),
        "got_two": ((6, T // 2, D), bf16),
        "got_three": ((6, T // 2, D), bf16),
        "got_act": ((6, T // 2, D), bf16),
        "got_conv": ((6, M // 2, CW), bf16),
        "mixed": ((M, CW), bf16),
        "hidden": ((M, CF), bf16),
        "d_pair": ((M, 2 * CF), bf16),
        "d_gu": ((M, 2 * CW), bf16),
        "d_pre": ((M, 2 * CW), bf16),
        "pair": ((M, 2 * CF), f32),
        "u": ((PLANE, T + 8, CW), f32),
        "state": ((PLANE, T + 8, CW), f32),
        "d_conv": ((PLANE, T + 8, CW), f32),
        **{name: ((M, CW), f32) for name in ("gated", "slope", "rgate", "igate", "decay", "work", "cum")},
        "x_one": ((T, D), f32),
        "d_one": ((T, D), f32),
        "carry_f": ((RING * NL, 2 * PLANE, CW), f32),
        "carry_b": ((RING * NL, 2 * PLANE, CW), f32),
        **{name: ((2 * PLANE, CW), f32) for name in ("own_f", "sib_f", "own_b", "sib_b")},
        "halo_out": ((16, CW), f32),
        "halo_in": ((16, CW), f32),
        "into": ((8, CW), f32),
        "x_all": ((PLANE, T, D), bf16),
        "x_halo": ((PLANE, 16, D), bf16),
        "n_halo": ((PLANE, 16, D), bf16),
        "g_dn": ((CF, D), bf16),
        "masks": ((7, M, 128), f32),
        "pack": ((16, 128), bf16),
        "pr": ((2 * RING, 16, 128), bf16),
        "pp": ((PLANE, 2 * RING, 16, 128), bf16),
        "act": ((T, D), bf16),
        "d_x": ((T, D), f32),
        "t_o": ((RW, D), f32),
        "t_dn": ((RF, D), f32),
        "small_sum": ((16, 128), f32),
        "chan_sum": ((8, CW), f32),
        "gains": ((8, D), f32),
        "chan": ((8, CW), f32),
        "ggain": ((8, D), f32),
        "gchan": ((8, CW), f32),
        "gg": ((2 * RING, 8, GL), f32),
        "gp": ((PLANE, 8, GL), f32),
        "gc": ((2 * RING, 8, CW), f32),
    }
    dims = SimpleNamespace(
        T=T, D=D, W=W, F=F, CW=CW, CF=CF, RD=RD, RW=RW, RF=RF, NL=NL, SEGS=SEGS, receives=RECEIVES + 2 * RING * NL, names=[*ins, *outs, *scratch, "ss", "rs"]
    )
    flops = 3 * 2 * M * (D * 2 * CW + W * 2 * CW + CW * D + 3 * D * CF)
    results = pl.pallas_call(
        partial(layer, dims),
        out_shape=[jax.ShapeDtypeStruct(shape, kind) for shape, kind in outs.values()],
        in_specs=[hbm] * (3 + len(WEIGHTS)),
        out_specs=[hbm] * len(outs),
        scratch_shapes=[pltpu.VMEM(shape, kind) for shape, kind in scratch.values()]
        + [pltpu.SemaphoreType.DMA((SENDS,)), pltpu.SemaphoreType.DMA((dims.receives,))],
        compiler_params=pltpu.CompilerParams(
            collective_id=0, has_side_effects=True, vmem_limit_bytes=62 * 2**20
        ),
        cost_estimate=pl.CostEstimate(flops=flops, bytes_accessed=8 * 2**20, transcendentals=M * CW * 16),
        name="griffin_layer",
    )(tokens, cotangent, pack, *[weights[name] for name in WEIGHTS])
    return finish(dict(zip(outs, results, strict=True)), PLANE, CW, CF)


def finish(got, blocks, CW, CF):
    hbm = pl.BlockSpec(memory_space=pl.ANY)
    pairs = (
        ("grads_ib", ("grad_input_weight", "grad_branch_weight"), CW),
        ("grads_di", ("grad_decay_weight", "grad_inject_weight"), CW),
        ("grads_gu", ("grad_mlp_gate", "grad_mlp_up"), CF),
    )
    plain = ("d_tokens", "activations", "grad_output_weight", "grad_mlp_down")
    names = [*[name for name, _, _ in pairs], *plain]
    shapes = {name: got[name] for name in plain}
    for name, outs, C in pairs:
        for out in outs:
            shapes[out] = jax.ShapeDtypeStruct((got[name].shape[1], blocks * C), f32)
    scratch = [pltpu.VMEM(got[name].shape, got[name].dtype) for name in names]
    scratch += [pltpu.VMEM(shapes[out].shape, f32) for _, outs, _ in pairs for out in outs]
    count = 2 * len(plain) + 3 * len(pairs)

    def body(*refs):
        ins = dict(zip(names, refs[: len(names)], strict=True))
        outs = dict(zip(shapes, refs[len(names) : len(names) + len(shapes)], strict=True))
        held, sems = refs[len(names) + len(shapes) : -1], refs[-1]
        copies = []

        def copy(src, dst):
            copies.append(pltpu.make_async_copy(src, dst, sems.at[len(copies)]))
            copies[-1].start()
            return copies[-1]

        loads = [copy(ins[name], held[i]) for i, name in enumerate(names)]
        stores = []
        for i, (_, targets, C) in enumerate(pairs):
            loads[i].wait()
            for j, target in enumerate(targets):
                wide = held[len(names) + 2 * i + j]
                for k in range(blocks):
                    wide[:, k * C : (k + 1) * C] = held[i][k, :, j * C : (j + 1) * C].astype(f32)
                stores.append(copy(wide, outs[target]))
        for i, name in enumerate(plain):
            loads[len(pairs) + i].wait()
            stores.append(copy(held[len(pairs) + i], outs[name]))
        for store in stores:
            store.wait()

    results = pl.pallas_call(
        body,
        out_shape=[jax.ShapeDtypeStruct(like.shape, like.dtype) for like in shapes.values()],
        in_specs=[hbm] * len(names),
        out_specs=[hbm] * len(shapes),
        scratch_shapes=[*scratch, pltpu.SemaphoreType.DMA((count,))],
        compiler_params=pltpu.CompilerParams(vmem_limit_bytes=62 * 2**20),
        name="finish",
    )(*[got[name] for name in names])
    return {**got, **dict(zip(shapes, results, strict=True))}


def local(
    sizes,
    tokens,
    cotangent,
    doc_lengths,
    decay_exponent,
    branch_weight,
    input_weight,
    decay_weight,
    inject_weight,
    output_weight,
    mlp_gate,
    mlp_up,
    mlp_down,
    first_gain,
    second_gain,
    conv_taps,
    conv_bias,
    decay_bias,
    inject_bias,
):
    devices = math.prod(sizes.values())
    width = branch_weight.shape[1]
    at = {name: lax.axis_index(name) for name in AXES}
    mine = at["yl"] * 2 + at["xl"]
    ring = at["zh"] * 2 + at["c"]
    share = ring * PLANE + mine
    groups = devices // SHARES

    def pooled(value, axis=0):
        if groups == 1:
            return value
        whole = lax.all_gather(value, AXES, axis=axis, tiled=True)
        size = whole.shape[axis] // SHARES
        return lax.dynamic_slice_in_dim(whole, share * size, size, axis)

    def rows(value):
        value = value.astype(bf16)
        return jnp.pad(value, ((0, 0), (0, 128 - value.shape[1])))

    gains = pooled(jnp.stack([first_gain, second_gain]), 1)
    chan = pooled(jnp.concatenate([conv_taps.T, jnp.stack([conv_bias, decay_bias, inject_bias])]), 1)
    RD, RW = gains.shape[1], chan.shape[1]
    rates = lax.dynamic_slice_in_dim(decay_exponent, mine * (width // PLANE), width // PLANE).reshape(-1, 128)
    lengths = jnp.concatenate([doc_lengths // 256, doc_lengths % 256])
    pack = jnp.concatenate([rows(gains), rows(chan), rows(lengths), rows(rates)])
    pack = jnp.pad(pack, ((0, 16 - pack.shape[0]), (0, 0)))

    weights = dict(
        zip(
            WEIGHTS,
            (branch_weight, input_weight, decay_weight, inject_weight, output_weight, mlp_gate, mlp_up, mlp_down),
            strict=True,
        )
    )
    weights = {name: pooled(value) for name, value in weights.items()}
    got = run_layer(sizes["zl"], doc_lengths.shape[1], tokens[0], cotangent[0], pack, weights)

    def returned(value, axis=0):
        if groups == 1:
            return value
        shape = list(value.shape)
        size = shape[axis]
        shape[axis] = size * SHARES
        whole = lax.dynamic_update_slice_in_dim(jnp.zeros(shape, bf16), value.astype(bf16), share * size, axis)
        return lax.psum_scatter(whole, AXES, scatter_dimension=axis, tiled=True).astype(f32)

    grads = [returned(got["grad_" + name]) for name in WEIGHTS]
    gain_sum = returned(got["small_out"][:2, :RD], 1)
    chan_sum = returned(got["small_out"][8:15, :RW], 1)
    return (
        got["activations"][None],
        got["d_tokens"][None],
        *grads,
        gain_sum[0],
        gain_sum[1],
        chan_sum[:4].T,
        chan_sum[4],
        chan_sum[5],
        chan_sum[6],
    )


def solution(mesh):
    seq, dp = mesh.shape["seq"], mesh.shape["dp"]
    across = 1 << ((dp.bit_length() - 1) // 2)
    sizes = dict(zip(AXES, (RING, seq // (2 * RING), 2, dp // across // 2, 2, across // 2, 2), strict=True))
    split = Mesh(mesh.devices.reshape(tuple(sizes.values())), AXES)
    along_seq, along_dp = AXES[:3], AXES[3:]
    rows = P(along_dp, along_seq, None)
    in_specs = (rows, rows, P(along_dp, None), P(), *[P(AXES, None)] * 8, P(AXES), P(AXES), P(AXES, None), *[P(AXES)] * 3)
    out_specs = (rows, rows, *[P(AXES, None)] * 8, P(AXES), P(AXES), P(AXES, None), *[P(AXES)] * 3)
    return jax.shard_map(partial(local, sizes), mesh=split, in_specs=in_specs, out_specs=out_specs, check_vma=False)
```

```python
import itertools
import math
from functools import partial
from types import SimpleNamespace

import jax
import jax.numpy as jnp
from jax import lax
from jax.experimental import pallas as pl
from jax.experimental.pallas import tpu as pltpu
from jax.sharding import Mesh, PartitionSpec as P

f32, bf16 = jnp.float32, jnp.bfloat16
MESH = pl.DeviceIdType.MESH
AXES = ("zh", "zl", "c", "yh", "yl", "xh", "xl")
RING = 4
PLANE = 4
SHARES = RING * 2 * PLANE
SENDS = 72
RECEIVES = 181

eps_norm = 1e-06
floor_gap = 1e-05
rate_scale = 8.0
gelu_root = math.sqrt(2.0 / math.pi)
gelu_cube = 0.044715


def dot(left, right):
    return jnp.dot(left, right, preferred_element_type=f32)


def dot_nt(left, right):
    return lax.dot_general(left, right, (((1,), (1,)), ((), ())), preferred_element_type=f32)


def dot_tn(left, right):
    return lax.dot_general(left, right, (((0,), (0,)), ((), ())), preferred_element_type=f32)


def gelu_parts(v):
    t = jnp.tanh(gelu_root * (v + gelu_cube * v * v * v))
    half = 0.5 * (1.0 + t)
    slope = half + 0.5 * v * (1.0 - t * t) * gelu_root * (1.0 + 3.0 * gelu_cube * v * v)
    return v * half, slope


def minus_expm1(y):
    poly = jnp.full_like(y, 1.0 / 8.0)
    poly = 1.0 + y * poly
    for k in (7, 6, 5, 4, 3, 2):
        poly = 1.0 + y * poly * (1.0 / k)
    return jnp.where(y > -0.35, -y * poly, 1.0 - jnp.exp(y))


def inverse_rms(v):
    return lax.rsqrt(jnp.mean(v * v, axis=-1, keepdims=True) + eps_norm)


def loop(total, step, body):
    def run(j, _):
        body(pl.multiple_of(j * step, step))
        return 0

    lax.fori_loop(0, total // step, run, 0)


def layer(dims, *refs):
    T, D, W, F, CW, CF = dims.T, dims.D, dims.W, dims.F, dims.CW, dims.CF
    RD, RW, RF, NL = dims.RD, dims.RW, dims.RF, dims.NL
    M = PLANE * T
    r = SimpleNamespace(**dict(zip(dims.names, refs, strict=True)))

    zh, zl, c = lax.axis_index("zh"), lax.axis_index("zl"), lax.axis_index("c")
    yl, xl = lax.axis_index("yl"), lax.axis_index("xl")
    p = yl * 2 + xl
    px, py, pd = yl * 2 + (1 - xl), (1 - yl) * 2 + xl, (1 - yl) * 2 + (1 - xl)
    to_x, to_y, to_d = {"xl": 1 - xl}, {"yl": 1 - yl}, {"yl": 1 - yl, "xl": 1 - xl}
    plane_peers = ((px, to_x), (py, to_y), (pd, to_d))
    to_core = {"c": 1 - c}
    flat_z = zh * NL + zl
    places = RING * NL * 2
    pos = flat_z * 2 + c

    def place(at):
        return {"zh": at // (2 * NL), "zl": (at // 2) % NL, "c": at % 2}

    count = itertools.count()

    def new(n=1):
        first = next(count)
        for _ in range(n - 1):
            next(count)
        assert first + n <= dims.receives
        return first

    spare = list(range(SENDS))
    sent = []

    def push(src, dst, dev, rsem, pred=None):
        i = spare.pop(0)

        def make():
            return pltpu.make_async_remote_copy(
                src, dst, r.ss.at[i], r.rs.at[rsem], device_id=dev, device_id_type=MESH
            )

        if pred is None:
            make().start()
        else:
            pl.when(pred)(lambda: make().start())
        entry = (make, pred, i)
        sent.append(entry)
        return entry

    def settle(*entries):
        for entry in entries:
            make, pred, i = entry
            if pred is None:
                make().wait_send()
            else:
                pl.when(pred)(lambda make=make: make().wait_send())
            sent.remove(entry)
            spare.append(i)

    def arrived(dst, rsem, pred=None):
        def wait():
            pltpu.make_async_remote_copy(
                dst, dst, r.ss.at[0], r.rs.at[rsem], device_id=to_core, device_id_type=MESH
            ).wait_recv()

        if pred is None:
            wait()
        else:
            pl.when(pred)(wait)

    def keep_local(src, dst, rsem):
        pltpu.make_async_copy(src, dst, r.rs.at[rsem]).start()

    def local_wait(src, dst, rsem):
        pltpu.make_async_copy(src, dst, r.rs.at[rsem]).wait()

    results = []

    def deliver(src, dst):
        sem = new()
        keep_local(src, dst, sem)
        results.append((src, dst, sem))

    def ds(start, size, unit):
        return pl.ds(pl.multiple_of(start, unit), size)

    class Gather:
        def __init__(self, buf):
            self.buf, half = buf, buf.shape[1] // 2
            self.h0, self.h1 = pl.ds(0, half), pl.ds(half, half)
            self.rx0, self.rx1, self.ry0, self.ry1, self.rd = (new() for _ in range(5))
            self.out = []

        def start(self):
            b = self.buf
            own0, own1 = b.at[p, self.h0], b.at[p, self.h1]
            self.out.append(push(own0, own0, to_x, self.rx0))
            self.out.append(push(own1, own1, to_y, self.ry1))
            self.out.append(push(own1, own1, to_x, self.rx1))
            self.out.append(push(own0, own0, to_y, self.ry0))

        def mid(self):
            b = self.buf
            got0, got1 = b.at[px, self.h0], b.at[py, self.h1]
            arrived(got0, self.rx0)
            self.out.append(push(got0, got0, to_y, self.rd))
            arrived(got1, self.ry1)
            self.out.append(push(got1, got1, to_x, self.rd))

        def wait_x(self):
            arrived(self.buf.at[px, self.h1], self.rx1)

        def wait_y(self):
            arrived(self.buf.at[py, self.h0], self.ry0)

        def wait_d(self):
            arrived(self.buf.at[pd], self.rd)

        def end(self):
            self.wait_x()
            self.wait_y()
            self.wait_d()
            settle(*self.out)

    class Scatter:
        def __init__(self, buf, recv):
            self.buf, self.recv = buf, recv
            self.half = buf.shape[1] // 2
            self.h0, self.h1 = pl.ds(0, self.half), pl.ds(self.half, self.half)
            self.sems = [new(), new(), *[new()] * 4]
            self.out = []

        def start(self):
            b, v, s = self.buf, self.recv, self.sems
            self.out.append(push(b.at[pd, self.h0], v.at[0], to_x, s[0]))
            self.out.append(push(b.at[pd, self.h1], v.at[1], to_y, s[1]))
            self.out.append(push(b.at[px, self.h0], v.at[2], to_x, s[2]))
            self.out.append(push(b.at[py, self.h1], v.at[3], to_y, s[3]))

        def mid(self):
            b, v, s = self.buf, self.recv, self.sems
            arrived(v.at[0], s[0])
            step = 16

            def add0(o):
                b[py, pl.ds(o, step)] = (b[py, pl.ds(o, step)].astype(f32) + v[0, pl.ds(o, step)].astype(f32)).astype(bf16)

            loop(self.half, step, add0)
            self.out.append(push(b.at[py, self.h0], v.at[4], to_y, s[4]))
            arrived(v.at[1], s[1])

            def add1(o):
                q = pl.ds(pl.multiple_of(self.half + o, step), step)
                b[px, q] = (b[px, q].astype(f32) + v[1, pl.ds(o, step)].astype(f32)).astype(bf16)

            loop(self.half, step, add1)
            self.out.append(push(b.at[px, self.h1], v.at[5], to_x, s[5]))

        def end(self):
            arrived(self.recv.at[pl.ds(2, 4)], self.sems[2])
            settle(*self.out)

        def total(self, half, o, step):
            b, v = self.buf, self.recv
            own = b[p, pl.ds(pl.multiple_of(half * self.half + o, step), step)].astype(f32)
            q = pl.ds(o, step)
            return own + v[2 + half, q].astype(f32) + v[4 + half, q].astype(f32)

        def each(self, step, body):
            for half in (0, 1):
                loop(self.half, step, lambda o: body(pl.multiple_of(half * self.half + o, step), self.total(half, o, step)))

    def z_send(src, block, rz):
        out = []
        for s in (2, 1):
            out.append(push(src, block(zh), {"zh": zh + s}, rz + zh, zh + s < RING))
            out.append(push(src, block(zh), {"zh": zh - s}, rz + zh, zh - s >= 0))
        return out

    def z_forward(block, rz):
        last = RING - 1
        arrived(block(0), rz, zh == last - 1)
        one = push(block(0), block(0), {"zh": zh + 1}, rz, zh == last - 1)
        arrived(block(last), rz + last, zh == 1)
        two = push(block(last), block(last), {"zh": zh - 1}, rz + last, zh == 1)
        return [one, two]

    def z_wait(block, rz):
        last = RING - 1
        arrived(block(0), rz, (zh == 1) | (zh == last))
        arrived(block(1), rz + 1, zh != 1)
        arrived(block(2), rz + 2, zh != 2)
        arrived(block(last), rz + last, (zh == 0) | (zh == last - 1))

    class ZSum:
        def __init__(self, block, slot, add):
            self.block, self.slot, self.add = block, slot, add
            self.sems = new(4)
            self.out = []

        def send(self):
            b, v, s = self.block, self.slot, self.sems
            last = RING - 1
            o = self.out
            o.append(push(b(last), v(1), {"zh": zh + 1}, s + 1, zh == 0))
            o.append(push(b(0), v(3), {"zh": zh - 1}, s + 3, zh == last))
            o.append(push(b(zh + 2), v(1), {"zh": zh + 2}, s + 1, zh == 0))
            o.append(push(b(zh - 2), v(3), {"zh": zh - 2}, s + 3, zh == last))
            o.append(push(b(zh + 1), v(0), {"zh": zh + 1}, s + 0, zh < last))
            o.append(push(b(zh - 1), v(2), {"zh": zh - 1}, s + 2, zh > 0))

        def forward(self):
            b, v, s = self.block, self.slot, self.sems
            last = RING - 1

            def up():
                arrived(v(1), s + 1)
                self.add(last, 1)

            def down():
                arrived(v(3), s + 3)
                self.add(0, 3)

            pl.when(zh == 1)(up)
            self.out.append(push(b(last), v(1), {"zh": zh + 2}, s + 1, zh == 1))
            pl.when(zh == last - 1)(down)
            self.out.append(push(b(0), v(3), {"zh": zh - 2}, s + 3, zh == last - 1))

        def end(self):
            v, s = self.slot, self.sems
            arrived(v(0), s, zh >= 1)
            arrived(v(1), s + 1, zh >= 2)
            arrived(v(2), s + 2, zh <= 2)
            arrived(v(3), s + 3, zh <= 1)
            settle(*self.out)

        def total(self, own, parts):
            for part, pred in zip(parts, (zh >= 1, zh >= 2, zh <= 2, zh <= 1), strict=True):
                own = own + jnp.where(pred, part.astype(f32), 0.0)
            return own

    class Column:
        def __init__(self, src, raw, sorted_, w, R, C, lane0):
            self.src, self.raw, self.sorted = src, raw, sorted_
            self.w, self.R, self.C, self.lanes = w, R, C, pl.ds(lane0, C)
            self.rl, self.ra, self.rz, self.rc = new(), new(), new(4), new()
            self.out = []

        def load(self):
            keep_local(self.src, self.raw, self.rl)

        def prepare(self):
            local_wait(self.src, self.raw, self.rl)
            value, part = self.raw[...], self.C // (2 * RING)
            for k in range(PLANE):
                first = [(g * PLANE + k) * part for g in range(2 * RING)]
                self.sorted[k] = jnp.concatenate([value[:, at : at + part] for at in first], axis=1)

        def spread(self):
            dst = self.w.at[zh, c, ds(p * self.R, self.R, 16), self.lanes]
            for k, dev in plane_peers:
                self.out.append(push(self.sorted.at[k], dst, dev, self.ra))
            keep_local(self.sorted.at[p], dst, self.ra)

        def block(self, z):
            return self.w.at[z, c, :, self.lanes]

        def z_send(self):
            arrived(self.block(zh), self.ra)
            self.out += z_send(self.block(zh), self.block, self.rz)

        def z_forward(self):
            self.out += z_forward(self.block, self.rz)

        def z_wait(self):
            z_wait(self.block, self.rz)
            half = self.w.at[:, c, :, self.lanes]
            self.out.append(push(half, half, to_core, self.rc))

        def end(self):
            arrived(self.w.at[:, 1 - c, :, self.lanes], self.rc)
            settle(*self.out)

    class Row(Column):
        def __init__(self, src, w):
            self.src, self.w, self.lanes = src, w, pl.ds(0, w.shape[3])
            self.ra, self.rz, self.rc = new(), new(4), new()
            self.out = []

        def z_send(self):
            keep_local(self.src, self.block(zh), self.ra)
            self.out += z_send(self.src, self.block, self.rz)

        def z_wait(self):
            local_wait(self.src, self.block(zh), self.ra)
            super().z_wait()

    class ColumnsGrad:
        def __init__(self, g, other, slots, land, R, lane0, lanes, result):
            self.g, self.other, self.slots, self.land = g, other, slots, land
            self.R, self.lanes, self.result = R, pl.ds(lane0, lanes), result
            self.rows = PLANE * R
            self.rc, self.rl = new(), new()
            self.zsum = ZSum(
                lambda z: g.at[z, c, :, self.lanes], lambda k: slots.at[k, :, self.lanes], self.add_slot
            )

        def add_slot(self, z, k):
            g, q = self.g, self.lanes

            def add(o):
                s = pl.ds(o, 16)
                g[z, c, s, q] = (g[z, c, s, q].astype(f32) + self.slots[k, s, q].astype(f32)).astype(bf16)

            loop(self.rows, 16, add)

        def core_send(self):
            self.pushed = push(
                self.g.at[:, 1 - c, :, self.lanes], self.other.at[:, :, self.lanes], to_core, self.rc
            )

        def z_send(self):
            g, q = self.g, self.lanes
            arrived(self.other.at[:, :, q], self.rc)
            for z in range(RING):

                def add(o):
                    s = pl.ds(o, 16)
                    g[z, c, s, q] = (g[z, c, s, q].astype(f32) + self.other[z, s, q].astype(f32)).astype(bf16)

                loop(self.rows, 16, add)
            self.zsum.send()

        def z_forward(self):
            self.zsum.forward()

        def plane_send(self):
            g, q, R = self.g, self.lanes, self.R
            self.zsum.end()

            def add(o):
                s = pl.ds(o, 16)
                parts = [self.slots[k, s, q] for k in range(4)]
                g[zh, c, s, q] = self.zsum.total(g[zh, c, s, q].astype(f32), parts).astype(bf16)

            loop(PLANE * R, 16, add)
            dst = self.land.at[p, :, q]
            self.out = [self.pushed]
            for k, dev in plane_peers:
                self.out.append(push(g.at[zh, c, ds(k * R, R, 16), q], dst, dev, self.rl))
            keep_local(g.at[zh, c, ds(p * R, R, 16), q], dst, self.rl)

        def end(self):
            arrived(self.land.at[:, :, self.lanes], self.rl)
            settle(*self.out)
            deliver(self.land.at[:, :, self.lanes], self.result.at[:, :, self.lanes])

    class RowsGrad(ColumnsGrad):
        def __init__(self, g, other, slots, total, result):
            super().__init__(g, other, slots, None, 0, 0, g.shape[3], result)
            self.rows, self.sum = g.shape[2], total

        def end(self):
            self.zsum.end()
            settle(self.pushed)

            def add(o):
                s = pl.ds(o, 16)
                self.sum[s] = self.zsum.total(self.g[zh, c, s].astype(f32), [self.slots[k, s] for k in range(4)])

            loop(self.rows, 16, add)
            deliver(self.sum, self.result)

    class Carry:
        def __init__(self, own, sib, buf, later):
            self.own, self.sib, self.buf, self.later = own, sib, buf, later
            self.rc, self.rz = new(), new(RING * NL)
            self.out = []

        def order(self):
            return range(RING * NL) if self.later else reversed(range(RING * NL))

        def send_core(self):
            self.out.append(push(self.own, self.sib, to_core, self.rc))

        def send(self):
            arrived(self.sib, self.rc)
            own, sib = self.own[...], self.sib[...]
            near = (c == 0) if self.later else (c == 1)
            head, tail = jnp.where(near, own, sib), jnp.where(near, sib, own)
            self.buf[flat_z, 0:PLANE] = tail[0:PLANE] * head[0:PLANE]
            self.buf[flat_z, PLANE : 2 * PLANE] = (
                tail[0:PLANE] * head[PLANE : 2 * PLANE] + tail[PLANE : 2 * PLANE]
            )
            part = self.buf.at[flat_z]
            for at in self.order():
                pred = (flat_z < at) if self.later else (flat_z > at)
                self.out.append(push(part, part, {"zh": at // NL, "zl": at % NL}, self.rz + flat_z, pred))

        def fold(self, into):
            into[...] = jnp.zeros_like(into)

            def take(part):
                into[0:PLANE] = part[0:PLANE] * into[0:PLANE] + part[PLANE : 2 * PLANE]

            for at in self.order():
                pred = (flat_z > at) if self.later else (flat_z < at)

                def chip(at=at):
                    arrived(self.buf.at[at], self.rz + at)
                    take(self.buf[at])

                pl.when(pred)(chip)
            pl.when((c == 1) if self.later else (c == 0))(lambda: take(self.sib[...]))
            settle(*self.out)

    GL = PLANE * RD
    ring = zh * 2 + c

    def ring_place(at):
        return {"zh": at // 2, "c": at % 2}

    class Small:
        def __init__(self):
            self.rr, self.rk = new(), new()
            self.out = []

        def one(self):
            for at in range(2 * RING):
                self.out.append(push(r.pack, r.pr.at[ring], ring_place(at), self.rr, ring != at))
            keep_local(r.pack, r.pr.at[ring], self.rr)

        def two(self):
            arrived(r.pr, self.rr)
            for _, dev in plane_peers:
                self.out.append(push(r.pr, r.pp.at[p], dev, self.rk))
            keep_local(r.pr, r.pp.at[p], self.rk)

        def three(self):
            arrived(r.pp, self.rk)
            from_row = lax.broadcasted_iota(jnp.int32, (128, GL), 0)
            to_lane = lax.broadcasted_iota(jnp.int32, (128, GL), 1)
            whole = jnp.zeros((2 * RING * 16, GL), f32)
            for k in range(PLANE):
                move = ((to_lane == from_row + k * RD) & (from_row < RD)).astype(bf16)
                whole = whole + dot(r.pp[k].reshape(2 * RING * 16, 128), move)
            for at in range(2 * RING):
                r.gains[0:2, at * GL : (at + 1) * GL] = whole[at * 16 : at * 16 + 2]
            whole = jnp.concatenate([r.pr[at, :, 0:RW].astype(f32) for at in range(2 * RING)], axis=1)
            r.chan[...] = whole[2:10]
            rate = r.pack[...].astype(f32)
            for k in range(CW // 128):
                r.chan[7:8, k * 128 : (k + 1) * 128] = jnp.exp2(-rate[11 + k : 12 + k])

        def four(self):
            where = lax.broadcasted_iota(jnp.int32, (T, 128), 0).astype(f32) + (pos * T).astype(f32)
            for k in range(PLANE):
                part = r.pp[k, 0].astype(f32)
                starts, ends = [], []
                total = jnp.zeros((1, 1), f32)
                for j in range(dims.SEGS):
                    starts.append(total)
                    total = total + part[9:10, j : j + 1] * 256.0 + part[10:11, j : j + 1]
                    ends.append(total)

                def seg(shift):
                    at = where + float(shift)
                    value = jnp.zeros((T, 128), f32)
                    for end in ends:
                        value = value + jnp.where(at >= end, 1.0, 0.0)
                    return jnp.where((at < 0.0) | (at >= float(T * places)), -1.0, value)

                here = seg(0)
                rows = pl.ds(k * T, T)
                first = jnp.zeros((T, 128), f32)
                for start in starts:
                    first = jnp.where(where == start, 1.0, first)
                r.masks[0, rows] = first
                for j in (1, 2, 3):
                    r.masks[j, rows] = jnp.where(seg(-j) == here, 1.0, 0.0)
                    r.masks[3 + j, rows] = jnp.where(seg(j) == here, 1.0, 0.0)
            settle(*self.out)

    class SmallGrad:
        def __init__(self):
            self.rg, self.rp = new(2 * RING), new(PLANE)
            self.out = []

        def one(self):
            for at in range(2 * RING):
                own = jnp.concatenate([r.gchan[:, at * RW : (at + 1) * RW], jnp.zeros((8, 128 - RW), f32)], axis=1)
                r.gs[at, 0:8], r.gs[at, 8:16] = r.ggain[:, at * GL : (at + 1) * GL], own
            for at in range(2 * RING):
                self.out.append(push(r.gs.at[at], r.gg.at[ring], ring_place(at), self.rg + ring, ring != at))

        def two(self):
            r.gg[ring] = r.gs[ring]
            for at in range(2 * RING):
                arrived(r.gg.at[at], self.rg + at, ring != at)
            value = r.gg[0]
            for at in range(1, 2 * RING):
                value = value + r.gg[at]
            r.small_sum[...] = value
            r.gp[p] = value[0:8]
            for _, dev in plane_peers:
                self.out.append(push(r.gp.at[p], r.gp.at[p], dev, self.rp + p))

        def end(self):
            for k, _ in plane_peers:
                arrived(r.gp.at[k], self.rp + k)
            gains = (r.gp[0] + r.gp[1]) + (r.gp[2] + r.gp[3])
            from_lane = lax.broadcasted_iota(jnp.int32, (GL, 128), 0)
            to_lane = lax.broadcasted_iota(jnp.int32, (GL, 128), 1)
            move = (from_lane == to_lane + p * RD).astype(f32)
            r.small_sum[0:8] = jnp.dot(gains, move, precision=lax.Precision.HIGHEST)
            deliver(r.small_sum, r.small_out)
            settle(*self.out)

    barrier = pltpu.get_barrier_semaphore()
    for _, dev in plane_peers:
        pl.semaphore_signal(barrier, 1, device_id=dev, device_id_type=MESH)
    for at in range(places):

        @pl.when(pos != at)
        def _(at=at):
            pl.semaphore_signal(barrier, 1, device_id=place(at), device_id_type=MESH)

    first_loads = [
        (src, dst, new())
        for src, dst in (
            (r.pack_in, r.pack),
            (r.tokens, r.x_all.at[p]),
            (r.cotangent, r.cot_all.at[p]),
        )
    ]
    for load in first_loads:
        keep_local(*load)

    w_i = Column(r.input_weight, r.raw_i, r.sort_i, r.w_ib, RD, CW, 0)
    w_b = Column(r.branch_weight, r.raw_b, r.sort_b, r.w_ib, RD, CW, CW)
    w_d = Column(r.decay_weight, r.raw_d, r.sort_d, r.w_di, RW, CW, 0)
    w_j = Column(r.inject_weight, r.raw_j, r.sort_j, r.w_di, RW, CW, CW)
    w_g = Column(r.mlp_gate, r.raw_g, r.sort_g, r.w_gu, RD, CF, 0)
    w_u = Column(r.mlp_up, r.raw_u, r.sort_u, r.w_gu, RD, CF, CF)
    w_o, w_dn = Row(r.output_weight, r.w_o), Row(r.mlp_down, r.w_dn)
    ag_x, ag_conv, ag_two = Gather(r.x_all), Gather(r.conv), Gather(r.n_two)
    ag_cot, ag_out = Gather(r.cot_all), Gather(r.d_out)
    small, small_grad = Small(), SmallGrad()
    after, before = flat_z + c, flat_z - (1 - c)
    to_next = {"zh": after // NL, "zl": after % NL, "c": 1 - c}
    to_prev = {"zh": before // NL, "zl": before % NL, "c": 1 - c}
    step = 256
    chunk = PLANE * RD * 2

    for w in (w_i, w_d, w_j, w_b, w_g, w_u):
        w.load()
    w_i.prepare()
    pl.semaphore_wait(barrier, len(plane_peers) + places - 1)
    local_wait(*first_loads[0])
    small.one()
    w_i.spread()
    local_wait(*first_loads[1])
    ag_x.start()
    halo_x = new()
    sent_x = push(r.x_all.at[p, pl.ds(T - 16, 16)], r.x_halo.at[p], to_next, halo_x, pos < places - 1)
    w_d.prepare()
    w_d.spread()
    w_i.z_send()
    w_o.z_send()
    small.two()
    w_j.prepare()
    w_b.prepare()

    @pl.when(pos == 0)
    def _():
        r.x_halo[p] = jnp.zeros((16, D), bf16)

    arrived(r.x_halo.at[p], halo_x, pos > 0)
    halo_p = new(PLANE)
    sent_p = [push(r.x_halo.at[p], r.x_halo.at[p], dev, halo_p + p) for _, dev in plane_peers]
    ag_x.mid()
    w_j.spread()
    w_b.spread()
    w_g.prepare()
    local_wait(*first_loads[2])
    small.three()

    def norm_block(k):
        def norm_one(o):
            s = pl.ds(o, 32)
            v = r.x_all[k, s].astype(f32)
            r.n_one[k, s] = (v * inverse_rms(v) * r.gains[0:1]).astype(bf16)

        loop(T, 32, norm_one)

    norm_block(p)
    w_i.z_forward()
    ag_x.wait_x()
    norm_block(px)
    ag_x.wait_y()
    norm_block(py)
    w_d.z_send()
    small.four()
    for k, _ in plane_peers:
        arrived(r.x_halo.at[k], halo_p + k)
    v = r.x_halo[...].reshape(PLANE * 16, D).astype(f32)
    r.n_halo[...] = (v * inverse_rms(v) * r.gains[0:1]).astype(bf16).reshape(PLANE, 16, D)
    ag_x.wait_d()
    norm_block(pd)
    settle(*ag_x.out, sent_x, *sent_p)
    w_g.spread()
    w_o.z_forward()
    w_i.z_wait()
    w_u.prepare()
    w_i.end()

    def weight_ib(lanes):
        return r.w_ib[:, :, :, lanes].reshape(D, CW)

    lanes_a, lanes_b = pl.ds(0, CW), pl.ds(CW, CW)
    halo = dot(r.n_halo[...].reshape(PLANE * 16, D), weight_ib(lanes_a)).astype(bf16).astype(f32)
    body = dot(r.n_one[...].reshape(M, D), weight_ib(lanes_a)).astype(bf16).astype(f32)
    for k in range(PLANE):
        r.u[k, 0:8] = halo[k * 16 + 8 : (k + 1) * 16]
        r.u[k, 8 : 8 + T] = body[k * T : (k + 1) * T]

    def wide(j, rows):
        return jnp.concatenate([r.masks[j, rows]] * (CW // 128), axis=1) > 0.5

    def convolve(o):
        for k in range(PLANE):
            ext = r.u[k, pl.ds(o, 24)]
            rows = ds(k * T + o, 16, 16)
            total = r.chan[4:5] + r.chan[0:1] * ext[8:24]
            for j in range(1, 4):
                total = total + jnp.where(wide(j, rows), r.chan[j : j + 1] * ext[8 - j : 24 - j], 0.0)
            r.conv[p, rows] = total.astype(bf16)

    loop(T, 16, convolve)
    ag_conv.start()
    w_d.z_forward()
    w_j.z_send()
    ag_conv.mid()
    w_d.z_wait()
    w_b.z_send()
    w_d.end()

    def pre(q, lanes):
        return dot(r.conv[q], r.w_di[:, :, ds(q * RW, RW, 16), lanes].reshape(CW, CW))

    r.pair[:, 0:CW] = pre(p, lanes_a)
    ag_conv.wait_x()
    r.pair[:, 0:CW] += pre(px, lanes_a)
    ag_conv.wait_y()
    r.pair[:, 0:CW] += pre(py, lanes_a)
    w_j.z_forward()
    ag_conv.wait_d()
    r.pair[:, 0:CW] += pre(pd, lanes_a)
    settle(*ag_conv.out)
    w_u.spread()
    ag_cot.start()
    w_b.z_forward()
    w_g.z_send()
    w_j.z_wait()
    w_o.z_wait()
    w_j.end()
    r.pair[:, CW : 2 * CW] = pre(0, lanes_b)
    for q in range(1, PLANE):
        r.pair[:, CW : 2 * CW] += pre(q, lanes_b)

    def decay_terms(s, rg):
        log_a = -rate_scale * rg * r.chan[7:8]
        gap = minus_expm1(2.0 * log_a)
        first = wide(0, s)
        return log_a, gap, jnp.where(first, 1.0, jnp.sqrt(jnp.maximum(gap, floor_gap))), first

    def gates_two(o):
        s = pl.ds(o, 16)
        rg = jax.nn.sigmoid(r.pair[s, 0:CW] + r.chan[5:6])
        ig = jax.nn.sigmoid(r.pair[s, CW : 2 * CW] + r.chan[6:7])
        log_a, _, mult, first = decay_terms(s, rg)
        r.rgate[s], r.igate[s] = rg, ig
        r.decay[s] = jnp.where(first, 0.0, jnp.exp(log_a))
        r.work[s] = mult * ig * r.conv[p, s].astype(f32)

    loop(M, 16, gates_two)
    row = lax.broadcasted_iota(jnp.int32, (8, CW), 0)

    def scan_forward(j, carry):
        out = []
        for k in range(PLANE):
            s = ds(k * T + j * 8, 8, 8)
            a, b = r.decay[s], r.work[s]
            for n in (1, 2, 4):
                a_b = jnp.where(row >= n, pltpu.roll(a, n, 0), 1.0)
                b_b = jnp.where(row >= n, pltpu.roll(b, n, 0), 0.0)
                a, b = a * a_b, a * b_b + b
            total, prod = b + a * carry[2 * k], a * carry[2 * k + 1]
            r.state[k, ds(8 + j * 8, 8, 8)] = total
            r.cum[s] = prod
            out += [total[7:8], prod[7:8]]
        return tuple(out)

    zero, one = jnp.zeros((1, CW), f32), jnp.ones((1, CW), f32)
    ends = lax.fori_loop(0, T // 8, scan_forward, (zero, one) * PLANE)
    carry_f = Carry(r.own_f, r.sib_f, r.carry_f, True)
    for k in range(PLANE):
        r.own_f[k : k + 1] = ends[2 * k + 1]
        r.own_f[PLANE + k : PLANE + k + 1] = ends[2 * k]
    carry_f.send_core()
    ag_cot.mid()
    carry_f.send()
    w_b.z_wait()
    w_g.z_forward()
    w_b.end()
    r.work[...] = dot(r.n_one[...].reshape(M, D), weight_ib(lanes_b))

    def gates_one(o):
        s = pl.ds(o, 16)
        r.gated[s], r.slope[s] = gelu_parts(r.work[s])

    loop(M, 16, gates_one)
    w_o.end()
    carry_f.fold(r.into)
    w_u.z_send()
    for k in range(PLANE):
        r.state[k, 0:8] = jnp.broadcast_to(r.into[k : k + 1], (8, CW))

    def mix(o):
        for k in range(PLANE):
            s, t = ds(k * T + o, 16, 16), ds(8 + o, 16, 8)
            state = r.state[k, t] + r.cum[s] * r.into[k : k + 1]
            r.state[k, t] = state
            r.mixed[s] = (state * r.gated[s]).astype(bf16)

    loop(T, 16, mix)

    def out_part(o):
        q = pl.ds(o, step)
        r.part[:, :, q] = dot(r.mixed[...], r.w_o[:, :, :, q].reshape(CW, step)).astype(bf16).reshape(PLANE, T, step)

    loop(D, step, out_part)
    rs_one = Scatter(r.part, r.got_one)
    rs_one.start()
    ag_cot.end()
    w_g.z_wait()
    rs_one.mid()
    w_u.z_forward()
    w_dn.z_send()
    rs_one.end()

    def norm_two(o, summed):
        s = pl.ds(o, 16)
        v = r.x_all[p, s].astype(f32) + summed
        r.x_one[s] = v
        r.n_two[p, s] = (v * inverse_rms(v) * r.gains[1:2]).astype(bf16)

    rs_one.each(16, norm_two)
    ag_two.start()
    ag_two.mid()
    w_u.z_wait()
    w_g.end()
    w_dn.z_forward()
    ag_two.end()

    def mlp_in(o):
        q = pl.ds(o, step)
        r.pair[:, q] = dot(r.n_two[...].reshape(M, D), r.w_gu[:, :, :, q].reshape(D, step))

    loop(CF, step, mlp_in)
    w_u.end()
    loop(CF, step, lambda o: mlp_in(pl.multiple_of(CF + o, step)))

    def gates_mlp(o):
        s = pl.ds(o, 16)
        value, slope = gelu_parts(r.pair[s, 0:CF])
        up = r.pair[s, CF : 2 * CF]
        r.hidden[s] = (value * up).astype(bf16)
        r.pair[s, 0:CF] = slope * up
        r.pair[s, CF : 2 * CF] = value

    loop(M, 16, gates_mlp)
    w_dn.z_wait()

    half = CF // 2
    for k in (0, 1):
        for o in range(0, D, D // 2):
            value = dot_tn(r.hidden[:, k * half : (k + 1) * half], r.cot_all[:, :, o : o + D // 2].reshape(M, D // 2))
            r.g_dn[k * RING // 2 : (k + 1) * RING // 2, :, :, o : o + D // 2] = value.astype(bf16).reshape(
                RING // 2, 2, RF, D // 2
            )
    g_dn = RowsGrad(r.g_dn, r.h_dn, r.z_dn, r.t_dn, r.grad_mlp_down)
    g_dn.core_send()
    w_dn.end()

    for k in range(CF // step):
        back = dot_nt(r.cot_all[...].reshape(M, D), r.w_dn[...].reshape(CF, D)[k * step : (k + 1) * step])
        r.d_pair[:, k * step : (k + 1) * step] = (back * r.pair[:, k * step : (k + 1) * step]).astype(bf16)
        r.d_pair[:, CF + k * step : CF + (k + 1) * step] = (
            back * r.pair[:, CF + k * step : CF + (k + 1) * step]
        ).astype(bf16)

    def d_two_part(z, _):
        q = ds(z * chunk, chunk, chunk)
        r.part[:, :, q] = (
            dot_nt(r.d_pair[...], r.w_gu[z].reshape(chunk, 2 * CF)).astype(bf16).reshape(PLANE, T, chunk)
        )
        return 0

    lax.fori_loop(0, RING, d_two_part, 0)
    rs_two = Scatter(r.part, r.got_two)
    rs_two.start()
    g_dn.z_send()

    def grad_gate_up(lane0):
        lanes = pl.ds(lane0, CF)

        def run(z, _):
            q = ds(z * chunk, chunk, chunk)
            value = dot_tn(r.n_two[:, :, q].reshape(M, chunk), r.d_pair[:, lanes])
            r.w_gu[z, :, :, lanes] = value.astype(bf16).reshape(2, chunk // 2, CF)
            return 0

        lax.fori_loop(0, RING, run, 0)

    grad_gate_up(0)
    g_g = ColumnsGrad(r.w_gu, r.h_gu, r.z_gu, r.l_gu, RD, 0, CF, r.grads_gu)
    g_g.core_send()
    rs_two.mid()
    grad_gate_up(CF)
    g_u = ColumnsGrad(r.w_gu, r.h_gu, r.z_gu, r.l_gu, RD, CF, CF, r.grads_gu)
    g_u.core_send()
    g_dn.z_forward()
    g_g.z_send()

    def act_part(o):
        q = pl.ds(o, step)
        r.part_act[:, :, q] = dot(r.hidden[...], r.w_dn[:, :, :, q].reshape(CF, step)).astype(bf16).reshape(PLANE, T, step)

    loop(D, step, act_part)
    r.ggain[...] = jnp.zeros_like(r.ggain)
    r.gchan[...] = jnp.zeros_like(r.gchan)
    rs_two.end()

    def norm_two_back(o, d_two):
        s = pl.ds(o, 16)
        v = r.x_one[s]
        rs = inverse_rms(v)
        z = v * rs
        dz = d_two * r.gains[1:2]
        r.ggain[1:2] += jnp.sum(d_two * z, axis=0, keepdims=True)
        d_one = r.cot_all[p, s].astype(f32) + rs * (dz - z * jnp.mean(dz * z, axis=-1, keepdims=True))
        r.d_one[s] = d_one
        r.d_out[p, s] = d_one.astype(bf16)

    rs_two.each(16, norm_two_back)
    ag_out.start()
    ag_out.mid()
    g_g.z_forward()
    ag_out.end()
    rs_act = Scatter(r.part_act, r.got_act)
    rs_act.start()

    r.work[...] = dot_nt(r.d_out[...].reshape(M, D), r.w_o[...].reshape(CW, D))

    def split(o):
        for k in range(PLANE):
            s = ds(k * T + o, 16, 16)
            d_mixed = r.work[s]
            r.d_gu[s, CW : 2 * CW] = (d_mixed * r.state[k, ds(8 + o, 16, 8)] * r.slope[s]).astype(bf16)
            r.work[s] = d_mixed * r.gated[s]

    loop(T, 16, split)

    def scan_backward(i, carry):
        j = T // 8 - 1 - i
        out = []
        for k in range(PLANE):
            s = ds(k * T + j * 8, 8, 8)
            decay, b = r.decay[s], r.work[s]
            a = jnp.where(row < 7, pltpu.roll(decay, 7, 0), carry[3 * k + 2])
            for n in (1, 2, 4):
                a_b = jnp.where(row < 8 - n, pltpu.roll(a, 8 - n, 0), 1.0)
                b_b = jnp.where(row < 8 - n, pltpu.roll(b, 8 - n, 0), 0.0)
                a, b = a * a_b, a * b_b + b
            total, prod = b + a * carry[3 * k], a * carry[3 * k + 1]
            r.work[s], r.cum[s] = total, prod
            out += [total[0:1], prod[0:1], decay[0:1]]
        return tuple(out)

    heads = lax.fori_loop(0, T // 8, scan_backward, (zero, one, one) * PLANE)
    carry_b = Carry(r.own_b, r.sib_b, r.carry_b, False)
    for k in range(PLANE):
        r.own_b[k : k + 1] = r.own_f[k : k + 1]
        r.own_b[PLANE + k : PLANE + k + 1] = heads[3 * k] * heads[3 * k + 2]
    carry_b.send_core()

    def grad_out(o):
        q = pl.ds(o, D // 2)
        value = dot_tn(r.mixed[...], r.d_out[:, :, q].reshape(M, D // 2))
        r.w_o[:, :, :, q] = value.astype(bf16).reshape(RING, 2, RW, D // 2)

    loop(D, D // 2, grad_out)
    g_o = RowsGrad(r.w_o, r.h_o, r.z_o, r.t_o, r.grad_output_weight)
    g_o.core_send()
    carry_b.send()
    rs_act.mid()

    def d_branch_part(z, _):
        q = ds(z * chunk, chunk, chunk)
        r.part[:, :, q] = (
            dot_nt(r.d_gu[:, lanes_b], r.w_ib[z, :, :, lanes_b].reshape(chunk, CW))
            .astype(bf16)
            .reshape(PLANE, T, chunk)
        )
        value = dot_tn(r.n_one[:, :, q].reshape(M, chunk), r.d_gu[:, lanes_b])
        r.w_ib[z, :, :, lanes_b] = value.astype(bf16).reshape(2, chunk // 2, CW)
        return 0

    lax.fori_loop(0, RING, d_branch_part, 0)
    g_b = ColumnsGrad(r.w_ib, r.h_ib, r.z_ib, r.l_ib, RD, CW, CW, r.grads_ib)
    g_b.core_send()
    g_g.plane_send()
    carry_b.fold(r.into)
    g_u.z_send()

    def back(o):
        sums = [jnp.zeros((1, CW), f32)] * 2
        for k in range(PLANE):
            s = ds(k * T + o, 16, 16)
            adjoint = r.work[s] + r.cum[s] * r.into[k : k + 1]
            previous = r.state[k, pl.ds(o, 24)][7:23]
            rg, ig, decay, conv = r.rgate[s], r.igate[s], r.decay[s], r.conv[p, s].astype(f32)
            _, gap, mult, first = decay_terms(s, rg)
            d_mult = jnp.where(first, 0.0, adjoint * ig * conv)
            d_log = adjoint * previous * decay - jnp.where(gap > floor_gap, (1.0 - gap) * d_mult / mult, 0.0)
            d_decay = (-rate_scale * r.chan[7:8] * d_log * rg * (1.0 - rg)).astype(bf16)
            d_inject = (adjoint * mult * conv * ig * (1.0 - ig)).astype(bf16)
            r.d_pre[s, 0:CW] = d_decay
            r.d_pre[s, CW : 2 * CW] = d_inject
            sums[0] = sums[0] + jnp.sum(d_decay.astype(f32), axis=0, keepdims=True)
            sums[1] = sums[1] + jnp.sum(d_inject.astype(f32), axis=0, keepdims=True)
            r.d_conv[k, pl.ds(o, 16)] = adjoint * mult * ig
        r.gchan[5:6] += sums[0]
        r.gchan[6:7] += sums[1]

    loop(T, 16, back)

    def conv_part(q, _):
        r.part_conv[q] = dot_nt(r.d_pre[...], r.w_di[:, :, ds(q * RW, RW, 16), :].reshape(CW, 2 * CW)).astype(bf16)
        return 0

    lax.fori_loop(0, RING, conv_part, 0)
    rs_act.end()
    rs_conv = Scatter(r.part_conv, r.got_conv)
    rs_conv.start()

    def finish_act(o, summed):
        s = pl.ds(o, 16)
        r.act[s] = (r.x_one[s] + summed).astype(bf16)

    rs_act.each(16, finish_act)
    deliver(r.act, r.activations)
    g_o.z_send()
    g_b.z_send()
    g_u.z_forward()
    g_dn.end()

    def grad_dec_inj(lanes):
        def run(q, _):
            value = dot_tn(r.conv[q], r.d_pre[:, lanes])
            r.w_di[:, :, ds(q * RW, RW, 16), lanes] = value.astype(bf16).reshape(RING, 2, RW, CW)
            return 0

        lax.fori_loop(0, RING, run, 0)

    grad_dec_inj(lanes_a)
    g_d = ColumnsGrad(r.w_di, r.h_di, r.z_di, r.l_di, RW, 0, CW, r.grads_di)
    g_d.core_send()
    rs_conv.mid()
    grad_dec_inj(lanes_b)
    g_j = ColumnsGrad(r.w_di, r.h_di, r.z_di, r.l_di, RW, CW, CW, r.grads_di)
    g_j.core_send()
    g_b.z_forward()
    rs_conv.end()

    for half in (0, 1):

        def add_conv(o, half=half):
            for k in (2 * half, 2 * half + 1):
                at = (k - 2 * half) * T + o
                r.d_conv[k, pl.ds(o, 16)] += rs_conv.total(half, pl.multiple_of(at, 16), 16)

        loop(T, 16, add_conv)
    halo_b = new()
    for k in range(PLANE):
        r.halo_out[4 * k : 4 * k + 4] = r.d_conv[k, 0:4]
    sent_b = push(r.halo_out, r.halo_in, to_prev, halo_b, pos > 0)
    g_d.z_send()

    def taps_back(o):
        sums = [jnp.zeros((1, CW), f32)] * 5
        for k in range(PLANE):
            ext = r.u[k, pl.ds(o, 24)]
            rows = ds(k * T + o, 16, 16)
            dc = r.d_conv[k, pl.ds(o, 16)]
            sums[4] = sums[4] + jnp.sum(dc, axis=0, keepdims=True)
            sums[0] = sums[0] + jnp.sum(dc * ext[8:24], axis=0, keepdims=True)
            for j in range(1, 4):
                term = jnp.where(wide(j, rows), dc * ext[8 - j : 24 - j], 0.0)
                sums[j] = sums[j] + jnp.sum(term, axis=0, keepdims=True)
        for j in range(5):
            r.gchan[j : j + 1] += sums[j]

    loop(T, 16, taps_back)

    @pl.when(pos == places - 1)
    def _():
        r.halo_in[...] = jnp.zeros((16, CW), f32)

    arrived(r.halo_in, halo_b, pos < places - 1)
    g_j.z_send()
    for k in range(PLANE):
        r.d_conv[k, T : T + 8] = jnp.concatenate([r.halo_in[4 * k : 4 * k + 4], jnp.zeros((4, CW), f32)], axis=0)

    def conv_back(o):
        for k in range(PLANE):
            ext = r.d_conv[k, pl.ds(o, 24)]
            rows = ds(k * T + o, 16, 16)
            total = r.chan[0:1] * ext[0:16]
            for j in range(1, 4):
                total = total + jnp.where(wide(3 + j, rows), r.chan[j : j + 1] * ext[j : 16 + j], 0.0)
            r.d_gu[rows, 0:CW] = total.astype(bf16)

    loop(T, 16, conv_back)

    def d_input_part(z, _):
        q = ds(z * chunk, chunk, chunk)
        value = dot_nt(r.d_gu[:, lanes_a], r.w_ib[z, :, :, lanes_a].reshape(chunk, CW)).reshape(PLANE, T, chunk)
        r.part[:, :, q] = (r.part[:, :, q].astype(f32) + value).astype(bf16)
        return 0

    lax.fori_loop(0, RING, d_input_part, 0)
    rs_three = Scatter(r.part, r.got_three)
    rs_three.start()

    def grad_input(z, _):
        q = ds(z * chunk, chunk, chunk)
        value = dot_tn(r.n_one[:, :, q].reshape(M, chunk), r.d_gu[:, lanes_a])
        r.w_ib[z, :, :, lanes_a] = value.astype(bf16).reshape(2, chunk // 2, CW)
        return 0

    lax.fori_loop(0, RING, grad_input, 0)
    g_i = ColumnsGrad(r.w_ib, r.h_ib, r.z_ib, r.l_ib, RD, 0, CW, r.grads_ib)
    g_i.core_send()
    rs_three.mid()
    g_o.z_forward()
    g_i.z_send()
    g_u.plane_send()
    g_d.z_forward()
    g_b.plane_send()
    rs_three.end()

    def norm_one_back(o, d_n):
        s = pl.ds(o, 16)
        v = r.x_all[p, s].astype(f32)
        rs = inverse_rms(v)
        z = v * rs
        dz = d_n * r.gains[0:1]
        r.ggain[0:1] += jnp.sum(d_n * z, axis=0, keepdims=True)
        r.d_x[s] = r.d_one[s] + rs * (dz - z * jnp.mean(dz * z, axis=-1, keepdims=True))

    rs_three.each(16, norm_one_back)
    deliver(r.d_x, r.d_tokens)
    small_grad.one()
    settle(sent_b)
    g_j.z_forward()
    g_i.z_forward()
    g_g.end()
    g_u.end()
    g_d.plane_send()
    g_o.end()
    small_grad.two()
    g_b.end()
    g_j.plane_send()
    g_i.plane_send()
    g_d.end()
    small_grad.end()
    g_j.end()
    g_i.end()
    assert not sent
    for result in results:
        local_wait(*result)


WEIGHTS = (
    "branch_weight",
    "input_weight",
    "decay_weight",
    "inject_weight",
    "output_weight",
    "mlp_gate",
    "mlp_up",
    "mlp_down",
)


def run_layer(NL, SEGS, tokens, cotangent, pack, weights):
    T, D = tokens.shape
    W, F = weights["branch_weight"].shape[1], weights["mlp_gate"].shape[1]
    CW, CF = W // PLANE, F // PLANE
    RD, RW, RF = D // SHARES, W // SHARES, F // SHARES
    GL, M, places = PLANE * RD, PLANE * T, RING * NL * 2
    hbm = pl.BlockSpec(memory_space=pl.ANY)
    ins = ["tokens", "cotangent", "pack_in", *WEIGHTS]
    outs = {
        "activations": ((T, D), bf16),
        "d_tokens": ((T, D), f32),
        "grads_ib": ((PLANE, RD, 2 * CW), bf16),
        "grads_di": ((PLANE, RW, 2 * CW), bf16),
        "grads_gu": ((PLANE, RD, 2 * CF), bf16),
        "grad_output_weight": ((RW, D), f32),
        "grad_mlp_down": ((RF, D), f32),
        "small_out": ((16, 128), f32),
    }
    columns = (("i", RD, CW), ("b", RD, CW), ("d", RW, CW), ("j", RW, CW), ("g", RD, CF), ("u", RD, CF))
    scratch = {
        "w_ib": ((RING, 2, PLANE * RD, 2 * CW), bf16),
        "w_di": ((RING, 2, PLANE * RW, 2 * CW), bf16),
        "w_gu": ((RING, 2, PLANE * RD, 2 * CF), bf16),
        "w_o": ((RING, 2, RW, D), bf16),
        "w_dn": ((RING, 2, RF, D), bf16),
        **{"raw_" + n: ((R, PLANE * C), bf16) for n, R, C in columns},
        **{"sort_" + n: ((PLANE, R, C), bf16) for n, R, C in columns},
        "h_ib": ((RING, PLANE * RD, 2 * CW), bf16),
        "h_di": ((RING, PLANE * RW, 2 * CW), bf16),
        "h_gu": ((RING, PLANE * RD, 2 * CF), bf16),
        "h_o": ((RING, RW, D), bf16),
        "h_dn": ((RING, RF, D), bf16),
        "z_ib": ((4, PLANE * RD, 2 * CW), bf16),
        "z_di": ((4, PLANE * RW, 2 * CW), bf16),
        "z_gu": ((4, PLANE * RD, 2 * CF), bf16),
        "z_o": ((4, RW, D), bf16),
        "z_dn": ((4, RF, D), bf16),
        "l_ib": ((PLANE, RD, 2 * CW), bf16),
        "l_di": ((PLANE, RW, 2 * CW), bf16),
        "l_gu": ((PLANE, RD, 2 * CF), bf16),
        "n_one": ((PLANE, T, D), bf16),
        "n_two": ((PLANE, T, D), bf16),
        "cot_all": ((PLANE, T, D), bf16),
        "d_out": ((PLANE, T, D), bf16),
        "conv": ((PLANE, M, CW), bf16),
        "part": ((PLANE, T, D), bf16),
        "part_act": ((PLANE, T, D), bf16),
        "part_conv": ((PLANE, M, CW), bf16),
        "got_one": ((6, T // 2, D), bf16),
        "got_two": ((6, T // 2, D), bf16),
        "got_three": ((6, T // 2, D), bf16),
        "got_act": ((6, T // 2, D), bf16),
        "got_conv": ((6, M // 2, CW), bf16),
        "mixed": ((M, CW), bf16),
        "hidden": ((M, CF), bf16),
        "d_pair": ((M, 2 * CF), bf16),
        "d_gu": ((M, 2 * CW), bf16),
        "d_pre": ((M, 2 * CW), bf16),
        "pair": ((M, 2 * CF), f32),
        "u": ((PLANE, T + 8, CW), f32),
        "state": ((PLANE, T + 8, CW), f32),
        "d_conv": ((PLANE, T + 8, CW), f32),
        **{name: ((M, CW), f32) for name in ("gated", "slope", "rgate", "igate", "decay", "work", "cum")},
        "x_one": ((T, D), f32),
        "d_one": ((T, D), f32),
        "carry_f": ((RING * NL, 2 * PLANE, CW), f32),
        "carry_b": ((RING * NL, 2 * PLANE, CW), f32),
        **{name: ((2 * PLANE, CW), f32) for name in ("own_f", "sib_f", "own_b", "sib_b")},
        "halo_out": ((16, CW), f32),
        "halo_in": ((16, CW), f32),
        "into": ((8, CW), f32),
        "x_all": ((PLANE, T, D), bf16),
        "x_halo": ((PLANE, 16, D), bf16),
        "n_halo": ((PLANE, 16, D), bf16),
        "g_dn": ((RING, 2, RF, D), bf16),
        "masks": ((7, M, 128), f32),
        "pack": ((16, 128), bf16),
        "pr": ((2 * RING, 16, 128), bf16),
        "pp": ((PLANE, 2 * RING, 16, 128), bf16),
        "act": ((T, D), bf16),
        "d_x": ((T, D), f32),
        "t_o": ((RW, D), f32),
        "t_dn": ((RF, D), f32),
        "small_sum": ((16, 128), f32),
        "gains": ((8, D), f32),
        "chan": ((8, CW), f32),
        "ggain": ((8, D), f32),
        "gchan": ((8, CW), f32),
        "gs": ((2 * RING, 16, 128), f32),
        "gg": ((2 * RING, 16, 128), f32),
        "gp": ((PLANE, 8, GL), f32),
    }
    dims = SimpleNamespace(
        T=T, D=D, W=W, F=F, CW=CW, CF=CF, RD=RD, RW=RW, RF=RF, NL=NL, SEGS=SEGS, receives=RECEIVES + 2 * RING * NL, names=[*ins, *outs, *scratch, "ss", "rs"]
    )
    flops = 3 * 2 * M * (D * 2 * CW + W * 2 * CW + CW * D + 3 * D * CF)
    results = pl.pallas_call(
        partial(layer, dims),
        out_shape=[jax.ShapeDtypeStruct(shape, kind) for shape, kind in outs.values()],
        in_specs=[hbm] * (3 + len(WEIGHTS)),
        out_specs=[hbm] * len(outs),
        scratch_shapes=[pltpu.VMEM(shape, kind) for shape, kind in scratch.values()]
        + [pltpu.SemaphoreType.DMA((SENDS,)), pltpu.SemaphoreType.DMA((dims.receives,))],
        compiler_params=pltpu.CompilerParams(
            collective_id=0, has_side_effects=True, vmem_limit_bytes=62 * 2**20
        ),
        cost_estimate=pl.CostEstimate(flops=flops, bytes_accessed=8 * 2**20, transcendentals=M * CW * 16),
        name="griffin_layer",
    )(tokens, cotangent, pack, *[weights[name] for name in WEIGHTS])
    return finish(dict(zip(outs, results, strict=True)), PLANE, CW, CF)


def finish(got, blocks, CW, CF):
    hbm = pl.BlockSpec(memory_space=pl.ANY)
    pairs = (
        ("grads_ib", ("grad_input_weight", "grad_branch_weight"), CW),
        ("grads_di", ("grad_decay_weight", "grad_inject_weight"), CW),
        ("grads_gu", ("grad_mlp_gate", "grad_mlp_up"), CF),
    )
    plain = ("d_tokens", "activations", "grad_output_weight", "grad_mlp_down")
    names = [*[name for name, _, _ in pairs], *plain]
    shapes = {name: got[name] for name in plain}
    for name, outs, C in pairs:
        for out in outs:
            shapes[out] = jax.ShapeDtypeStruct((got[name].shape[1], blocks * C), f32)
    scratch = [pltpu.VMEM(got[name].shape, got[name].dtype) for name in names]
    scratch += [pltpu.VMEM(shapes[out].shape, f32) for _, outs, _ in pairs for out in outs]
    count = 2 * len(plain) + 3 * len(pairs)

    def body(*refs):
        ins = dict(zip(names, refs[: len(names)], strict=True))
        outs = dict(zip(shapes, refs[len(names) : len(names) + len(shapes)], strict=True))
        held, sems = refs[len(names) + len(shapes) : -1], refs[-1]
        copies = []

        def copy(src, dst):
            copies.append(pltpu.make_async_copy(src, dst, sems.at[len(copies)]))
            copies[-1].start()
            return copies[-1]

        loads = [copy(ins[name], held[i]) for i, name in enumerate(names)]
        stores = []
        for i, (_, targets, C) in enumerate(pairs):
            loads[i].wait()
            for j, target in enumerate(targets):
                wide = held[len(names) + 2 * i + j]
                part = C // (2 * RING)
                values = [held[i][k, :, j * C : (j + 1) * C].astype(f32) for k in range(blocks)]
                wide[...] = jnp.concatenate(
                    [value[:, g * part : (g + 1) * part] for g in range(2 * RING) for value in values], axis=1
                )
                stores.append(copy(wide, outs[target]))
        for i, name in enumerate(plain):
            loads[len(pairs) + i].wait()
            stores.append(copy(held[len(pairs) + i], outs[name]))
        for store in stores:
            store.wait()

    results = pl.pallas_call(
        body,
        out_shape=[jax.ShapeDtypeStruct(like.shape, like.dtype) for like in shapes.values()],
        in_specs=[hbm] * len(names),
        out_specs=[hbm] * len(shapes),
        scratch_shapes=[*scratch, pltpu.SemaphoreType.DMA((count,))],
        compiler_params=pltpu.CompilerParams(vmem_limit_bytes=62 * 2**20),
        name="finish",
    )(*[got[name] for name in names])
    return {**got, **dict(zip(shapes, results, strict=True))}


def local(
    sizes,
    tokens,
    cotangent,
    doc_lengths,
    decay_exponent,
    branch_weight,
    input_weight,
    decay_weight,
    inject_weight,
    output_weight,
    mlp_gate,
    mlp_up,
    mlp_down,
    first_gain,
    second_gain,
    conv_taps,
    conv_bias,
    decay_bias,
    inject_bias,
):
    devices = math.prod(sizes.values())
    width = branch_weight.shape[1]
    at = {name: lax.axis_index(name) for name in AXES}
    mine = at["yl"] * 2 + at["xl"]
    ring = at["zh"] * 2 + at["c"]
    share = ring * PLANE + mine
    groups = devices // SHARES

    def pooled(value, axis=0):
        if groups == 1:
            return value
        whole = lax.all_gather(value, AXES, axis=axis, tiled=True)
        size = whole.shape[axis] // SHARES
        return lax.dynamic_slice_in_dim(whole, share * size, size, axis)

    def rows(value):
        value = value.astype(bf16)
        return jnp.pad(value, ((0, 0), (0, 128 - value.shape[1])))

    gains = pooled(jnp.stack([first_gain, second_gain]), 1)
    chan = pooled(jnp.concatenate([conv_taps.T, jnp.stack([conv_bias, decay_bias, inject_bias])]), 1)
    RD, RW = gains.shape[1], chan.shape[1]
    rates = decay_exponent.reshape(2 * RING, PLANE, width // SHARES)
    rates = lax.dynamic_index_in_dim(rates, mine, 1, keepdims=False).reshape(-1, 128)
    lengths = jnp.concatenate([doc_lengths // 256, doc_lengths % 256])
    pack = jnp.concatenate([rows(gains), rows(chan), rows(lengths), rows(rates)])
    pack = jnp.pad(pack, ((0, 16 - pack.shape[0]), (0, 0)))

    weights = dict(
        zip(
            WEIGHTS,
            (branch_weight, input_weight, decay_weight, inject_weight, output_weight, mlp_gate, mlp_up, mlp_down),
            strict=True,
        )
    )
    weights = {name: pooled(value) for name, value in weights.items()}
    got = run_layer(sizes["zl"], doc_lengths.shape[1], tokens[0], cotangent[0], pack, weights)

    def returned(value, axis=0):
        if groups == 1:
            return value
        shape = list(value.shape)
        size = shape[axis]
        shape[axis] = size * SHARES
        whole = lax.dynamic_update_slice_in_dim(jnp.zeros(shape, bf16), value.astype(bf16), share * size, axis)
        return lax.psum_scatter(whole, AXES, scatter_dimension=axis, tiled=True).astype(f32)

    grads = [returned(got["grad_" + name]) for name in WEIGHTS]
    gain_sum = returned(got["small_out"][:2, :RD], 1)
    chan_sum = returned(got["small_out"][8:15, :RW], 1)
    return (
        got["activations"][None],
        got["d_tokens"][None],
        *grads,
        gain_sum[0],
        gain_sum[1],
        chan_sum[:4].T,
        chan_sum[4],
        chan_sum[5],
        chan_sum[6],
    )


def solution(mesh):
    seq, dp = mesh.shape["seq"], mesh.shape["dp"]
    across = 1 << ((dp.bit_length() - 1) // 2)
    sizes = dict(zip(AXES, (RING, seq // (2 * RING), 2, dp // across // 2, 2, across // 2, 2), strict=True))
    split = Mesh(mesh.devices.reshape(tuple(sizes.values())), AXES)
    along_seq, along_dp = AXES[:3], AXES[3:]
    rows = P(along_dp, along_seq, None)
    in_specs = (rows, rows, P(along_dp, None), P(), *[P(AXES, None)] * 8, P(AXES), P(AXES), P(AXES, None), *[P(AXES)] * 3)
    out_specs = (rows, rows, *[P(AXES, None)] * 8, P(AXES), P(AXES), P(AXES, None), *[P(AXES)] * 3)
    return jax.shard_map(partial(local, sizes), mesh=split, in_specs=in_specs, out_specs=out_specs, check_vma=False)
```

```python
import itertools
import math
from functools import partial
from types import SimpleNamespace

import jax
import jax.numpy as jnp
from jax import lax
from jax.experimental import pallas as pl
from jax.experimental.pallas import tpu as pltpu
from jax.sharding import Mesh, PartitionSpec as P

f32, bf16 = jnp.float32, jnp.bfloat16
MESH = pl.DeviceIdType.MESH
AXES = ("zh", "zl", "c", "yh", "yl", "xh", "xl")
RING = 4
PLANE = 4
SHARES = RING * 2 * PLANE
SENDS = 60
RECEIVES = 188

eps_norm = 1e-06
floor_gap = 1e-05
rate_scale = 8.0
gelu_root = math.sqrt(2.0 / math.pi)
gelu_cube = 0.044715


def dot(left, right):
    return jnp.dot(left, right, preferred_element_type=f32)


def dot_nt(left, right):
    return lax.dot_general(left, right, (((1,), (1,)), ((), ())), preferred_element_type=f32)


def dot_tn(left, right):
    return lax.dot_general(left, right, (((0,), (0,)), ((), ())), preferred_element_type=f32)


def gelu_parts(v):
    t = jnp.tanh(gelu_root * (v + gelu_cube * v * v * v))
    half = 0.5 * (1.0 + t)
    slope = half + 0.5 * v * (1.0 - t * t) * gelu_root * (1.0 + 3.0 * gelu_cube * v * v)
    return v * half, slope


def minus_expm1(y, root):
    poly = 1.0 + y * (1.0 / 7.0)
    for k in (6, 5, 4, 3, 2):
        poly = 1.0 + y * poly * (1.0 / k)
    return jnp.where(y > -0.35, -y * poly, 1.0 - root * root)


def inverse_rms(v):
    return lax.rsqrt(jnp.mean(v * v, axis=-1, keepdims=True) + eps_norm)


def loop(total, step, body):
    def run(j, _):
        body(pl.multiple_of(j * step, step))
        return 0

    lax.fori_loop(0, total // step, run, 0)


def layer(dims, *refs):
    T, D, W, F, CW, CF = dims.T, dims.D, dims.W, dims.F, dims.CW, dims.CF
    RD, RW, RF, NL = dims.RD, dims.RW, dims.RF, dims.NL
    M = PLANE * T
    r = SimpleNamespace(**dict(zip(dims.names, refs, strict=True)))

    zh, zl, c = lax.axis_index("zh"), lax.axis_index("zl"), lax.axis_index("c")
    yl, xl = lax.axis_index("yl"), lax.axis_index("xl")
    p = yl * 2 + xl
    px, py, pd = yl * 2 + (1 - xl), (1 - yl) * 2 + xl, (1 - yl) * 2 + (1 - xl)
    to_x, to_y, to_d = {"xl": 1 - xl}, {"yl": 1 - yl}, {"yl": 1 - yl, "xl": 1 - xl}
    plane_peers = ((px, to_x), (py, to_y), (pd, to_d))
    to_core = {"c": 1 - c}
    flat_z = zh * NL + zl
    places = RING * NL * 2
    pos = flat_z * 2 + c

    def place(at):
        return {"zh": at // (2 * NL), "zl": (at // 2) % NL, "c": at % 2}

    count = itertools.count()

    def new(n=1):
        first = next(count)
        for _ in range(n - 1):
            next(count)
        assert first + n <= dims.receives
        return first

    spare = list(range(SENDS))
    sent = []

    def push(src, dst, dev, rsem, pred=None, instead=None):
        i = spare.pop(0) if instead is None else instead[2]

        def make():
            return pltpu.make_async_remote_copy(
                src, dst, r.ss.at[i], r.rs.at[rsem], device_id=dev, device_id_type=MESH
            )

        if pred is None:
            make().start()
        else:
            pl.when(pred)(lambda: make().start())
        entry = (make, pred, i, instead is None)
        sent.append(entry)
        return entry

    def settle(*entries):
        for entry in entries:
            make, pred, i, owner = entry
            if pred is None:
                make().wait_send()
            else:
                pl.when(pred)(lambda make=make: make().wait_send())
            sent.remove(entry)
            if owner:
                spare.append(i)

    def arrived(dst, rsem, pred=None):
        def wait():
            pltpu.make_async_remote_copy(
                dst, dst, r.ss.at[0], r.rs.at[rsem], device_id=to_core, device_id_type=MESH
            ).wait_recv()

        if pred is None:
            wait()
        else:
            pl.when(pred)(wait)

    def keep_local(src, dst, rsem):
        pltpu.make_async_copy(src, dst, r.rs.at[rsem]).start()

    def local_wait(src, dst, rsem):
        pltpu.make_async_copy(src, dst, r.rs.at[rsem]).wait()

    results = []

    def deliver(src, dst):
        sem = new()
        keep_local(src, dst, sem)
        results.append((src, dst, sem))

    def ds(start, size, unit):
        return pl.ds(pl.multiple_of(start, unit), size)

    class Gather:
        def __init__(self, buf):
            self.buf, half = buf, buf.shape[1] // 2
            self.h0, self.h1 = pl.ds(0, half), pl.ds(half, half)
            self.rx0, self.rx1, self.ry0, self.ry1, self.rd = (new() for _ in range(5))
            self.out = []

        def start(self):
            b = self.buf
            own0, own1 = b.at[p, self.h0], b.at[p, self.h1]
            self.out.append(push(own0, own0, to_x, self.rx0))
            self.out.append(push(own1, own1, to_y, self.ry1))
            self.out.append(push(own1, own1, to_x, self.rx1))
            self.out.append(push(own0, own0, to_y, self.ry0))

        def mid(self):
            b = self.buf
            got0, got1 = b.at[px, self.h0], b.at[py, self.h1]
            arrived(got0, self.rx0)
            self.out.append(push(got0, got0, to_y, self.rd))
            arrived(got1, self.ry1)
            self.out.append(push(got1, got1, to_x, self.rd))

        def wait_x(self):
            arrived(self.buf.at[px, self.h1], self.rx1)

        def wait_y(self):
            arrived(self.buf.at[py, self.h0], self.ry0)

        def wait_d(self):
            arrived(self.buf.at[pd], self.rd)

        def end(self):
            self.wait_x()
            self.wait_y()
            self.wait_d()
            settle(*self.out)

    class Scatter:
        def __init__(self, buf, recv):
            self.buf, self.recv = buf, recv
            self.half = buf.shape[1] // 2
            self.h0, self.h1 = pl.ds(0, self.half), pl.ds(self.half, self.half)
            self.sems = [new(), new(), *[new()] * 4]
            self.out = []

        def start(self):
            self.start_far()
            self.start_near()

        def start_far(self):
            b, v, s = self.buf, self.recv, self.sems
            self.out.append(push(b.at[pd, self.h0], v.at[0], to_x, s[0]))
            self.out.append(push(b.at[pd, self.h1], v.at[1], to_y, s[1]))

        def start_near(self):
            b, v, s = self.buf, self.recv, self.sems
            self.out.append(push(b.at[px, self.h0], v.at[2], to_x, s[2]))
            self.out.append(push(b.at[py, self.h1], v.at[3], to_y, s[3]))

        def mid(self):
            b, v, s = self.buf, self.recv, self.sems
            arrived(v.at[0], s[0])
            step = 16

            def add0(o):
                b[py, pl.ds(o, step)] = (b[py, pl.ds(o, step)].astype(f32) + v[0, pl.ds(o, step)].astype(f32)).astype(bf16)

            loop(self.half, step, add0)
            self.out.append(push(b.at[py, self.h0], v.at[4], to_y, s[4]))
            arrived(v.at[1], s[1])

            def add1(o):
                q = pl.ds(pl.multiple_of(self.half + o, step), step)
                b[px, q] = (b[px, q].astype(f32) + v[1, pl.ds(o, step)].astype(f32)).astype(bf16)

            loop(self.half, step, add1)
            self.out.append(push(b.at[px, self.h1], v.at[5], to_x, s[5]))

        def end(self):
            arrived(self.recv.at[pl.ds(2, 4)], self.sems[2])
            settle(*self.out)

        def total(self, half, o, step):
            b, v = self.buf, self.recv
            own = b[p, pl.ds(pl.multiple_of(half * self.half + o, step), step)].astype(f32)
            q = pl.ds(o, step)
            return own + v[2 + half, q].astype(f32) + v[4 + half, q].astype(f32)

        def each(self, step, body, init=None):
            for half in (0, 1):

                def run(j, carry, half=half):
                    o = pl.multiple_of(j * step, step)
                    return body(pl.multiple_of(half * self.half + o, step), self.total(half, o, step), carry)

                init = lax.fori_loop(0, self.half // step, run, init)
            return init

    def z_send(src, block, rz):
        out = []
        out.append(push(src, block(zh), {"zh": zh + 2}, rz + zh, zh + 2 < RING))
        out.append(push(src, block(zh), {"zh": zh - 2}, rz + zh, zh - 2 >= 0, out[-1]))
        out.append(push(src, block(zh), {"zh": zh + 1}, rz + zh, zh + 1 < RING))
        out.append(push(src, block(zh), {"zh": zh - 1}, rz + zh, zh - 1 >= 0))
        return out

    def z_forward(block, rz):
        last = RING - 1
        arrived(block(0), rz, zh == last - 1)
        one = push(block(0), block(0), {"zh": zh + 1}, rz, zh == last - 1)
        arrived(block(last), rz + last, zh == 1)
        two = push(block(last), block(last), {"zh": zh - 1}, rz + last, zh == 1, one)
        return [one, two]

    def z_wait(block, rz):
        last = RING - 1
        arrived(block(0), rz, (zh == 1) | (zh == last))
        arrived(block(1), rz + 1, zh != 1)
        arrived(block(2), rz + 2, zh != 2)
        arrived(block(last), rz + last, (zh == 0) | (zh == last - 1))

    class ZSum:
        def __init__(self, block, slot, add):
            self.block, self.slot, self.add = block, slot, add
            self.sems = new(4)
            self.out = []

        def send(self):
            b, v, s = self.block, self.slot, self.sems
            last = RING - 1
            o = self.out
            o.append(push(b(last), v(1), {"zh": zh + 1}, s + 1, zh == 0))
            o.append(push(b(0), v(3), {"zh": zh - 1}, s + 3, zh == last, o[-1]))
            o.append(push(b(zh + 2), v(1), {"zh": zh + 2}, s + 1, zh == 0))
            o.append(push(b(zh - 2), v(3), {"zh": zh - 2}, s + 3, zh == last, o[-1]))
            o.append(push(b(zh + 1), v(0), {"zh": zh + 1}, s + 0, zh < last))
            o.append(push(b(zh - 1), v(2), {"zh": zh - 1}, s + 2, zh > 0))

        def forward(self):
            b, v, s = self.block, self.slot, self.sems
            last = RING - 1

            def up():
                arrived(v(1), s + 1)
                self.add(last, 1)

            def down():
                arrived(v(3), s + 3)
                self.add(0, 3)

            pl.when(zh == 1)(up)
            self.out.append(push(b(last), v(1), {"zh": zh + 2}, s + 1, zh == 1))
            pl.when(zh == last - 1)(down)
            self.out.append(push(b(0), v(3), {"zh": zh - 2}, s + 3, zh == last - 1, self.out[-1]))

        def end(self):
            v, s = self.slot, self.sems
            arrived(v(0), s, zh >= 1)
            arrived(v(1), s + 1, zh >= 2)
            arrived(v(2), s + 2, zh <= 2)
            arrived(v(3), s + 3, zh <= 1)
            settle(*self.out)

        def total(self, own, parts):
            for part, pred in zip(parts, (zh >= 1, zh >= 2, zh <= 2, zh <= 1), strict=True):
                own = own + jnp.where(pred, part.astype(f32), 0.0)
            return own

    class Column:
        def __init__(self, src, raw, sorted_, w, R, C, lane0):
            self.src, self.raw, self.sorted = src, raw, sorted_
            self.w, self.R, self.C, self.lanes = w, R, C, pl.ds(lane0, C)
            self.rl, self.ra, self.rz, self.rc = new(), new(), new(4), new()
            self.out = []

        def halves(self):
            out = []
            for k in (0, 1):
                part = Column(self.src, self.raw, self.sorted, self.w, self.R, self.C, 0)
                part.lanes = pl.ds(self.lanes.start + k * self.C // 2, self.C // 2)
                out.append(part)
            return out

        def spread_wait(self):
            arrived(self.block(zh), self.ra)
            settle(*self.out)
            self.out = []

        def load(self):
            keep_local(self.src, self.raw, self.rl)

        def prepare(self):
            local_wait(self.src, self.raw, self.rl)
            value, part = self.raw[...], self.C // (2 * RING)
            for k in range(PLANE):
                first = [(g * PLANE + k) * part for g in range(2 * RING)]
                self.sorted[k] = jnp.concatenate([value[:, at : at + part] for at in first], axis=1)

        def spread(self):
            dst = self.w.at[zh, c, ds(p * self.R, self.R, 16), self.lanes]
            for k, dev in plane_peers:
                self.out.append(push(self.sorted.at[k], dst, dev, self.ra))
            keep_local(self.sorted.at[p], dst, self.ra)

        def block(self, z):
            return self.w.at[z, c, :, self.lanes]

        def z_send(self, spread=True):
            if spread:
                arrived(self.block(zh), self.ra)
            self.out += z_send(self.block(zh), self.block, self.rz)

        def z_forward(self):
            self.out += z_forward(self.block, self.rz)

        def z_wait(self):
            z_wait(self.block, self.rz)
            half = self.w.at[:, c, :, self.lanes]
            self.out.append(push(half, half, to_core, self.rc))

        def end(self):
            arrived(self.w.at[:, 1 - c, :, self.lanes], self.rc)
            settle(*self.out)

    class Row(Column):
        def __init__(self, src, w):
            self.src, self.w, self.lanes = src, w, pl.ds(0, w.shape[3])
            self.ra, self.rz, self.rc = new(), new(4), new()
            self.out = []

        def z_send(self):
            keep_local(self.src, self.block(zh), self.ra)
            self.out += z_send(self.src, self.block, self.rz)

        def z_wait(self):
            local_wait(self.src, self.block(zh), self.ra)
            super().z_wait()

    class ColumnsGrad:
        def __init__(self, g, other, slots, land, R, lane0, lanes, result):
            self.g, self.other, self.slots, self.land = g, other, slots, land
            self.R, self.lanes, self.result = R, pl.ds(lane0, lanes), result
            self.rows = PLANE * R
            self.rc, self.rl = new(), new()
            self.zsum = ZSum(
                lambda z: g.at[z, c, :, self.lanes], lambda k: slots.at[k, :, self.lanes], self.add_slot
            )

        def add_slot(self, z, k):
            g, q = self.g, self.lanes

            def add(o):
                s = pl.ds(o, 16)
                g[z, c, s, q] = (g[z, c, s, q].astype(f32) + self.slots[k, s, q].astype(f32)).astype(bf16)

            loop(self.rows, 16, add)

        def core_send(self):
            self.pushed = push(
                self.g.at[:, 1 - c, :, self.lanes], self.other.at[:, :, self.lanes], to_core, self.rc
            )

        def z_send(self):
            g, q = self.g, self.lanes
            arrived(self.other.at[:, :, q], self.rc)
            for z in range(RING):

                def add(o):
                    s = pl.ds(o, 16)
                    g[z, c, s, q] = (g[z, c, s, q].astype(f32) + self.other[z, s, q].astype(f32)).astype(bf16)

                loop(self.rows, 16, add)
            self.zsum.send()

        def z_forward(self):
            self.zsum.forward()

        def plane_send(self):
            g, q, R = self.g, self.lanes, self.R
            self.zsum.end()

            def add(o):
                s = pl.ds(o, 16)
                parts = [self.slots[k, s, q] for k in range(4)]
                g[zh, c, s, q] = self.zsum.total(g[zh, c, s, q].astype(f32), parts).astype(bf16)

            loop(PLANE * R, 16, add)
            dst = self.land.at[p, :, q]
            self.out = [self.pushed]
            for k, dev in plane_peers:
                self.out.append(push(g.at[zh, c, ds(k * R, R, 16), q], dst, dev, self.rl))
            keep_local(g.at[zh, c, ds(p * R, R, 16), q], dst, self.rl)

        def end(self):
            arrived(self.land.at[:, :, self.lanes], self.rl)
            settle(*self.out)
            deliver(self.land.at[:, :, self.lanes], self.result.at[:, :, self.lanes])

    class RowsGrad(ColumnsGrad):
        def __init__(self, g, other, slots, total, result):
            super().__init__(g, other, slots, None, 0, 0, g.shape[3], result)
            self.rows, self.sum = g.shape[2], total

        def end(self):
            self.zsum.end()
            settle(self.pushed)

            def add(o):
                s = pl.ds(o, 16)
                self.sum[s] = self.zsum.total(self.g[zh, c, s].astype(f32), [self.slots[k, s] for k in range(4)])

            loop(self.rows, 16, add)
            deliver(self.sum, self.result)

    class Carry:
        def __init__(self, own, sib, buf, later):
            self.own, self.sib, self.buf, self.later = own, sib, buf, later
            self.rc, self.rz = new(), new(RING * NL)
            self.out = []

        def order(self):
            return range(RING * NL) if self.later else reversed(range(RING * NL))

        def send_core(self):
            self.out.append(push(self.own, self.sib, to_core, self.rc))

        def send(self):
            arrived(self.sib, self.rc)
            own, sib = self.own[...], self.sib[...]
            near = (c == 0) if self.later else (c == 1)
            head, tail = jnp.where(near, own, sib), jnp.where(near, sib, own)
            self.buf[flat_z, 0:PLANE] = tail[0:PLANE] * head[0:PLANE]
            self.buf[flat_z, PLANE : 2 * PLANE] = (
                tail[0:PLANE] * head[PLANE : 2 * PLANE] + tail[PLANE : 2 * PLANE]
            )
            part = self.buf.at[flat_z]
            for at in self.order():
                pred = (flat_z < at) if self.later else (flat_z > at)
                self.out.append(push(part, part, {"zh": at // NL, "zl": at % NL}, self.rz + flat_z, pred))

        def fold(self, into):
            into[...] = jnp.zeros_like(into)

            def take(part):
                into[0:PLANE] = part[0:PLANE] * into[0:PLANE] + part[PLANE : 2 * PLANE]

            for at in self.order():
                pred = (flat_z > at) if self.later else (flat_z < at)

                def chip(at=at):
                    arrived(self.buf.at[at], self.rz + at)
                    take(self.buf[at])

                pl.when(pred)(chip)
            pl.when((c == 1) if self.later else (c == 0))(lambda: take(self.sib[...]))
            settle(*self.out)

    GL = PLANE * RD
    ring = zh * 2 + c

    def ring_place(at):
        return {"zh": at // 2, "c": at % 2}

    class Small:
        def __init__(self):
            self.rr, self.rk = new(), new()
            self.out = []

        def one(self):
            for at in range(2 * RING):
                self.out.append(push(r.pack, r.pr.at[ring], ring_place(at), self.rr, ring != at))
            keep_local(r.pack, r.pr.at[ring], self.rr)

        def two(self):
            arrived(r.pr, self.rr)
            lines = []
            for at in range(2 * RING):
                tile = r.pr[at].astype(f32)
                lines.append(jnp.concatenate([tile[row : row + 1, 0:32] for row in (0, 1, 9, 10)], axis=1))
            r.line[...] = jnp.concatenate([*lines, jnp.zeros((16 - 2 * RING, 128), f32)], axis=0).astype(bf16)
            for _, dev in plane_peers:
                self.out.append(push(r.line, r.pp.at[p], dev, self.rk))
            keep_local(r.line, r.pp.at[p], self.rk)

        def three(self):
            arrived(r.pp, self.rk)
            parts = [r.pp[k].astype(f32) for k in range(PLANE)]
            for row in (0, 1):
                lanes = slice(row * 32, row * 32 + RD)
                wide = jnp.concatenate([part[:, lanes] for part in parts], axis=1)
                for at in range(2 * RING):
                    r.gains[row : row + 1, at * GL : (at + 1) * GL] = wide[at : at + 1]
            whole = jnp.concatenate([r.pr[at, :, 0:RW].astype(f32) for at in range(2 * RING)], axis=1)
            r.chan[...] = whole[2:10]
            rate = r.pack[...].astype(f32)
            for k in range(CW // 128):
                r.chan[7:8, k * 128 : (k + 1) * 128] = jnp.exp2(-rate[11 + k : 12 + k])

        def four(self):
            where = lax.broadcasted_iota(jnp.int32, (T, 128), 0).astype(f32) + (pos * T).astype(f32)
            for k in range(PLANE):
                part = r.pp[k].astype(f32)
                starts, ends = [], []
                total = jnp.zeros((1, 1), f32)
                for j in range(dims.SEGS):
                    starts.append(total)
                    total = total + part[0:1, 64 + j : 65 + j] * 256.0 + part[0:1, 96 + j : 97 + j]
                    ends.append(total)

                def seg(shift):
                    at = where + float(shift)
                    value = jnp.zeros((T, 128), f32)
                    for end in ends:
                        value = value + jnp.where(at >= end, 1.0, 0.0)
                    return jnp.where((at < 0.0) | (at >= float(T * places)), -1.0, value)

                here = seg(0)
                rows = pl.ds(k * T, T)
                first = jnp.zeros((T, 128), f32)
                for start in starts:
                    first = jnp.where(where == start, 1.0, first)
                r.masks[0, rows] = first
                for j in (1, 2, 3):
                    r.masks[j, rows] = jnp.where(seg(-j) == here, 1.0, 0.0)
                    r.masks[3 + j, rows] = jnp.where(seg(j) == here, 1.0, 0.0)
            settle(*self.out)

    class SmallGrad:
        def __init__(self):
            self.rg = new()
            self.out = []

        def one(self):
            for at in range(2 * RING):
                own = jnp.concatenate([r.gchan[:, at * RW : (at + 1) * RW], jnp.zeros((8, 128 - RW), f32)], axis=1)
                r.gs[at] = own
            for at in range(2 * RING):
                self.out.append(push(r.gs.at[at], r.gg.at[ring], ring_place(at), self.rg, ring != at))
            keep_local(r.gs.at[ring], r.gg.at[ring], self.rg)

        def two(self):
            arrived(r.gg, self.rg)
            value = r.gg[0]
            for at in range(1, 2 * RING):
                value = value + r.gg[at]
            r.small_sum[...] = value
            deliver(r.small_sum, r.small_out)
            settle(*self.out)

    barrier = pltpu.get_barrier_semaphore()
    for _, dev in plane_peers:
        pl.semaphore_signal(barrier, 1, device_id=dev, device_id_type=MESH)
    for at in range(places):

        @pl.when(pos != at)
        def _(at=at):
            pl.semaphore_signal(barrier, 1, device_id=place(at), device_id_type=MESH)

    first_loads = [
        (src, dst, new())
        for src, dst in (
            (r.pack_in, r.pack),
            (r.tokens, r.x_all.at[p]),
            (r.cotangent, r.cot_all.at[p]),
        )
    ]
    for load in first_loads:
        keep_local(*load)

    w_i = Column(r.input_weight, r.raw_i, r.sort_i, r.w_ib, RD, CW, 0)
    w_b = Column(r.branch_weight, r.raw_b, r.sort_b, r.w_ib, RD, CW, CW)
    w_d = Column(r.decay_weight, r.raw_d, r.sort_d, r.w_di, RW, CW, 0)
    w_j = Column(r.inject_weight, r.raw_j, r.sort_j, r.w_di, RW, CW, CW)
    w_g = Column(r.mlp_gate, r.raw_g, r.sort_g, r.w_gu, RD, CF, 0)
    w_u = Column(r.mlp_up, r.raw_u, r.sort_u, r.w_gu, RD, CF, CF)
    w_g1, w_g2 = w_g.halves()
    w_o, w_dn = Row(r.output_weight, r.w_o), Row(r.mlp_down, r.w_dn)
    ag_x, ag_conv, ag_two = Gather(r.x_all), Gather(r.conv), Gather(r.n_two)
    ag_cot, ag_out = Gather(r.cot_all), Gather(r.d_out)
    small, small_grad = Small(), SmallGrad()
    after, before = flat_z + c, flat_z - (1 - c)
    to_next = {"zh": after // NL, "zl": after % NL, "c": 1 - c}
    to_prev = {"zh": before // NL, "zl": before % NL, "c": 1 - c}
    step = 256
    chunk = PLANE * RD * 2

    for w in (w_i, w_d, w_j, w_b, w_g, w_u):
        w.load()
    w_i.prepare()
    w_d.prepare()
    pl.semaphore_wait(barrier, len(plane_peers) + places - 1)
    local_wait(*first_loads[0])
    small.one()
    w_o.z_send()
    w_i.spread()
    w_d.spread()
    local_wait(*first_loads[1])
    ag_x.start()
    halo_x = new()
    sent_x = push(r.x_all.at[p, pl.ds(T - 16, 16)], r.x_halo.at[p], to_next, halo_x, pos < places - 1)
    w_j.prepare()
    w_i.z_send()
    small.two()
    w_b.prepare()

    @pl.when(pos == 0)
    def _():
        r.x_halo[p] = jnp.zeros((16, D), bf16)

    arrived(r.x_halo.at[p], halo_x, pos > 0)
    halo_p = new(PLANE)
    sent_p = [push(r.x_halo.at[p], r.x_halo.at[p], dev, halo_p + p) for _, dev in plane_peers]
    ag_x.mid()
    w_i.z_forward()
    w_g.prepare()
    local_wait(*first_loads[2])
    small.three()

    def norm_block(k):
        def norm_one(o):
            s = pl.ds(o, 32)
            v = r.x_all[k, s].astype(f32)
            r.n_one[k, s] = (v * inverse_rms(v) * r.gains[0:1]).astype(bf16)

        loop(T, 32, norm_one)

    norm_block(p)
    w_d.z_send()
    ag_x.wait_x()
    norm_block(px)
    ag_x.wait_y()
    norm_block(py)
    w_j.spread()
    small.four()
    for k, _ in plane_peers:
        arrived(r.x_halo.at[k], halo_p + k)
    v = r.x_halo[...].reshape(PLANE * 16, D).astype(f32)
    r.n_halo[...] = (v * inverse_rms(v) * r.gains[0:1]).astype(bf16).reshape(PLANE, 16, D)
    ag_x.wait_d()
    norm_block(pd)
    settle(*ag_x.out, sent_x, *sent_p)
    w_b.spread()
    w_g.spread()
    w_o.z_forward()
    w_i.z_wait()
    w_u.prepare()
    w_j.z_send()
    w_i.end()

    def weight_ib(lanes):
        return r.w_ib[:, :, :, lanes].reshape(D, CW)

    lanes_a, lanes_b = pl.ds(0, CW), pl.ds(CW, CW)
    halo = dot(r.n_halo[...].reshape(PLANE * 16, D), weight_ib(lanes_a)).astype(bf16).astype(f32)
    body = dot(r.n_one[...].reshape(M, D), weight_ib(lanes_a)).astype(bf16).astype(f32)
    for k in range(PLANE):
        r.u[k, 0:8] = halo[k * 16 + 8 : (k + 1) * 16]
        r.u[k, 8 : 8 + T] = body[k * T : (k + 1) * T]

    def wide(j, rows):
        return jnp.concatenate([r.masks[j, rows]] * (CW // 128), axis=1) > 0.5

    def convolve(o):
        for k in range(PLANE):
            ext = r.u[k, pl.ds(o, 24)]
            rows = ds(k * T + o, 16, 16)
            total = r.chan[4:5] + r.chan[0:1] * ext[8:24]
            for j in range(1, 4):
                total = total + jnp.where(wide(j, rows), r.chan[j : j + 1] * ext[8 - j : 24 - j], 0.0)
            r.conv[p, rows] = total.astype(bf16)

    loop(T, 16, convolve)
    ag_conv.start()
    w_d.z_forward()
    w_b.z_send()
    ag_conv.mid()
    w_j.z_forward()
    w_d.z_wait()
    w_d.end()

    def pre(q, lanes):
        return dot(r.conv[q], r.w_di[:, :, ds(q * RW, RW, 16), lanes].reshape(CW, CW))

    r.pair[:, 0:CW] = pre(p, lanes_a)
    ag_conv.wait_x()
    r.pair[:, 0:CW] += pre(px, lanes_a)
    ag_conv.wait_y()
    r.pair[:, 0:CW] += pre(py, lanes_a)
    w_b.z_forward()
    ag_conv.wait_d()
    r.pair[:, 0:CW] += pre(pd, lanes_a)
    settle(*ag_conv.out)
    w_g.spread_wait()
    w_g1.z_send(False)
    w_j.z_wait()
    w_u.spread()
    ag_cot.start()
    w_o.z_wait()
    w_j.end()
    r.pair[:, CW : 2 * CW] = (pre(0, lanes_b) + pre(1, lanes_b)) + (pre(2, lanes_b) + pre(3, lanes_b))

    def decay_terms(s, rg):
        log_a = -rate_scale * rg * r.chan[7:8]
        root = jnp.exp(log_a)
        gap = minus_expm1(2.0 * log_a, root)
        first = wide(0, s)
        return root, gap, jnp.where(first, 1.0, jnp.sqrt(jnp.maximum(gap, floor_gap))), first

    def gates_two(o):
        s = pl.ds(o, 16)
        rg = jax.nn.sigmoid(r.pair[s, 0:CW] + r.chan[5:6])
        ig = jax.nn.sigmoid(r.pair[s, CW : 2 * CW] + r.chan[6:7])
        root, _, mult, first = decay_terms(s, rg)
        r.rgate[s], r.igate[s] = rg, ig
        r.decay[s] = jnp.where(first, 0.0, root)
        r.work[s] = mult * ig * r.conv[p, s].astype(f32)

    loop(M, 16, gates_two)
    row = lax.broadcasted_iota(jnp.int32, (8, CW), 0)

    def scan_forward(j, carry):
        out = []
        for k in range(PLANE):
            s = ds(k * T + j * 8, 8, 8)
            a, b = r.decay[s], r.work[s]
            for n in (1, 2, 4):
                a_b = jnp.where(row >= n, pltpu.roll(a, n, 0), 1.0)
                b_b = jnp.where(row >= n, pltpu.roll(b, n, 0), 0.0)
                a, b = a * a_b, a * b_b + b
            total, prod = b + a * carry[2 * k], a * carry[2 * k + 1]
            r.state[k, ds(8 + j * 8, 8, 8)] = total
            r.cum[s] = prod
            out += [total[7:8], prod[7:8]]
        return tuple(out)

    zero, one = jnp.zeros((1, CW), f32), jnp.ones((1, CW), f32)
    ends = lax.fori_loop(0, T // 8, scan_forward, (zero, one) * PLANE)
    carry_f = Carry(r.own_f, r.sib_f, r.carry_f, True)
    for k in range(PLANE):
        r.own_f[k : k + 1] = ends[2 * k + 1]
        r.own_f[PLANE + k : PLANE + k + 1] = ends[2 * k]
    carry_f.send_core()
    w_b.z_wait()
    carry_f.send()
    w_g1.z_forward()
    w_g2.z_send(False)
    w_b.end()
    r.work[...] = dot(r.n_one[...].reshape(M, D), weight_ib(lanes_b))

    def gates_one(o):
        s = pl.ds(o, 16)
        r.gated[s], r.slope[s] = gelu_parts(r.work[s])

    loop(M, 16, gates_one)
    ag_cot.mid()
    carry_f.fold(r.into)
    for k in range(PLANE):
        r.state[k, 0:8] = jnp.broadcast_to(r.into[k : k + 1], (8, CW))

    def mix(o):
        for k in range(PLANE):
            s, t = ds(k * T + o, 16, 16), ds(8 + o, 16, 8)
            state = r.state[k, t] + r.cum[s] * r.into[k : k + 1]
            r.state[k, t] = state
            r.mixed[s] = (state * r.gated[s]).astype(bf16)

    loop(T, 16, mix)

    w_o.end()

    def out_part(o):
        q = pl.ds(o, step)
        r.part[:, :, q] = dot(r.mixed[...], r.w_o[:, :, :, q].reshape(CW, step)).astype(bf16).reshape(PLANE, T, step)

    loop(D, step, out_part)
    rs_one = Scatter(r.part, r.got_one)
    rs_one.start()
    w_g1.z_wait()
    w_g2.z_forward()
    w_u.z_send()
    ag_cot.end()
    rs_one.mid()
    rs_one.end()

    def norm_two(o, summed, _):
        s = pl.ds(o, 32)
        v = r.x_all[p, s].astype(f32) + summed
        r.x_one[s] = v
        r.n_two[p, s] = (v * inverse_rms(v) * r.gains[1:2]).astype(bf16)

    rs_one.each(32, norm_two)
    ag_two.start()
    w_u.z_forward()
    w_dn.z_send()
    ag_two.mid()
    w_g2.z_wait()
    w_g1.end()
    w_g2.end()
    ag_two.end()

    def mlp_in(o):
        q = pl.ds(o, step)
        r.pair[:, q] = dot(r.n_two[...].reshape(M, D), r.w_gu[:, :, :, q].reshape(D, step))

    loop(CF, step, mlp_in)
    w_dn.z_forward()
    w_u.z_wait()
    w_u.end()
    loop(CF, step, lambda o: mlp_in(pl.multiple_of(CF + o, step)))

    def gates_mlp(o):
        s = pl.ds(o, 16)
        value, slope = gelu_parts(r.pair[s, 0:CF])
        up = r.pair[s, CF : 2 * CF]
        r.hidden[s] = (value * up).astype(bf16)
        r.pair[s, 0:CF] = slope * up
        r.pair[s, CF : 2 * CF] = value

    loop(M, 16, gates_mlp)

    half = CF // 2
    for k in (0, 1):
        for o in range(0, D, D // 2):
            value = dot_tn(r.hidden[:, k * half : (k + 1) * half], r.cot_all[:, :, o : o + D // 2].reshape(M, D // 2))
            r.g_dn[k * RING // 2 : (k + 1) * RING // 2, :, :, o : o + D // 2] = value.astype(bf16).reshape(
                RING // 2, 2, RF, D // 2
            )
    g_dn = RowsGrad(r.g_dn, r.h_dn, r.z_dn, r.t_dn, r.grad_mlp_down)
    g_dn.core_send()
    w_dn.z_wait()
    g_dn.z_send()
    w_dn.end()

    for k in range(CF // step):
        back = dot_nt(r.cot_all[...].reshape(M, D), r.w_dn[...].reshape(CF, D)[k * step : (k + 1) * step])
        r.d_pair[:, k * step : (k + 1) * step] = (back * r.pair[:, k * step : (k + 1) * step]).astype(bf16)
        r.d_pair[:, CF + k * step : CF + (k + 1) * step] = (
            back * r.pair[:, CF + k * step : CF + (k + 1) * step]
        ).astype(bf16)

    def d_two_part(z, _):
        q = ds(z * chunk, chunk, chunk)
        r.part[:, :, q] = (
            dot_nt(r.d_pair[...], r.w_gu[z].reshape(chunk, 2 * CF)).astype(bf16).reshape(PLANE, T, chunk)
        )
        return 0

    lax.fori_loop(0, RING, d_two_part, 0)
    rs_two = Scatter(r.part, r.got_two)
    rs_two.start()

    def grad_gate_up(lane0):
        lanes = pl.ds(lane0, CF)

        def run(z, _):
            q = ds(z * chunk, chunk, chunk)
            value = dot_tn(r.n_two[:, :, q].reshape(M, chunk), r.d_pair[:, lanes])
            r.w_gu[z, :, :, lanes] = value.astype(bf16).reshape(2, chunk // 2, CF)
            return 0

        lax.fori_loop(0, RING, run, 0)

    grad_gate_up(0)
    g_g = ColumnsGrad(r.w_gu, r.h_gu, r.z_gu, r.l_gu, RD, 0, CF, r.grads_gu)
    g_g.core_send()
    rs_two.mid()
    g_dn.z_forward()
    g_g.z_send()
    grad_gate_up(CF)
    g_u, g_v = (
        ColumnsGrad(r.w_gu, r.h_gu, r.z_gu, r.l_gu, RD, lane0, CF // 2, r.grads_gu) for lane0 in (CF, CF + CF // 2)
    )
    g_u.core_send()
    g_v.core_send()

    def act_part(o):
        q = pl.ds(o, step)
        r.part_act[:, :, q] = dot(r.hidden[...], r.w_dn[:, :, :, q].reshape(CF, step)).astype(bf16).reshape(PLANE, T, step)

    loop(D, step, act_part)
    r.gchan[...] = jnp.zeros_like(r.gchan)
    rs_two.end()

    def norm_two_back(o, d_two, _):
        s = pl.ds(o, 32)
        v = r.x_one[s]
        rs = inverse_rms(v)
        z = v * rs
        dz = d_two * r.gains[1:2]
        d_one = r.cot_all[p, s].astype(f32) + rs * (dz - z * jnp.mean(dz * z, axis=-1, keepdims=True))
        r.d_one[s] = d_one
        r.d_out[p, s] = d_one.astype(bf16)

    rs_two.each(32, norm_two_back)
    ag_out.start()
    g_g.z_forward()
    g_u.z_send()
    ag_out.mid()
    ag_out.end()
    rs_act = Scatter(r.part_act, r.got_act)
    rs_act.start()
    g_u.z_forward()

    r.work[...] = dot_nt(r.d_out[...].reshape(M, D), r.w_o[...].reshape(CW, D))

    def split(o):
        for k in range(PLANE):
            s = ds(k * T + o, 16, 16)
            d_mixed = r.work[s]
            r.d_gu[s, CW : 2 * CW] = (d_mixed * r.state[k, ds(8 + o, 16, 8)] * r.slope[s]).astype(bf16)
            r.work[s] = d_mixed * r.gated[s]

    loop(T, 16, split)

    def scan_backward(i, carry):
        j = T // 8 - 1 - i
        out = []
        for k in range(PLANE):
            s = ds(k * T + j * 8, 8, 8)
            decay, b = r.decay[s], r.work[s]
            a = jnp.where(row < 7, pltpu.roll(decay, 7, 0), carry[3 * k + 2])
            for n in (1, 2, 4):
                a_b = jnp.where(row < 8 - n, pltpu.roll(a, 8 - n, 0), 1.0)
                b_b = jnp.where(row < 8 - n, pltpu.roll(b, 8 - n, 0), 0.0)
                a, b = a * a_b, a * b_b + b
            total, prod = b + a * carry[3 * k], a * carry[3 * k + 1]
            r.work[s], r.cum[s] = total, prod
            out += [total[0:1], prod[0:1], decay[0:1]]
        return tuple(out)

    heads = lax.fori_loop(0, T // 8, scan_backward, (zero, one, one) * PLANE)
    carry_b = Carry(r.own_b, r.sib_b, r.carry_b, False)
    for k in range(PLANE):
        r.own_b[k : k + 1] = r.own_f[k : k + 1]
        r.own_b[PLANE + k : PLANE + k + 1] = heads[3 * k] * heads[3 * k + 2]
    carry_b.send_core()

    def grad_out(o):
        q = pl.ds(o, D // 2)
        value = dot_tn(r.mixed[...], r.d_out[:, :, q].reshape(M, D // 2))
        r.w_o[:, :, :, q] = value.astype(bf16).reshape(RING, 2, RW, D // 2)

    loop(D, D // 2, grad_out)
    g_o = RowsGrad(r.w_o, r.h_o, r.z_o, r.t_o, r.grad_output_weight)
    g_o.core_send()
    carry_b.send()
    g_v.z_send()
    rs_act.mid()

    def d_branch_part(z, _):
        q = ds(z * chunk, chunk, chunk)
        r.part[:, :, q] = (
            dot_nt(r.d_gu[:, lanes_b], r.w_ib[z, :, :, lanes_b].reshape(chunk, CW))
            .astype(bf16)
            .reshape(PLANE, T, chunk)
        )
        value = dot_tn(r.n_one[:, :, q].reshape(M, chunk), r.d_gu[:, lanes_b])
        r.w_ib[z, :, :, lanes_b] = value.astype(bf16).reshape(2, chunk // 2, CW)
        return 0

    lax.fori_loop(0, RING, d_branch_part, 0)
    g_b = ColumnsGrad(r.w_ib, r.h_ib, r.z_ib, r.l_ib, RD, CW, CW, r.grads_ib)
    g_b.core_send()
    g_g.plane_send()
    carry_b.fold(r.into)
    g_b.z_send()

    def back(o):
        sums = [jnp.zeros((1, CW), f32)] * 2
        for k in range(PLANE):
            s = ds(k * T + o, 16, 16)
            adjoint = r.work[s] + r.cum[s] * r.into[k : k + 1]
            previous = r.state[k, pl.ds(o, 24)][7:23]
            rg, ig, decay, conv = r.rgate[s], r.igate[s], r.decay[s], r.conv[p, s].astype(f32)
            _, gap, mult, first = decay_terms(s, rg)
            d_mult = jnp.where(first, 0.0, adjoint * ig * conv)
            d_log = adjoint * previous * decay - jnp.where(gap > floor_gap, (1.0 - gap) * d_mult / mult, 0.0)
            d_decay = (-rate_scale * r.chan[7:8] * d_log * rg * (1.0 - rg)).astype(bf16)
            d_inject = (adjoint * mult * conv * ig * (1.0 - ig)).astype(bf16)
            r.d_pre[s, 0:CW] = d_decay
            r.d_pre[s, CW : 2 * CW] = d_inject
            sums[0] = sums[0] + jnp.sum(d_decay.astype(f32), axis=0, keepdims=True)
            sums[1] = sums[1] + jnp.sum(d_inject.astype(f32), axis=0, keepdims=True)
            r.d_conv[k, pl.ds(o, 16)] = adjoint * mult * ig
        r.gchan[5:6] += sums[0]
        r.gchan[6:7] += sums[1]

    loop(T, 16, back)

    def conv_part(q):
        r.part_conv[q] = dot_nt(r.d_pre[...], r.w_di[:, :, ds(q * RW, RW, 16), :].reshape(CW, 2 * CW)).astype(bf16)

    rs_conv = Scatter(r.part_conv, r.got_conv)
    conv_part(pd)
    rs_act.end()
    rs_conv.start_far()
    conv_part(px)
    conv_part(py)
    rs_conv.start_near()
    conv_part(p)
    g_v.z_forward()

    def finish_act(o, summed, _):
        s = pl.ds(o, 16)
        r.act[s] = (r.x_one[s] + summed).astype(bf16)

    rs_act.each(16, finish_act)
    deliver(r.act, r.activations)
    g_o.z_send()
    g_dn.end()

    def grad_dec_inj(lanes):
        def run(q, _):
            value = dot_tn(r.conv[q], r.d_pre[:, lanes])
            r.w_di[:, :, ds(q * RW, RW, 16), lanes] = value.astype(bf16).reshape(RING, 2, RW, CW)
            return 0

        lax.fori_loop(0, RING, run, 0)

    grad_dec_inj(lanes_a)
    g_d = ColumnsGrad(r.w_di, r.h_di, r.z_di, r.l_di, RW, 0, CW - 128, r.grads_di)
    g_d.core_send()
    rs_conv.mid()
    grad_dec_inj(lanes_b)
    g_j = ColumnsGrad(r.w_di, r.h_di, r.z_di, r.l_di, RW, CW - 128, CW + 128, r.grads_di)
    g_j.core_send()
    g_b.z_forward()
    g_d.z_send()
    rs_conv.end()

    for half in (0, 1):

        def add_conv(o, half=half):
            for k in (2 * half, 2 * half + 1):
                at = (k - 2 * half) * T + o
                r.d_conv[k, pl.ds(o, 16)] += rs_conv.total(half, pl.multiple_of(at, 16), 16)

        loop(T, 16, add_conv)
    halo_b = new()
    for k in range(PLANE):
        r.halo_out[4 * k : 4 * k + 4] = r.d_conv[k, 0:4]
    sent_b = push(r.halo_out, r.halo_in, to_prev, halo_b, pos > 0)
    g_o.z_forward()

    def taps_back(o):
        sums = [jnp.zeros((1, CW), f32)] * 5
        for k in range(PLANE):
            ext = r.u[k, pl.ds(o, 24)]
            rows = ds(k * T + o, 16, 16)
            dc = r.d_conv[k, pl.ds(o, 16)]
            sums[4] = sums[4] + jnp.sum(dc, axis=0, keepdims=True)
            sums[0] = sums[0] + jnp.sum(dc * ext[8:24], axis=0, keepdims=True)
            for j in range(1, 4):
                term = jnp.where(wide(j, rows), dc * ext[8 - j : 24 - j], 0.0)
                sums[j] = sums[j] + jnp.sum(term, axis=0, keepdims=True)
        for j in range(5):
            r.gchan[j : j + 1] += sums[j]

    loop(T, 16, taps_back)
    small_grad.one()

    @pl.when(pos == places - 1)
    def _():
        r.halo_in[...] = jnp.zeros((16, CW), f32)

    arrived(r.halo_in, halo_b, pos < places - 1)
    g_d.z_forward()
    g_j.z_send()
    for k in range(PLANE):
        r.d_conv[k, T : T + 8] = jnp.concatenate([r.halo_in[4 * k : 4 * k + 4], jnp.zeros((4, CW), f32)], axis=0)

    def conv_back(o):
        for k in range(PLANE):
            ext = r.d_conv[k, pl.ds(o, 24)]
            rows = ds(k * T + o, 16, 16)
            total = r.chan[0:1] * ext[0:16]
            for j in range(1, 4):
                total = total + jnp.where(wide(3 + j, rows), r.chan[j : j + 1] * ext[j : 16 + j], 0.0)
            r.d_gu[rows, 0:CW] = total.astype(bf16)

    loop(T, 16, conv_back)

    def d_input_part(z, _):
        q = ds(z * chunk, chunk, chunk)
        value = dot_nt(r.d_gu[:, lanes_a], r.w_ib[z, :, :, lanes_a].reshape(chunk, CW)).reshape(PLANE, T, chunk)
        r.part[:, :, q] = (r.part[:, :, q].astype(f32) + value).astype(bf16)
        return 0

    lax.fori_loop(0, RING, d_input_part, 0)
    rs_three = Scatter(r.part, r.got_three)
    rs_three.start()

    def grad_input(z, _):
        q = ds(z * chunk, chunk, chunk)
        value = dot_tn(r.n_one[:, :, q].reshape(M, chunk), r.d_gu[:, lanes_a])
        r.w_ib[z, :, :, lanes_a] = value.astype(bf16).reshape(2, chunk // 2, CW)
        return 0

    lax.fori_loop(0, RING, grad_input, 0)
    g_i = ColumnsGrad(r.w_ib, r.h_ib, r.z_ib, r.l_ib, RD, 0, CW, r.grads_ib)
    g_i.core_send()
    rs_three.mid()
    g_j.z_forward()
    g_i.z_send()
    g_u.plane_send()
    g_v.plane_send()
    rs_three.end()

    def norm_one_back(o, d_n, _):
        s = pl.ds(o, 32)
        v = r.x_all[p, s].astype(f32)
        rs = inverse_rms(v)
        z = v * rs
        dz = d_n * r.gains[0:1]
        r.d_x[s] = r.d_one[s] + rs * (dz - z * jnp.mean(dz * z, axis=-1, keepdims=True))

    rs_three.each(32, norm_one_back)
    deliver(r.d_x, r.d_tokens)
    settle(sent_b)
    g_g.end()
    g_b.plane_send()
    g_o.end()
    g_u.end()
    g_v.end()
    g_i.z_forward()
    g_d.plane_send()
    g_b.end()
    g_j.plane_send()
    g_i.plane_send()
    small_grad.two()
    g_d.end()
    g_j.end()
    g_i.end()
    assert not sent
    for result in results:
        local_wait(*result)


WEIGHTS = (
    "branch_weight",
    "input_weight",
    "decay_weight",
    "inject_weight",
    "output_weight",
    "mlp_gate",
    "mlp_up",
    "mlp_down",
)


def run_layer(NL, SEGS, tokens, cotangent, pack, weights):
    T, D = tokens.shape
    W, F = weights["branch_weight"].shape[1], weights["mlp_gate"].shape[1]
    CW, CF = W // PLANE, F // PLANE
    RD, RW, RF = D // SHARES, W // SHARES, F // SHARES
    GL, M, places = PLANE * RD, PLANE * T, RING * NL * 2
    hbm = pl.BlockSpec(memory_space=pl.ANY)
    ins = ["tokens", "cotangent", "pack_in", *WEIGHTS]
    outs = {
        "activations": ((T, D), bf16),
        "d_tokens": ((T, D), f32),
        "grads_ib": ((PLANE, RD, 2 * CW), bf16),
        "grads_di": ((PLANE, RW, 2 * CW), bf16),
        "grads_gu": ((PLANE, RD, 2 * CF), bf16),
        "grad_output_weight": ((RW, D), f32),
        "grad_mlp_down": ((RF, D), f32),
        "small_out": ((8, 128), f32),
    }
    columns = (("i", RD, CW), ("b", RD, CW), ("d", RW, CW), ("j", RW, CW), ("g", RD, CF), ("u", RD, CF))
    scratch = {
        "w_ib": ((RING, 2, PLANE * RD, 2 * CW), bf16),
        "w_di": ((RING, 2, PLANE * RW, 2 * CW), bf16),
        "w_gu": ((RING, 2, PLANE * RD, 2 * CF), bf16),
        "w_o": ((RING, 2, RW, D), bf16),
        "w_dn": ((RING, 2, RF, D), bf16),
        **{"raw_" + n: ((R, PLANE * C), bf16) for n, R, C in columns},
        **{"sort_" + n: ((PLANE, R, C), bf16) for n, R, C in columns},
        "h_ib": ((RING, PLANE * RD, 2 * CW), bf16),
        "h_di": ((RING, PLANE * RW, 2 * CW), bf16),
        "h_gu": ((RING, PLANE * RD, 2 * CF), bf16),
        "h_o": ((RING, RW, D), bf16),
        "h_dn": ((RING, RF, D), bf16),
        "z_ib": ((4, PLANE * RD, 2 * CW), bf16),
        "z_di": ((4, PLANE * RW, 2 * CW), bf16),
        "z_gu": ((4, PLANE * RD, 2 * CF), bf16),
        "z_o": ((4, RW, D), bf16),
        "z_dn": ((4, RF, D), bf16),
        "l_ib": ((PLANE, RD, 2 * CW), bf16),
        "l_di": ((PLANE, RW, 2 * CW), bf16),
        "l_gu": ((PLANE, RD, 2 * CF), bf16),
        "n_one": ((PLANE, T, D), bf16),
        "n_two": ((PLANE, T, D), bf16),
        "cot_all": ((PLANE, T, D), bf16),
        "d_out": ((PLANE, T, D), bf16),
        "conv": ((PLANE, M, CW), bf16),
        "part": ((PLANE, T, D), bf16),
        "part_act": ((PLANE, T, D), bf16),
        "part_conv": ((PLANE, M, CW), bf16),
        "got_one": ((6, T // 2, D), bf16),
        "got_two": ((6, T // 2, D), bf16),
        "got_three": ((6, T // 2, D), bf16),
        "got_act": ((6, T // 2, D), bf16),
        "got_conv": ((6, M // 2, CW), bf16),
        "mixed": ((M, CW), bf16),
        "hidden": ((M, CF), bf16),
        "d_pair": ((M, 2 * CF), bf16),
        "d_gu": ((M, 2 * CW), bf16),
        "d_pre": ((M, 2 * CW), bf16),
        "pair": ((M, 2 * CF), f32),
        "u": ((PLANE, T + 8, CW), f32),
        "state": ((PLANE, T + 8, CW), f32),
        "d_conv": ((PLANE, T + 8, CW), f32),
        **{name: ((M, CW), f32) for name in ("gated", "slope", "rgate", "igate", "decay", "work", "cum")},
        "x_one": ((T, D), f32),
        "d_one": ((T, D), f32),
        "carry_f": ((RING * NL, 2 * PLANE, CW), f32),
        "carry_b": ((RING * NL, 2 * PLANE, CW), f32),
        **{name: ((2 * PLANE, CW), f32) for name in ("own_f", "sib_f", "own_b", "sib_b")},
        "halo_out": ((16, CW), f32),
        "halo_in": ((16, CW), f32),
        "into": ((8, CW), f32),
        "x_all": ((PLANE, T, D), bf16),
        "x_halo": ((PLANE, 16, D), bf16),
        "n_halo": ((PLANE, 16, D), bf16),
        "g_dn": ((RING, 2, RF, D), bf16),
        "masks": ((7, M, 128), f32),
        "pack": ((16, 128), bf16),
        "pr": ((2 * RING, 16, 128), bf16),
        "line": ((16, 128), bf16),
        "pp": ((PLANE, 16, 128), bf16),
        "act": ((T, D), bf16),
        "d_x": ((T, D), f32),
        "t_o": ((RW, D), f32),
        "t_dn": ((RF, D), f32),
        "small_sum": ((8, 128), f32),
        "gains": ((8, D), f32),
        "chan": ((8, CW), f32),
        "gchan": ((8, CW), f32),
        "gs": ((2 * RING, 8, 128), f32),
        "gg": ((2 * RING, 8, 128), f32),
    }
    dims = SimpleNamespace(
        T=T, D=D, W=W, F=F, CW=CW, CF=CF, RD=RD, RW=RW, RF=RF, NL=NL, SEGS=SEGS, receives=RECEIVES + 2 * RING * NL, names=[*ins, *outs, *scratch, "ss", "rs"]
    )
    flops = 3 * 2 * M * (D * 2 * CW + W * 2 * CW + CW * D + 3 * D * CF)
    results = pl.pallas_call(
        partial(layer, dims),
        out_shape=[jax.ShapeDtypeStruct(shape, kind) for shape, kind in outs.values()],
        in_specs=[hbm] * (3 + len(WEIGHTS)),
        out_specs=[hbm] * len(outs),
        scratch_shapes=[pltpu.VMEM(shape, kind) for shape, kind in scratch.values()]
        + [pltpu.SemaphoreType.DMA((SENDS,)), pltpu.SemaphoreType.DMA((dims.receives,))],
        compiler_params=pltpu.CompilerParams(
            collective_id=0, has_side_effects=True, vmem_limit_bytes=62 * 2**20
        ),
        cost_estimate=pl.CostEstimate(flops=flops, bytes_accessed=8 * 2**20, transcendentals=M * CW * 16),
        name="griffin_layer",
    )(tokens, cotangent, pack, *[weights[name] for name in WEIGHTS])
    return finish({**dict(zip(outs, results, strict=True)), "pack": pack}, weights, CW, CF)


def finish(got, weights, CW, CF):
    hbm = pl.BlockSpec(memory_space=pl.ANY)
    pairs = (
        ("grads_ib", ("input_weight", "branch_weight"), CW),
        ("grads_gu", ("mlp_gate", "mlp_up"), CF),
        ("grads_di", ("decay_weight", "inject_weight"), CW),
    )
    gains = ("first_gain", "second_gain")
    RD, RW = got["grads_ib"].shape[1], got["grads_di"].shape[1]
    channels = {"conv_taps": (0, 4), "conv_bias": (4, 5), "decay_bias": (5, 6), "inject_bias": (6, 7)}
    plain = ("d_tokens", "activations", "grad_output_weight", "grad_mlp_down")
    shared = [name for _, names, _ in pairs[:2] for name in names]
    source = {**got, **{name: weights[name] for name in shared}}
    names = ["small_out", "pack", *[name for name, _, _ in pairs], *shared, *plain]
    shapes = {name: got[name] for name in plain}
    for name, targets, C in pairs:
        for target in targets:
            shapes["grad_" + target] = jax.ShapeDtypeStruct((got[name].shape[1], PLANE * C), f32)
    for name in gains:
        shapes["grad_" + name] = jax.ShapeDtypeStruct((1, RD), f32)
    for name, (low, high) in channels.items():
        shapes["grad_" + name] = jax.ShapeDtypeStruct((high - low, RW), f32)
    scratch = {name: (source[name].shape, source[name].dtype) for name in names}
    scratch.update({name: (like.shape, f32) for name, like in shapes.items() if name not in plain})

    def body(*refs):
        ins = dict(zip(names, refs[: len(names)], strict=True))
        outs = dict(zip(shapes, refs[len(names) : len(names) + len(shapes)], strict=True))
        held, sems = dict(zip(scratch, refs[len(names) + len(shapes) : -1], strict=True)), refs[-1]
        copies = []

        def copy(src, dst):
            copies.append(pltpu.make_async_copy(src, dst, sems.at[len(copies)]))
            copies[-1].start()
            return copies[-1]

        loads = {name: copy(ins[name], held[name]) for name in names}
        stores = []
        loads["small_out"].wait()
        loads["pack"].wait()
        for name, (low, high) in channels.items():
            held["grad_" + name][...] = held["small_out"][low:high, 0:RW]
            stores.append(copy(held["grad_" + name], outs["grad_" + name]))
        for i, (name, targets, C) in enumerate(pairs):
            loads[name].wait()
            part, sums = C // (2 * RING), None
            for j, target in enumerate(targets):
                values = [held[name][k, :, j * C : (j + 1) * C].astype(f32) for k in range(PLANE)]
                wide = jnp.concatenate(
                    [value[:, g * part : (g + 1) * part] for g in range(2 * RING) for value in values], axis=1
                )
                held["grad_" + target][...] = wide
                stores.append(copy(held["grad_" + target], outs["grad_" + target]))
                if target in shared:
                    loads[target].wait()
                    product = wide * held[target][...].astype(f32)
                    lanes = sum(product[:, k * 128 : (k + 1) * 128] for k in range(product.shape[1] // 128))
                    sums = lanes if sums is None else sums + lanes
            if sums is not None:
                total = lax.dot_general(
                    jnp.ones((8, 128), f32),
                    sums,
                    (((1,), (1,)), ((), ())),
                    precision=lax.Precision.HIGHEST,
                    preferred_element_type=f32,
                )
                target = "grad_" + gains[i]
                held[target][...] = total[0:1] / held["pack"][...].astype(f32)[i : i + 1, 0:RD]
                stores.append(copy(held[target], outs[target]))
        for name in plain:
            loads[name].wait()
            stores.append(copy(held[name], outs[name]))
        for store in stores:
            store.wait()

    results = pl.pallas_call(
        body,
        out_shape=[jax.ShapeDtypeStruct(like.shape, like.dtype) for like in shapes.values()],
        in_specs=[hbm] * len(names),
        out_specs=[hbm] * len(shapes),
        scratch_shapes=[
            *[pltpu.VMEM(shape, kind) for shape, kind in scratch.values()],
            pltpu.SemaphoreType.DMA((len(names) + len(shapes),)),
        ],
        compiler_params=pltpu.CompilerParams(vmem_limit_bytes=62 * 2**20),
        name="finish",
    )(*[source[name] for name in names])
    return {**got, **dict(zip(shapes, results, strict=True))}


def local(
    sizes,
    tokens,
    cotangent,
    doc_lengths,
    decay_exponent,
    branch_weight,
    input_weight,
    decay_weight,
    inject_weight,
    output_weight,
    mlp_gate,
    mlp_up,
    mlp_down,
    first_gain,
    second_gain,
    conv_taps,
    conv_bias,
    decay_bias,
    inject_bias,
):
    devices = math.prod(sizes.values())
    width = branch_weight.shape[1]
    at = {name: lax.axis_index(name) for name in AXES}
    mine = at["yl"] * 2 + at["xl"]
    ring = at["zh"] * 2 + at["c"]
    share = ring * PLANE + mine
    groups = devices // SHARES

    def pooled(value, axis=0):
        if groups == 1:
            return value
        whole = lax.all_gather(value, AXES, axis=axis, tiled=True)
        size = whole.shape[axis] // SHARES
        return lax.dynamic_slice_in_dim(whole, share * size, size, axis)

    def rows(value):
        value = value.astype(bf16)
        return jnp.pad(value, ((0, 0), (0, 128 - value.shape[1])))

    gains = pooled(jnp.stack([first_gain, second_gain]), 1)
    chan = pooled(jnp.concatenate([conv_taps.T, jnp.stack([conv_bias, decay_bias, inject_bias])]), 1)
    RD, RW = gains.shape[1], chan.shape[1]
    rates = decay_exponent.reshape(2 * RING, PLANE, width // SHARES)
    rates = lax.dynamic_index_in_dim(rates, mine, 1, keepdims=False).reshape(-1, 128)
    lengths = jnp.concatenate([doc_lengths // 256, doc_lengths % 256])
    pack = jnp.concatenate([rows(gains), rows(chan), rows(lengths), rows(rates)])
    pack = jnp.pad(pack, ((0, 16 - pack.shape[0]), (0, 0)))

    weights = dict(
        zip(
            WEIGHTS,
            (branch_weight, input_weight, decay_weight, inject_weight, output_weight, mlp_gate, mlp_up, mlp_down),
            strict=True,
        )
    )
    weights = {name: pooled(value) for name, value in weights.items()}
    got = run_layer(sizes["zl"], doc_lengths.shape[1], tokens[0], cotangent[0], pack, weights)

    def returned(value, axis=0):
        if groups == 1:
            return value
        shape = list(value.shape)
        size = shape[axis]
        shape[axis] = size * SHARES
        whole = lax.dynamic_update_slice_in_dim(jnp.zeros(shape, bf16), value.astype(bf16), share * size, axis)
        return lax.psum_scatter(whole, AXES, scatter_dimension=axis, tiled=True).astype(f32)

    grads = [returned(got["grad_" + name]) for name in WEIGHTS]
    first, second, taps, *biases = (
        returned(got["grad_" + name], 1)
        for name in ("first_gain", "second_gain", "conv_taps", "conv_bias", "decay_bias", "inject_bias")
    )
    return (
        got["activations"][None],
        got["d_tokens"][None],
        *grads,
        first[0],
        second[0],
        taps.T,
        *[bias[0] for bias in biases],
    )


def solution(mesh):
    seq, dp = mesh.shape["seq"], mesh.shape["dp"]
    across = 1 << ((dp.bit_length() - 1) // 2)
    sizes = dict(zip(AXES, (RING, seq // (2 * RING), 2, dp // across // 2, 2, across // 2, 2), strict=True))
    split = Mesh(mesh.devices.reshape(tuple(sizes.values())), AXES)
    along_seq, along_dp = AXES[:3], AXES[3:]
    rows = P(along_dp, along_seq, None)
    in_specs = (rows, rows, P(along_dp, None), P(), *[P(AXES, None)] * 8, P(AXES), P(AXES), P(AXES, None), *[P(AXES)] * 3)
    out_specs = (rows, rows, *[P(AXES, None)] * 8, P(AXES), P(AXES), P(AXES, None), *[P(AXES)] * 3)
    return jax.shard_map(partial(local, sizes), mesh=split, in_specs=in_specs, out_specs=out_specs, check_vma=False)
```

```python
import itertools
import math
from functools import cached_property, partial
from types import SimpleNamespace

import jax
import jax.numpy as jnp
from jax import lax
from jax.experimental import pallas as pl
from jax.experimental.pallas import tpu as pltpu
from jax.sharding import Mesh, PartitionSpec as P

f32, bf16 = jnp.float32, jnp.bfloat16
MESH = pl.DeviceIdType.MESH
AXES = ("zh", "zl", "c", "yh", "yl", "xh", "xl")
RING = 4
PLANE = 4
SHARES = RING * 2 * PLANE
SENDS = 60
RECEIVES = 174

eps_norm = 1e-06
floor_gap = 1e-05
rate_scale = 8.0
gelu_root = math.sqrt(2.0 / math.pi)
gelu_cube = 0.044715


def dot(left, right):
    return jnp.dot(left, right, preferred_element_type=f32)


def dot_nt(left, right):
    return lax.dot_general(left, right, (((1,), (1,)), ((), ())), preferred_element_type=f32)


def dot_tn(left, right):
    return lax.dot_general(left, right, (((0,), (0,)), ((), ())), preferred_element_type=f32)


def gelu_parts(v):
    t = jnp.tanh(gelu_root * (v + gelu_cube * v * v * v))
    half = 0.5 * (1.0 + t)
    slope = half + 0.5 * v * (1.0 - t * t) * gelu_root * (1.0 + 3.0 * gelu_cube * v * v)
    return v * half, slope


def minus_expm1(y, root):
    poly = 1.0 + y * (1.0 / 7.0)
    for k in (6, 5, 4, 3, 2):
        poly = 1.0 + y * poly * (1.0 / k)
    return jnp.where(y > -0.35, -y * poly, 1.0 - root * root)


def inverse_rms(v):
    return lax.rsqrt(jnp.mean(v * v, axis=-1, keepdims=True) + eps_norm)


def loop(total, step, body):
    def run(j, _):
        body(pl.multiple_of(j * step, step))
        return 0

    lax.fori_loop(0, total // step, run, 0)


def layer(dims, *refs):
    T, D, W, F, CW, CF = dims.T, dims.D, dims.W, dims.F, dims.CW, dims.CF
    RD, RW, RF, NL = dims.RD, dims.RW, dims.RF, dims.NL
    M = PLANE * T
    r = SimpleNamespace(**dict(zip(dims.names, refs, strict=True)))

    zh, zl, c = lax.axis_index("zh"), lax.axis_index("zl"), lax.axis_index("c")
    yl, xl = lax.axis_index("yl"), lax.axis_index("xl")
    p = yl * 2 + xl
    px, py, pd = yl * 2 + (1 - xl), (1 - yl) * 2 + xl, (1 - yl) * 2 + (1 - xl)
    to_x, to_y, to_d = {"xl": 1 - xl}, {"yl": 1 - yl}, {"yl": 1 - yl, "xl": 1 - xl}
    plane_peers = ((px, to_x), (py, to_y), (pd, to_d))
    to_core = {"c": 1 - c}
    flat_z = zh * NL + zl
    places = RING * NL * 2
    pos = flat_z * 2 + c

    def place(at):
        return {"zh": at // (2 * NL), "zl": (at // 2) % NL, "c": at % 2}

    count = itertools.count()

    def new(n=1):
        first = next(count)
        for _ in range(n - 1):
            next(count)
        assert first + n <= dims.receives
        return first

    spare = list(range(SENDS))
    sent = []

    def push(src, dst, dev, rsem, pred=None, instead=None):
        i = spare.pop(0) if instead is None else instead[2]

        def make():
            return pltpu.make_async_remote_copy(
                src, dst, r.ss.at[i], r.rs.at[rsem], device_id=dev, device_id_type=MESH
            )

        if pred is None:
            make().start()
        else:
            pl.when(pred)(lambda: make().start())
        entry = (make, pred, i, instead is None)
        sent.append(entry)
        return entry

    def settle(*entries):
        for entry in entries:
            make, pred, i, owner = entry
            if pred is None:
                make().wait_send()
            else:
                pl.when(pred)(lambda make=make: make().wait_send())
            sent.remove(entry)
            if owner:
                spare.append(i)

    def arrived(dst, rsem, pred=None):
        def wait():
            pltpu.make_async_remote_copy(
                dst, dst, r.ss.at[0], r.rs.at[rsem], device_id=to_core, device_id_type=MESH
            ).wait_recv()

        if pred is None:
            wait()
        else:
            pl.when(pred)(wait)

    def keep_local(src, dst, rsem):
        pltpu.make_async_copy(src, dst, r.rs.at[rsem]).start()

    idle = []

    def local_wait(src, dst, rsem):
        pltpu.make_async_copy(src, dst, r.rs.at[rsem]).wait()
        idle.append(rsem)

    results = []

    def deliver(src, dst):
        sem = idle.pop() if idle else new()
        keep_local(src, dst, sem)
        results.append((src, dst, sem))

    def ds(start, size, unit):
        return pl.ds(pl.multiple_of(start, unit), size)

    class Gather:
        def __init__(self, buf):
            self.buf, half = buf, buf.shape[1] // 2
            self.h0, self.h1 = pl.ds(0, half), pl.ds(half, half)
            self.rx0, self.rx1, self.ry0, self.ry1, self.rd = (new() for _ in range(5))
            self.out = []

        def start(self):
            b = self.buf
            own0, own1 = b.at[p, self.h0], b.at[p, self.h1]
            self.out.append(push(own0, own0, to_x, self.rx0))
            self.out.append(push(own1, own1, to_y, self.ry1))
            self.out.append(push(own1, own1, to_x, self.rx1))
            self.out.append(push(own0, own0, to_y, self.ry0))

        def mid(self):
            b = self.buf
            got0, got1 = b.at[px, self.h0], b.at[py, self.h1]
            arrived(got0, self.rx0)
            self.out.append(push(got0, got0, to_y, self.rd))
            arrived(got1, self.ry1)
            self.out.append(push(got1, got1, to_x, self.rd))

        def wait_x(self):
            arrived(self.buf.at[px, self.h1], self.rx1)

        def wait_y(self):
            arrived(self.buf.at[py, self.h0], self.ry0)

        def wait_d(self):
            arrived(self.buf.at[pd], self.rd)

        def end(self):
            self.wait_x()
            self.wait_y()
            self.wait_d()
            settle(*self.out)

    class Scatter:
        def __init__(self, buf, recv):
            self.buf, self.recv = buf, recv
            self.half = buf.shape[1] // 2
            self.h0, self.h1 = pl.ds(0, self.half), pl.ds(self.half, self.half)
            self.sems = [new(), new(), *[new()] * 4]
            self.out = []

        def start(self):
            self.start_far()
            self.start_near()

        def start_far(self):
            b, v, s = self.buf, self.recv, self.sems
            self.out.append(push(b.at[pd, self.h0], v.at[0], to_x, s[0]))
            self.out.append(push(b.at[pd, self.h1], v.at[1], to_y, s[1]))

        def start_near(self):
            b, v, s = self.buf, self.recv, self.sems
            self.out.append(push(b.at[px, self.h0], v.at[2], to_x, s[2]))
            self.out.append(push(b.at[py, self.h1], v.at[3], to_y, s[3]))

        def mid(self):
            b, v, s = self.buf, self.recv, self.sems
            arrived(v.at[0], s[0])
            step = 16

            def add0(o):
                b[py, pl.ds(o, step)] = (b[py, pl.ds(o, step)].astype(f32) + v[0, pl.ds(o, step)].astype(f32)).astype(bf16)

            loop(self.half, step, add0)
            self.out.append(push(b.at[py, self.h0], v.at[4], to_y, s[4]))
            arrived(v.at[1], s[1])

            def add1(o):
                q = pl.ds(pl.multiple_of(self.half + o, step), step)
                b[px, q] = (b[px, q].astype(f32) + v[1, pl.ds(o, step)].astype(f32)).astype(bf16)

            loop(self.half, step, add1)
            self.out.append(push(b.at[px, self.h1], v.at[5], to_x, s[5]))

        def end(self):
            arrived(self.recv.at[pl.ds(2, 4)], self.sems[2])
            settle(*self.out)

        def total(self, half, o, step):
            b, v = self.buf, self.recv
            own = b[p, pl.ds(pl.multiple_of(half * self.half + o, step), step)].astype(f32)
            q = pl.ds(o, step)
            return own + v[2 + half, q].astype(f32) + v[4 + half, q].astype(f32)

        def each(self, step, body, init=None):
            for half in (0, 1):

                def run(j, carry, half=half):
                    o = pl.multiple_of(j * step, step)
                    return body(pl.multiple_of(half * self.half + o, step), self.total(half, o, step), carry)

                init = lax.fori_loop(0, self.half // step, run, init)
            return init

    def z_send(src, block, rz):
        out = []
        out.append(push(src, block(zh), {"zh": zh + 2}, rz + zh, zh + 2 < RING))
        out.append(push(src, block(zh), {"zh": zh - 2}, rz + zh, zh - 2 >= 0, out[-1]))
        out.append(push(src, block(zh), {"zh": zh + 1}, rz + zh, zh + 1 < RING))
        out.append(push(src, block(zh), {"zh": zh - 1}, rz + zh, zh - 1 >= 0))
        return out

    def z_forward(block, rz):
        last = RING - 1
        arrived(block(0), rz, zh == last - 1)
        one = push(block(0), block(0), {"zh": zh + 1}, rz, zh == last - 1)
        arrived(block(last), rz + last, zh == 1)
        two = push(block(last), block(last), {"zh": zh - 1}, rz + last, zh == 1, one)
        return [one, two]

    def z_wait(block, rz):
        last = RING - 1
        arrived(block(0), rz, (zh == 1) | (zh == last))
        arrived(block(1), rz + 1, zh != 1)
        arrived(block(2), rz + 2, zh != 2)
        arrived(block(last), rz + last, (zh == 0) | (zh == last - 1))

    class ZSum:
        def __init__(self, block, slot, add, direct):
            self.block, self.slot, self.add, self.direct = block, slot, add, direct
            self.valid = (direct | (zh >= 1), zh >= 2, direct | (zh <= 2), zh <= 1)
            self.sems = new(4)
            self.out = []

        def send(self):
            b, v, s = self.block, self.slot, self.sems
            last = RING - 1
            o = self.out
            if self.direct:
                o.append(push(b(last), v(2), {"zh": zh + last}, s + 2, zh == 0))
                o.append(push(b(0), v(0), {"zh": zh - last}, s + 0, zh == last, o[-1]))
                o.append(push(b(zh + 2), v(1), {"zh": zh + 2}, s + 1, zh <= 1))
                o.append(push(b(zh - 2), v(3), {"zh": zh - 2}, s + 3, zh >= 2, o[-1]))
            else:
                o.append(push(b(last), v(1), {"zh": zh + 1}, s + 1, zh == 0))
                o.append(push(b(0), v(3), {"zh": zh - 1}, s + 3, zh == last, o[-1]))
                o.append(push(b(zh + 2), v(1), {"zh": zh + 2}, s + 1, zh == 0))
                o.append(push(b(zh - 2), v(3), {"zh": zh - 2}, s + 3, zh == last, o[-1]))
            o.append(push(b(zh + 1), v(0), {"zh": zh + 1}, s + 0, zh < last))
            o.append(push(b(zh - 1), v(2), {"zh": zh - 1}, s + 2, zh > 0))

        def forward(self):
            b, v, s = self.block, self.slot, self.sems
            last = RING - 1

            def up():
                arrived(v(1), s + 1)
                self.add(last, 1)

            def down():
                arrived(v(3), s + 3)
                self.add(0, 3)

            pl.when(zh == 1)(up)
            self.out.append(push(b(last), v(1), {"zh": zh + 2}, s + 1, zh == 1))
            pl.when(zh == last - 1)(down)
            self.out.append(push(b(0), v(3), {"zh": zh - 2}, s + 3, zh == last - 1, self.out[-1]))

        def end(self):
            for k, valid in enumerate(self.valid):
                arrived(self.slot(k), self.sems + k, valid)
            settle(*self.out)

        def total(self, own, parts):
            for part, pred in zip(parts, self.valid, strict=True):
                own = own + jnp.where(pred, part.astype(f32), 0.0)
            return own

    class Column:
        def __init__(self, src, raw, sorted_, w, R, C, lane0):
            self.src, self.raw, self.sorted = src, raw, sorted_
            self.w, self.R, self.C, self.lanes = w, R, C, pl.ds(lane0, C)
            self.out = []

        rl = cached_property(lambda self: new())
        ra = cached_property(lambda self: new())
        rz = cached_property(lambda self: new(4))
        rc = cached_property(lambda self: new())

        def halves(self):
            out = []
            for k in (0, 1):
                part = Column(self.src, self.raw, self.sorted, self.w, self.R, self.C, 0)
                part.lanes = pl.ds(self.lanes.start + k * self.C // 2, self.C // 2)
                out.append(part)
            return out

        def spread_wait(self):
            arrived(self.block(zh), self.ra)
            settle(*self.out)
            self.out = []

        def load(self):
            keep_local(self.src, self.raw, self.rl)

        def prepare(self):
            local_wait(self.src, self.raw, self.rl)
            value, part = self.raw[...], self.C // (2 * RING)
            for k in range(PLANE):
                first = [(g * PLANE + k) * part for g in range(2 * RING)]
                self.sorted[k] = jnp.concatenate([value[:, at : at + part] for at in first], axis=1)

        def spread(self):
            dst = self.w.at[zh, c, ds(p * self.R, self.R, 16), self.lanes]
            for k, dev in plane_peers:
                self.out.append(push(self.sorted.at[k], dst, dev, self.ra))
            keep_local(self.sorted.at[p], dst, self.ra)

        def block(self, z):
            return self.w.at[z, c, :, self.lanes]

        def z_send(self, spread=True):
            if spread:
                arrived(self.block(zh), self.ra)
            self.out += z_send(self.block(zh), self.block, self.rz)

        def z_forward(self):
            self.out += z_forward(self.block, self.rz)

        def z_wait(self):
            z_wait(self.block, self.rz)
            half = self.w.at[:, c, :, self.lanes]
            self.out.append(push(half, half, to_core, self.rc))

        def end(self):
            arrived(self.w.at[:, 1 - c, :, self.lanes], self.rc)
            settle(*self.out)

    class Row(Column):
        def __init__(self, src, w):
            self.src, self.w, self.lanes = src, w, pl.ds(0, w.shape[3])
            self.out = []

        def z_send(self):
            keep_local(self.src, self.block(zh), self.ra)
            self.out += z_send(self.src, self.block, self.rz)

        def z_wait(self):
            pltpu.make_async_copy(self.src, self.block(zh), r.rs.at[self.ra]).wait()
            super().z_wait()

    class ColumnsGrad:
        def __init__(self, g, other, slots, land, R, lane0, lanes, result, direct=False):
            self.g, self.other, self.slots, self.land = g, other, slots, land
            self.R, self.lanes, self.result = R, pl.ds(lane0, lanes), result
            self.rows = PLANE * R
            self.rc, self.rl = new(), new()
            self.zsum = ZSum(
                lambda z: g.at[z, c, :, self.lanes], lambda k: slots.at[k, :, self.lanes], self.add_slot, direct
            )

        def add_slot(self, z, k):
            g, q = self.g, self.lanes

            def add(o):
                s = pl.ds(o, 16)
                g[z, c, s, q] = (g[z, c, s, q].astype(f32) + self.slots[k, s, q].astype(f32)).astype(bf16)

            loop(self.rows, 16, add)

        def core_send(self):
            self.pushed = push(
                self.g.at[:, 1 - c, :, self.lanes], self.other.at[:, :, self.lanes], to_core, self.rc
            )

        def z_send(self):
            g, q = self.g, self.lanes
            arrived(self.other.at[:, :, q], self.rc)
            for z in range(RING):

                def add(o):
                    s = pl.ds(o, 16)
                    g[z, c, s, q] = (g[z, c, s, q].astype(f32) + self.other[z, s, q].astype(f32)).astype(bf16)

                loop(self.rows, 16, add)
            self.zsum.send()

        def z_forward(self):
            self.zsum.forward()

        def plane_send(self):
            g, q, R = self.g, self.lanes, self.R
            self.zsum.end()

            def add(o):
                s = pl.ds(o, 16)
                parts = [self.slots[k, s, q] for k in range(4)]
                g[zh, c, s, q] = self.zsum.total(g[zh, c, s, q].astype(f32), parts).astype(bf16)

            loop(PLANE * R, 16, add)
            dst = self.land.at[p, :, q]
            self.out = [self.pushed]
            for k, dev in plane_peers:
                self.out.append(push(g.at[zh, c, ds(k * R, R, 16), q], dst, dev, self.rl))
            keep_local(g.at[zh, c, ds(p * R, R, 16), q], dst, self.rl)

        def end(self):
            arrived(self.land.at[:, :, self.lanes], self.rl)
            settle(*self.out)
            deliver(self.land.at[:, :, self.lanes], self.result.at[:, :, self.lanes])

    class RowsGrad(ColumnsGrad):
        def __init__(self, g, other, slots, total, result):
            super().__init__(g, other, slots, None, 0, 0, g.shape[3], result)
            self.rows, self.sum = g.shape[2], total

        def end(self):
            self.zsum.end()
            settle(self.pushed)

            def add(o):
                s = pl.ds(o, 16)
                self.sum[s] = self.zsum.total(self.g[zh, c, s].astype(f32), [self.slots[k, s] for k in range(4)])

            loop(self.rows, 16, add)
            deliver(self.sum, self.result)

    class Carry:
        def __init__(self, own, sib, buf, later):
            self.own, self.sib, self.buf, self.later = own, sib, buf, later
            self.rc, self.rz = new(), new(RING * NL)
            self.out = []

        def order(self):
            return range(RING * NL) if self.later else reversed(range(RING * NL))

        def send_core(self):
            self.out.append(push(self.own, self.sib, to_core, self.rc))

        def send(self):
            arrived(self.sib, self.rc)
            own, sib = self.own[...], self.sib[...]
            near = (c == 0) if self.later else (c == 1)
            head, tail = jnp.where(near, own, sib), jnp.where(near, sib, own)
            self.buf[flat_z, 0:PLANE] = tail[0:PLANE] * head[0:PLANE]
            self.buf[flat_z, PLANE : 2 * PLANE] = (
                tail[0:PLANE] * head[PLANE : 2 * PLANE] + tail[PLANE : 2 * PLANE]
            )
            part = self.buf.at[flat_z]
            for at in self.order():
                pred = (flat_z < at) if self.later else (flat_z > at)
                self.out.append(push(part, part, {"zh": at // NL, "zl": at % NL}, self.rz + flat_z, pred))

        def fold(self, into):
            into[...] = jnp.zeros_like(into)

            def take(part):
                into[0:PLANE] = part[0:PLANE] * into[0:PLANE] + part[PLANE : 2 * PLANE]

            for at in self.order():
                pred = (flat_z > at) if self.later else (flat_z < at)

                def chip(at=at):
                    arrived(self.buf.at[at], self.rz + at)
                    take(self.buf[at])

                pl.when(pred)(chip)
            pl.when((c == 1) if self.later else (c == 0))(lambda: take(self.sib[...]))
            settle(*self.out)

    GL = PLANE * RD
    ring = zh * 2 + c

    def ring_place(at):
        return {"zh": at // 2, "c": at % 2}

    class Small:
        def __init__(self):
            self.rr, self.rk = new(), new()
            self.out = []

        def pack(self):
            for load in small_loads:
                local_wait(*load)
            lengths = r.lens[...]
            rows = [r.gain_a[...], r.gain_b[...], r.taps[...], r.bias_a[...], r.bias_b[...], r.bias_c[...]]
            rows += [lax.shift_right_logical(lengths, 8), lengths & 255]
            rows = [row.astype(f32) for row in rows]
            rows = [jnp.concatenate([row, jnp.zeros((row.shape[0], 128 - row.shape[1]), f32)], axis=1) for row in rows]
            r.pack[...] = jnp.concatenate([*rows, jnp.zeros((5, 128), f32)], axis=0).astype(bf16)

        def one(self):
            for at in range(2 * RING):
                self.out.append(push(r.pack, r.pr.at[ring], ring_place(at), self.rr, ring != at))
            keep_local(r.pack, r.pr.at[ring], self.rr)

        def two(self):
            arrived(r.pr, self.rr)
            lines = []
            for at in range(2 * RING):
                tile = r.pr[at].astype(f32)
                lines.append(jnp.concatenate([tile[row : row + 1, 0:32] for row in (0, 1, 9, 10)], axis=1))
            r.line[...] = jnp.concatenate([*lines, jnp.zeros((16 - 2 * RING, 128), f32)], axis=0).astype(bf16)
            for _, dev in plane_peers:
                self.out.append(push(r.line, r.pp.at[p], dev, self.rk))
            keep_local(r.line, r.pp.at[p], self.rk)

        def three(self):
            arrived(r.pp, self.rk)
            parts = [r.pp[k].astype(f32) for k in range(PLANE)]
            for row in (0, 1):
                lanes = slice(row * 32, row * 32 + RD)
                wide = jnp.concatenate([part[:, lanes] for part in parts], axis=1)
                for at in range(2 * RING):
                    r.gains[row : row + 1, at * GL : (at + 1) * GL] = wide[at : at + 1]
            whole = jnp.concatenate([r.pr[at, :, 0:RW].astype(f32) for at in range(2 * RING)], axis=1)
            r.chan[...] = whole[2:10]
            rates = r.rates[...].astype(f32)
            rates = jnp.concatenate([rates[k : k + 1] for k in range(W // 128)], axis=1)
            mine = jnp.zeros((1, CW), f32)
            for k in range(PLANE):
                at = [(g * PLANE + k) * RW for g in range(2 * RING)]
                mine = jnp.where(p == k, jnp.concatenate([rates[:, o : o + RW] for o in at], axis=1), mine)
            r.chan[7:8] = jnp.exp2(-mine)

        def four(self):
            where = lax.broadcasted_iota(jnp.int32, (T, 128), 0).astype(f32) + (pos * T).astype(f32)
            for k in range(PLANE):
                part = r.pp[k].astype(f32)
                starts, ends = [], []
                total = jnp.zeros((1, 1), f32)
                for j in range(dims.SEGS):
                    starts.append(total)
                    total = total + part[0:1, 64 + j : 65 + j] * 256.0 + part[0:1, 96 + j : 97 + j]
                    ends.append(total)

                def seg(shift):
                    at = where + float(shift)
                    value = jnp.zeros((T, 128), f32)
                    for end in ends:
                        value = value + jnp.where(at >= end, 1.0, 0.0)
                    return jnp.where((at < 0.0) | (at >= float(T * places)), -1.0, value)

                here = seg(0)
                rows = pl.ds(k * T, T)
                first = jnp.zeros((T, 128), f32)
                for start in starts:
                    first = jnp.where(where == start, 1.0, first)
                r.masks[0, rows] = first
                for j in (1, 2, 3):
                    r.masks[j, rows] = jnp.where(seg(-j) == here, 1.0, 0.0)
                    r.masks[3 + j, rows] = jnp.where(seg(j) == here, 1.0, 0.0)
            settle(*self.out)

    class SmallGrad:
        def __init__(self):
            self.rg = new()
            self.out = []

        def one(self):
            for at in range(2 * RING):
                own = jnp.concatenate([r.gchan[:, at * RW : (at + 1) * RW], jnp.zeros((8, 128 - RW), f32)], axis=1)
                r.gs[at] = own
            for at in range(2 * RING):
                self.out.append(push(r.gs.at[at], r.gg.at[ring], ring_place(at), self.rg, ring != at))
            keep_local(r.gs.at[ring], r.gg.at[ring], self.rg)

        def two(self):
            arrived(r.gg, self.rg)
            value = r.gg[0]
            for at in range(1, 2 * RING):
                value = value + r.gg[at]
            r.small_sum[...] = value
            deliver(r.small_sum, r.small_out)
            settle(*self.out)

    barrier = pltpu.get_barrier_semaphore()
    for _, dev in plane_peers:
        pl.semaphore_signal(barrier, 1, device_id=dev, device_id_type=MESH)
    for at in range(places):

        @pl.when(pos != at)
        def _(at=at):
            pl.semaphore_signal(barrier, 1, device_id=place(at), device_id_type=MESH)

    first_loads = [
        (src, dst, new())
        for src, dst in (
            (r.tokens, r.x_all.at[p]),
            (r.cotangent, r.cot_all.at[p]),
        )
    ]
    small_loads = [
        (src, dst, new())
        for src, dst in (
            (r.first_gain, r.gain_a),
            (r.second_gain, r.gain_b),
            (r.conv_taps, r.taps),
            (r.conv_bias, r.bias_a),
            (r.decay_bias, r.bias_b),
            (r.inject_bias, r.bias_c),
            (r.doc_lengths, r.lens),
            (r.decay_exponent, r.rates),
        )
    ]
    for load in small_loads + first_loads:
        keep_local(*load)

    w_i = Column(r.input_weight, r.raw_i, r.sort_i, r.w_ib, RD, CW, 0)
    w_b = Column(r.branch_weight, r.raw_b, r.sort_b, r.w_ib, RD, CW, CW)
    w_d = Column(r.decay_weight, r.raw_d, r.sort_d, r.w_di, RW, CW, 0)
    w_j = Column(r.inject_weight, r.raw_j, r.sort_j, r.w_di, RW, CW, CW)
    w_g = Column(r.mlp_gate, r.raw_g, r.sort_g, r.w_gu, RD, CF, 0)
    w_u = Column(r.mlp_up, r.raw_u, r.sort_u, r.w_gu, RD, CF, CF)
    w_g1, w_g2 = w_g.halves()
    w_o, w_dn = Row(r.output_weight, r.w_o), Row(r.mlp_down, r.w_dn)
    ag_x, ag_conv, ag_two = Gather(r.x_all), Gather(r.conv), Gather(r.n_two)
    ag_cot, ag_out = Gather(r.cot_all), Gather(r.d_out)
    small, small_grad = Small(), SmallGrad()
    after, before = flat_z + c, flat_z - (1 - c)
    to_next = {"zh": after // NL, "zl": after % NL, "c": 1 - c}
    to_prev = {"zh": before // NL, "zl": before % NL, "c": 1 - c}
    step = 256
    chunk = PLANE * RD * 2

    for w in (w_i, w_d, w_j, w_b, w_g, w_u):
        w.load()
    small.pack()
    w_i.prepare()
    w_d.prepare()
    pl.semaphore_wait(barrier, len(plane_peers) + places - 1)
    small.one()
    w_o.z_send()
    w_i.spread()
    w_d.spread()
    local_wait(*first_loads[0])
    ag_x.start()
    halo_x = new()
    sent_x = push(r.x_all.at[p, pl.ds(T - 16, 16)], r.x_halo.at[p], to_next, halo_x, pos < places - 1)
    w_j.prepare()
    w_i.z_send()
    small.two()
    w_b.prepare()

    @pl.when(pos == 0)
    def _():
        r.x_halo[p] = jnp.zeros((16, D), bf16)

    arrived(r.x_halo.at[p], halo_x, pos > 0)
    halo_p = new(PLANE)
    sent_p = [push(r.x_halo.at[p], r.x_halo.at[p], dev, halo_p + p) for _, dev in plane_peers]
    ag_x.mid()
    w_i.z_forward()
    w_g.prepare()
    local_wait(*first_loads[1])
    small.three()

    def norm_block(k):
        def norm_one(o):
            s = pl.ds(o, 32)
            v = r.x_all[k, s].astype(f32)
            r.n_one[k, s] = (v * inverse_rms(v) * r.gains[0:1]).astype(bf16)

        loop(T, 32, norm_one)

    norm_block(p)
    w_d.z_send()
    ag_x.wait_x()
    norm_block(px)
    ag_x.wait_y()
    norm_block(py)
    w_j.spread()
    small.four()
    for k, _ in plane_peers:
        arrived(r.x_halo.at[k], halo_p + k)
    v = r.x_halo[...].reshape(PLANE * 16, D).astype(f32)
    r.n_halo[...] = (v * inverse_rms(v) * r.gains[0:1]).astype(bf16).reshape(PLANE, 16, D)
    ag_x.wait_d()
    norm_block(pd)
    settle(*ag_x.out, sent_x, *sent_p)
    w_b.spread()
    w_g.spread()
    w_o.z_forward()
    w_i.z_wait()
    w_u.prepare()
    w_j.z_send()
    w_i.end()

    def weight_ib(lanes):
        return r.w_ib[:, :, :, lanes].reshape(D, CW)

    lanes_a, lanes_b = pl.ds(0, CW), pl.ds(CW, CW)
    halo = dot(r.n_halo[...].reshape(PLANE * 16, D), weight_ib(lanes_a)).astype(bf16).astype(f32)
    body = dot(r.n_one[...].reshape(M, D), weight_ib(lanes_a)).astype(bf16).astype(f32)
    for k in range(PLANE):
        r.u[k, 0:8] = halo[k * 16 + 8 : (k + 1) * 16]
        r.u[k, 8 : 8 + T] = body[k * T : (k + 1) * T]

    def wide(j, rows):
        return jnp.concatenate([r.masks[j, rows]] * (CW // 128), axis=1) > 0.5

    def convolve(o):
        for k in range(PLANE):
            ext = r.u[k, pl.ds(o, 24)]
            rows = ds(k * T + o, 16, 16)
            total = r.chan[4:5] + r.chan[0:1] * ext[8:24]
            for j in range(1, 4):
                total = total + jnp.where(wide(j, rows), r.chan[j : j + 1] * ext[8 - j : 24 - j], 0.0)
            r.conv[p, rows] = total.astype(bf16)

    loop(T, 16, convolve)
    ag_conv.start()
    w_d.z_forward()
    w_b.z_send()
    ag_conv.mid()
    w_j.z_forward()
    w_d.z_wait()
    w_d.end()

    def pre(q, lanes):
        return dot(r.conv[q], r.w_di[:, :, ds(q * RW, RW, 16), lanes].reshape(CW, CW))

    r.pair[:, 0:CW] = pre(p, lanes_a)
    ag_conv.wait_x()
    r.pair[:, 0:CW] += pre(px, lanes_a)
    ag_conv.wait_y()
    r.pair[:, 0:CW] += pre(py, lanes_a)
    w_b.z_forward()
    ag_conv.wait_d()
    r.pair[:, 0:CW] += pre(pd, lanes_a)
    settle(*ag_conv.out)
    w_g.spread_wait()
    w_g1.z_send(False)
    w_j.z_wait()
    w_u.spread()
    ag_cot.start()
    w_o.z_wait()
    w_j.end()
    r.pair[:, CW : 2 * CW] = (pre(0, lanes_b) + pre(1, lanes_b)) + (pre(2, lanes_b) + pre(3, lanes_b))

    def decay_terms(s, rg):
        log_a = -rate_scale * rg * r.chan[7:8]
        root = jnp.exp(log_a)
        gap = minus_expm1(2.0 * log_a, root)
        first = wide(0, s)
        return root, gap, jnp.where(first, 1.0, jnp.sqrt(jnp.maximum(gap, floor_gap))), first

    def gates_two(o):
        s = pl.ds(o, 16)
        rg = jax.nn.sigmoid(r.pair[s, 0:CW] + r.chan[5:6])
        ig = jax.nn.sigmoid(r.pair[s, CW : 2 * CW] + r.chan[6:7])
        root, _, mult, first = decay_terms(s, rg)
        r.rgate[s], r.igate[s] = rg, ig
        r.decay[s] = jnp.where(first, 0.0, root)
        r.work[s] = mult * ig * r.conv[p, s].astype(f32)

    loop(M, 16, gates_two)
    row = lax.broadcasted_iota(jnp.int32, (8, CW), 0)

    def scan_forward(j, carry):
        out = []
        for k in range(PLANE):
            s = ds(k * T + j * 8, 8, 8)
            a, b = r.decay[s], r.work[s]
            for n in (1, 2, 4):
                a_b = jnp.where(row >= n, pltpu.roll(a, n, 0), 1.0)
                b_b = jnp.where(row >= n, pltpu.roll(b, n, 0), 0.0)
                a, b = a * a_b, a * b_b + b
            total, prod = b + a * carry[2 * k], a * carry[2 * k + 1]
            r.state[k, ds(8 + j * 8, 8, 8)] = total
            r.cum[s] = prod
            out += [total[7:8], prod[7:8]]
        return tuple(out)

    zero, one = jnp.zeros((1, CW), f32), jnp.ones((1, CW), f32)
    ends = lax.fori_loop(0, T // 8, scan_forward, (zero, one) * PLANE)
    carry_f = Carry(r.own_f, r.sib_f, r.carry_f, True)
    for k in range(PLANE):
        r.own_f[k : k + 1] = ends[2 * k + 1]
        r.own_f[PLANE + k : PLANE + k + 1] = ends[2 * k]
    carry_f.send_core()
    w_b.z_wait()
    carry_f.send()
    w_g1.z_forward()
    w_g2.z_send(False)
    w_b.end()
    r.work[...] = dot(r.n_one[...].reshape(M, D), weight_ib(lanes_b))

    def gates_one(o):
        s = pl.ds(o, 16)
        r.gated[s], r.slope[s] = gelu_parts(r.work[s])

    loop(M, 16, gates_one)
    ag_cot.mid()
    carry_f.fold(r.into)
    for k in range(PLANE):
        r.state[k, 0:8] = jnp.broadcast_to(r.into[k : k + 1], (8, CW))

    def mix(o):
        for k in range(PLANE):
            s, t = ds(k * T + o, 16, 16), ds(8 + o, 16, 8)
            state = r.state[k, t] + r.cum[s] * r.into[k : k + 1]
            r.state[k, t] = state
            r.mixed[s] = (state * r.gated[s]).astype(bf16)

    loop(T, 16, mix)

    w_o.end()

    def out_part(o):
        q = pl.ds(o, step)
        r.part[:, :, q] = dot(r.mixed[...], r.w_o[:, :, :, q].reshape(CW, step)).astype(bf16).reshape(PLANE, T, step)

    loop(D, step, out_part)
    rs_one = Scatter(r.part, r.got_one)
    rs_one.start()
    w_g1.z_wait()
    w_g2.z_forward()
    w_u.z_send()
    ag_cot.end()
    rs_one.mid()
    rs_one.end()

    def norm_two(o, summed, _):
        s = pl.ds(o, 32)
        v = r.x_all[p, s].astype(f32) + summed
        r.x_one[s] = v
        r.n_two[p, s] = (v * inverse_rms(v) * r.gains[1:2]).astype(bf16)

    rs_one.each(32, norm_two)
    ag_two.start()
    w_u.z_forward()
    w_dn.z_send()
    ag_two.mid()
    w_g2.z_wait()
    w_g1.end()
    w_g2.end()
    ag_two.end()

    def mlp_in(o):
        q = pl.ds(o, step)
        r.pair[:, q] = dot(r.n_two[...].reshape(M, D), r.w_gu[:, :, :, q].reshape(D, step))

    loop(CF, step, mlp_in)
    w_dn.z_forward()
    w_u.z_wait()
    w_u.end()
    loop(CF, step, lambda o: mlp_in(pl.multiple_of(CF + o, step)))

    def gates_mlp(o):
        s = pl.ds(o, 16)
        value, slope = gelu_parts(r.pair[s, 0:CF])
        up = r.pair[s, CF : 2 * CF]
        r.hidden[s] = (value * up).astype(bf16)
        r.pair[s, 0:CF] = slope * up
        r.pair[s, CF : 2 * CF] = value

    loop(M, 16, gates_mlp)

    half = CF // 2
    for k in (0, 1):
        for o in range(0, D, D // 2):
            value = dot_tn(r.hidden[:, k * half : (k + 1) * half], r.cot_all[:, :, o : o + D // 2].reshape(M, D // 2))
            r.g_dn[k * RING // 2 : (k + 1) * RING // 2, :, :, o : o + D // 2] = value.astype(bf16).reshape(
                RING // 2, 2, RF, D // 2
            )
    g_dn = RowsGrad(r.g_dn, r.h_dn, r.z_dn, r.t_dn, r.grad_mlp_down)
    g_dn.core_send()
    w_dn.z_wait()
    g_dn.z_send()
    w_dn.end()

    for k in range(CF // step):
        back = dot_nt(r.cot_all[...].reshape(M, D), r.w_dn[...].reshape(CF, D)[k * step : (k + 1) * step])
        r.d_pair[:, k * step : (k + 1) * step] = (back * r.pair[:, k * step : (k + 1) * step]).astype(bf16)
        r.d_pair[:, CF + k * step : CF + (k + 1) * step] = (
            back * r.pair[:, CF + k * step : CF + (k + 1) * step]
        ).astype(bf16)

    def d_two_part(z, _):
        q = ds(z * chunk, chunk, chunk)
        r.part[:, :, q] = (
            dot_nt(r.d_pair[...], r.w_gu[z].reshape(chunk, 2 * CF)).astype(bf16).reshape(PLANE, T, chunk)
        )
        return 0

    lax.fori_loop(0, RING, d_two_part, 0)
    rs_two = Scatter(r.part, r.got_two)
    rs_two.start()

    def grad_gate_up(lane0):
        lanes = pl.ds(lane0, CF)

        def run(z, _):
            q = ds(z * chunk, chunk, chunk)
            value = dot_tn(r.n_two[:, :, q].reshape(M, chunk), r.d_pair[:, lanes])
            r.w_gu[z, :, :, lanes] = value.astype(bf16).reshape(2, chunk // 2, CF)
            return 0

        lax.fori_loop(0, RING, run, 0)

    grad_gate_up(0)
    g_g = ColumnsGrad(r.w_gu, r.h_gu, r.z_gu, r.l_gu, RD, 0, CF, r.grads_gu)
    g_g.core_send()
    rs_two.mid()
    g_dn.z_forward()
    g_g.z_send()
    grad_gate_up(CF)
    g_u, g_v = (
        ColumnsGrad(r.w_gu, r.h_gu, r.z_gu, r.l_gu, RD, lane0, CF // 2, r.grads_gu) for lane0 in (CF, CF + CF // 2)
    )
    g_u.core_send()
    g_v.core_send()

    def act_part(o):
        q = pl.ds(o, step)
        r.part_act[:, :, q] = dot(r.hidden[...], r.w_dn[:, :, :, q].reshape(CF, step)).astype(bf16).reshape(PLANE, T, step)

    loop(D, step, act_part)
    r.gchan[...] = jnp.zeros_like(r.gchan)
    rs_two.end()

    def norm_two_back(o, d_two, _):
        s = pl.ds(o, 32)
        v = r.x_one[s]
        rs = inverse_rms(v)
        z = v * rs
        dz = d_two * r.gains[1:2]
        d_one = r.cot_all[p, s].astype(f32) + rs * (dz - z * jnp.mean(dz * z, axis=-1, keepdims=True))
        r.d_one[s] = d_one
        r.d_out[p, s] = d_one.astype(bf16)

    rs_two.each(32, norm_two_back)
    ag_out.start()
    ag_out.mid()
    g_g.z_forward()
    g_u.z_send()
    ag_out.end()
    rs_act = Scatter(r.part_act, r.got_act)
    rs_act.start()

    r.work[...] = dot_nt(r.d_out[...].reshape(M, D), r.w_o[...].reshape(CW, D))

    def split(o):
        for k in range(PLANE):
            s = ds(k * T + o, 16, 16)
            d_mixed = r.work[s]
            r.d_gu[s, CW : 2 * CW] = (d_mixed * r.state[k, ds(8 + o, 16, 8)] * r.slope[s]).astype(bf16)
            r.work[s] = d_mixed * r.gated[s]

    loop(T, 16, split)

    def scan_backward(i, carry):
        j = T // 8 - 1 - i
        out = []
        for k in range(PLANE):
            s = ds(k * T + j * 8, 8, 8)
            decay, b = r.decay[s], r.work[s]
            a = jnp.where(row < 7, pltpu.roll(decay, 7, 0), carry[3 * k + 2])
            for n in (1, 2, 4):
                a_b = jnp.where(row < 8 - n, pltpu.roll(a, 8 - n, 0), 1.0)
                b_b = jnp.where(row < 8 - n, pltpu.roll(b, 8 - n, 0), 0.0)
                a, b = a * a_b, a * b_b + b
            total, prod = b + a * carry[3 * k], a * carry[3 * k + 1]
            r.work[s], r.cum[s] = total, prod
            out += [total[0:1], prod[0:1], decay[0:1]]
        return tuple(out)

    heads = lax.fori_loop(0, T // 8, scan_backward, (zero, one, one) * PLANE)
    carry_b = Carry(r.own_b, r.sib_b, r.carry_b, False)
    for k in range(PLANE):
        r.own_b[k : k + 1] = r.own_f[k : k + 1]
        r.own_b[PLANE + k : PLANE + k + 1] = heads[3 * k] * heads[3 * k + 2]
    carry_b.send_core()

    def grad_out(o):
        q = pl.ds(o, D // 2)
        value = dot_tn(r.mixed[...], r.d_out[:, :, q].reshape(M, D // 2))
        r.w_o[:, :, :, q] = value.astype(bf16).reshape(RING, 2, RW, D // 2)

    loop(D, D // 2, grad_out)
    g_o = RowsGrad(r.w_o, r.h_o, r.z_o, r.t_o, r.grad_output_weight)
    g_o.core_send()
    carry_b.send()
    g_u.z_forward()
    g_v.z_send()
    rs_act.mid()

    def d_branch_part(z, _):
        q = ds(z * chunk, chunk, chunk)
        r.part[:, :, q] = (
            dot_nt(r.d_gu[:, lanes_b], r.w_ib[z, :, :, lanes_b].reshape(chunk, CW))
            .astype(bf16)
            .reshape(PLANE, T, chunk)
        )
        value = dot_tn(r.n_one[:, :, q].reshape(M, chunk), r.d_gu[:, lanes_b])
        r.w_ib[z, :, :, lanes_b] = value.astype(bf16).reshape(2, chunk // 2, CW)
        return 0

    lax.fori_loop(0, RING, d_branch_part, 0)
    g_b = ColumnsGrad(r.w_ib, r.h_ib, r.z_ib, r.l_ib, RD, CW, CW, r.grads_ib)
    g_b.core_send()
    g_g.plane_send()
    carry_b.fold(r.into)
    g_b.z_send()

    def back(o):
        sums = [jnp.zeros((1, CW), f32)] * 2
        for k in range(PLANE):
            s = ds(k * T + o, 16, 16)
            adjoint = r.work[s] + r.cum[s] * r.into[k : k + 1]
            previous = r.state[k, pl.ds(o, 24)][7:23]
            rg, ig, decay, conv = r.rgate[s], r.igate[s], r.decay[s], r.conv[p, s].astype(f32)
            _, gap, mult, first = decay_terms(s, rg)
            d_mult = jnp.where(first, 0.0, adjoint * ig * conv)
            d_log = adjoint * previous * decay - jnp.where(gap > floor_gap, (1.0 - gap) * d_mult / mult, 0.0)
            d_decay = (-rate_scale * r.chan[7:8] * d_log * rg * (1.0 - rg)).astype(bf16)
            d_inject = (adjoint * mult * conv * ig * (1.0 - ig)).astype(bf16)
            r.d_pre[s, 0:CW] = d_decay
            r.d_pre[s, CW : 2 * CW] = d_inject
            sums[0] = sums[0] + jnp.sum(d_decay.astype(f32), axis=0, keepdims=True)
            sums[1] = sums[1] + jnp.sum(d_inject.astype(f32), axis=0, keepdims=True)
            r.d_conv[k, pl.ds(o, 16)] = adjoint * mult * ig
        r.gchan[5:6] += sums[0]
        r.gchan[6:7] += sums[1]

    loop(T, 16, back)

    def conv_part(q):
        r.part_conv[q] = dot_nt(r.d_pre[...], r.w_di[:, :, ds(q * RW, RW, 16), :].reshape(CW, 2 * CW)).astype(bf16)

    rs_conv = Scatter(r.part_conv, r.got_conv)
    conv_part(pd)
    rs_act.end()
    rs_conv.start_far()
    conv_part(px)
    conv_part(py)
    rs_conv.start_near()
    conv_part(p)
    g_v.z_forward()

    def finish_act(o, summed, _):
        s = pl.ds(o, 16)
        r.act[s] = (r.x_one[s] + summed).astype(bf16)

    rs_act.each(16, finish_act)
    deliver(r.act, r.activations)
    g_o.z_send()
    g_dn.end()

    def grad_dec_inj(lanes):
        def run(q, _):
            value = dot_tn(r.conv[q], r.d_pre[:, lanes])
            r.w_di[:, :, ds(q * RW, RW, 16), lanes] = value.astype(bf16).reshape(RING, 2, RW, CW)
            return 0

        lax.fori_loop(0, RING, run, 0)

    grad_dec_inj(lanes_a)
    g_d = ColumnsGrad(r.w_di, r.h_di, r.z_di, r.l_di, RW, 0, CW - 128, r.grads_di)
    g_d.core_send()
    rs_conv.mid()
    grad_dec_inj(lanes_b)
    g_j = ColumnsGrad(r.w_di, r.h_di, r.z_di, r.l_di, RW, CW - 128, CW + 128, r.grads_di)
    g_j.core_send()
    g_b.z_forward()
    g_d.z_send()
    rs_conv.end()

    for half in (0, 1):

        def add_conv(o, half=half):
            for k in (2 * half, 2 * half + 1):
                at = (k - 2 * half) * T + o
                r.d_conv[k, pl.ds(o, 16)] += rs_conv.total(half, pl.multiple_of(at, 16), 16)

        loop(T, 16, add_conv)
    halo_b = new()
    for k in range(PLANE):
        r.halo_out[4 * k : 4 * k + 4] = r.d_conv[k, 0:4]
    sent_b = push(r.halo_out, r.halo_in, to_prev, halo_b, pos > 0)
    g_o.z_forward()

    def taps_back(o):
        sums = [jnp.zeros((1, CW), f32)] * 5
        for k in range(PLANE):
            ext = r.u[k, pl.ds(o, 24)]
            rows = ds(k * T + o, 16, 16)
            dc = r.d_conv[k, pl.ds(o, 16)]
            sums[4] = sums[4] + jnp.sum(dc, axis=0, keepdims=True)
            sums[0] = sums[0] + jnp.sum(dc * ext[8:24], axis=0, keepdims=True)
            for j in range(1, 4):
                term = jnp.where(wide(j, rows), dc * ext[8 - j : 24 - j], 0.0)
                sums[j] = sums[j] + jnp.sum(term, axis=0, keepdims=True)
        for j in range(5):
            r.gchan[j : j + 1] += sums[j]

    loop(T, 16, taps_back)
    small_grad.one()

    @pl.when(pos == places - 1)
    def _():
        r.halo_in[...] = jnp.zeros((16, CW), f32)

    g_d.z_forward()
    g_j.z_send()
    arrived(r.halo_in, halo_b, pos < places - 1)
    for k in range(PLANE):
        r.d_conv[k, T : T + 8] = jnp.concatenate([r.halo_in[4 * k : 4 * k + 4], jnp.zeros((4, CW), f32)], axis=0)

    def conv_back(o):
        for k in range(PLANE):
            ext = r.d_conv[k, pl.ds(o, 24)]
            rows = ds(k * T + o, 16, 16)
            total = r.chan[0:1] * ext[0:16]
            for j in range(1, 4):
                total = total + jnp.where(wide(3 + j, rows), r.chan[j : j + 1] * ext[j : 16 + j], 0.0)
            r.d_gu[rows, 0:CW] = total.astype(bf16)

    loop(T, 16, conv_back)

    def d_input_part(z, _):
        q = ds(z * chunk, chunk, chunk)
        value = dot_nt(r.d_gu[:, lanes_a], r.w_ib[z, :, :, lanes_a].reshape(chunk, CW)).reshape(PLANE, T, chunk)
        r.part[:, :, q] = (r.part[:, :, q].astype(f32) + value).astype(bf16)
        return 0

    lax.fori_loop(0, RING, d_input_part, 0)
    rs_three = Scatter(r.part, r.got_three)
    rs_three.start()

    def grad_input(z, _):
        q = ds(z * chunk, chunk, chunk)
        value = dot_tn(r.n_one[:, :, q].reshape(M, chunk), r.d_gu[:, lanes_a])
        r.w_ib[z, :, :, lanes_a] = value.astype(bf16).reshape(2, chunk // 2, CW)
        return 0

    lax.fori_loop(0, RING, grad_input, 0)
    g_i = ColumnsGrad(r.w_ib, r.h_ib, r.z_ib, r.l_ib, RD, 0, CW, r.grads_ib, True)
    g_i.core_send()
    rs_three.mid()
    g_j.z_forward()
    g_i.z_send()
    g_u.plane_send()
    g_v.plane_send()
    rs_three.end()

    def norm_one_back(o, d_n, _):
        s = pl.ds(o, 32)
        v = r.x_all[p, s].astype(f32)
        rs = inverse_rms(v)
        z = v * rs
        dz = d_n * r.gains[0:1]
        r.d_x[s] = r.d_one[s] + rs * (dz - z * jnp.mean(dz * z, axis=-1, keepdims=True))

    rs_three.each(32, norm_one_back)
    deliver(r.d_x, r.d_tokens)
    settle(sent_b)
    g_g.end()
    g_b.plane_send()
    g_o.end()
    g_u.end()
    g_v.end()
    g_d.plane_send()
    g_b.end()
    g_j.plane_send()
    g_i.plane_send()
    small_grad.two()
    g_d.end()
    g_j.end()
    g_i.end()
    assert not sent
    for result in results:
        local_wait(*result)


WEIGHTS = (
    "branch_weight",
    "input_weight",
    "decay_weight",
    "inject_weight",
    "output_weight",
    "mlp_gate",
    "mlp_up",
    "mlp_down",
)


def run_layer(NL, tokens, cotangent, small, weights):
    T, D = tokens.shape
    SEGS = small["doc_lengths"].shape[1]
    W, F = weights["branch_weight"].shape[1], weights["mlp_gate"].shape[1]
    CW, CF = W // PLANE, F // PLANE
    RD, RW, RF = D // SHARES, W // SHARES, F // SHARES
    GL, M, places = PLANE * RD, PLANE * T, RING * NL * 2
    hbm = pl.BlockSpec(memory_space=pl.ANY)
    ins = ["tokens", "cotangent", *small, *WEIGHTS]
    outs = dict(
        activations=((T, D), bf16),
        d_tokens=((T, D), f32),
        grads_ib=((PLANE, RD, 2 * CW), bf16),
        grads_di=((PLANE, RW, 2 * CW), bf16),
        grads_gu=((PLANE, RD, 2 * CF), bf16),
        grad_output_weight=((RW, D), f32),
        grad_mlp_down=((RF, D), f32),
        small_out=((8, 128), f32),
    )
    columns = (("i", RD, CW), ("b", RD, CW), ("d", RW, CW), ("j", RW, CW), ("g", RD, CF), ("u", RD, CF))
    scratch = dict(
        w_ib=((RING, 2, PLANE * RD, 2 * CW), bf16),
        w_di=((RING, 2, PLANE * RW, 2 * CW), bf16),
        w_gu=((RING, 2, PLANE * RD, 2 * CF), bf16),
        w_o=((RING, 2, RW, D), bf16),
        w_dn=((RING, 2, RF, D), bf16),
        **{"raw_" + n: ((R, PLANE * C), bf16) for n, R, C in columns},
        **{"sort_" + n: ((PLANE, R, C), bf16) for n, R, C in columns},
        h_ib=((RING, PLANE * RD, 2 * CW), bf16),
        h_di=((RING, PLANE * RW, 2 * CW), bf16),
        h_gu=((RING, PLANE * RD, 2 * CF), bf16),
        h_o=((RING, RW, D), bf16),
        h_dn=((RING, RF, D), bf16),
        z_ib=((4, PLANE * RD, 2 * CW), bf16),
        z_di=((4, PLANE * RW, 2 * CW), bf16),
        z_gu=((4, PLANE * RD, 2 * CF), bf16),
        z_o=((4, RW, D), bf16),
        z_dn=((4, RF, D), bf16),
        l_ib=((PLANE, RD, 2 * CW), bf16),
        l_di=((PLANE, RW, 2 * CW), bf16),
        l_gu=((PLANE, RD, 2 * CF), bf16),
        n_one=((PLANE, T, D), bf16),
        n_two=((PLANE, T, D), bf16),
        cot_all=((PLANE, T, D), bf16),
        d_out=((PLANE, T, D), bf16),
        conv=((PLANE, M, CW), bf16),
        part=((PLANE, T, D), bf16),
        part_act=((PLANE, T, D), bf16),
        part_conv=((PLANE, M, CW), bf16),
        got_one=((6, T // 2, D), bf16),
        got_two=((6, T // 2, D), bf16),
        got_three=((6, T // 2, D), bf16),
        got_act=((6, T // 2, D), bf16),
        got_conv=((6, M // 2, CW), bf16),
        mixed=((M, CW), bf16),
        hidden=((M, CF), bf16),
        d_pair=((M, 2 * CF), bf16),
        d_gu=((M, 2 * CW), bf16),
        d_pre=((M, 2 * CW), bf16),
        pair=((M, 2 * CF), f32),
        u=((PLANE, T + 8, CW), f32),
        state=((PLANE, T + 8, CW), f32),
        d_conv=((PLANE, T + 8, CW), f32),
        **{name: ((M, CW), f32) for name in ("gated", "slope", "rgate", "igate", "decay", "work", "cum")},
        x_one=((T, D), f32),
        d_one=((T, D), f32),
        carry_f=((RING * NL, 2 * PLANE, CW), f32),
        carry_b=((RING * NL, 2 * PLANE, CW), f32),
        **{name: ((2 * PLANE, CW), f32) for name in ("own_f", "sib_f", "own_b", "sib_b")},
        halo_out=((16, CW), f32),
        halo_in=((16, CW), f32),
        into=((8, CW), f32),
        x_all=((PLANE, T, D), bf16),
        x_halo=((PLANE, 16, D), bf16),
        n_halo=((PLANE, 16, D), bf16),
        g_dn=((RING, 2, RF, D), bf16),
        masks=((7, M, 128), f32),
        pack=((16, 128), bf16),
        gain_a=((1, RD), bf16),
        gain_b=((1, RD), bf16),
        taps=((4, RW), bf16),
        bias_a=((1, RW), bf16),
        bias_b=((1, RW), bf16),
        bias_c=((1, RW), bf16),
        lens=((1, SEGS), jnp.int32),
        rates=((W // 128, 128), jnp.int32),
        pr=((2 * RING, 16, 128), bf16),
        line=((16, 128), bf16),
        pp=((PLANE, 16, 128), bf16),
        act=((T, D), bf16),
        d_x=((T, D), f32),
        t_o=((RW, D), f32),
        t_dn=((RF, D), f32),
        small_sum=((8, 128), f32),
        gains=((8, D), f32),
        chan=((8, CW), f32),
        gchan=((8, CW), f32),
        gs=((2 * RING, 8, 128), f32),
        gg=((2 * RING, 8, 128), f32),
    )
    dims = SimpleNamespace(
        T=T, D=D, W=W, F=F, CW=CW, CF=CF, RD=RD, RW=RW, RF=RF, NL=NL, SEGS=SEGS, receives=RECEIVES + 2 * RING * NL, names=[*ins, *outs, *scratch, "ss", "rs"]
    )
    flops = 3 * 2 * M * (D * 2 * CW + W * 2 * CW + CW * D + 3 * D * CF)
    results = pl.pallas_call(
        partial(layer, dims),
        out_shape=[jax.ShapeDtypeStruct(shape, kind) for shape, kind in outs.values()],
        in_specs=[hbm] * len(ins),
        out_specs=[hbm] * len(outs),
        scratch_shapes=[pltpu.VMEM(shape, kind) for shape, kind in scratch.values()]
        + [pltpu.SemaphoreType.DMA((SENDS,)), pltpu.SemaphoreType.DMA((dims.receives,))],
        compiler_params=pltpu.CompilerParams(
            collective_id=0, has_side_effects=True, vmem_limit_bytes=62 * 2**20
        ),
        cost_estimate=pl.CostEstimate(flops=flops, bytes_accessed=8 * 2**20, transcendentals=M * CW * 16),
        name="griffin_layer",
    )(tokens, cotangent, *small.values(), *[weights[name] for name in WEIGHTS])
    return finish({**small, **dict(zip(outs, results, strict=True))}, weights, CW, CF)


def finish(got, weights, CW, CF):
    hbm = pl.BlockSpec(memory_space=pl.ANY)
    pairs = (
        ("grads_ib", ("input_weight", "branch_weight"), CW),
        ("grads_gu", ("mlp_gate", "mlp_up"), CF),
        ("grads_di", ("decay_weight", "inject_weight"), CW),
    )
    gains = ("first_gain", "second_gain")
    RD, RW = got["grads_ib"].shape[1], got["grads_di"].shape[1]
    channels = {"conv_taps": (0, 4), "conv_bias": (4, 5), "decay_bias": (5, 6), "inject_bias": (6, 7)}
    plain = ("d_tokens", "activations", "grad_output_weight", "grad_mlp_down")
    shared = [name for _, names, _ in pairs[:2] for name in names]
    source = {**got, **{name: weights[name] for name in shared}}
    names = ["small_out", *gains, *[name for name, _, _ in pairs], *shared, *plain]
    shapes = {name: got[name] for name in plain}
    for name, targets, C in pairs:
        for target in targets:
            shapes["grad_" + target] = jax.ShapeDtypeStruct((got[name].shape[1], PLANE * C), f32)
    for name in gains:
        shapes["grad_" + name] = jax.ShapeDtypeStruct((1, RD), f32)
    for name, (low, high) in channels.items():
        shapes["grad_" + name] = jax.ShapeDtypeStruct((high - low, RW), f32)
    scratch = {name: (source[name].shape, source[name].dtype) for name in names}
    scratch.update({name: (like.shape, f32) for name, like in shapes.items() if name not in plain})

    def body(*refs):
        ins = dict(zip(names, refs[: len(names)], strict=True))
        outs = dict(zip(shapes, refs[len(names) : len(names) + len(shapes)], strict=True))
        held, sems = dict(zip(scratch, refs[len(names) + len(shapes) : -1], strict=True)), refs[-1]
        copies = []

        def copy(src, dst):
            copies.append(pltpu.make_async_copy(src, dst, sems.at[len(copies)]))
            copies[-1].start()
            return copies[-1]

        loads = {name: copy(ins[name], held[name]) for name in names}
        stores = []
        loads["small_out"].wait()
        for name, (low, high) in channels.items():
            held["grad_" + name][...] = held["small_out"][low:high, 0:RW]
            stores.append(copy(held["grad_" + name], outs["grad_" + name]))
        for i, (name, targets, C) in enumerate(pairs):
            loads[name].wait()
            part, sums = C // (2 * RING), None
            for j, target in enumerate(targets):
                values = [held[name][k, :, j * C : (j + 1) * C].astype(f32) for k in range(PLANE)]
                wide = jnp.concatenate(
                    [value[:, g * part : (g + 1) * part] for g in range(2 * RING) for value in values], axis=1
                )
                held["grad_" + target][...] = wide
                stores.append(copy(held["grad_" + target], outs["grad_" + target]))
                if target in shared:
                    loads[target].wait()
                    product = wide * held[target][...].astype(f32)
                    lanes = sum(product[:, k * 128 : (k + 1) * 128] for k in range(product.shape[1] // 128))
                    sums = lanes if sums is None else sums + lanes
            if sums is not None:
                total = lax.dot_general(
                    jnp.ones((8, 128), f32),
                    sums,
                    (((1,), (1,)), ((), ())),
                    precision=lax.Precision.HIGHEST,
                    preferred_element_type=f32,
                )
                target = "grad_" + gains[i]
                loads[gains[i]].wait()
                held[target][...] = total[0:1] / held[gains[i]][...].astype(f32)
                stores.append(copy(held[target], outs[target]))
        for name in plain:
            loads[name].wait()
            stores.append(copy(held[name], outs[name]))
        for store in stores:
            store.wait()

    results = pl.pallas_call(
        body,
        out_shape=[jax.ShapeDtypeStruct(like.shape, like.dtype) for like in shapes.values()],
        in_specs=[hbm] * len(names),
        out_specs=[hbm] * len(shapes),
        scratch_shapes=[
            *[pltpu.VMEM(shape, kind) for shape, kind in scratch.values()],
            pltpu.SemaphoreType.DMA((len(names) + len(shapes),)),
        ],
        compiler_params=pltpu.CompilerParams(vmem_limit_bytes=62 * 2**20),
        name="finish",
    )(*[source[name] for name in names])
    return {**got, **dict(zip(shapes, results, strict=True))}


def local(
    sizes,
    tokens,
    cotangent,
    doc_lengths,
    decay_exponent,
    branch_weight,
    input_weight,
    decay_weight,
    inject_weight,
    output_weight,
    mlp_gate,
    mlp_up,
    mlp_down,
    first_gain,
    second_gain,
    conv_taps,
    conv_bias,
    decay_bias,
    inject_bias,
):
    devices = math.prod(sizes.values())
    at = {name: lax.axis_index(name) for name in AXES}
    mine = at["yl"] * 2 + at["xl"]
    ring = at["zh"] * 2 + at["c"]
    share = ring * PLANE + mine
    groups = devices // SHARES

    def pooled(value, axis=0):
        if groups == 1:
            return value
        whole = lax.all_gather(value, AXES, axis=axis, tiled=True)
        size = whole.shape[axis] // SHARES
        return lax.dynamic_slice_in_dim(whole, share * size, size, axis)

    small = dict(
        first_gain=pooled(first_gain[None], 1),
        second_gain=pooled(second_gain[None], 1),
        conv_taps=pooled(conv_taps.T, 1),
        conv_bias=pooled(conv_bias[None], 1),
        decay_bias=pooled(decay_bias[None], 1),
        inject_bias=pooled(inject_bias[None], 1),
        doc_lengths=doc_lengths,
        decay_exponent=decay_exponent.reshape(-1, 128),
    )
    weights = dict(
        zip(
            WEIGHTS,
            (branch_weight, input_weight, decay_weight, inject_weight, output_weight, mlp_gate, mlp_up, mlp_down),
            strict=True,
        )
    )
    weights = {name: pooled(value) for name, value in weights.items()}
    got = run_layer(sizes["zl"], tokens[0], cotangent[0], small, weights)

    def returned(value, axis=0):
        if groups == 1:
            return value
        shape = list(value.shape)
        size = shape[axis]
        shape[axis] = size * SHARES
        whole = lax.dynamic_update_slice_in_dim(jnp.zeros(shape, bf16), value.astype(bf16), share * size, axis)
        return lax.psum_scatter(whole, AXES, scatter_dimension=axis, tiled=True).astype(f32)

    grads = [returned(got["grad_" + name]) for name in WEIGHTS]
    first, second, taps, *biases = (
        returned(got["grad_" + name], 1)
        for name in ("first_gain", "second_gain", "conv_taps", "conv_bias", "decay_bias", "inject_bias")
    )
    return (
        got["activations"][None],
        got["d_tokens"][None],
        *grads,
        first[0],
        second[0],
        taps.T,
        *[bias[0] for bias in biases],
    )


def solution(mesh):
    seq, dp = mesh.shape["seq"], mesh.shape["dp"]
    across = 1 << ((dp.bit_length() - 1) // 2)
    sizes = dict(zip(AXES, (RING, seq // (2 * RING), 2, dp // across // 2, 2, across // 2, 2), strict=True))
    split = Mesh(mesh.devices.reshape(tuple(sizes.values())), AXES)
    along_seq, along_dp = AXES[:3], AXES[3:]
    rows = P(along_dp, along_seq, None)
    in_specs = (rows, rows, P(along_dp, None), P(), *[P(AXES, None)] * 8, P(AXES), P(AXES), P(AXES, None), *[P(AXES)] * 3)
    out_specs = (rows, rows, *[P(AXES, None)] * 8, P(AXES), P(AXES), P(AXES, None), *[P(AXES)] * 3)
    return jax.shard_map(partial(local, sizes), mesh=split, in_specs=in_specs, out_specs=out_specs, check_vma=False)
```

```python
import itertools
import math
from functools import cached_property, partial
from types import SimpleNamespace

import jax
import jax.numpy as jnp
from jax import lax
from jax.experimental import pallas as pl
from jax.experimental.pallas import tpu as pltpu
from jax.sharding import Mesh, PartitionSpec as P

f32, bf16 = jnp.float32, jnp.bfloat16
MESH = pl.DeviceIdType.MESH
AXES = ("zh", "zl", "c", "yh", "yl", "xh", "xl")
RING = 4
PLANE = 4
SHARES = RING * 2 * PLANE
SENDS = 57
RECEIVES = 180

eps_norm = 1e-06
floor_gap = 1e-05
rate_scale = 8.0
gelu_root = math.sqrt(2.0 / math.pi)
gelu_cube = 0.044715


def dot(left, right):
    return jnp.dot(left, right, preferred_element_type=f32)


def dot_nt(left, right):
    return lax.dot_general(left, right, (((1,), (1,)), ((), ())), preferred_element_type=f32)


def dot_tn(left, right):
    return lax.dot_general(left, right, (((0,), (0,)), ((), ())), preferred_element_type=f32)


def gelu_parts(v):
    t = jnp.tanh(gelu_root * (v + gelu_cube * v * v * v))
    half = 0.5 * (1.0 + t)
    slope = half + 0.5 * v * (1.0 - t * t) * gelu_root * (1.0 + 3.0 * gelu_cube * v * v)
    return v * half, slope


def minus_expm1(y, root):
    poly = 1.0 + y * (1.0 / 7.0)
    for k in (6, 5, 4, 3, 2):
        poly = 1.0 + y * poly * (1.0 / k)
    return jnp.where(y > -0.35, -y * poly, 1.0 - root * root)


def inverse_rms(v):
    return lax.rsqrt(jnp.mean(v * v, axis=-1, keepdims=True) + eps_norm)


def unsorted(parts):
    size = parts[0].shape[1] // (2 * RING)
    return jnp.concatenate([part[:, g * size : (g + 1) * size] for g in range(2 * RING) for part in parts], axis=1)


def loop(total, step, body):
    def run(j, _):
        body(pl.multiple_of(j * step, step))
        return 0

    lax.fori_loop(0, total // step, run, 0)


def layer(dims, *refs):
    T, D, W, F, CW, CF = dims.T, dims.D, dims.W, dims.F, dims.CW, dims.CF
    RD, RW, RF, NL = dims.RD, dims.RW, dims.RF, dims.NL
    M = PLANE * T
    r = SimpleNamespace(**dict(zip(dims.names, refs, strict=True)))

    zh, zl, c = lax.axis_index("zh"), lax.axis_index("zl"), lax.axis_index("c")
    yl, xl = lax.axis_index("yl"), lax.axis_index("xl")
    p = yl * 2 + xl
    px, py, pd = yl * 2 + (1 - xl), (1 - yl) * 2 + xl, (1 - yl) * 2 + (1 - xl)
    to_x, to_y, to_d = {"xl": 1 - xl}, {"yl": 1 - yl}, {"yl": 1 - yl, "xl": 1 - xl}
    plane_peers = ((px, to_x), (py, to_y), (pd, to_d))
    to_core = {"c": 1 - c}
    flat_z = zh * NL + zl
    places = RING * NL * 2
    pos = flat_z * 2 + c

    def place(at):
        return {"zh": at // (2 * NL), "zl": (at // 2) % NL, "c": at % 2}

    count = itertools.count()

    def new(n=1):
        first = next(count)
        for _ in range(n - 1):
            next(count)
        assert first + n <= dims.receives
        return first

    spare = list(range(SENDS))
    sent = []

    def push(src, dst, dev, rsem, pred=None, instead=None):
        i = spare.pop(0) if instead is None else instead[2]

        def make():
            return pltpu.make_async_remote_copy(
                src, dst, r.ss.at[i], r.rs.at[rsem], device_id=dev, device_id_type=MESH
            )

        if pred is None:
            make().start()
        else:
            pl.when(pred)(lambda: make().start())
        entry = (make, pred, i, instead is None)
        sent.append(entry)
        return entry

    def settle(*entries):
        for entry in entries:
            make, pred, i, owner = entry
            if pred is None:
                make().wait_send()
            else:
                pl.when(pred)(lambda make=make: make().wait_send())
            sent.remove(entry)
            if owner:
                spare.append(i)

    def arrived(dst, rsem, pred=None):
        def wait():
            pltpu.make_async_remote_copy(
                dst, dst, r.ss.at[0], r.rs.at[rsem], device_id=to_core, device_id_type=MESH
            ).wait_recv()

        if pred is None:
            wait()
        else:
            pl.when(pred)(wait)

    def keep_local(src, dst, rsem):
        pltpu.make_async_copy(src, dst, r.rs.at[rsem]).start()

    idle = []

    def local_wait(src, dst, rsem):
        pltpu.make_async_copy(src, dst, r.rs.at[rsem]).wait()
        idle.append(rsem)

    results = []

    def deliver(src, dst):
        sem = idle.pop() if idle else new()
        keep_local(src, dst, sem)
        results.append((src, dst, sem))

    def ds(start, size, unit):
        return pl.ds(pl.multiple_of(start, unit), size)

    class Gather:
        def __init__(self, buf):
            self.buf, half = buf, buf.shape[1] // 2
            self.h0, self.h1 = pl.ds(0, half), pl.ds(half, half)
            self.rx0, self.rx1, self.ry0, self.ry1, self.rd = (new() for _ in range(5))
            self.out = []

        def start(self):
            b = self.buf
            own0, own1 = b.at[p, self.h0], b.at[p, self.h1]
            self.out.append(push(own0, own0, to_x, self.rx0))
            self.out.append(push(own1, own1, to_y, self.ry1))
            self.out.append(push(own1, own1, to_x, self.rx1))
            self.out.append(push(own0, own0, to_y, self.ry0))

        def mid(self):
            b = self.buf
            got0, got1 = b.at[px, self.h0], b.at[py, self.h1]
            arrived(got0, self.rx0)
            self.out.append(push(got0, got0, to_y, self.rd))
            arrived(got1, self.ry1)
            self.out.append(push(got1, got1, to_x, self.rd))

        def wait_x(self):
            arrived(self.buf.at[px, self.h1], self.rx1)

        def wait_y(self):
            arrived(self.buf.at[py, self.h0], self.ry0)

        def wait_d(self):
            arrived(self.buf.at[pd], self.rd)

        def end(self):
            self.wait_x()
            self.wait_y()
            self.wait_d()
            settle(*self.out)

    class Scatter:
        def __init__(self, buf, recv):
            self.buf, self.recv = buf, recv
            self.half = buf.shape[1] // 2
            self.h0, self.h1 = pl.ds(0, self.half), pl.ds(self.half, self.half)
            self.sems = [new(), new(), *[new()] * 4]
            self.out = []

        def start(self):
            self.start_far()
            self.start_near()

        def start_far(self):
            b, v, s = self.buf, self.recv, self.sems
            self.out.append(push(b.at[pd, self.h0], v.at[0], to_x, s[0]))
            self.out.append(push(b.at[pd, self.h1], v.at[1], to_y, s[1]))

        def start_near(self):
            b, v, s = self.buf, self.recv, self.sems
            self.out.append(push(b.at[px, self.h0], v.at[2], to_x, s[2]))
            self.out.append(push(b.at[py, self.h1], v.at[3], to_y, s[3]))

        def mid(self):
            b, v, s = self.buf, self.recv, self.sems
            arrived(v.at[0], s[0])
            step = 16

            def add0(o):
                b[py, pl.ds(o, step)] = (b[py, pl.ds(o, step)].astype(f32) + v[0, pl.ds(o, step)].astype(f32)).astype(bf16)

            loop(self.half, step, add0)
            self.out.append(push(b.at[py, self.h0], v.at[4], to_y, s[4]))
            arrived(v.at[1], s[1])

            def add1(o):
                q = pl.ds(pl.multiple_of(self.half + o, step), step)
                b[px, q] = (b[px, q].astype(f32) + v[1, pl.ds(o, step)].astype(f32)).astype(bf16)

            loop(self.half, step, add1)
            self.out.append(push(b.at[px, self.h1], v.at[5], to_x, s[5]))

        def end(self):
            arrived(self.recv.at[pl.ds(2, 4)], self.sems[2])
            settle(*self.out)

        def total(self, half, o, step):
            b, v = self.buf, self.recv
            own = b[p, pl.ds(pl.multiple_of(half * self.half + o, step), step)].astype(f32)
            q = pl.ds(o, step)
            return own + v[2 + half, q].astype(f32) + v[4 + half, q].astype(f32)

        def each(self, step, body, init=None):
            for half in (0, 1):

                def run(j, carry, half=half):
                    o = pl.multiple_of(j * step, step)
                    return body(pl.multiple_of(half * self.half + o, step), self.total(half, o, step), carry)

                init = lax.fori_loop(0, self.half // step, run, init)
            return init

    def z_send(src, block, rz, away=(2, 1)):
        out = []
        if 2 in away:
            out.append(push(src, block(zh), {"zh": zh + 2}, rz + zh, zh + 2 < RING))
            out.append(push(src, block(zh), {"zh": zh - 2}, rz + zh, zh - 2 >= 0, out[-1]))
        if 1 in away:
            out.append(push(src, block(zh), {"zh": zh + 1}, rz + zh, zh + 1 < RING))
            out.append(push(src, block(zh), {"zh": zh - 1}, rz + zh, zh - 1 >= 0))
        return out

    def z_forward(block, rz):
        last = RING - 1
        arrived(block(0), rz, zh == last - 1)
        one = push(block(0), block(0), {"zh": zh + 1}, rz, zh == last - 1)
        arrived(block(last), rz + last, zh == 1)
        two = push(block(last), block(last), {"zh": zh - 1}, rz + last, zh == 1, one)
        return [one, two]

    def z_wait(block, rz, use):
        last = RING - 1

        def take(k, pred, waited=None, instead=None):
            arrived(block(k), rz + k, pred if waited is None else pred & ~waited)
            return use(block(k), pred, instead)

        out = [take(zh - 1, zh >= 1), take(zh + 1, zh < last)]
        out.append(take(zh - 2, zh >= 2, zh == last - 1))
        out.append(take(zh + 2, zh <= 1, zh == 1, out[-1]))
        out.append(take(0, zh == last))
        out.append(take(last, zh == 0, None, out[-1]))
        return out

    class ZSum:
        def __init__(self, block, slot, add, direct):
            self.block, self.slot, self.add, self.direct = block, slot, add, direct
            self.valid = (direct | (zh >= 1), zh >= 2, direct | (zh <= 2), zh <= 1)
            self.sems = new(4)
            self.out = []

        def send(self):
            b, v, s = self.block, self.slot, self.sems
            last = RING - 1
            o = self.out
            if self.direct:
                o.append(push(b(last), v(2), {"zh": zh + last}, s + 2, zh == 0))
                o.append(push(b(0), v(0), {"zh": zh - last}, s + 0, zh == last, o[-1]))
                o.append(push(b(zh + 2), v(1), {"zh": zh + 2}, s + 1, zh <= 1))
                o.append(push(b(zh - 2), v(3), {"zh": zh - 2}, s + 3, zh >= 2, o[-1]))
            else:
                o.append(push(b(last), v(1), {"zh": zh + 1}, s + 1, zh == 0))
                o.append(push(b(0), v(3), {"zh": zh - 1}, s + 3, zh == last, o[-1]))
                o.append(push(b(zh + 2), v(1), {"zh": zh + 2}, s + 1, zh == 0))
                o.append(push(b(zh - 2), v(3), {"zh": zh - 2}, s + 3, zh == last, o[-1]))
            o.append(push(b(zh + 1), v(0), {"zh": zh + 1}, s + 0, zh < last))
            o.append(push(b(zh - 1), v(2), {"zh": zh - 1}, s + 2, zh > 0))

        def forward(self):
            b, v, s = self.block, self.slot, self.sems
            last = RING - 1

            def up():
                arrived(v(1), s + 1)
                self.add(last, 1)

            def down():
                arrived(v(3), s + 3)
                self.add(0, 3)

            pl.when(zh == 1)(up)
            self.out.append(push(b(last), v(1), {"zh": zh + 2}, s + 1, zh == 1))
            pl.when(zh == last - 1)(down)
            self.out.append(push(b(0), v(3), {"zh": zh - 2}, s + 3, zh == last - 1, self.out[-1]))

        def end(self):
            for k, valid in enumerate(self.valid):
                arrived(self.slot(k), self.sems + k, valid)
            settle(*self.out)

        def total(self, own, parts):
            for part, pred in zip(parts, self.valid, strict=True):
                own = own + jnp.where(pred, part.astype(f32), 0.0)
            return own

    class Column:
        def __init__(self, src, raw, sorted_, w, R, C, lane0):
            self.src, self.raw, self.sorted = src, raw, sorted_
            self.w, self.R, self.C, self.lanes = w, R, C, pl.ds(lane0, C)
            self.out = []

        rl = cached_property(lambda self: new())
        ra = cached_property(lambda self: new())
        rz = cached_property(lambda self: new(4))
        rc = cached_property(lambda self: new())

        def halves(self):
            out = []
            for k in (0, 1):
                part = Column(self.src, self.raw, self.sorted, self.w, self.R, self.C, 0)
                part.lanes = pl.ds(self.lanes.start + k * self.C // 2, self.C // 2)
                out.append(part)
            return out

        def spread_wait(self):
            arrived(self.block(zh), self.ra)
            settle(*self.out)
            self.out = []

        def load(self):
            keep_local(self.src, self.raw, self.rl)

        def prepare(self):
            local_wait(self.src, self.raw, self.rl)
            value, part = self.raw[...], self.C // (2 * RING)
            for k in range(PLANE):
                first = [(g * PLANE + k) * part for g in range(2 * RING)]
                self.sorted[k] = jnp.concatenate([value[:, at : at + part] for at in first], axis=1)

        def spread(self):
            dst = self.w.at[zh, c, ds(p * self.R, self.R, 16), self.lanes]
            for k, dev in plane_peers:
                self.out.append(push(self.sorted.at[k], dst, dev, self.ra))
            keep_local(self.sorted.at[p], dst, self.ra)

        def block(self, z):
            return self.w.at[z, c, :, self.lanes]

        def z_send(self, spread=True):
            if spread:
                arrived(self.block(zh), self.ra)
            self.out += z_send(self.block(zh), self.block, self.rz)
            self.out.append(self.core_push(self.block(zh)))

        def z_forward(self):
            self.out += z_forward(self.block, self.rz)

        def core_push(self, block, pred=None, instead=None):
            return push(block, block, to_core, self.rc, pred, instead)

        def z_wait(self):
            self.out += z_wait(self.block, self.rz, self.core_push)

        def end(self):
            arrived(self.w.at[:, 1 - c, :, self.lanes], self.rc)
            settle(*self.out)

    class Row(Column):
        def __init__(self, src, w):
            self.src, self.w, self.lanes = src, w, pl.ds(0, w.shape[3])
            self.out = []

        def z_send(self, away=(2, 1)):
            if 2 in away:
                keep_local(self.src, self.block(zh), self.ra)
            self.out += z_send(self.src, self.block, self.rz, away)

        def z_wait(self):
            pltpu.make_async_copy(self.src, self.block(zh), r.rs.at[self.ra]).wait()
            self.out.append(self.core_push(self.block(zh)))
            super().z_wait()

    class ColumnsGrad:
        def __init__(self, g, other, slots, land, R, lane0, lanes, direct=False):
            self.g, self.other, self.slots, self.land = g, other, slots, land
            self.R, self.lanes = R, pl.ds(lane0, lanes)
            self.rows = PLANE * R
            self.rc, self.rl = new(), new()
            self.zsum = ZSum(
                lambda z: g.at[z, c, :, self.lanes], lambda k: slots.at[k, :, self.lanes], self.add_slot, direct
            )

        def add_slot(self, z, k):
            g, q = self.g, self.lanes

            def add(o):
                s = pl.ds(o, 16)
                g[z, c, s, q] = (g[z, c, s, q].astype(f32) + self.slots[k, s, q].astype(f32)).astype(bf16)

            loop(self.rows, 16, add)

        def core_send(self):
            self.pushed = push(
                self.g.at[:, 1 - c, :, self.lanes], self.other.at[:, :, self.lanes], to_core, self.rc
            )

        def core_sum(self):
            g, q = self.g, self.lanes
            arrived(self.other.at[:, :, q], self.rc)
            settle(self.pushed)
            for z in range(RING):

                def add(o):
                    s = pl.ds(o, 16)
                    g[z, c, s, q] = (g[z, c, s, q].astype(f32) + self.other[z, s, q].astype(f32)).astype(bf16)

                loop(self.rows, 16, add)

        def z_send(self):
            self.core_sum()
            self.zsum.send()

        def z_forward(self):
            self.zsum.forward()

        def plane_send(self):
            g, q, R = self.g, self.lanes, self.R
            self.zsum.end()

            def add(o):
                s = pl.ds(o, 16)
                parts = [self.slots[k, s, q] for k in range(4)]
                g[zh, c, s, q] = self.zsum.total(g[zh, c, s, q].astype(f32), parts).astype(bf16)

            loop(PLANE * R, 16, add)
            dst = self.land.at[p, :, q]
            self.out = []
            for k, dev in plane_peers:
                self.out.append(push(g.at[zh, c, ds(k * R, R, 16), q], dst, dev, self.rl))
            keep_local(g.at[zh, c, ds(p * R, R, 16), q], dst, self.rl)

        def end(self):
            arrived(self.land.at[:, :, self.lanes], self.rl)
            settle(*self.out)

    def in_order(land, lane0, C, held, result):
        held[...] = unsorted([land[k, :, lane0 : lane0 + C].astype(f32) for k in range(PLANE)])
        deliver(held, result)

    class LastGrad(ColumnsGrad):
        def __init__(self, g, other, stage, slots, R, lane0, lanes, total, result):
            super().__init__(g, other, slots, None, R, lane0, lanes)
            self.stage, self.sum, self.result = stage, total, result
            self.zsum.block, self.zsum.slot = (lambda z: stage.at[:, z]), (lambda k: slots.at[k])

        def add_slot(self, z, k):
            for q in range(PLANE):
                self.stage[q, z] = (self.stage[q, z].astype(f32) + self.slots[k, q].astype(f32)).astype(bf16)

        def plane_send(self):
            R, dst = self.R, self.stage.at[p]
            self.core_sum()
            self.out = []
            for k, dev in plane_peers:
                self.out.append(push(self.g.at[:, c, ds(k * R, R, 16), self.lanes], dst, dev, self.rl))
            keep_local(self.g.at[:, c, ds(p * R, R, 16), self.lanes], dst, self.rl)

        def z_send(self):
            arrived(self.stage, self.rl)
            self.zsum.send()

        def end(self):
            self.zsum.end()
            settle(*self.out)
            values = [
                self.zsum.total(self.stage[q, zh].astype(f32), [self.slots[k, q] for k in range(4)]) for q in range(PLANE)
            ]
            self.sum[...] = unsorted(values)
            deliver(self.sum, self.result)

    class RowsGrad(ColumnsGrad):
        def __init__(self, g, other, slots, total, result):
            super().__init__(g, other, slots, None, 0, 0, g.shape[3])
            self.rows, self.sum, self.result = g.shape[2], total, result

        def end(self):
            self.zsum.end()

            def add(o):
                s = pl.ds(o, 16)
                self.sum[s] = self.zsum.total(self.g[zh, c, s].astype(f32), [self.slots[k, s] for k in range(4)])

            loop(self.rows, 16, add)
            deliver(self.sum, self.result)

    class Carry:
        def __init__(self, own, sib, buf, later):
            self.own, self.sib, self.buf, self.later = own, sib, buf, later
            self.rc, self.rz = new(), new(RING * NL)
            self.out = []

        def order(self):
            return range(RING * NL) if self.later else reversed(range(RING * NL))

        def send_core(self):
            self.out.append(push(self.own, self.sib, to_core, self.rc))

        def send(self):
            arrived(self.sib, self.rc)
            own, sib = self.own[...], self.sib[...]
            near = (c == 0) if self.later else (c == 1)
            head, tail = jnp.where(near, own, sib), jnp.where(near, sib, own)
            self.buf[flat_z, 0:PLANE] = tail[0:PLANE] * head[0:PLANE]
            self.buf[flat_z, PLANE : 2 * PLANE] = (
                tail[0:PLANE] * head[PLANE : 2 * PLANE] + tail[PLANE : 2 * PLANE]
            )
            part = self.buf.at[flat_z]
            for at in self.order():
                pred = (flat_z < at) if self.later else (flat_z > at)
                self.out.append(push(part, part, {"zh": at // NL, "zl": at % NL}, self.rz + flat_z, pred))

        def fold(self, into):
            into[...] = jnp.zeros_like(into)

            def take(part):
                into[0:PLANE] = part[0:PLANE] * into[0:PLANE] + part[PLANE : 2 * PLANE]

            for at in self.order():
                pred = (flat_z > at) if self.later else (flat_z < at)

                def chip(at=at):
                    arrived(self.buf.at[at], self.rz + at)
                    take(self.buf[at])

                pl.when(pred)(chip)
            pl.when((c == 1) if self.later else (c == 0))(lambda: take(self.sib[...]))
            settle(*self.out)

    GL = PLANE * RD
    ring = zh * 2 + c

    def ring_place(at):
        return {"zh": at // 2, "c": at % 2}

    class Small:
        def __init__(self):
            self.rr, self.rk = new(), new()
            self.out = []

        def pack(self):
            for load in small_loads:
                local_wait(*load)
            lengths = r.lens[...]
            rows = [r.gain_a[...], r.gain_b[...], r.taps[...], r.bias_a[...], r.bias_b[...], r.bias_c[...]]
            rows += [lax.shift_right_logical(lengths, 8), lengths & 255]
            rows = [row.astype(f32) for row in rows]
            rows = [jnp.concatenate([row, jnp.zeros((row.shape[0], 128 - row.shape[1]), f32)], axis=1) for row in rows]
            r.pack[...] = jnp.concatenate([*rows, jnp.zeros((5, 128), f32)], axis=0).astype(bf16)

        def one(self):
            for at in range(2 * RING):
                self.out.append(push(r.pack, r.pr.at[ring], ring_place(at), self.rr, ring != at))
            keep_local(r.pack, r.pr.at[ring], self.rr)

        def two(self):
            arrived(r.pr, self.rr)
            lines = []
            for at in range(2 * RING):
                tile = r.pr[at].astype(f32)
                lines.append(jnp.concatenate([tile[row : row + 1, 0:32] for row in (0, 1, 9, 10)], axis=1))
            r.line[...] = jnp.concatenate([*lines, jnp.zeros((16 - 2 * RING, 128), f32)], axis=0).astype(bf16)
            for _, dev in plane_peers:
                self.out.append(push(r.line, r.pp.at[p], dev, self.rk))
            keep_local(r.line, r.pp.at[p], self.rk)

        def three(self):
            arrived(r.pp, self.rk)
            parts = [r.pp[k].astype(f32) for k in range(PLANE)]
            for row in (0, 1):
                lanes = slice(row * 32, row * 32 + RD)
                wide = jnp.concatenate([part[:, lanes] for part in parts], axis=1)
                for at in range(2 * RING):
                    r.gains[row : row + 1, at * GL : (at + 1) * GL] = wide[at : at + 1]
            whole = jnp.concatenate([r.pr[at, :, 0:RW].astype(f32) for at in range(2 * RING)], axis=1)
            r.chan[...] = whole[2:10]
            rates = r.rates[...].astype(f32)
            rates = jnp.concatenate([rates[k : k + 1] for k in range(W // 128)], axis=1)
            mine = jnp.zeros((1, CW), f32)
            for k in range(PLANE):
                at = [(g * PLANE + k) * RW for g in range(2 * RING)]
                mine = jnp.where(p == k, jnp.concatenate([rates[:, o : o + RW] for o in at], axis=1), mine)
            r.chan[7:8] = jnp.exp2(-mine)

        def four(self):
            where = lax.broadcasted_iota(jnp.int32, (T, 128), 0).astype(f32) + (pos * T).astype(f32)
            for k in range(PLANE):
                part = r.pp[k].astype(f32)
                starts, ends = [], []
                total = jnp.zeros((1, 1), f32)
                for j in range(dims.SEGS):
                    starts.append(total)
                    total = total + part[0:1, 64 + j : 65 + j] * 256.0 + part[0:1, 96 + j : 97 + j]
                    ends.append(total)

                def seg(shift):
                    at = where + float(shift)
                    value = jnp.zeros((T, 128), f32)
                    for end in ends:
                        value = value + jnp.where(at >= end, 1.0, 0.0)
                    return jnp.where((at < 0.0) | (at >= float(T * places)), -1.0, value)

                here = seg(0)
                rows = pl.ds(k * T, T)
                first = jnp.zeros((T, 128), f32)
                for start in starts:
                    first = jnp.where(where == start, 1.0, first)
                r.masks[0, rows] = first
                for j in (1, 2, 3):
                    r.masks[j, rows] = jnp.where(seg(-j) == here, 1.0, 0.0)
                    r.masks[3 + j, rows] = jnp.where(seg(j) == here, 1.0, 0.0)
            settle(*self.out)

    class SmallGrad:
        def __init__(self):
            self.rg = new()
            self.out = []

        def one(self):
            for at in range(2 * RING):
                own = jnp.concatenate([r.gchan[:, at * RW : (at + 1) * RW], jnp.zeros((8, 128 - RW), f32)], axis=1)
                r.gs[at] = own
            for at in range(2 * RING):
                self.out.append(push(r.gs.at[at], r.gg.at[ring], ring_place(at), self.rg, ring != at))
            keep_local(r.gs.at[ring], r.gg.at[ring], self.rg)

        def two(self):
            arrived(r.gg, self.rg)
            value = r.gg[0]
            for at in range(1, 2 * RING):
                value = value + r.gg[at]
            r.small_sum[...] = value
            deliver(r.small_sum, r.small_out)
            settle(*self.out)

    barrier = pltpu.get_barrier_semaphore()
    for _, dev in plane_peers:
        pl.semaphore_signal(barrier, 1, device_id=dev, device_id_type=MESH)
    for at in range(places):

        @pl.when(pos != at)
        def _(at=at):
            pl.semaphore_signal(barrier, 1, device_id=place(at), device_id_type=MESH)

    first_loads = [
        (src, dst, new())
        for src, dst in (
            (r.tokens, r.x_all.at[p]),
            (r.cotangent, r.cot_all.at[p]),
        )
    ]
    small_loads = [
        (src, dst, new())
        for src, dst in (
            (r.first_gain, r.gain_a),
            (r.second_gain, r.gain_b),
            (r.conv_taps, r.taps),
            (r.conv_bias, r.bias_a),
            (r.decay_bias, r.bias_b),
            (r.inject_bias, r.bias_c),
            (r.doc_lengths, r.lens),
            (r.decay_exponent, r.rates),
        )
    ]
    for load in small_loads + first_loads:
        keep_local(*load)

    w_i = Column(r.input_weight, r.raw_i, r.sort_i, r.w_ib, RD, CW, 0)
    w_b = Column(r.branch_weight, r.raw_b, r.sort_b, r.w_ib, RD, CW, CW)
    w_d = Column(r.decay_weight, r.raw_d, r.sort_d, r.w_di, RW, CW, 0)
    w_j = Column(r.inject_weight, r.raw_j, r.sort_j, r.w_di, RW, CW, CW)
    w_g = Column(r.mlp_gate, r.raw_g, r.sort_g, r.w_gu, RD, CF, 0)
    w_u = Column(r.mlp_up, r.raw_u, r.sort_u, r.w_gu, RD, CF, CF)
    w_g1, w_g2 = w_g.halves()
    w_o, w_dn = Row(r.output_weight, r.w_o), Row(r.mlp_down, r.w_dn)
    ag_x, ag_conv, ag_two = Gather(r.x_all), Gather(r.conv), Gather(r.n_two)
    ag_cot, ag_out = Gather(r.cot_all), Gather(r.d_out)
    small, small_grad = Small(), SmallGrad()
    after, before = flat_z + c, flat_z - (1 - c)
    to_next = {"zh": after // NL, "zl": after % NL, "c": 1 - c}
    to_prev = {"zh": before // NL, "zl": before % NL, "c": 1 - c}
    step = 256
    chunk = PLANE * RD * 2

    for w in (w_i, w_d, w_j, w_b, w_g, w_u):
        w.load()
    small.pack()
    w_i.prepare()
    w_d.prepare()
    pl.semaphore_wait(barrier, len(plane_peers) + places - 1)
    small.one()
    local_wait(*first_loads[0])
    halo_x = new()
    sent_x = push(r.x_all.at[p, pl.ds(T - 16, 16)], r.x_halo.at[p], to_next, halo_x, pos < places - 1)
    w_o.z_send((2,))
    w_i.spread()
    w_d.spread()
    ag_x.start()
    w_j.prepare()
    w_i.z_send()
    small.two()
    w_b.prepare()

    @pl.when(pos == 0)
    def _():
        r.x_halo[p] = jnp.zeros((16, D), bf16)

    arrived(r.x_halo.at[p], halo_x, pos > 0)
    halo_p = new(PLANE)
    sent_p = [push(r.x_halo.at[p], r.x_halo.at[p], dev, halo_p + p) for _, dev in plane_peers]
    ag_x.mid()
    w_i.z_forward()
    w_o.z_send((1,))
    w_g.prepare()
    local_wait(*first_loads[1])
    small.three()

    def norm_block(k):
        def norm_one(o):
            s = pl.ds(o, 32)
            v = r.x_all[k, s].astype(f32)
            r.n_one[k, s] = (v * inverse_rms(v) * r.gains[0:1]).astype(bf16)

        loop(T, 32, norm_one)

    norm_block(p)
    w_d.z_send()
    ag_x.wait_x()
    norm_block(px)
    ag_x.wait_y()
    norm_block(py)
    w_j.spread()
    small.four()
    for k, _ in plane_peers:
        arrived(r.x_halo.at[k], halo_p + k)
    v = r.x_halo[...].reshape(PLANE * 16, D).astype(f32)
    r.n_halo[...] = (v * inverse_rms(v) * r.gains[0:1]).astype(bf16).reshape(PLANE, 16, D)
    ag_x.wait_d()
    norm_block(pd)
    settle(*ag_x.out, sent_x, *sent_p)
    w_b.spread()
    w_g.spread()
    w_o.z_forward()
    w_i.z_wait()
    w_u.prepare()
    w_j.z_send()
    w_i.end()

    def weight_ib(lanes):
        return r.w_ib[:, :, :, lanes].reshape(D, CW)

    lanes_a, lanes_b = pl.ds(0, CW), pl.ds(CW, CW)
    halo = dot(r.n_halo[...].reshape(PLANE * 16, D), weight_ib(lanes_a)).astype(bf16).astype(f32)
    body = dot(r.n_one[...].reshape(M, D), weight_ib(lanes_a)).astype(bf16).astype(f32)
    for k in range(PLANE):
        r.u[k, 0:8] = halo[k * 16 + 8 : (k + 1) * 16]
        r.u[k, 8 : 8 + T] = body[k * T : (k + 1) * T]

    def wide(j, rows):
        return jnp.concatenate([r.masks[j, rows]] * (CW // 128), axis=1) > 0.5

    def convolve(o):
        for k in range(PLANE):
            ext = r.u[k, pl.ds(o, 24)]
            rows = ds(k * T + o, 16, 16)
            total = r.chan[4:5] + r.chan[0:1] * ext[8:24]
            for j in range(1, 4):
                total = total + jnp.where(wide(j, rows), r.chan[j : j + 1] * ext[8 - j : 24 - j], 0.0)
            r.conv[p, rows] = total.astype(bf16)

    loop(T, 16, convolve)
    ag_conv.start()
    w_d.z_forward()
    ag_conv.mid()
    w_j.z_forward()
    w_b.z_send()
    w_d.z_wait()
    w_d.end()

    def pre(q, lanes):
        return dot(r.conv[q], r.w_di[:, :, ds(q * RW, RW, 16), lanes].reshape(CW, CW))

    r.pair[:, 0:CW] = pre(p, lanes_a)
    ag_conv.wait_x()
    r.pair[:, 0:CW] += pre(px, lanes_a)
    ag_conv.wait_y()
    r.pair[:, 0:CW] += pre(py, lanes_a)
    w_b.z_forward()
    ag_conv.wait_d()
    r.pair[:, 0:CW] += pre(pd, lanes_a)
    settle(*ag_conv.out)
    w_g.spread_wait()
    w_g1.z_send(False)
    w_j.z_wait()
    w_u.spread()
    ag_cot.start()
    w_o.z_wait()
    w_j.end()
    r.pair[:, CW : 2 * CW] = (pre(0, lanes_b) + pre(1, lanes_b)) + (pre(2, lanes_b) + pre(3, lanes_b))

    def decay_terms(s, rg):
        log_a = -rate_scale * rg * r.chan[7:8]
        root = jnp.exp(log_a)
        gap = minus_expm1(2.0 * log_a, root)
        first = wide(0, s)
        return root, gap, jnp.where(first, 1.0, jnp.sqrt(jnp.maximum(gap, floor_gap))), first

    def gates_two(o):
        s = pl.ds(o, 16)
        rg = jax.nn.sigmoid(r.pair[s, 0:CW] + r.chan[5:6])
        ig = jax.nn.sigmoid(r.pair[s, CW : 2 * CW] + r.chan[6:7])
        root, _, mult, first = decay_terms(s, rg)
        r.rgate[s], r.igate[s] = rg, ig
        r.decay[s] = jnp.where(first, 0.0, root)
        r.work[s] = mult * ig * r.conv[p, s].astype(f32)

    loop(M, 16, gates_two)
    row = lax.broadcasted_iota(jnp.int32, (8, CW), 0)

    def scan_forward(j, carry):
        out = []
        for k in range(PLANE):
            s = ds(k * T + j * 8, 8, 8)
            a, b = r.decay[s], r.work[s]
            for n in (1, 2, 4):
                a_b = jnp.where(row >= n, pltpu.roll(a, n, 0), 1.0)
                b_b = jnp.where(row >= n, pltpu.roll(b, n, 0), 0.0)
                a, b = a * a_b, a * b_b + b
            total, prod = b + a * carry[2 * k], a * carry[2 * k + 1]
            r.state[k, ds(8 + j * 8, 8, 8)] = total
            r.cum[s] = prod
            out += [total[7:8], prod[7:8]]
        return tuple(out)

    zero, one = jnp.zeros((1, CW), f32), jnp.ones((1, CW), f32)
    ends = lax.fori_loop(0, T // 8, scan_forward, (zero, one) * PLANE)
    carry_f = Carry(r.own_f, r.sib_f, r.carry_f, True)
    for k in range(PLANE):
        r.own_f[k : k + 1] = ends[2 * k + 1]
        r.own_f[PLANE + k : PLANE + k + 1] = ends[2 * k]
    carry_f.send_core()
    w_b.z_wait()
    carry_f.send()
    w_g1.z_forward()
    w_g2.z_send(False)
    w_b.end()
    r.work[...] = dot(r.n_one[...].reshape(M, D), weight_ib(lanes_b))

    def gates_one(o):
        s = pl.ds(o, 16)
        r.gated[s], r.slope[s] = gelu_parts(r.work[s])

    loop(M, 16, gates_one)
    ag_cot.mid()
    carry_f.fold(r.into)
    for k in range(PLANE):
        r.state[k, 0:8] = jnp.broadcast_to(r.into[k : k + 1], (8, CW))

    def mix(o):
        for k in range(PLANE):
            s, t = ds(k * T + o, 16, 16), ds(8 + o, 16, 8)
            state = r.state[k, t] + r.cum[s] * r.into[k : k + 1]
            r.state[k, t] = state
            r.mixed[s] = (state * r.gated[s]).astype(bf16)

    loop(T, 16, mix)

    w_o.end()

    def out_part(o):
        q = pl.ds(o, step)
        r.part[:, :, q] = dot(r.mixed[...], r.w_o[:, :, :, q].reshape(CW, step)).astype(bf16).reshape(PLANE, T, step)

    loop(D, step, out_part)
    rs_one = Scatter(r.part, r.got_one)
    rs_one.start()
    w_g1.z_wait()
    w_g2.z_forward()
    w_u.z_send()
    ag_cot.end()
    rs_one.mid()
    rs_one.end()

    def norm_two(o, summed, _):
        s = pl.ds(o, 32)
        v = r.x_all[p, s].astype(f32) + summed
        r.x_one[s] = v
        r.n_two[p, s] = (v * inverse_rms(v) * r.gains[1:2]).astype(bf16)

    rs_one.each(32, norm_two)
    ag_two.start()
    w_u.z_forward()
    ag_two.mid()
    w_dn.z_send()
    w_g2.z_wait()
    w_g1.end()
    w_u.z_wait()
    w_g2.end()
    ag_two.end()

    def mlp_in(o):
        q = pl.ds(o, step)
        r.pair[:, q] = dot(r.n_two[...].reshape(M, D), r.w_gu[:, :, :, q].reshape(D, step))

    loop(CF, step, mlp_in)
    w_dn.z_forward()
    w_u.end()
    loop(CF, step, lambda o: mlp_in(pl.multiple_of(CF + o, step)))

    def gates_mlp(o):
        s = pl.ds(o, 16)
        value, slope = gelu_parts(r.pair[s, 0:CF])
        up = r.pair[s, CF : 2 * CF]
        r.hidden[s] = (value * up).astype(bf16)
        r.pair[s, 0:CF] = slope * up
        r.pair[s, CF : 2 * CF] = value

    loop(M, 16, gates_mlp)

    half = CF // 2
    for k in (0, 1):
        for o in range(0, D, D // 2):
            value = dot_tn(r.hidden[:, k * half : (k + 1) * half], r.cot_all[:, :, o : o + D // 2].reshape(M, D // 2))
            r.g_dn[k * RING // 2 : (k + 1) * RING // 2, :, :, o : o + D // 2] = value.astype(bf16).reshape(
                RING // 2, 2, RF, D // 2
            )
    g_dn = RowsGrad(r.g_dn, r.h_dn, r.z_dn, r.t_dn, r.grad_mlp_down)
    g_dn.core_send()
    g_dn.z_send()
    w_dn.z_wait()
    w_dn.end()

    for k in range(CF // step):
        back = dot_nt(r.cot_all[...].reshape(M, D), r.w_dn[...].reshape(CF, D)[k * step : (k + 1) * step])
        r.d_pair[:, k * step : (k + 1) * step] = (back * r.pair[:, k * step : (k + 1) * step]).astype(bf16)
        r.d_pair[:, CF + k * step : CF + (k + 1) * step] = (
            back * r.pair[:, CF + k * step : CF + (k + 1) * step]
        ).astype(bf16)

    def d_two_part(z, _):
        q = ds(z * chunk, chunk, chunk)
        r.part[:, :, q] = (
            dot_nt(r.d_pair[...], r.w_gu[z].reshape(chunk, 2 * CF)).astype(bf16).reshape(PLANE, T, chunk)
        )
        return 0

    lax.fori_loop(0, RING, d_two_part, 0)
    rs_two = Scatter(r.part, r.got_two)
    rs_two.start()

    def grad_gate_up(lane0):
        lanes = pl.ds(lane0, CF)

        def run(z, _):
            q = ds(z * chunk, chunk, chunk)
            value = dot_tn(r.n_two[:, :, q].reshape(M, chunk), r.d_pair[:, lanes])
            r.w_gu[z, :, :, lanes] = value.astype(bf16).reshape(2, chunk // 2, CF)
            return 0

        lax.fori_loop(0, RING, run, 0)

    grad_gate_up(0)
    g_g = ColumnsGrad(r.w_gu, r.h_gu, r.z_gu, r.l_gu, RD, 0, CF)
    g_g.core_send()
    rs_two.mid()
    g_dn.z_forward()
    g_g.z_send()
    grad_gate_up(CF)
    g_u, g_v = (
        ColumnsGrad(r.w_gu, r.h_gu, r.z_gu, r.l_gu, RD, lane0, CF // 2) for lane0 in (CF, CF + CF // 2)
    )
    g_u.core_send()
    g_v.core_send()

    def act_part(o):
        q = pl.ds(o, step)
        r.part_act[:, :, q] = dot(r.hidden[...], r.w_dn[:, :, :, q].reshape(CF, step)).astype(bf16).reshape(PLANE, T, step)

    loop(D, step, act_part)
    r.gchan[...] = jnp.zeros_like(r.gchan)
    rs_two.end()

    def norm_two_back(o, d_two, _):
        s = pl.ds(o, 32)
        v = r.x_one[s]
        rs = inverse_rms(v)
        z = v * rs
        dz = d_two * r.gains[1:2]
        d_one = r.cot_all[p, s].astype(f32) + rs * (dz - z * jnp.mean(dz * z, axis=-1, keepdims=True))
        r.d_one[s] = d_one
        r.d_out[p, s] = d_one.astype(bf16)

    rs_two.each(32, norm_two_back)
    ag_out.start()
    ag_out.mid()
    g_g.z_forward()
    g_u.z_send()
    ag_out.end()
    rs_act = Scatter(r.part_act, r.got_act)
    rs_act.start()

    r.work[...] = dot_nt(r.d_out[...].reshape(M, D), r.w_o[...].reshape(CW, D))

    def split(o):
        for k in range(PLANE):
            s = ds(k * T + o, 16, 16)
            d_mixed = r.work[s]
            r.d_gu[s, CW : 2 * CW] = (d_mixed * r.state[k, ds(8 + o, 16, 8)] * r.slope[s]).astype(bf16)
            r.work[s] = d_mixed * r.gated[s]

    loop(T, 16, split)

    def scan_backward(i, carry):
        j = T // 8 - 1 - i
        out = []
        for k in range(PLANE):
            s = ds(k * T + j * 8, 8, 8)
            decay, b = r.decay[s], r.work[s]
            a = jnp.where(row < 7, pltpu.roll(decay, 7, 0), carry[3 * k + 2])
            for n in (1, 2, 4):
                a_b = jnp.where(row < 8 - n, pltpu.roll(a, 8 - n, 0), 1.0)
                b_b = jnp.where(row < 8 - n, pltpu.roll(b, 8 - n, 0), 0.0)
                a, b = a * a_b, a * b_b + b
            total, prod = b + a * carry[3 * k], a * carry[3 * k + 1]
            r.work[s], r.cum[s] = total, prod
            out += [total[0:1], prod[0:1], decay[0:1]]
        return tuple(out)

    heads = lax.fori_loop(0, T // 8, scan_backward, (zero, one, one) * PLANE)
    carry_b = Carry(r.own_b, r.sib_b, r.carry_b, False)
    for k in range(PLANE):
        r.own_b[k : k + 1] = r.own_f[k : k + 1]
        r.own_b[PLANE + k : PLANE + k + 1] = heads[3 * k] * heads[3 * k + 2]
    carry_b.send_core()

    def grad_out(o):
        q = pl.ds(o, D // 2)
        value = dot_tn(r.mixed[...], r.d_out[:, :, q].reshape(M, D // 2))
        r.w_o[:, :, :, q] = value.astype(bf16).reshape(RING, 2, RW, D // 2)

    loop(D, D // 2, grad_out)
    g_o = RowsGrad(r.w_o, r.h_o, r.z_o, r.t_o, r.grad_output_weight)
    g_o.core_send()
    carry_b.send()
    g_u.z_forward()
    g_v.z_send()
    rs_act.mid()

    def d_branch_part(z, _):
        q = ds(z * chunk, chunk, chunk)
        r.part[:, :, q] = (
            dot_nt(r.d_gu[:, lanes_b], r.w_ib[z, :, :, lanes_b].reshape(chunk, CW))
            .astype(bf16)
            .reshape(PLANE, T, chunk)
        )
        value = dot_tn(r.n_one[:, :, q].reshape(M, chunk), r.d_gu[:, lanes_b])
        r.w_ib[z, :, :, lanes_b] = value.astype(bf16).reshape(2, chunk // 2, CW)
        return 0

    lax.fori_loop(0, RING, d_branch_part, 0)
    g_b = ColumnsGrad(r.w_ib, r.h_ib, r.z_ib, r.l_ib, RD, CW, CW)
    g_b.core_send()
    g_g.plane_send()
    carry_b.fold(r.into)
    g_o.z_send()

    def back(o):
        sums = [jnp.zeros((1, CW), f32)] * 2
        for k in range(PLANE):
            s = ds(k * T + o, 16, 16)
            adjoint = r.work[s] + r.cum[s] * r.into[k : k + 1]
            previous = r.state[k, pl.ds(o, 24)][7:23]
            rg, ig, decay, conv = r.rgate[s], r.igate[s], r.decay[s], r.conv[p, s].astype(f32)
            _, gap, mult, first = decay_terms(s, rg)
            d_mult = jnp.where(first, 0.0, adjoint * ig * conv)
            d_log = adjoint * previous * decay - jnp.where(gap > floor_gap, (1.0 - gap) * d_mult / mult, 0.0)
            d_decay = (-rate_scale * r.chan[7:8] * d_log * rg * (1.0 - rg)).astype(bf16)
            d_inject = (adjoint * mult * conv * ig * (1.0 - ig)).astype(bf16)
            r.d_pre[s, 0:CW] = d_decay
            r.d_pre[s, CW : 2 * CW] = d_inject
            sums[0] = sums[0] + jnp.sum(d_decay.astype(f32), axis=0, keepdims=True)
            sums[1] = sums[1] + jnp.sum(d_inject.astype(f32), axis=0, keepdims=True)
            r.d_conv[k, pl.ds(o, 16)] = adjoint * mult * ig
        r.gchan[5:6] += sums[0]
        r.gchan[6:7] += sums[1]

    loop(T, 16, back)

    def conv_part(q):
        r.part_conv[q] = dot_nt(r.d_pre[...], r.w_di[:, :, ds(q * RW, RW, 16), :].reshape(CW, 2 * CW)).astype(bf16)

    rs_conv = Scatter(r.part_conv, r.got_conv)
    conv_part(pd)
    rs_act.end()
    rs_conv.start_far()
    conv_part(px)
    conv_part(py)
    rs_conv.start_near()
    conv_part(p)
    g_v.z_forward()

    def finish_act(o, summed, _):
        s = pl.ds(o, 16)
        r.act[s] = (r.x_one[s] + summed).astype(bf16)

    rs_act.each(16, finish_act)
    deliver(r.act, r.activations)
    g_b.z_send()
    g_dn.end()

    def grad_dec_inj(lanes):
        def run(q, _):
            value = dot_tn(r.conv[q], r.d_pre[:, lanes])
            r.w_di[:, :, ds(q * RW, RW, 16), lanes] = value.astype(bf16).reshape(RING, 2, RW, CW)
            return 0

        lax.fori_loop(0, RING, run, 0)

    grad_dec_inj(lanes_a)
    g_d = ColumnsGrad(r.w_di, r.h_di, r.z_di, r.l_di, RW, 0, CW - 128)
    g_d.core_send()
    rs_conv.mid()
    grad_dec_inj(lanes_b)
    g_j, g_k = (
        ColumnsGrad(r.w_di, r.h_di, r.z_di, r.l_di, RW, lane0, lanes)
        for lane0, lanes in ((CW - 128, 256), (CW + 128, CW - 128))
    )
    g_j.core_send()
    g_k.core_send()
    g_o.z_forward()
    g_d.z_send()
    rs_conv.end()

    for half in (0, 1):

        def add_conv(o, half=half):
            for k in (2 * half, 2 * half + 1):
                at = (k - 2 * half) * T + o
                r.d_conv[k, pl.ds(o, 16)] += rs_conv.total(half, pl.multiple_of(at, 16), 16)

        loop(T, 16, add_conv)
    halo_b = new()
    for k in range(PLANE):
        r.halo_out[4 * k : 4 * k + 4] = r.d_conv[k, 0:4]
    sent_b = push(r.halo_out, r.halo_in, to_prev, halo_b, pos > 0)
    g_b.z_forward()

    def taps_back(o):
        sums = [jnp.zeros((1, CW), f32)] * 5
        for k in range(PLANE):
            ext = r.u[k, pl.ds(o, 24)]
            rows = ds(k * T + o, 16, 16)
            dc = r.d_conv[k, pl.ds(o, 16)]
            sums[4] = sums[4] + jnp.sum(dc, axis=0, keepdims=True)
            sums[0] = sums[0] + jnp.sum(dc * ext[8:24], axis=0, keepdims=True)
            for j in range(1, 4):
                term = jnp.where(wide(j, rows), dc * ext[8 - j : 24 - j], 0.0)
                sums[j] = sums[j] + jnp.sum(term, axis=0, keepdims=True)
        for j in range(5):
            r.gchan[j : j + 1] += sums[j]

    loop(T, 16, taps_back)
    small_grad.one()

    @pl.when(pos == places - 1)
    def _():
        r.halo_in[...] = jnp.zeros((16, CW), f32)

    g_d.z_forward()
    g_j.z_send()
    arrived(r.halo_in, halo_b, pos < places - 1)
    for k in range(PLANE):
        r.d_conv[k, T : T + 8] = jnp.concatenate([r.halo_in[4 * k : 4 * k + 4], jnp.zeros((4, CW), f32)], axis=0)

    def conv_back(o):
        for k in range(PLANE):
            ext = r.d_conv[k, pl.ds(o, 24)]
            rows = ds(k * T + o, 16, 16)
            total = r.chan[0:1] * ext[0:16]
            for j in range(1, 4):
                total = total + jnp.where(wide(3 + j, rows), r.chan[j : j + 1] * ext[j : 16 + j], 0.0)
            r.d_gu[rows, 0:CW] = total.astype(bf16)

    loop(T, 16, conv_back)

    def d_input_part(z, _):
        q = ds(z * chunk, chunk, chunk)
        value = dot_nt(r.d_gu[:, lanes_a], r.w_ib[z, :, :, lanes_a].reshape(chunk, CW)).reshape(PLANE, T, chunk)
        r.part[:, :, q] = (r.part[:, :, q].astype(f32) + value).astype(bf16)
        return 0

    lax.fori_loop(0, RING, d_input_part, 0)
    rs_three = Scatter(r.part, r.got_three)
    rs_three.start()

    def grad_input(z, _):
        q = ds(z * chunk, chunk, chunk)
        value = dot_tn(r.n_one[:, :, q].reshape(M, chunk), r.d_gu[:, lanes_a])
        r.w_ib[z, :, :, lanes_a] = value.astype(bf16).reshape(2, chunk // 2, CW)
        return 0

    lax.fori_loop(0, RING, grad_input, 0)
    g_i = LastGrad(r.w_ib, r.h_ib, r.st_i, r.z_i, RD, 0, CW, r.t_i, r.grad_input_weight)
    g_i.core_send()
    g_j.z_forward()
    g_k.z_send()
    rs_three.mid()
    g_i.plane_send()
    g_k.z_forward()
    g_u.plane_send()
    g_v.plane_send()
    rs_three.end()
    g_i.z_send()
    g_b.plane_send()
    g_d.plane_send()
    g_j.plane_send()

    def norm_one_back(o, d_n, _):
        s = pl.ds(o, 32)
        v = r.x_all[p, s].astype(f32)
        rs = inverse_rms(v)
        z = v * rs
        dz = d_n * r.gains[0:1]
        r.d_x[s] = r.d_one[s] + rs * (dz - z * jnp.mean(dz * z, axis=-1, keepdims=True))

    rs_three.each(32, norm_one_back)
    deliver(r.d_x, r.d_tokens)
    settle(sent_b)
    g_i.z_forward()
    g_k.plane_send()
    g_g.end()
    in_order(r.l_gu, 0, CF, r.t_g, r.grad_mlp_gate)
    g_u.end()
    g_v.end()
    in_order(r.l_gu, CF, CF, r.t_u, r.grad_mlp_up)
    g_b.end()
    in_order(r.l_ib, CW, CW, r.t_b, r.grad_branch_weight)
    g_o.end()
    small_grad.two()
    g_d.end()
    g_j.end()
    in_order(r.l_di, 0, CW, r.t_d, r.grad_decay_weight)
    g_k.end()
    in_order(r.l_di, CW, CW, r.t_j, r.grad_inject_weight)
    g_i.end()
    assert not sent
    for result in results:
        local_wait(*result)


WEIGHTS = (
    "branch_weight",
    "input_weight",
    "decay_weight",
    "inject_weight",
    "output_weight",
    "mlp_gate",
    "mlp_up",
    "mlp_down",
)


def run_layer(NL, tokens, cotangent, small, weights):
    T, D = tokens.shape
    SEGS = small["doc_lengths"].shape[1]
    W, F = weights["branch_weight"].shape[1], weights["mlp_gate"].shape[1]
    CW, CF = W // PLANE, F // PLANE
    RD, RW, RF = D // SHARES, W // SHARES, F // SHARES
    GL, M, places = PLANE * RD, PLANE * T, RING * NL * 2
    hbm = pl.BlockSpec(memory_space=pl.ANY)
    ins = ["tokens", "cotangent", *small, *WEIGHTS]
    outs = dict(
        activations=((T, D), bf16),
        d_tokens=((T, D), f32),
        grad_input_weight=((RD, W), f32),
        grad_branch_weight=((RD, W), f32),
        grad_decay_weight=((RW, W), f32),
        grad_inject_weight=((RW, W), f32),
        grad_output_weight=((RW, D), f32),
        grad_mlp_gate=((RD, F), f32),
        grad_mlp_up=((RD, F), f32),
        grad_mlp_down=((RF, D), f32),
        small_out=((8, 128), f32),
    )
    columns = (("i", RD, CW), ("b", RD, CW), ("d", RW, CW), ("j", RW, CW), ("g", RD, CF), ("u", RD, CF))
    scratch = dict(
        w_ib=((RING, 2, PLANE * RD, 2 * CW), bf16),
        w_di=((RING, 2, PLANE * RW, 2 * CW), bf16),
        w_gu=((RING, 2, PLANE * RD, 2 * CF), bf16),
        w_o=((RING, 2, RW, D), bf16),
        w_dn=((RING, 2, RF, D), bf16),
        **{"raw_" + n: ((R, PLANE * C), bf16) for n, R, C in columns},
        **{"sort_" + n: ((PLANE, R, C), bf16) for n, R, C in columns},
        h_ib=((RING, PLANE * RD, 2 * CW), bf16),
        h_di=((RING, PLANE * RW, 2 * CW), bf16),
        h_gu=((RING, PLANE * RD, 2 * CF), bf16),
        h_o=((RING, RW, D), bf16),
        h_dn=((RING, RF, D), bf16),
        z_ib=((4, PLANE * RD, 2 * CW), bf16),
        z_di=((4, PLANE * RW, 2 * CW), bf16),
        z_gu=((4, PLANE * RD, 2 * CF), bf16),
        z_o=((4, RW, D), bf16),
        z_dn=((4, RF, D), bf16),
        l_ib=((PLANE, RD, 2 * CW), bf16),
        l_di=((PLANE, RW, 2 * CW), bf16),
        l_gu=((PLANE, RD, 2 * CF), bf16),
        n_one=((PLANE, T, D), bf16),
        n_two=((PLANE, T, D), bf16),
        cot_all=((PLANE, T, D), bf16),
        d_out=((PLANE, T, D), bf16),
        conv=((PLANE, M, CW), bf16),
        part=((PLANE, T, D), bf16),
        part_act=((PLANE, T, D), bf16),
        part_conv=((PLANE, M, CW), bf16),
        got_one=((6, T // 2, D), bf16),
        got_two=((6, T // 2, D), bf16),
        got_three=((6, T // 2, D), bf16),
        got_act=((6, T // 2, D), bf16),
        got_conv=((6, M // 2, CW), bf16),
        mixed=((M, CW), bf16),
        hidden=((M, CF), bf16),
        d_pair=((M, 2 * CF), bf16),
        d_gu=((M, 2 * CW), bf16),
        d_pre=((M, 2 * CW), bf16),
        pair=((M, 2 * CF), f32),
        u=((PLANE, T + 8, CW), f32),
        state=((PLANE, T + 8, CW), f32),
        d_conv=((PLANE, T + 8, CW), f32),
        **{name: ((M, CW), f32) for name in ("gated", "slope", "rgate", "igate", "decay", "work", "cum")},
        x_one=((T, D), f32),
        d_one=((T, D), f32),
        carry_f=((RING * NL, 2 * PLANE, CW), f32),
        carry_b=((RING * NL, 2 * PLANE, CW), f32),
        **{name: ((2 * PLANE, CW), f32) for name in ("own_f", "sib_f", "own_b", "sib_b")},
        halo_out=((16, CW), f32),
        halo_in=((16, CW), f32),
        into=((8, CW), f32),
        x_all=((PLANE, T, D), bf16),
        x_halo=((PLANE, 16, D), bf16),
        n_halo=((PLANE, 16, D), bf16),
        g_dn=((RING, 2, RF, D), bf16),
        masks=((7, M, 128), f32),
        pack=((16, 128), bf16),
        gain_a=((1, RD), bf16),
        gain_b=((1, RD), bf16),
        taps=((4, RW), bf16),
        bias_a=((1, RW), bf16),
        bias_b=((1, RW), bf16),
        bias_c=((1, RW), bf16),
        lens=((1, SEGS), jnp.int32),
        rates=((W // 128, 128), jnp.int32),
        pr=((2 * RING, 16, 128), bf16),
        line=((16, 128), bf16),
        pp=((PLANE, 16, 128), bf16),
        act=((T, D), bf16),
        d_x=((T, D), f32),
        t_i=((RD, W), f32),
        t_b=((RD, W), f32),
        st_i=((PLANE, RING, RD, CW), bf16),
        z_i=((4, PLANE, RD, CW), bf16),
        t_d=((RW, W), f32),
        t_j=((RW, W), f32),
        t_g=((RD, F), f32),
        t_u=((RD, F), f32),
        t_o=((RW, D), f32),
        t_dn=((RF, D), f32),
        small_sum=((8, 128), f32),
        gains=((8, D), f32),
        chan=((8, CW), f32),
        gchan=((8, CW), f32),
        gs=((2 * RING, 8, 128), f32),
        gg=((2 * RING, 8, 128), f32),
    )
    dims = SimpleNamespace(
        T=T, D=D, W=W, F=F, CW=CW, CF=CF, RD=RD, RW=RW, RF=RF, NL=NL, SEGS=SEGS, receives=RECEIVES + 2 * RING * NL, names=[*ins, *outs, *scratch, "ss", "rs"]
    )
    flops = 3 * 2 * M * (D * 2 * CW + W * 2 * CW + CW * D + 3 * D * CF)
    results = pl.pallas_call(
        partial(layer, dims),
        out_shape=[jax.ShapeDtypeStruct(shape, kind) for shape, kind in outs.values()],
        in_specs=[hbm] * len(ins),
        out_specs=[hbm] * len(outs),
        scratch_shapes=[pltpu.VMEM(shape, kind) for shape, kind in scratch.values()]
        + [pltpu.SemaphoreType.DMA((SENDS,)), pltpu.SemaphoreType.DMA((dims.receives,))],
        compiler_params=pltpu.CompilerParams(
            collective_id=0, has_side_effects=True, vmem_limit_bytes=62 * 2**20
        ),
        cost_estimate=pl.CostEstimate(flops=flops, bytes_accessed=8 * 2**20, transcendentals=M * CW * 16),
        name="griffin_layer",
    )(tokens, cotangent, *small.values(), *[weights[name] for name in WEIGHTS])
    return finish({**small, **dict(zip(outs, results, strict=True))}, weights)


def finish(got, weights):
    hbm = pl.BlockSpec(memory_space=pl.ANY)
    behind = {"first_gain": ("input_weight", "branch_weight"), "second_gain": ("mlp_gate", "mlp_up")}
    RD, RW = got["grad_input_weight"].shape[0], got["grad_decay_weight"].shape[0]
    channels = {"conv_taps": (0, 4), "conv_bias": (4, 5), "decay_bias": (5, 6), "inject_bias": (6, 7)}
    shared = [name for names in behind.values() for name in names]
    rest = ["grad_" + name for name in WEIGHTS if name not in shared]
    plain = [*["grad_" + name for name in shared], *rest, "d_tokens", "activations"]
    source = {**got, **{name: weights[name] for name in shared}}
    names = ["small_out", *behind, *shared, *plain]
    shapes = {name: got[name] for name in plain}
    for name in behind:
        shapes["grad_" + name] = jax.ShapeDtypeStruct((1, RD), f32)
    for name, (low, high) in channels.items():
        shapes["grad_" + name] = jax.ShapeDtypeStruct((high - low, RW), f32)
    scratch = {name: (source[name].shape, source[name].dtype) for name in names}
    scratch.update({name: (like.shape, f32) for name, like in shapes.items() if name not in plain})

    def body(*refs):
        ins = dict(zip(names, refs[: len(names)], strict=True))
        outs = dict(zip(shapes, refs[len(names) : len(names) + len(shapes)], strict=True))
        held, sems = dict(zip(scratch, refs[len(names) + len(shapes) : -1], strict=True)), refs[-1]
        copies = []

        def copy(src, dst):
            copies.append(pltpu.make_async_copy(src, dst, sems.at[len(copies)]))
            copies[-1].start()
            return copies[-1]

        loads = {name: copy(ins[name], held[name]) for name in names}
        stores = []

        def store(name):
            stores.append(copy(held[name], outs[name]))

        loads["small_out"].wait()
        for name, (low, high) in channels.items():
            held["grad_" + name][...] = held["small_out"][low:high, 0:RW]
            store("grad_" + name)
        for name in plain:
            loads[name].wait()
            store(name)
        for gain, pair in behind.items():
            sums = jnp.zeros((RD, 128), f32)
            for name in pair:
                loads[name].wait()
                product = held["grad_" + name][...] * held[name][...].astype(f32)
                sums = sums + sum(product[:, k * 128 : (k + 1) * 128] for k in range(product.shape[1] // 128))
            total = lax.dot_general(
                jnp.ones((8, 128), f32),
                sums,
                (((1,), (1,)), ((), ())),
                precision=lax.Precision.HIGHEST,
                preferred_element_type=f32,
            )
            loads[gain].wait()
            held["grad_" + gain][...] = total[0:1] / held[gain][...].astype(f32)
            store("grad_" + gain)
        for each in stores:
            each.wait()

    results = pl.pallas_call(
        body,
        out_shape=[jax.ShapeDtypeStruct(like.shape, like.dtype) for like in shapes.values()],
        in_specs=[hbm] * len(names),
        out_specs=[hbm] * len(shapes),
        scratch_shapes=[
            *[pltpu.VMEM(shape, kind) for shape, kind in scratch.values()],
            pltpu.SemaphoreType.DMA((len(names) + len(shapes),)),
        ],
        compiler_params=pltpu.CompilerParams(vmem_limit_bytes=62 * 2**20),
        name="finish",
    )(*[source[name] for name in names])
    return {**got, **dict(zip(shapes, results, strict=True))}


def local(
    sizes,
    tokens,
    cotangent,
    doc_lengths,
    decay_exponent,
    branch_weight,
    input_weight,
    decay_weight,
    inject_weight,
    output_weight,
    mlp_gate,
    mlp_up,
    mlp_down,
    first_gain,
    second_gain,
    conv_taps,
    conv_bias,
    decay_bias,
    inject_bias,
):
    devices = math.prod(sizes.values())
    at = {name: lax.axis_index(name) for name in AXES}
    mine = at["yl"] * 2 + at["xl"]
    ring = at["zh"] * 2 + at["c"]
    share = ring * PLANE + mine
    groups = devices // SHARES

    def pooled(value, axis=0):
        if groups == 1:
            return value
        whole = lax.all_gather(value, AXES, axis=axis, tiled=True)
        size = whole.shape[axis] // SHARES
        return lax.dynamic_slice_in_dim(whole, share * size, size, axis)

    small = dict(
        first_gain=pooled(first_gain[None], 1),
        second_gain=pooled(second_gain[None], 1),
        conv_taps=pooled(conv_taps.T, 1),
        conv_bias=pooled(conv_bias[None], 1),
        decay_bias=pooled(decay_bias[None], 1),
        inject_bias=pooled(inject_bias[None], 1),
        doc_lengths=doc_lengths,
        decay_exponent=decay_exponent.reshape(-1, 128),
    )
    weights = dict(
        zip(
            WEIGHTS,
            (branch_weight, input_weight, decay_weight, inject_weight, output_weight, mlp_gate, mlp_up, mlp_down),
            strict=True,
        )
    )
    weights = {name: pooled(value) for name, value in weights.items()}
    got = run_layer(sizes["zl"], tokens[0], cotangent[0], small, weights)

    def returned(value, axis=0):
        if groups == 1:
            return value
        shape = list(value.shape)
        size = shape[axis]
        shape[axis] = size * SHARES
        whole = lax.dynamic_update_slice_in_dim(jnp.zeros(shape, bf16), value.astype(bf16), share * size, axis)
        return lax.psum_scatter(whole, AXES, scatter_dimension=axis, tiled=True).astype(f32)

    grads = [returned(got["grad_" + name]) for name in WEIGHTS]
    first, second, taps, *biases = (
        returned(got["grad_" + name], 1)
        for name in ("first_gain", "second_gain", "conv_taps", "conv_bias", "decay_bias", "inject_bias")
    )
    return (
        got["activations"][None],
        got["d_tokens"][None],
        *grads,
        first[0],
        second[0],
        taps.T,
        *[bias[0] for bias in biases],
    )


def solution(mesh):
    seq, dp = mesh.shape["seq"], mesh.shape["dp"]
    across = 1 << ((dp.bit_length() - 1) // 2)
    sizes = dict(zip(AXES, (RING, seq // (2 * RING), 2, dp // across // 2, 2, across // 2, 2), strict=True))
    split = Mesh(mesh.devices.reshape(tuple(sizes.values())), AXES)
    along_seq, along_dp = AXES[:3], AXES[3:]
    rows = P(along_dp, along_seq, None)
    in_specs = (rows, rows, P(along_dp, None), P(), *[P(AXES, None)] * 8, P(AXES), P(AXES), P(AXES, None), *[P(AXES)] * 3)
    out_specs = (rows, rows, *[P(AXES, None)] * 8, P(AXES), P(AXES), P(AXES, None), *[P(AXES)] * 3)
    return jax.shard_map(partial(local, sizes), mesh=split, in_specs=in_specs, out_specs=out_specs, check_vma=False)
```

```python
import itertools
import math
from functools import cached_property, partial
from types import SimpleNamespace

import jax
import jax.numpy as jnp
from jax import lax
from jax.experimental import pallas as pl
from jax.experimental.pallas import tpu as pltpu
from jax.sharding import Mesh, PartitionSpec as P

f32, bf16 = jnp.float32, jnp.bfloat16
MESH = pl.DeviceIdType.MESH
AXES = ("zh", "zl", "c", "yh", "yl", "xh", "xl")
RING = 4
PLANE = 4
SHARES = RING * 2 * PLANE
SENDS = 53
RECEIVES = 180

eps_norm = 1e-06
floor_gap = 1e-05
rate_scale = 8.0
gelu_root = math.sqrt(2.0 / math.pi)
gelu_cube = 0.044715


def dot(left, right):
    return jnp.dot(left, right, preferred_element_type=f32)


def dot_nt(left, right):
    return lax.dot_general(left, right, (((1,), (1,)), ((), ())), preferred_element_type=f32)


def dot_tn(left, right):
    return lax.dot_general(left, right, (((0,), (0,)), ((), ())), preferred_element_type=f32)


def gelu_parts(v):
    t = jnp.tanh(gelu_root * (v + gelu_cube * v * v * v))
    half = 0.5 * (1.0 + t)
    slope = half + 0.5 * v * (1.0 - t * t) * gelu_root * (1.0 + 3.0 * gelu_cube * v * v)
    return v * half, slope


def minus_expm1(y, root):
    poly = 1.0 + y * (1.0 / 7.0)
    for k in (6, 5, 4, 3, 2):
        poly = 1.0 + y * poly * (1.0 / k)
    return jnp.where(y > -0.35, -y * poly, 1.0 - root * root)


def inverse_rms(v):
    return lax.rsqrt(jnp.mean(v * v, axis=-1, keepdims=True) + eps_norm)


def unsorted(parts):
    size = parts[0].shape[1] // (2 * RING)
    return jnp.concatenate([part[:, g * size : (g + 1) * size] for g in range(2 * RING) for part in parts], axis=1)


def loop(total, step, body):
    def run(j, _):
        body(pl.multiple_of(j * step, step))
        return 0

    lax.fori_loop(0, total // step, run, 0)


def layer(dims, *refs):
    T, D, W, F, CW, CF = dims.T, dims.D, dims.W, dims.F, dims.CW, dims.CF
    RD, RW, RF, NL = dims.RD, dims.RW, dims.RF, dims.NL
    M = PLANE * T
    r = SimpleNamespace(**dict(zip(dims.names, refs, strict=True)))

    zh, zl, c = lax.axis_index("zh"), lax.axis_index("zl"), lax.axis_index("c")
    yl, xl = lax.axis_index("yl"), lax.axis_index("xl")
    p = yl * 2 + xl
    px, py, pd = yl * 2 + (1 - xl), (1 - yl) * 2 + xl, (1 - yl) * 2 + (1 - xl)
    to_x, to_y, to_d = {"xl": 1 - xl}, {"yl": 1 - yl}, {"yl": 1 - yl, "xl": 1 - xl}
    plane_peers = ((px, to_x), (py, to_y), (pd, to_d))
    to_core = {"c": 1 - c}
    flat_z = zh * NL + zl
    places = RING * NL * 2
    pos = flat_z * 2 + c

    def place(at):
        return {"zh": at // (2 * NL), "zl": (at // 2) % NL, "c": at % 2}

    count = itertools.count()

    def new(n=1):
        first = next(count)
        for _ in range(n - 1):
            next(count)
        assert first + n <= dims.receives
        return first

    spare = list(range(SENDS))
    sent = []

    def push(src, dst, dev, rsem, pred=None, instead=None):
        i = spare.pop(0) if instead is None else instead[2]

        def make():
            return pltpu.make_async_remote_copy(
                src, dst, r.ss.at[i], r.rs.at[rsem], device_id=dev, device_id_type=MESH
            )

        if pred is None:
            make().start()
        else:
            pl.when(pred)(lambda: make().start())
        entry = (make, pred, i, instead is None)
        sent.append(entry)
        return entry

    def settle(*entries):
        for entry in entries:
            make, pred, i, owner = entry
            if pred is None:
                make().wait_send()
            else:
                pl.when(pred)(lambda make=make: make().wait_send())
            sent.remove(entry)
            if owner:
                spare.append(i)

    def arrived(dst, rsem, pred=None):
        def wait():
            pltpu.make_async_remote_copy(
                dst, dst, r.ss.at[0], r.rs.at[rsem], device_id=to_core, device_id_type=MESH
            ).wait_recv()

        if pred is None:
            wait()
        else:
            pl.when(pred)(wait)

    def keep_local(src, dst, rsem):
        pltpu.make_async_copy(src, dst, r.rs.at[rsem]).start()

    idle = []

    def local_wait(src, dst, rsem):
        pltpu.make_async_copy(src, dst, r.rs.at[rsem]).wait()
        idle.append(rsem)

    results = []

    def deliver(src, dst):
        sem = idle.pop() if idle else new()
        keep_local(src, dst, sem)
        results.append((src, dst, sem))

    def ds(start, size, unit):
        return pl.ds(pl.multiple_of(start, unit), size)

    class Gather:
        def __init__(self, buf):
            self.buf, half = buf, buf.shape[1] // 2
            self.h0, self.h1 = pl.ds(0, half), pl.ds(half, half)
            self.rx0, self.rx1, self.ry0, self.ry1, self.rd = (new() for _ in range(5))
            self.out = []

        def start(self):
            b = self.buf
            own0, own1 = b.at[p, self.h0], b.at[p, self.h1]
            self.out.append(push(own0, own0, to_x, self.rx0))
            self.out.append(push(own1, own1, to_y, self.ry1))
            self.out.append(push(own1, own1, to_x, self.rx1))
            self.out.append(push(own0, own0, to_y, self.ry0))

        def mid(self):
            b = self.buf
            got0, got1 = b.at[px, self.h0], b.at[py, self.h1]
            arrived(got0, self.rx0)
            self.out.append(push(got0, got0, to_y, self.rd))
            arrived(got1, self.ry1)
            self.out.append(push(got1, got1, to_x, self.rd))

        def wait_x(self):
            arrived(self.buf.at[px, self.h1], self.rx1)

        def wait_y(self):
            arrived(self.buf.at[py, self.h0], self.ry0)

        def wait_d(self):
            arrived(self.buf.at[pd], self.rd)

        def end(self):
            self.wait_x()
            self.wait_y()
            self.wait_d()
            settle(*self.out)

    class Scatter:
        def __init__(self, buf, recv):
            self.buf, self.recv = buf, recv
            self.half = buf.shape[1] // 2
            self.h0, self.h1 = pl.ds(0, self.half), pl.ds(self.half, self.half)
            self.sems = [new(), new(), *[new()] * 4]
            self.out = []

        def start(self):
            self.start_far()
            self.start_near()

        def start_far(self):
            b, v, s = self.buf, self.recv, self.sems
            self.out.append(push(b.at[pd, self.h0], v.at[0], to_x, s[0]))
            self.out.append(push(b.at[pd, self.h1], v.at[1], to_y, s[1]))

        def start_near(self):
            b, v, s = self.buf, self.recv, self.sems
            self.out.append(push(b.at[px, self.h0], v.at[2], to_x, s[2]))
            self.out.append(push(b.at[py, self.h1], v.at[3], to_y, s[3]))

        def mid(self):
            b, v, s = self.buf, self.recv, self.sems
            arrived(v.at[0], s[0])
            step = 16

            def add0(o):
                b[py, pl.ds(o, step)] = (b[py, pl.ds(o, step)].astype(f32) + v[0, pl.ds(o, step)].astype(f32)).astype(bf16)

            loop(self.half, step, add0)
            self.out.append(push(b.at[py, self.h0], v.at[4], to_y, s[4]))
            arrived(v.at[1], s[1])

            def add1(o):
                q = pl.ds(pl.multiple_of(self.half + o, step), step)
                b[px, q] = (b[px, q].astype(f32) + v[1, pl.ds(o, step)].astype(f32)).astype(bf16)

            loop(self.half, step, add1)
            self.out.append(push(b.at[px, self.h1], v.at[5], to_x, s[5]))

        def end(self):
            arrived(self.recv.at[pl.ds(2, 4)], self.sems[2])
            settle(*self.out)

        def total(self, half, o, step):
            b, v = self.buf, self.recv
            own = b[p, pl.ds(pl.multiple_of(half * self.half + o, step), step)].astype(f32)
            q = pl.ds(o, step)
            return own + v[2 + half, q].astype(f32) + v[4 + half, q].astype(f32)

        def each(self, step, body, init=None):
            for half in (0, 1):

                def run(j, carry, half=half):
                    o = pl.multiple_of(j * step, step)
                    return body(pl.multiple_of(half * self.half + o, step), self.total(half, o, step), carry)

                init = lax.fori_loop(0, self.half // step, run, init)
            return init

    def z_send(src, block, rz, away=(2, 1)):
        out = []
        if 2 in away:
            out.append(push(src, block(zh), {"zh": zh + 2}, rz + zh, zh + 2 < RING))
            out.append(push(src, block(zh), {"zh": zh - 2}, rz + zh, zh - 2 >= 0, out[-1]))
        if 1 in away:
            out.append(push(src, block(zh), {"zh": zh + 1}, rz + zh, zh + 1 < RING))
            out.append(push(src, block(zh), {"zh": zh - 1}, rz + zh, zh - 1 >= 0))
        return out

    def z_forward(block, rz):
        last = RING - 1
        arrived(block(0), rz, zh == last - 1)
        one = push(block(0), block(0), {"zh": zh + 1}, rz, zh == last - 1)
        arrived(block(last), rz + last, zh == 1)
        two = push(block(last), block(last), {"zh": zh - 1}, rz + last, zh == 1, one)
        return [one, two]

    def z_wait(block, rz, use):
        last = RING - 1

        def take(k, pred, waited=None, instead=None):
            arrived(block(k), rz + k, pred if waited is None else pred & ~waited)
            return use(block(k), pred, instead)

        out = [take(zh - 1, zh >= 1), take(zh + 1, zh < last)]
        out.append(take(zh - 2, zh >= 2, zh == last - 1))
        out.append(take(zh + 2, zh <= 1, zh == 1, out[-1]))
        out.append(take(0, zh == last))
        out.append(take(last, zh == 0, None, out[-1]))
        return out

    class ZSum:
        def __init__(self, block, slot, add, direct):
            self.block, self.slot, self.add, self.direct = block, slot, add, direct
            self.valid = (direct | (zh >= 1), zh >= 2, direct | (zh <= 2), zh <= 1)
            self.sems = new(4)
            self.out = []

        def send(self):
            b, v, s = self.block, self.slot, self.sems
            last = RING - 1
            o = self.out
            if self.direct:
                o.append(push(b(last), v(2), {"zh": zh + last}, s + 2, zh == 0))
                o.append(push(b(0), v(0), {"zh": zh - last}, s + 0, zh == last, o[-1]))
                o.append(push(b(zh + 2), v(1), {"zh": zh + 2}, s + 1, zh <= 1))
                o.append(push(b(zh - 2), v(3), {"zh": zh - 2}, s + 3, zh >= 2, o[-1]))
            else:
                o.append(push(b(last), v(1), {"zh": zh + 1}, s + 1, zh == 0))
                o.append(push(b(0), v(3), {"zh": zh - 1}, s + 3, zh == last, o[-1]))
                o.append(push(b(zh + 2), v(1), {"zh": zh + 2}, s + 1, zh == 0))
                o.append(push(b(zh - 2), v(3), {"zh": zh - 2}, s + 3, zh == last, o[-1]))
            o.append(push(b(zh + 1), v(0), {"zh": zh + 1}, s + 0, zh < last))
            o.append(push(b(zh - 1), v(2), {"zh": zh - 1}, s + 2, zh > 0))

        def forward(self):
            b, v, s = self.block, self.slot, self.sems
            last = RING - 1

            def up():
                arrived(v(1), s + 1)
                self.add(last, 1)

            def down():
                arrived(v(3), s + 3)
                self.add(0, 3)

            pl.when(zh == 1)(up)
            self.out.append(push(b(last), v(1), {"zh": zh + 2}, s + 1, zh == 1))
            pl.when(zh == last - 1)(down)
            self.out.append(push(b(0), v(3), {"zh": zh - 2}, s + 3, zh == last - 1, self.out[-1]))

        def end(self):
            for k, valid in enumerate(self.valid):
                arrived(self.slot(k), self.sems + k, valid)
            settle(*self.out)

        def total(self, own, parts):
            for part, pred in zip(parts, self.valid, strict=True):
                own = own + jnp.where(pred, part.astype(f32), 0.0)
            return own

    class Column:
        def __init__(self, src, raw, sorted_, w, R, C, lane0):
            self.src, self.raw, self.sorted = src, raw, sorted_
            self.w, self.R, self.C, self.lanes = w, R, C, pl.ds(lane0, C)
            self.out = []

        rl = cached_property(lambda self: new())
        ra = cached_property(lambda self: new())
        rz = cached_property(lambda self: new(4))
        rc = cached_property(lambda self: new())

        def halves(self):
            out = []
            for k in (0, 1):
                part = Column(self.src, self.raw, self.sorted, self.w, self.R, self.C, 0)
                part.lanes = pl.ds(self.lanes.start + k * self.C // 2, self.C // 2)
                out.append(part)
            return out

        def spread_wait(self):
            arrived(self.block(zh), self.ra)
            settle(*self.out)
            self.out = []

        def load(self):
            keep_local(self.src, self.raw, self.rl)

        def prepare(self):
            local_wait(self.src, self.raw, self.rl)
            value, part = self.raw[...], self.C // (2 * RING)
            for k in range(PLANE):
                first = [(g * PLANE + k) * part for g in range(2 * RING)]
                self.sorted[k] = jnp.concatenate([value[:, at : at + part] for at in first], axis=1)

        def spread(self):
            dst = self.w.at[zh, c, ds(p * self.R, self.R, 16), self.lanes]
            for k, dev in plane_peers:
                self.out.append(push(self.sorted.at[k], dst, dev, self.ra))
            keep_local(self.sorted.at[p], dst, self.ra)

        def block(self, z):
            return self.w.at[z, c, :, self.lanes]

        def z_send(self, spread=True):
            if spread:
                arrived(self.block(zh), self.ra)
            self.out += z_send(self.block(zh), self.block, self.rz)
            self.out.append(self.core_push(self.block(zh)))

        def z_forward(self):
            self.out += z_forward(self.block, self.rz)

        def core_push(self, block, pred=None, instead=None):
            return push(block, block, to_core, self.rc, pred, instead)

        def z_wait(self):
            self.out += z_wait(self.block, self.rz, self.core_push)

        def end(self):
            arrived(self.w.at[:, 1 - c, :, self.lanes], self.rc)
            settle(*self.out)

    class Row(Column):
        def __init__(self, src, w):
            self.src, self.w, self.lanes = src, w, pl.ds(0, w.shape[3])
            self.out = []

        def z_send(self, away=(2, 1)):
            if 2 in away:
                keep_local(self.src, self.block(zh), self.ra)
            self.out += z_send(self.src, self.block, self.rz, away)

        def z_wait(self):
            pltpu.make_async_copy(self.src, self.block(zh), r.rs.at[self.ra]).wait()
            self.out.append(self.core_push(self.block(zh)))
            super().z_wait()

    class ColumnsGrad:
        def __init__(self, g, other, slots, land, R, lane0, lanes, direct=False):
            self.g, self.other, self.slots, self.land = g, other, slots, land
            self.R, self.lanes = R, pl.ds(lane0, lanes)
            self.rows = PLANE * R
            self.rc, self.rl = new(), new()
            self.zsum = ZSum(
                lambda z: g.at[z, c, :, self.lanes], lambda k: slots.at[k, :, self.lanes], self.add_slot, direct
            )

        def add_slot(self, z, k):
            g, q = self.g, self.lanes

            def add(o):
                s = pl.ds(o, 16)
                g[z, c, s, q] = (g[z, c, s, q].astype(f32) + self.slots[k, s, q].astype(f32)).astype(bf16)

            loop(self.rows, 16, add)

        def core_send(self):
            self.pushed = push(
                self.g.at[:, 1 - c, :, self.lanes], self.other.at[:, :, self.lanes], to_core, self.rc
            )

        def core_sum(self):
            g, q = self.g, self.lanes
            arrived(self.other.at[:, :, q], self.rc)
            settle(self.pushed)
            for z in range(RING):

                def add(o):
                    s = pl.ds(o, 16)
                    g[z, c, s, q] = (g[z, c, s, q].astype(f32) + self.other[z, s, q].astype(f32)).astype(bf16)

                loop(self.rows, 16, add)

        def z_send(self):
            self.core_sum()
            self.zsum.send()

        def z_forward(self):
            self.zsum.forward()

        def plane_send(self):
            g, q, R = self.g, self.lanes, self.R
            self.zsum.end()

            def add(o):
                s = pl.ds(o, 16)
                parts = [self.slots[k, s, q] for k in range(4)]
                g[zh, c, s, q] = self.zsum.total(g[zh, c, s, q].astype(f32), parts).astype(bf16)

            loop(PLANE * R, 16, add)
            dst = self.land.at[p, :, q]
            self.out = []
            for k, dev in plane_peers:
                self.out.append(push(g.at[zh, c, ds(k * R, R, 16), q], dst, dev, self.rl))
            keep_local(g.at[zh, c, ds(p * R, R, 16), q], dst, self.rl)

        def end(self):
            arrived(self.land.at[:, :, self.lanes], self.rl)
            settle(*self.out)

    def in_order(land, lane0, C, held, result):
        held[...] = unsorted([land[k, :, lane0 : lane0 + C].astype(f32) for k in range(PLANE)])
        deliver(held, result)

    class LastGrad(ColumnsGrad):
        def __init__(self, g, other, stage, slots, R, lane0, lanes, total, result):
            super().__init__(g, other, slots, None, R, lane0, lanes)
            self.stage, self.sum, self.result = stage, total, result
            self.zsum.block, self.zsum.slot = (lambda z: stage.at[:, z]), (lambda k: slots.at[k])

        def add_slot(self, z, k):
            for q in range(PLANE):
                self.stage[q, z] = (self.stage[q, z].astype(f32) + self.slots[k, q].astype(f32)).astype(bf16)

        def plane_send(self):
            R, dst = self.R, self.stage.at[p]
            self.core_sum()
            self.out = []
            for k, dev in plane_peers:
                self.out.append(push(self.g.at[:, c, ds(k * R, R, 16), self.lanes], dst, dev, self.rl))
            keep_local(self.g.at[:, c, ds(p * R, R, 16), self.lanes], dst, self.rl)

        def z_send(self):
            arrived(self.stage, self.rl)
            self.zsum.send()

        def end(self):
            self.zsum.end()
            settle(*self.out)
            values = [
                self.zsum.total(self.stage[q, zh].astype(f32), [self.slots[k, q] for k in range(4)]) for q in range(PLANE)
            ]
            self.sum[...] = unsorted(values)
            deliver(self.sum, self.result)

    class RowsGrad(ColumnsGrad):
        def __init__(self, g, other, slots, total, result):
            super().__init__(g, other, slots, None, 0, 0, g.shape[3])
            self.rows, self.sum, self.result = g.shape[2], total, result

        def end(self):
            self.zsum.end()

            def add(o):
                s = pl.ds(o, 16)
                self.sum[s] = self.zsum.total(self.g[zh, c, s].astype(f32), [self.slots[k, s] for k in range(4)])

            loop(self.rows, 16, add)
            deliver(self.sum, self.result)

    class Carry:
        def __init__(self, own, sib, buf, later):
            self.own, self.sib, self.buf, self.later = own, sib, buf, later
            self.rc, self.rz = new(), new(RING * NL)
            self.out = []

        def order(self):
            return range(RING * NL) if self.later else reversed(range(RING * NL))

        def send_core(self):
            self.out.append(push(self.own, self.sib, to_core, self.rc))

        def send(self):
            arrived(self.sib, self.rc)
            own, sib = self.own[...], self.sib[...]
            near = (c == 0) if self.later else (c == 1)
            head, tail = jnp.where(near, own, sib), jnp.where(near, sib, own)
            self.buf[flat_z, 0:PLANE] = tail[0:PLANE] * head[0:PLANE]
            self.buf[flat_z, PLANE : 2 * PLANE] = (
                tail[0:PLANE] * head[PLANE : 2 * PLANE] + tail[PLANE : 2 * PLANE]
            )
            part = self.buf.at[flat_z]
            for at in self.order():
                pred = (flat_z < at) if self.later else (flat_z > at)
                self.out.append(push(part, part, {"zh": at // NL, "zl": at % NL}, self.rz + flat_z, pred))

        def fold(self, into):
            into[...] = jnp.zeros_like(into)

            def take(part):
                into[0:PLANE] = part[0:PLANE] * into[0:PLANE] + part[PLANE : 2 * PLANE]

            for at in self.order():
                pred = (flat_z > at) if self.later else (flat_z < at)

                def chip(at=at):
                    arrived(self.buf.at[at], self.rz + at)
                    take(self.buf[at])

                pl.when(pred)(chip)
            pl.when((c == 1) if self.later else (c == 0))(lambda: take(self.sib[...]))
            settle(*self.out)

    GL = PLANE * RD
    ring = zh * 2 + c

    def ring_place(at):
        return {"zh": at // 2, "c": at % 2}

    class Small:
        def __init__(self):
            self.rr, self.rk = new(), new()
            self.out = []

        def pack(self):
            for load in small_loads:
                local_wait(*load)
            lengths = r.lens[...]
            rows = [r.gain_a[...], r.gain_b[...], r.taps[...], r.bias_a[...], r.bias_b[...], r.bias_c[...]]
            rows += [lax.shift_right_logical(lengths, 8), lengths & 255]
            rows = [row.astype(f32) for row in rows]
            rows = [jnp.concatenate([row, jnp.zeros((row.shape[0], 128 - row.shape[1]), f32)], axis=1) for row in rows]
            r.pack[...] = jnp.concatenate([*rows, jnp.zeros((5, 128), f32)], axis=0).astype(bf16)

        def one(self):
            for at in range(2 * RING):
                self.out.append(push(r.pack, r.pr.at[ring], ring_place(at), self.rr, ring != at))
            keep_local(r.pack, r.pr.at[ring], self.rr)

        def two(self):
            arrived(r.pr, self.rr)
            lines = []
            for at in range(2 * RING):
                tile = r.pr[at].astype(f32)
                lines.append(jnp.concatenate([tile[row : row + 1, 0:32] for row in (0, 1, 9, 10)], axis=1))
            r.line[...] = jnp.concatenate([*lines, jnp.zeros((16 - 2 * RING, 128), f32)], axis=0).astype(bf16)
            for _, dev in plane_peers:
                self.out.append(push(r.line, r.pp.at[p], dev, self.rk))
            keep_local(r.line, r.pp.at[p], self.rk)

        def three(self):
            arrived(r.pp, self.rk)
            parts = [r.pp[k].astype(f32) for k in range(PLANE)]
            for row in (0, 1):
                lanes = slice(row * 32, row * 32 + RD)
                wide = jnp.concatenate([part[:, lanes] for part in parts], axis=1)
                for at in range(2 * RING):
                    r.gains[row : row + 1, at * GL : (at + 1) * GL] = wide[at : at + 1]
            whole = jnp.concatenate([r.pr[at, :, 0:RW].astype(f32) for at in range(2 * RING)], axis=1)
            r.chan[...] = whole[2:10]
            rates = r.rates[...].astype(f32)
            rates = jnp.concatenate([rates[k : k + 1] for k in range(W // 128)], axis=1)
            mine = jnp.zeros((1, CW), f32)
            for k in range(PLANE):
                at = [(g * PLANE + k) * RW for g in range(2 * RING)]
                mine = jnp.where(p == k, jnp.concatenate([rates[:, o : o + RW] for o in at], axis=1), mine)
            r.chan[7:8] = jnp.exp2(-mine)

        def four(self):
            where = lax.broadcasted_iota(jnp.int32, (T, 128), 0).astype(f32) + (pos * T).astype(f32)
            for k in range(PLANE):
                part = r.pp[k].astype(f32)
                starts, ends = [], []
                total = jnp.zeros((1, 1), f32)
                for j in range(dims.SEGS):
                    starts.append(total)
                    total = total + part[0:1, 64 + j : 65 + j] * 256.0 + part[0:1, 96 + j : 97 + j]
                    ends.append(total)

                def seg(shift):
                    at = where + float(shift)
                    value = jnp.zeros((T, 128), f32)
                    for end in ends:
                        value = value + jnp.where(at >= end, 1.0, 0.0)
                    return jnp.where((at < 0.0) | (at >= float(T * places)), -1.0, value)

                here = seg(0)
                rows = pl.ds(k * T, T)
                first = jnp.zeros((T, 128), f32)
                for start in starts:
                    first = jnp.where(where == start, 1.0, first)
                r.masks[0, rows] = first
                for j in (1, 2, 3):
                    r.masks[j, rows] = jnp.where(seg(-j) == here, 1.0, 0.0)
                    r.masks[3 + j, rows] = jnp.where(seg(j) == here, 1.0, 0.0)
            settle(*self.out)

    class SmallGrad:
        def __init__(self):
            self.rg = new()
            self.out = []

        def one(self):
            for at in range(2 * RING):
                own = jnp.concatenate([r.gchan[:, at * RW : (at + 1) * RW], jnp.zeros((8, 128 - RW), f32)], axis=1)
                r.gs[at] = own
            for at in range(2 * RING):
                self.out.append(push(r.gs.at[at], r.gg.at[ring], ring_place(at), self.rg, ring != at))
            keep_local(r.gs.at[ring], r.gg.at[ring], self.rg)

        def two(self):
            arrived(r.gg, self.rg)
            value = r.gg[0]
            for at in range(1, 2 * RING):
                value = value + r.gg[at]
            r.small_sum[...] = value
            deliver(r.small_sum, r.small_out)
            settle(*self.out)

    barrier = pltpu.get_barrier_semaphore()
    for _, dev in plane_peers:
        pl.semaphore_signal(barrier, 1, device_id=dev, device_id_type=MESH)
    for at in range(places):

        @pl.when(pos != at)
        def _(at=at):
            pl.semaphore_signal(barrier, 1, device_id=place(at), device_id_type=MESH)

    first_loads = [
        (src, dst, new())
        for src, dst in (
            (r.tokens, r.x_all.at[p]),
            (r.cotangent, r.cot_all.at[p]),
        )
    ]
    small_loads = [
        (src, dst, new())
        for src, dst in (
            (r.first_gain, r.gain_a),
            (r.second_gain, r.gain_b),
            (r.conv_taps, r.taps),
            (r.conv_bias, r.bias_a),
            (r.decay_bias, r.bias_b),
            (r.inject_bias, r.bias_c),
            (r.doc_lengths, r.lens),
            (r.decay_exponent, r.rates),
        )
    ]
    for load in small_loads + first_loads:
        keep_local(*load)

    w_i = Column(r.input_weight, r.raw_i, r.sort_i, r.w_ib, RD, CW, 0)
    w_b = Column(r.branch_weight, r.raw_b, r.sort_b, r.w_ib, RD, CW, CW)
    w_d = Column(r.decay_weight, r.raw_d, r.sort_d, r.w_di, RW, CW, 0)
    w_j = Column(r.inject_weight, r.raw_j, r.sort_j, r.w_di, RW, CW, CW)
    w_g = Column(r.mlp_gate, r.raw_g, r.sort_g, r.w_gu, RD, CF, 0)
    w_u = Column(r.mlp_up, r.raw_u, r.sort_u, r.w_gu, RD, CF, CF)
    w_g1, w_g2 = w_g.halves()
    w_o, w_dn = Row(r.output_weight, r.w_o), Row(r.mlp_down, r.w_dn)
    ag_x, ag_conv, ag_two = Gather(r.x_all), Gather(r.conv), Gather(r.n_two)
    ag_cot, ag_out = Gather(r.cot_all), Gather(r.d_out)
    small, small_grad = Small(), SmallGrad()
    after, before = flat_z + c, flat_z - (1 - c)
    to_next = {"zh": after // NL, "zl": after % NL, "c": 1 - c}
    to_prev = {"zh": before // NL, "zl": before % NL, "c": 1 - c}
    step = 256
    chunk = PLANE * RD * 2

    for w in (w_i, w_d, w_j, w_b, w_g, w_u):
        w.load()
    small.pack()
    w_i.prepare()
    w_d.prepare()
    pl.semaphore_wait(barrier, len(plane_peers) + places - 1)
    small.one()
    local_wait(*first_loads[0])
    halo_x = new()
    sent_x = push(r.x_all.at[p, pl.ds(T - 16, 16)], r.x_halo.at[p], to_next, halo_x, pos < places - 1)
    w_o.z_send((2,))
    w_i.spread()
    w_d.spread()
    ag_x.start()
    w_j.prepare()
    w_i.z_send()
    small.two()
    w_b.prepare()

    @pl.when(pos == 0)
    def _():
        r.x_halo[p] = jnp.zeros((16, D), bf16)

    arrived(r.x_halo.at[p], halo_x, pos > 0)
    halo_p = new(PLANE)
    sent_p = [push(r.x_halo.at[p], r.x_halo.at[p], dev, halo_p + p) for _, dev in plane_peers]
    ag_x.mid()
    w_i.z_forward()
    w_o.z_send((1,))
    w_g.prepare()
    local_wait(*first_loads[1])
    small.three()

    def norm_block(k):
        def norm_one(o):
            s = pl.ds(o, 32)
            v = r.x_all[k, s].astype(f32)
            r.n_one[k, s] = (v * inverse_rms(v) * r.gains[0:1]).astype(bf16)

        loop(T, 32, norm_one)

    norm_block(p)
    w_d.z_send()
    ag_x.wait_x()
    norm_block(px)
    ag_x.wait_y()
    norm_block(py)
    w_j.spread()
    small.four()
    for k, _ in plane_peers:
        arrived(r.x_halo.at[k], halo_p + k)
    v = r.x_halo[...].reshape(PLANE * 16, D).astype(f32)
    r.n_halo[...] = (v * inverse_rms(v) * r.gains[0:1]).astype(bf16).reshape(PLANE, 16, D)
    ag_x.wait_d()
    norm_block(pd)
    settle(*ag_x.out, sent_x, *sent_p)
    w_b.spread()
    w_g.spread()
    w_o.z_forward()
    w_i.z_wait()
    w_u.prepare()
    w_j.z_send()
    w_i.end()

    def weight_ib(lanes):
        return r.w_ib[:, :, :, lanes].reshape(D, CW)

    lanes_a, lanes_b = pl.ds(0, CW), pl.ds(CW, CW)
    halo = dot(r.n_halo[...].reshape(PLANE * 16, D), weight_ib(lanes_a)).astype(bf16).astype(f32)
    body = dot(r.n_one[...].reshape(M, D), weight_ib(lanes_a)).astype(bf16).astype(f32)
    for k in range(PLANE):
        r.u[k, 0:8] = halo[k * 16 + 8 : (k + 1) * 16]
        r.u[k, 8 : 8 + T] = body[k * T : (k + 1) * T]

    def wide(j, rows):
        return jnp.concatenate([r.masks[j, rows]] * (CW // 128), axis=1) > 0.5

    def convolve(o):
        for k in range(PLANE):
            ext = r.u[k, pl.ds(o, 24)]
            rows = ds(k * T + o, 16, 16)
            total = r.chan[4:5] + r.chan[0:1] * ext[8:24]
            for j in range(1, 4):
                total = total + jnp.where(wide(j, rows), r.chan[j : j + 1] * ext[8 - j : 24 - j], 0.0)
            r.conv[p, rows] = total.astype(bf16)

    loop(T, 16, convolve)
    ag_conv.start()
    w_d.z_forward()
    ag_conv.mid()
    w_j.z_forward()
    w_b.z_send()
    w_d.z_wait()
    w_d.end()

    def pre(q, lanes):
        return dot(r.conv[q], r.w_di[:, :, ds(q * RW, RW, 16), lanes].reshape(CW, CW))

    r.pair[:, 0:CW] = pre(p, lanes_a)
    ag_conv.wait_x()
    r.pair[:, 0:CW] += pre(px, lanes_a)
    ag_conv.wait_y()
    r.pair[:, 0:CW] += pre(py, lanes_a)
    w_b.z_forward()
    ag_conv.wait_d()
    r.pair[:, 0:CW] += pre(pd, lanes_a)
    settle(*ag_conv.out)
    w_g.spread_wait()
    w_g1.z_send(False)
    w_j.z_wait()
    w_u.spread()
    ag_cot.start()
    w_o.z_wait()
    w_j.end()
    r.pair[:, CW : 2 * CW] = (pre(0, lanes_b) + pre(1, lanes_b)) + (pre(2, lanes_b) + pre(3, lanes_b))

    def decay_terms(s, rg):
        log_a = -rate_scale * rg * r.chan[7:8]
        root = jnp.exp(log_a)
        gap = minus_expm1(2.0 * log_a, root)
        first = wide(0, s)
        return root, gap, jnp.where(first, 1.0, jnp.sqrt(jnp.maximum(gap, floor_gap))), first

    def gates_two(o):
        s = pl.ds(o, 16)
        rg = jax.nn.sigmoid(r.pair[s, 0:CW] + r.chan[5:6])
        ig = jax.nn.sigmoid(r.pair[s, CW : 2 * CW] + r.chan[6:7])
        root, _, mult, first = decay_terms(s, rg)
        r.rgate[s], r.igate[s] = rg, ig
        r.decay[s] = jnp.where(first, 0.0, root)
        r.work[s] = mult * ig * r.conv[p, s].astype(f32)

    loop(M, 16, gates_two)
    row = lax.broadcasted_iota(jnp.int32, (8, CW), 0)

    def scan_forward(j, carry):
        out = []
        for k in range(PLANE):
            s = ds(k * T + j * 8, 8, 8)
            a, b = r.decay[s], r.work[s]
            for n in (1, 2, 4):
                a_b = jnp.where(row >= n, pltpu.roll(a, n, 0), 1.0)
                b_b = jnp.where(row >= n, pltpu.roll(b, n, 0), 0.0)
                a, b = a * a_b, a * b_b + b
            total, prod = b + a * carry[2 * k], a * carry[2 * k + 1]
            r.state[k, ds(8 + j * 8, 8, 8)] = total
            r.cum[s] = prod
            out += [total[7:8], prod[7:8]]
        return tuple(out)

    zero, one = jnp.zeros((1, CW), f32), jnp.ones((1, CW), f32)
    ends = lax.fori_loop(0, T // 8, scan_forward, (zero, one) * PLANE)
    carry_f = Carry(r.own_f, r.sib_f, r.carry_f, True)
    for k in range(PLANE):
        r.own_f[k : k + 1] = ends[2 * k + 1]
        r.own_f[PLANE + k : PLANE + k + 1] = ends[2 * k]
    carry_f.send_core()
    w_b.z_wait()
    carry_f.send()
    w_g1.z_forward()
    w_g2.z_send(False)
    w_b.end()
    r.work[...] = dot(r.n_one[...].reshape(M, D), weight_ib(lanes_b))

    def gates_one(o):
        s = pl.ds(o, 16)
        r.gated[s], r.slope[s] = gelu_parts(r.work[s])

    loop(M, 16, gates_one)
    ag_cot.mid()
    carry_f.fold(r.into)
    for k in range(PLANE):
        r.state[k, 0:8] = jnp.broadcast_to(r.into[k : k + 1], (8, CW))

    def mix(o):
        for k in range(PLANE):
            s, t = ds(k * T + o, 16, 16), ds(8 + o, 16, 8)
            state = r.state[k, t] + r.cum[s] * r.into[k : k + 1]
            r.state[k, t] = state
            r.mixed[s] = (state * r.gated[s]).astype(bf16)

    loop(T, 16, mix)

    w_o.end()

    def out_part(o):
        q = pl.ds(o, step)
        r.part[:, :, q] = dot(r.mixed[...], r.w_o[:, :, :, q].reshape(CW, step)).astype(bf16).reshape(PLANE, T, step)

    loop(D, step, out_part)
    rs_one = Scatter(r.part, r.got_one)
    rs_one.start()
    w_g1.z_wait()
    w_g2.z_forward()
    w_u.z_send()
    ag_cot.end()
    rs_one.mid()
    rs_one.end()

    def norm_two(o, summed, _):
        s = pl.ds(o, 32)
        v = r.x_all[p, s].astype(f32) + summed
        r.x_one[s] = v
        r.n_two[p, s] = (v * inverse_rms(v) * r.gains[1:2]).astype(bf16)

    rs_one.each(32, norm_two)
    ag_two.start()
    w_u.z_forward()
    ag_two.mid()
    w_dn.z_send()
    w_g2.z_wait()
    w_g1.end()
    w_u.z_wait()
    w_g2.end()
    ag_two.end()

    def mlp_in(o):
        q = pl.ds(o, step)
        r.pair[:, q] = dot(r.n_two[...].reshape(M, D), r.w_gu[:, :, :, q].reshape(D, step))

    loop(CF, step, mlp_in)
    w_dn.z_forward()
    w_u.end()
    loop(CF, step, lambda o: mlp_in(pl.multiple_of(CF + o, step)))

    def gates_mlp(o):
        s = pl.ds(o, 16)
        value, slope = gelu_parts(r.pair[s, 0:CF])
        up = r.pair[s, CF : 2 * CF]
        r.hidden[s] = (value * up).astype(bf16)
        r.pair[s, 0:CF] = slope * up
        r.pair[s, CF : 2 * CF] = value

    loop(M, 16, gates_mlp)

    half = CF // 2
    for k in (0, 1):
        for o in range(0, D, D // 2):
            value = dot_tn(r.hidden[:, k * half : (k + 1) * half], r.cot_all[:, :, o : o + D // 2].reshape(M, D // 2))
            r.g_dn[k * RING // 2 : (k + 1) * RING // 2, :, :, o : o + D // 2] = value.astype(bf16).reshape(
                RING // 2, 2, RF, D // 2
            )
    g_dn = RowsGrad(r.g_dn, r.h_dn, r.z_dn, r.t_dn, r.grad_mlp_down)
    g_dn.core_send()
    g_dn.z_send()
    w_dn.z_wait()
    w_dn.end()

    for k in range(CF // step):
        back = dot_nt(r.cot_all[...].reshape(M, D), r.w_dn[...].reshape(CF, D)[k * step : (k + 1) * step])
        r.d_pair[:, k * step : (k + 1) * step] = (back * r.pair[:, k * step : (k + 1) * step]).astype(bf16)
        r.d_pair[:, CF + k * step : CF + (k + 1) * step] = (
            back * r.pair[:, CF + k * step : CF + (k + 1) * step]
        ).astype(bf16)

    def d_two_part(z, _):
        q = ds(z * chunk, chunk, chunk)
        r.part[:, :, q] = (
            dot_nt(r.d_pair[...], r.w_gu[z].reshape(chunk, 2 * CF)).astype(bf16).reshape(PLANE, T, chunk)
        )
        return 0

    lax.fori_loop(0, RING, d_two_part, 0)
    rs_two = Scatter(r.part, r.got_two)
    rs_two.start()

    def grad_gate_up(lane0):
        lanes = pl.ds(lane0, CF)

        def run(z, _):
            q = ds(z * chunk, chunk, chunk)
            value = dot_tn(r.n_two[:, :, q].reshape(M, chunk), r.d_pair[:, lanes])
            r.w_gu[z, :, :, lanes] = value.astype(bf16).reshape(2, chunk // 2, CF)
            return 0

        lax.fori_loop(0, RING, run, 0)

    grad_gate_up(0)
    g_g = ColumnsGrad(r.w_gu, r.h_gu, r.z_gu, r.l_gu, RD, 0, CF)
    g_g.core_send()
    rs_two.mid()
    g_dn.z_forward()
    g_g.z_send()
    grad_gate_up(CF)
    g_u, g_v = (
        ColumnsGrad(r.w_gu, r.h_gu, r.z_gu, r.l_gu, RD, lane0, CF // 2) for lane0 in (CF, CF + CF // 2)
    )
    g_u.core_send()
    g_v.core_send()

    def act_part(o):
        q = pl.ds(o, step)
        r.part_act[:, :, q] = dot(r.hidden[...], r.w_dn[:, :, :, q].reshape(CF, step)).astype(bf16).reshape(PLANE, T, step)

    loop(D, step, act_part)
    r.gchan[...] = jnp.zeros_like(r.gchan)
    rs_two.end()

    def norm_two_back(o, d_two, _):
        s = pl.ds(o, 32)
        v = r.x_one[s]
        rs = inverse_rms(v)
        z = v * rs
        dz = d_two * r.gains[1:2]
        d_one = r.cot_all[p, s].astype(f32) + rs * (dz - z * jnp.mean(dz * z, axis=-1, keepdims=True))
        r.d_one[s] = d_one
        r.d_out[p, s] = d_one.astype(bf16)

    rs_two.each(32, norm_two_back)
    ag_out.start()
    ag_out.mid()
    g_g.z_forward()
    g_u.z_send()
    ag_out.end()
    rs_act = Scatter(r.part_act, r.got_act)
    rs_act.start()

    r.work[...] = dot_nt(r.d_out[...].reshape(M, D), r.w_o[...].reshape(CW, D))

    def split(o):
        for k in range(PLANE):
            s = ds(k * T + o, 16, 16)
            d_mixed = r.work[s]
            r.d_gu[s, CW : 2 * CW] = (d_mixed * r.state[k, ds(8 + o, 16, 8)] * r.slope[s]).astype(bf16)
            r.work[s] = d_mixed * r.gated[s]

    loop(T, 16, split)

    def scan_backward(i, carry):
        j = T // 8 - 1 - i
        out = []
        for k in range(PLANE):
            s = ds(k * T + j * 8, 8, 8)
            decay, b = r.decay[s], r.work[s]
            a = jnp.where(row < 7, pltpu.roll(decay, 7, 0), carry[3 * k + 2])
            for n in (1, 2, 4):
                a_b = jnp.where(row < 8 - n, pltpu.roll(a, 8 - n, 0), 1.0)
                b_b = jnp.where(row < 8 - n, pltpu.roll(b, 8 - n, 0), 0.0)
                a, b = a * a_b, a * b_b + b
            total, prod = b + a * carry[3 * k], a * carry[3 * k + 1]
            r.work[s], r.cum[s] = total, prod
            out += [total[0:1], prod[0:1], decay[0:1]]
        return tuple(out)

    heads = lax.fori_loop(0, T // 8, scan_backward, (zero, one, one) * PLANE)
    carry_b = Carry(r.own_b, r.sib_b, r.carry_b, False)
    for k in range(PLANE):
        r.own_b[k : k + 1] = r.own_f[k : k + 1]
        r.own_b[PLANE + k : PLANE + k + 1] = heads[3 * k] * heads[3 * k + 2]
    carry_b.send_core()

    def grad_out(o):
        q = pl.ds(o, D // 2)
        value = dot_tn(r.mixed[...], r.d_out[:, :, q].reshape(M, D // 2))
        r.w_o[:, :, :, q] = value.astype(bf16).reshape(RING, 2, RW, D // 2)

    loop(D, D // 2, grad_out)
    g_o = RowsGrad(r.w_o, r.h_o, r.z_o, r.t_o, r.grad_output_weight)
    g_o.core_send()
    carry_b.send()
    g_u.z_forward()
    g_v.z_send()
    rs_act.mid()

    def d_branch_part(z, _):
        q = ds(z * chunk, chunk, chunk)
        r.part[:, :, q] = (
            dot_nt(r.d_gu[:, lanes_b], r.w_ib[z, :, :, lanes_b].reshape(chunk, CW))
            .astype(bf16)
            .reshape(PLANE, T, chunk)
        )
        value = dot_tn(r.n_one[:, :, q].reshape(M, chunk), r.d_gu[:, lanes_b])
        r.w_ib[z, :, :, lanes_b] = value.astype(bf16).reshape(2, chunk // 2, CW)
        return 0

    lax.fori_loop(0, RING, d_branch_part, 0)
    g_b = ColumnsGrad(r.w_ib, r.h_ib, r.z_ib, r.l_ib, RD, CW, CW)
    g_b.core_send()
    g_g.plane_send()
    carry_b.fold(r.into)
    g_o.z_send()

    def back(o):
        sums = [jnp.zeros((1, CW), f32)] * 2
        for k in range(PLANE):
            s = ds(k * T + o, 16, 16)
            adjoint = r.work[s] + r.cum[s] * r.into[k : k + 1]
            previous = r.state[k, pl.ds(o, 24)][7:23]
            rg, ig, decay, conv = r.rgate[s], r.igate[s], r.decay[s], r.conv[p, s].astype(f32)
            _, gap, mult, first = decay_terms(s, rg)
            d_mult = jnp.where(first, 0.0, adjoint * ig * conv)
            d_log = adjoint * previous * decay - jnp.where(gap > floor_gap, (1.0 - gap) * d_mult / mult, 0.0)
            d_decay = (-rate_scale * r.chan[7:8] * d_log * rg * (1.0 - rg)).astype(bf16)
            d_inject = (adjoint * mult * conv * ig * (1.0 - ig)).astype(bf16)
            r.d_pre[s, 0:CW] = d_decay
            r.d_pre[s, CW : 2 * CW] = d_inject
            sums[0] = sums[0] + jnp.sum(d_decay.astype(f32), axis=0, keepdims=True)
            sums[1] = sums[1] + jnp.sum(d_inject.astype(f32), axis=0, keepdims=True)
            r.d_conv[k, pl.ds(o, 16)] = adjoint * mult * ig
        r.gchan[5:6] += sums[0]
        r.gchan[6:7] += sums[1]

    loop(T, 16, back)

    def conv_part(q):
        r.part_conv[q] = dot_nt(r.d_pre[...], r.w_di[:, :, ds(q * RW, RW, 16), :].reshape(CW, 2 * CW)).astype(bf16)

    rs_conv = Scatter(r.part_conv, r.got_conv)
    conv_part(pd)
    rs_act.end()
    rs_conv.start_far()
    conv_part(px)
    conv_part(py)
    rs_conv.start_near()
    conv_part(p)
    g_v.z_forward()

    def finish_act(o, summed, _):
        s = pl.ds(o, 16)
        r.act[s] = (r.x_one[s] + summed).astype(bf16)

    rs_act.each(16, finish_act)
    deliver(r.act, r.activations)
    g_b.z_send()
    g_dn.end()

    def grad_dec_inj(lanes):
        def run(q, _):
            value = dot_tn(r.conv[q], r.d_pre[:, lanes])
            r.w_di[:, :, ds(q * RW, RW, 16), lanes] = value.astype(bf16).reshape(RING, 2, RW, CW)
            return 0

        lax.fori_loop(0, RING, run, 0)

    grad_dec_inj(lanes_a)
    g_d, g_j, g_k = (
        ColumnsGrad(r.w_di, r.h_di, r.z_di, r.l_di, RW, lane0, lanes)
        for lane0, lanes in ((0, 128), (128, CW - 128), (CW, CW))
    )
    g_d.core_send()
    g_j.core_send()
    rs_conv.mid()
    grad_dec_inj(lanes_b)
    g_k.core_send()
    g_o.z_forward()
    g_d.z_send()
    rs_conv.end()

    for half in (0, 1):

        def add_conv(o, half=half):
            for k in (2 * half, 2 * half + 1):
                at = (k - 2 * half) * T + o
                r.d_conv[k, pl.ds(o, 16)] += rs_conv.total(half, pl.multiple_of(at, 16), 16)

        loop(T, 16, add_conv)
    halo_b = new()
    for k in range(PLANE):
        r.halo_out[4 * k : 4 * k + 4] = r.d_conv[k, 0:4]
    sent_b = push(r.halo_out, r.halo_in, to_prev, halo_b, pos > 0)
    g_b.z_forward()
    g_j.z_send()

    def taps_back(o):
        sums = [jnp.zeros((1, CW), f32)] * 5
        for k in range(PLANE):
            ext = r.u[k, pl.ds(o, 24)]
            rows = ds(k * T + o, 16, 16)
            dc = r.d_conv[k, pl.ds(o, 16)]
            sums[4] = sums[4] + jnp.sum(dc, axis=0, keepdims=True)
            sums[0] = sums[0] + jnp.sum(dc * ext[8:24], axis=0, keepdims=True)
            for j in range(1, 4):
                term = jnp.where(wide(j, rows), dc * ext[8 - j : 24 - j], 0.0)
                sums[j] = sums[j] + jnp.sum(term, axis=0, keepdims=True)
        for j in range(5):
            r.gchan[j : j + 1] += sums[j]

    loop(T, 16, taps_back)
    small_grad.one()

    @pl.when(pos == places - 1)
    def _():
        r.halo_in[...] = jnp.zeros((16, CW), f32)

    g_d.z_forward()
    g_u.plane_send()
    g_v.plane_send()
    arrived(r.halo_in, halo_b, pos < places - 1)
    for k in range(PLANE):
        r.d_conv[k, T : T + 8] = jnp.concatenate([r.halo_in[4 * k : 4 * k + 4], jnp.zeros((4, CW), f32)], axis=0)

    def conv_back(o):
        for k in range(PLANE):
            ext = r.d_conv[k, pl.ds(o, 24)]
            rows = ds(k * T + o, 16, 16)
            total = r.chan[0:1] * ext[0:16]
            for j in range(1, 4):
                total = total + jnp.where(wide(3 + j, rows), r.chan[j : j + 1] * ext[j : 16 + j], 0.0)
            r.d_gu[rows, 0:CW] = total.astype(bf16)

    loop(T, 16, conv_back)

    def d_input_part(z, _):
        q = ds(z * chunk, chunk, chunk)
        value = dot_nt(r.d_gu[:, lanes_a], r.w_ib[z, :, :, lanes_a].reshape(chunk, CW)).reshape(PLANE, T, chunk)
        r.part[:, :, q] = (r.part[:, :, q].astype(f32) + value).astype(bf16)
        return 0

    lax.fori_loop(0, RING, d_input_part, 0)
    rs_three = Scatter(r.part, r.got_three)
    rs_three.start()

    def grad_input(z, _):
        q = ds(z * chunk, chunk, chunk)
        value = dot_tn(r.n_one[:, :, q].reshape(M, chunk), r.d_gu[:, lanes_a])
        r.w_ib[z, :, :, lanes_a] = value.astype(bf16).reshape(2, chunk // 2, CW)
        return 0

    lax.fori_loop(0, RING, grad_input, 0)
    g_i = LastGrad(r.w_ib, r.h_ib, r.st_i, r.z_i, RD, 0, CW, r.t_i, r.grad_input_weight)
    g_i.core_send()
    g_j.z_forward()
    g_k.z_send()
    g_i.plane_send()
    rs_three.mid()
    g_k.z_forward()
    rs_three.end()
    g_i.z_send()
    g_b.plane_send()
    g_d.plane_send()
    g_j.plane_send()

    def norm_one_back(o, d_n, _):
        s = pl.ds(o, 32)
        v = r.x_all[p, s].astype(f32)
        rs = inverse_rms(v)
        z = v * rs
        dz = d_n * r.gains[0:1]
        r.d_x[s] = r.d_one[s] + rs * (dz - z * jnp.mean(dz * z, axis=-1, keepdims=True))

    rs_three.each(32, norm_one_back)
    deliver(r.d_x, r.d_tokens)
    settle(sent_b)
    g_i.z_forward()
    g_k.plane_send()
    g_g.end()
    in_order(r.l_gu, 0, CF, r.t_g, r.grad_mlp_gate)
    g_u.end()
    g_v.end()
    in_order(r.l_gu, CF, CF, r.t_u, r.grad_mlp_up)
    g_b.end()
    in_order(r.l_ib, CW, CW, r.t_b, r.grad_branch_weight)
    g_o.end()
    small_grad.two()
    g_d.end()
    g_j.end()
    in_order(r.l_di, 0, CW, r.t_d, r.grad_decay_weight)
    g_k.end()
    in_order(r.l_di, CW, CW, r.t_j, r.grad_inject_weight)
    g_i.end()
    assert not sent
    for result in results:
        local_wait(*result)


WEIGHTS = (
    "branch_weight",
    "input_weight",
    "decay_weight",
    "inject_weight",
    "output_weight",
    "mlp_gate",
    "mlp_up",
    "mlp_down",
)


def run_layer(NL, tokens, cotangent, small, weights):
    T, D = tokens.shape
    SEGS = small["doc_lengths"].shape[1]
    W, F = weights["branch_weight"].shape[1], weights["mlp_gate"].shape[1]
    CW, CF = W // PLANE, F // PLANE
    RD, RW, RF = D // SHARES, W // SHARES, F // SHARES
    GL, M, places = PLANE * RD, PLANE * T, RING * NL * 2
    hbm = pl.BlockSpec(memory_space=pl.ANY)
    ins = ["tokens", "cotangent", *small, *WEIGHTS]
    outs = dict(
        activations=((T, D), bf16),
        d_tokens=((T, D), f32),
        grad_input_weight=((RD, W), f32),
        grad_branch_weight=((RD, W), f32),
        grad_decay_weight=((RW, W), f32),
        grad_inject_weight=((RW, W), f32),
        grad_output_weight=((RW, D), f32),
        grad_mlp_gate=((RD, F), f32),
        grad_mlp_up=((RD, F), f32),
        grad_mlp_down=((RF, D), f32),
        small_out=((8, 128), f32),
    )
    columns = (("i", RD, CW), ("b", RD, CW), ("d", RW, CW), ("j", RW, CW), ("g", RD, CF), ("u", RD, CF))
    scratch = dict(
        w_ib=((RING, 2, PLANE * RD, 2 * CW), bf16),
        w_di=((RING, 2, PLANE * RW, 2 * CW), bf16),
        w_gu=((RING, 2, PLANE * RD, 2 * CF), bf16),
        w_o=((RING, 2, RW, D), bf16),
        w_dn=((RING, 2, RF, D), bf16),
        **{"raw_" + n: ((R, PLANE * C), bf16) for n, R, C in columns},
        **{"sort_" + n: ((PLANE, R, C), bf16) for n, R, C in columns},
        h_ib=((RING, PLANE * RD, 2 * CW), bf16),
        h_di=((RING, PLANE * RW, 2 * CW), bf16),
        h_gu=((RING, PLANE * RD, 2 * CF), bf16),
        h_o=((RING, RW, D), bf16),
        h_dn=((RING, RF, D), bf16),
        z_ib=((4, PLANE * RD, 2 * CW), bf16),
        z_di=((4, PLANE * RW, 2 * CW), bf16),
        z_gu=((4, PLANE * RD, 2 * CF), bf16),
        z_o=((4, RW, D), bf16),
        z_dn=((4, RF, D), bf16),
        l_ib=((PLANE, RD, 2 * CW), bf16),
        l_di=((PLANE, RW, 2 * CW), bf16),
        l_gu=((PLANE, RD, 2 * CF), bf16),
        n_one=((PLANE, T, D), bf16),
        n_two=((PLANE, T, D), bf16),
        cot_all=((PLANE, T, D), bf16),
        d_out=((PLANE, T, D), bf16),
        conv=((PLANE, M, CW), bf16),
        part=((PLANE, T, D), bf16),
        part_act=((PLANE, T, D), bf16),
        part_conv=((PLANE, M, CW), bf16),
        got_one=((6, T // 2, D), bf16),
        got_two=((6, T // 2, D), bf16),
        got_three=((6, T // 2, D), bf16),
        got_act=((6, T // 2, D), bf16),
        got_conv=((6, M // 2, CW), bf16),
        mixed=((M, CW), bf16),
        hidden=((M, CF), bf16),
        d_pair=((M, 2 * CF), bf16),
        d_gu=((M, 2 * CW), bf16),
        d_pre=((M, 2 * CW), bf16),
        pair=((M, 2 * CF), f32),
        u=((PLANE, T + 8, CW), f32),
        state=((PLANE, T + 8, CW), f32),
        d_conv=((PLANE, T + 8, CW), f32),
        **{name: ((M, CW), f32) for name in ("gated", "slope", "rgate", "igate", "decay", "work", "cum")},
        x_one=((T, D), f32),
        d_one=((T, D), f32),
        carry_f=((RING * NL, 2 * PLANE, CW), f32),
        carry_b=((RING * NL, 2 * PLANE, CW), f32),
        **{name: ((2 * PLANE, CW), f32) for name in ("own_f", "sib_f", "own_b", "sib_b")},
        halo_out=((16, CW), f32),
        halo_in=((16, CW), f32),
        into=((8, CW), f32),
        x_all=((PLANE, T, D), bf16),
        x_halo=((PLANE, 16, D), bf16),
        n_halo=((PLANE, 16, D), bf16),
        g_dn=((RING, 2, RF, D), bf16),
        masks=((7, M, 128), f32),
        pack=((16, 128), bf16),
        gain_a=((1, RD), bf16),
        gain_b=((1, RD), bf16),
        taps=((4, RW), bf16),
        bias_a=((1, RW), bf16),
        bias_b=((1, RW), bf16),
        bias_c=((1, RW), bf16),
        lens=((1, SEGS), jnp.int32),
        rates=((W // 128, 128), jnp.int32),
        pr=((2 * RING, 16, 128), bf16),
        line=((16, 128), bf16),
        pp=((PLANE, 16, 128), bf16),
        act=((T, D), bf16),
        d_x=((T, D), f32),
        t_i=((RD, W), f32),
        t_b=((RD, W), f32),
        st_i=((PLANE, RING, RD, CW), bf16),
        z_i=((4, PLANE, RD, CW), bf16),
        t_d=((RW, W), f32),
        t_j=((RW, W), f32),
        t_g=((RD, F), f32),
        t_u=((RD, F), f32),
        t_o=((RW, D), f32),
        t_dn=((RF, D), f32),
        small_sum=((8, 128), f32),
        gains=((8, D), f32),
        chan=((8, CW), f32),
        gchan=((8, CW), f32),
        gs=((2 * RING, 8, 128), f32),
        gg=((2 * RING, 8, 128), f32),
    )
    dims = SimpleNamespace(
        T=T, D=D, W=W, F=F, CW=CW, CF=CF, RD=RD, RW=RW, RF=RF, NL=NL, SEGS=SEGS, receives=RECEIVES + 2 * RING * NL, names=[*ins, *outs, *scratch, "ss", "rs"]
    )
    flops = 3 * 2 * M * (D * 2 * CW + W * 2 * CW + CW * D + 3 * D * CF)
    results = pl.pallas_call(
        partial(layer, dims),
        out_shape=[jax.ShapeDtypeStruct(shape, kind) for shape, kind in outs.values()],
        in_specs=[hbm] * len(ins),
        out_specs=[hbm] * len(outs),
        scratch_shapes=[pltpu.VMEM(shape, kind) for shape, kind in scratch.values()]
        + [pltpu.SemaphoreType.DMA((SENDS,)), pltpu.SemaphoreType.DMA((dims.receives,))],
        compiler_params=pltpu.CompilerParams(
            collective_id=0, has_side_effects=True, vmem_limit_bytes=62 * 2**20
        ),
        cost_estimate=pl.CostEstimate(flops=flops, bytes_accessed=8 * 2**20, transcendentals=M * CW * 16),
        name="griffin_layer",
    )(tokens, cotangent, *small.values(), *[weights[name] for name in WEIGHTS])
    return finish({**small, **dict(zip(outs, results, strict=True))}, weights)


def finish(got, weights):
    hbm = pl.BlockSpec(memory_space=pl.ANY)
    behind = {"first_gain": ("input_weight", "branch_weight"), "second_gain": ("mlp_gate", "mlp_up")}
    RD, RW = got["grad_input_weight"].shape[0], got["grad_decay_weight"].shape[0]
    channels = {"conv_taps": (0, 4), "conv_bias": (4, 5), "decay_bias": (5, 6), "inject_bias": (6, 7)}
    shared = [name for names in behind.values() for name in names]
    rest = ["grad_" + name for name in WEIGHTS if name not in shared]
    plain = [*["grad_" + name for name in shared], *rest, "d_tokens", "activations"]
    source = {**got, **{name: weights[name] for name in shared}}
    names = ["small_out", *behind, *shared, *plain]
    shapes = {name: got[name] for name in plain}
    for name in behind:
        shapes["grad_" + name] = jax.ShapeDtypeStruct((1, RD), f32)
    for name, (low, high) in channels.items():
        shapes["grad_" + name] = jax.ShapeDtypeStruct((high - low, RW), f32)
    scratch = {name: (source[name].shape, source[name].dtype) for name in names}
    scratch.update({name: (like.shape, f32) for name, like in shapes.items() if name not in plain})

    def body(*refs):
        ins = dict(zip(names, refs[: len(names)], strict=True))
        outs = dict(zip(shapes, refs[len(names) : len(names) + len(shapes)], strict=True))
        held, sems = dict(zip(scratch, refs[len(names) + len(shapes) : -1], strict=True)), refs[-1]
        copies = []

        def copy(src, dst):
            copies.append(pltpu.make_async_copy(src, dst, sems.at[len(copies)]))
            copies[-1].start()
            return copies[-1]

        loads = {name: copy(ins[name], held[name]) for name in names}
        stores = []

        def store(name):
            stores.append(copy(held[name], outs[name]))

        loads["small_out"].wait()
        for name, (low, high) in channels.items():
            held["grad_" + name][...] = held["small_out"][low:high, 0:RW]
            store("grad_" + name)
        for name in plain:
            loads[name].wait()
            store(name)
        for gain, pair in behind.items():
            sums = jnp.zeros((RD, 128), f32)
            for name in pair:
                loads[name].wait()
                product = held["grad_" + name][...] * held[name][...].astype(f32)
                sums = sums + sum(product[:, k * 128 : (k + 1) * 128] for k in range(product.shape[1] // 128))
            total = lax.dot_general(
                jnp.ones((8, 128), f32),
                sums,
                (((1,), (1,)), ((), ())),
                precision=lax.Precision.HIGHEST,
                preferred_element_type=f32,
            )
            loads[gain].wait()
            held["grad_" + gain][...] = total[0:1] / held[gain][...].astype(f32)
            store("grad_" + gain)
        for each in stores:
            each.wait()

    results = pl.pallas_call(
        body,
        out_shape=[jax.ShapeDtypeStruct(like.shape, like.dtype) for like in shapes.values()],
        in_specs=[hbm] * len(names),
        out_specs=[hbm] * len(shapes),
        scratch_shapes=[
            *[pltpu.VMEM(shape, kind) for shape, kind in scratch.values()],
            pltpu.SemaphoreType.DMA((len(names) + len(shapes),)),
        ],
        compiler_params=pltpu.CompilerParams(vmem_limit_bytes=62 * 2**20),
        name="finish",
    )(*[source[name] for name in names])
    return {**got, **dict(zip(shapes, results, strict=True))}


def local(
    sizes,
    tokens,
    cotangent,
    doc_lengths,
    decay_exponent,
    branch_weight,
    input_weight,
    decay_weight,
    inject_weight,
    output_weight,
    mlp_gate,
    mlp_up,
    mlp_down,
    first_gain,
    second_gain,
    conv_taps,
    conv_bias,
    decay_bias,
    inject_bias,
):
    devices = math.prod(sizes.values())
    at = {name: lax.axis_index(name) for name in AXES}
    mine = at["yl"] * 2 + at["xl"]
    ring = at["zh"] * 2 + at["c"]
    share = ring * PLANE + mine
    groups = devices // SHARES

    def pooled(value, axis=0):
        if groups == 1:
            return value
        whole = lax.all_gather(value, AXES, axis=axis, tiled=True)
        size = whole.shape[axis] // SHARES
        return lax.dynamic_slice_in_dim(whole, share * size, size, axis)

    small = dict(
        first_gain=pooled(first_gain[None], 1),
        second_gain=pooled(second_gain[None], 1),
        conv_taps=pooled(conv_taps.T, 1),
        conv_bias=pooled(conv_bias[None], 1),
        decay_bias=pooled(decay_bias[None], 1),
        inject_bias=pooled(inject_bias[None], 1),
        doc_lengths=doc_lengths,
        decay_exponent=decay_exponent.reshape(-1, 128),
    )
    weights = dict(
        zip(
            WEIGHTS,
            (branch_weight, input_weight, decay_weight, inject_weight, output_weight, mlp_gate, mlp_up, mlp_down),
            strict=True,
        )
    )
    weights = {name: pooled(value) for name, value in weights.items()}
    got = run_layer(sizes["zl"], tokens[0], cotangent[0], small, weights)

    def returned(value, axis=0):
        if groups == 1:
            return value
        shape = list(value.shape)
        size = shape[axis]
        shape[axis] = size * SHARES
        whole = lax.dynamic_update_slice_in_dim(jnp.zeros(shape, bf16), value.astype(bf16), share * size, axis)
        return lax.psum_scatter(whole, AXES, scatter_dimension=axis, tiled=True).astype(f32)

    grads = [returned(got["grad_" + name]) for name in WEIGHTS]
    first, second, taps, *biases = (
        returned(got["grad_" + name], 1)
        for name in ("first_gain", "second_gain", "conv_taps", "conv_bias", "decay_bias", "inject_bias")
    )
    return (
        got["activations"][None],
        got["d_tokens"][None],
        *grads,
        first[0],
        second[0],
        taps.T,
        *[bias[0] for bias in biases],
    )


def solution(mesh):
    seq, dp = mesh.shape["seq"], mesh.shape["dp"]
    across = 1 << ((dp.bit_length() - 1) // 2)
    sizes = dict(zip(AXES, (RING, seq // (2 * RING), 2, dp // across // 2, 2, across // 2, 2), strict=True))
    split = Mesh(mesh.devices.reshape(tuple(sizes.values())), AXES)
    along_seq, along_dp = AXES[:3], AXES[3:]
    rows = P(along_dp, along_seq, None)
    in_specs = (rows, rows, P(along_dp, None), P(), *[P(AXES, None)] * 8, P(AXES), P(AXES), P(AXES, None), *[P(AXES)] * 3)
    out_specs = (rows, rows, *[P(AXES, None)] * 8, P(AXES), P(AXES), P(AXES, None), *[P(AXES)] * 3)
    return jax.shard_map(partial(local, sizes), mesh=split, in_specs=in_specs, out_specs=out_specs, check_vma=False)
```

```python
import itertools
import math
from functools import cached_property, partial
from types import SimpleNamespace

import jax
import jax.numpy as jnp
from jax import lax
from jax.experimental import pallas as pl
from jax.experimental.pallas import tpu as pltpu
from jax.sharding import Mesh, PartitionSpec as P

f32, bf16 = jnp.float32, jnp.bfloat16
MESH = pl.DeviceIdType.MESH
AXES = ("zh", "zl", "c", "yh", "yl", "xh", "xl")
RING = 4
PLANE = 4
SHARES = RING * 2 * PLANE
SENDS = 53
RECEIVES = 180

eps_norm = 1e-06
floor_gap = 1e-05
rate_scale = 8.0
gelu_root = math.sqrt(2.0 / math.pi)
gelu_cube = 0.044715


def dot(left, right):
    return jnp.dot(left, right, preferred_element_type=f32)


def dot_nt(left, right):
    return lax.dot_general(left, right, (((1,), (1,)), ((), ())), preferred_element_type=f32)


def dot_tn(left, right):
    return lax.dot_general(left, right, (((0,), (0,)), ((), ())), preferred_element_type=f32)


def gelu_parts(v):
    t = jnp.tanh(gelu_root * (v + gelu_cube * v * v * v))
    half = 0.5 * (1.0 + t)
    slope = half + 0.5 * v * (1.0 - t * t) * gelu_root * (1.0 + 3.0 * gelu_cube * v * v)
    return v * half, slope


def minus_expm1(y, root):
    poly = 1.0 + y * (1.0 / 7.0)
    for k in (6, 5, 4, 3, 2):
        poly = 1.0 + y * poly * (1.0 / k)
    return jnp.where(y > -0.35, -y * poly, 1.0 - root * root)


def inverse_rms(v):
    return lax.rsqrt(jnp.mean(v * v, axis=-1, keepdims=True) + eps_norm)


def unsorted(parts):
    size = parts[0].shape[1] // (2 * RING)
    return jnp.concatenate([part[:, g * size : (g + 1) * size] for g in range(2 * RING) for part in parts], axis=1)


def loop(total, step, body):
    def run(j, _):
        body(pl.multiple_of(j * step, step))
        return 0

    lax.fori_loop(0, total // step, run, 0)


def layer(dims, *refs):
    T, D, W, F, CW, CF = dims.T, dims.D, dims.W, dims.F, dims.CW, dims.CF
    RD, RW, RF, NL = dims.RD, dims.RW, dims.RF, dims.NL
    M = PLANE * T
    r = SimpleNamespace(**dict(zip(dims.names, refs, strict=True)))

    zh, zl, c = lax.axis_index("zh"), lax.axis_index("zl"), lax.axis_index("c")
    yl, xl = lax.axis_index("yl"), lax.axis_index("xl")
    p = yl * 2 + xl
    px, py, pd = yl * 2 + (1 - xl), (1 - yl) * 2 + xl, (1 - yl) * 2 + (1 - xl)
    to_x, to_y, to_d = {"xl": 1 - xl}, {"yl": 1 - yl}, {"yl": 1 - yl, "xl": 1 - xl}
    plane_peers = ((px, to_x), (py, to_y), (pd, to_d))
    to_core = {"c": 1 - c}
    flat_z = zh * NL + zl
    places = RING * NL * 2
    pos = flat_z * 2 + c

    def place(at):
        return {"zh": at // (2 * NL), "zl": (at // 2) % NL, "c": at % 2}

    count = itertools.count()

    def new(n=1):
        first = next(count)
        for _ in range(n - 1):
            next(count)
        assert first + n <= dims.receives
        return first

    spare = list(range(SENDS))
    sent = []

    def push(src, dst, dev, rsem, pred=None, instead=None):
        i = spare.pop(0) if instead is None else instead[2]

        def make():
            return pltpu.make_async_remote_copy(
                src, dst, r.ss.at[i], r.rs.at[rsem], device_id=dev, device_id_type=MESH
            )

        if pred is None:
            make().start()
        else:
            pl.when(pred)(lambda: make().start())
        entry = (make, pred, i, instead is None)
        sent.append(entry)
        return entry

    def settle(*entries):
        for entry in entries:
            make, pred, i, owner = entry
            if pred is None:
                make().wait_send()
            else:
                pl.when(pred)(lambda make=make: make().wait_send())
            sent.remove(entry)
            if owner:
                spare.append(i)

    def arrived(dst, rsem, pred=None):
        def wait():
            pltpu.make_async_remote_copy(
                dst, dst, r.ss.at[0], r.rs.at[rsem], device_id=to_core, device_id_type=MESH
            ).wait_recv()

        if pred is None:
            wait()
        else:
            pl.when(pred)(wait)

    def keep_local(src, dst, rsem):
        pltpu.make_async_copy(src, dst, r.rs.at[rsem]).start()

    def local_wait(src, dst, rsem):
        pltpu.make_async_copy(src, dst, r.rs.at[rsem]).wait()

    def ds(start, size, unit):
        return pl.ds(pl.multiple_of(start, unit), size)

    class Gather:
        def __init__(self, buf):
            self.buf, half = buf, buf.shape[1] // 2
            self.h0, self.h1 = pl.ds(0, half), pl.ds(half, half)
            self.rx0, self.rx1, self.ry0, self.ry1, self.rd = (new() for _ in range(5))
            self.out = []

        def start(self):
            b = self.buf
            own0, own1 = b.at[p, self.h0], b.at[p, self.h1]
            self.out.append(push(own0, own0, to_x, self.rx0))
            self.out.append(push(own1, own1, to_y, self.ry1))
            self.out.append(push(own1, own1, to_x, self.rx1))
            self.out.append(push(own0, own0, to_y, self.ry0))

        def mid(self):
            b = self.buf
            got0, got1 = b.at[px, self.h0], b.at[py, self.h1]
            arrived(got0, self.rx0)
            self.out.append(push(got0, got0, to_y, self.rd))
            arrived(got1, self.ry1)
            self.out.append(push(got1, got1, to_x, self.rd))

        def wait_x(self):
            arrived(self.buf.at[px, self.h1], self.rx1)

        def wait_y(self):
            arrived(self.buf.at[py, self.h0], self.ry0)

        def wait_d(self):
            arrived(self.buf.at[pd], self.rd)

        def end(self):
            self.wait_x()
            self.wait_y()
            self.wait_d()
            settle(*self.out)

    class Scatter:
        def __init__(self, buf, recv):
            self.buf, self.recv = buf, recv
            self.half = buf.shape[1] // 2
            self.h0, self.h1 = pl.ds(0, self.half), pl.ds(self.half, self.half)
            self.sems = [new(), new(), *[new()] * 4]
            self.out = []

        def start(self):
            self.start_far()
            self.start_near()

        def start_far(self):
            b, v, s = self.buf, self.recv, self.sems
            self.out.append(push(b.at[pd, self.h0], v.at[0], to_x, s[0]))
            self.out.append(push(b.at[pd, self.h1], v.at[1], to_y, s[1]))

        def start_near(self):
            b, v, s = self.buf, self.recv, self.sems
            self.out.append(push(b.at[px, self.h0], v.at[2], to_x, s[2]))
            self.out.append(push(b.at[py, self.h1], v.at[3], to_y, s[3]))

        def mid(self):
            b, v, s = self.buf, self.recv, self.sems
            arrived(v.at[0], s[0])
            step = 16

            def add0(o):
                b[py, pl.ds(o, step)] = (b[py, pl.ds(o, step)].astype(f32) + v[0, pl.ds(o, step)].astype(f32)).astype(bf16)

            loop(self.half, step, add0)
            self.out.append(push(b.at[py, self.h0], v.at[4], to_y, s[4]))
            arrived(v.at[1], s[1])

            def add1(o):
                q = pl.ds(pl.multiple_of(self.half + o, step), step)
                b[px, q] = (b[px, q].astype(f32) + v[1, pl.ds(o, step)].astype(f32)).astype(bf16)

            loop(self.half, step, add1)
            self.out.append(push(b.at[px, self.h1], v.at[5], to_x, s[5]))

        def end(self):
            arrived(self.recv.at[pl.ds(2, 4)], self.sems[2])
            settle(*self.out)

        def total(self, half, o, step):
            b, v = self.buf, self.recv
            own = b[p, pl.ds(pl.multiple_of(half * self.half + o, step), step)].astype(f32)
            q = pl.ds(o, step)
            return own + v[2 + half, q].astype(f32) + v[4 + half, q].astype(f32)

        def each(self, step, body, init=None):
            for half in (0, 1):

                def run(j, carry, half=half):
                    o = pl.multiple_of(j * step, step)
                    return body(pl.multiple_of(half * self.half + o, step), self.total(half, o, step), carry)

                init = lax.fori_loop(0, self.half // step, run, init)
            return init

    def z_send(src, block, rz, away=(2, 1)):
        out = []
        if 2 in away:
            out.append(push(src, block(zh), {"zh": zh + 2}, rz + zh, zh + 2 < RING))
            out.append(push(src, block(zh), {"zh": zh - 2}, rz + zh, zh - 2 >= 0, out[-1]))
        if 1 in away:
            out.append(push(src, block(zh), {"zh": zh + 1}, rz + zh, zh + 1 < RING))
            out.append(push(src, block(zh), {"zh": zh - 1}, rz + zh, zh - 1 >= 0))
        return out

    def z_forward(block, rz):
        last = RING - 1
        arrived(block(0), rz, zh == last - 1)
        one = push(block(0), block(0), {"zh": zh + 1}, rz, zh == last - 1)
        arrived(block(last), rz + last, zh == 1)
        two = push(block(last), block(last), {"zh": zh - 1}, rz + last, zh == 1, one)
        return [one, two]

    def z_wait(block, rz, use):
        last = RING - 1

        def take(k, pred, waited=None, instead=None):
            arrived(block(k), rz + k, pred if waited is None else pred & ~waited)
            return use(block(k), pred, instead)

        out = [take(zh - 1, zh >= 1), take(zh + 1, zh < last)]
        out.append(take(zh - 2, zh >= 2, zh == last - 1))
        out.append(take(zh + 2, zh <= 1, zh == 1, out[-1]))
        out.append(take(0, zh == last))
        out.append(take(last, zh == 0, None, out[-1]))
        return out

    class ZSum:
        def __init__(self, block, slot, add, direct):
            self.block, self.slot, self.add, self.direct = block, slot, add, direct
            self.valid = (direct | (zh >= 1), zh >= 2, direct | (zh <= 2), zh <= 1)
            self.sems = new(4)
            self.out = []

        def send(self):
            b, v, s = self.block, self.slot, self.sems
            last = RING - 1
            o = self.out
            if self.direct:
                o.append(push(b(last), v(2), {"zh": zh + last}, s + 2, zh == 0))
                o.append(push(b(0), v(0), {"zh": zh - last}, s + 0, zh == last, o[-1]))
                o.append(push(b(zh + 2), v(1), {"zh": zh + 2}, s + 1, zh <= 1))
                o.append(push(b(zh - 2), v(3), {"zh": zh - 2}, s + 3, zh >= 2, o[-1]))
            else:
                o.append(push(b(last), v(1), {"zh": zh + 1}, s + 1, zh == 0))
                o.append(push(b(0), v(3), {"zh": zh - 1}, s + 3, zh == last, o[-1]))
                o.append(push(b(zh + 2), v(1), {"zh": zh + 2}, s + 1, zh == 0))
                o.append(push(b(zh - 2), v(3), {"zh": zh - 2}, s + 3, zh == last, o[-1]))
            o.append(push(b(zh + 1), v(0), {"zh": zh + 1}, s + 0, zh < last))
            o.append(push(b(zh - 1), v(2), {"zh": zh - 1}, s + 2, zh > 0))

        def forward(self):
            b, v, s = self.block, self.slot, self.sems
            last = RING - 1

            def up():
                arrived(v(1), s + 1)
                self.add(last, 1)

            def down():
                arrived(v(3), s + 3)
                self.add(0, 3)

            pl.when(zh == 1)(up)
            self.out.append(push(b(last), v(1), {"zh": zh + 2}, s + 1, zh == 1))
            pl.when(zh == last - 1)(down)
            self.out.append(push(b(0), v(3), {"zh": zh - 2}, s + 3, zh == last - 1, self.out[-1]))

        def end(self):
            for k, valid in enumerate(self.valid):
                arrived(self.slot(k), self.sems + k, valid)
            settle(*self.out)

        def total(self, own, parts):
            for part, pred in zip(parts, self.valid, strict=True):
                own = own + jnp.where(pred, part.astype(f32), 0.0)
            return own

    class Column:
        def __init__(self, src, raw, sorted_, w, R, C, lane0):
            self.src, self.raw, self.sorted = src, raw, sorted_
            self.w, self.R, self.C, self.lanes = w, R, C, pl.ds(lane0, C)
            self.out = []

        rl = cached_property(lambda self: new())
        ra = cached_property(lambda self: new())
        rz = cached_property(lambda self: new(4))
        rc = cached_property(lambda self: new())

        def halves(self):
            out = []
            for k in (0, 1):
                part = Column(self.src, self.raw, self.sorted, self.w, self.R, self.C, 0)
                part.lanes = pl.ds(self.lanes.start + k * self.C // 2, self.C // 2)
                out.append(part)
            return out

        def spread_wait(self):
            arrived(self.block(zh), self.ra)
            settle(*self.out)
            self.out = []

        def load(self):
            keep_local(self.src, self.raw, self.rl)

        def prepare(self):
            local_wait(self.src, self.raw, self.rl)
            value, part = self.raw[...], self.C // (2 * RING)
            for k in range(PLANE):
                first = [(g * PLANE + k) * part for g in range(2 * RING)]
                self.sorted[k] = jnp.concatenate([value[:, at : at + part] for at in first], axis=1)

        def spread(self):
            dst = self.w.at[zh, c, ds(p * self.R, self.R, 16), self.lanes]
            for k, dev in plane_peers:
                self.out.append(push(self.sorted.at[k], dst, dev, self.ra))
            keep_local(self.sorted.at[p], dst, self.ra)

        def block(self, z):
            return self.w.at[z, c, :, self.lanes]

        def z_send(self, spread=True):
            if spread:
                arrived(self.block(zh), self.ra)
            self.out += z_send(self.block(zh), self.block, self.rz)
            self.out.append(self.core_push(self.block(zh)))

        def z_forward(self):
            self.out += z_forward(self.block, self.rz)

        def core_push(self, block, pred=None, instead=None):
            return push(block, block, to_core, self.rc, pred, instead)

        def z_wait(self):
            self.out += z_wait(self.block, self.rz, self.core_push)

        def end(self):
            arrived(self.w.at[:, 1 - c, :, self.lanes], self.rc)
            settle(*self.out)

    class Row(Column):
        def __init__(self, src, w):
            self.src, self.w, self.lanes = src, w, pl.ds(0, w.shape[3])
            self.out = []

        def z_send(self, away=(2, 1)):
            if 2 in away:
                keep_local(self.src, self.block(zh), self.ra)
            self.out += z_send(self.src, self.block, self.rz, away)

        def z_wait(self):
            pltpu.make_async_copy(self.src, self.block(zh), r.rs.at[self.ra]).wait()
            self.out.append(self.core_push(self.block(zh)))
            super().z_wait()

    class ColumnsGrad:
        def __init__(self, g, other, slots, land, R, lane0, lanes, direct=False):
            self.g, self.other, self.slots, self.land = g, other, slots, land
            self.R, self.lanes = R, pl.ds(lane0, lanes)
            self.rows = PLANE * R
            self.rc, self.rl = new(), new()
            self.zsum = ZSum(
                lambda z: g.at[z, c, :, self.lanes], lambda k: slots.at[k, :, self.lanes], self.add_slot, direct
            )

        def add_slot(self, z, k):
            g, q = self.g, self.lanes

            def add(o):
                s = pl.ds(o, 16)
                g[z, c, s, q] = (g[z, c, s, q].astype(f32) + self.slots[k, s, q].astype(f32)).astype(bf16)

            loop(self.rows, 16, add)

        def core_send(self):
            self.pushed = push(
                self.g.at[:, 1 - c, :, self.lanes], self.other.at[:, :, self.lanes], to_core, self.rc
            )

        def core_sum(self):
            g, q = self.g, self.lanes
            arrived(self.other.at[:, :, q], self.rc)
            settle(self.pushed)
            for z in range(RING):

                def add(o):
                    s = pl.ds(o, 16)
                    g[z, c, s, q] = (g[z, c, s, q].astype(f32) + self.other[z, s, q].astype(f32)).astype(bf16)

                loop(self.rows, 16, add)

        def z_send(self):
            self.core_sum()
            self.zsum.send()

        def z_forward(self):
            self.zsum.forward()

        def plane_send(self):
            g, q, R = self.g, self.lanes, self.R
            self.zsum.end()

            def add(o):
                s = pl.ds(o, 16)
                parts = [self.slots[k, s, q] for k in range(4)]
                g[zh, c, s, q] = self.zsum.total(g[zh, c, s, q].astype(f32), parts).astype(bf16)

            loop(PLANE * R, 16, add)
            dst = self.land.at[p, :, q]
            self.out = []
            for k, dev in plane_peers:
                self.out.append(push(g.at[zh, c, ds(k * R, R, 16), q], dst, dev, self.rl))
            keep_local(g.at[zh, c, ds(p * R, R, 16), q], dst, self.rl)

        def end(self):
            arrived(self.land.at[:, :, self.lanes], self.rl)
            settle(*self.out)

    def in_order(land, lane0, C, held, result):
        held[...] = unsorted([land[k, :, lane0 : lane0 + C].astype(f32) for k in range(PLANE)])

    class LastGrad(ColumnsGrad):
        def __init__(self, g, other, stage, slots, R, lane0, lanes, total, result):
            super().__init__(g, other, slots, None, R, lane0, lanes)
            self.stage, self.sum, self.result = stage, total, result
            self.zsum.block, self.zsum.slot = (lambda z: stage.at[:, z]), (lambda k: slots.at[k])

        def add_slot(self, z, k):
            for q in range(PLANE):
                self.stage[q, z] = (self.stage[q, z].astype(f32) + self.slots[k, q].astype(f32)).astype(bf16)

        def plane_send(self):
            R, dst = self.R, self.stage.at[p]
            self.core_sum()
            self.out = []
            for k, dev in plane_peers:
                self.out.append(push(self.g.at[:, c, ds(k * R, R, 16), self.lanes], dst, dev, self.rl))
            keep_local(self.g.at[:, c, ds(p * R, R, 16), self.lanes], dst, self.rl)

        def z_send(self):
            arrived(self.stage, self.rl)
            self.zsum.send()

        def end(self):
            self.zsum.end()
            settle(*self.out)
            values = [
                self.zsum.total(self.stage[q, zh].astype(f32), [self.slots[k, q] for k in range(4)]) for q in range(PLANE)
            ]
            self.sum[...] = unsorted(values)

    class RowsGrad(ColumnsGrad):
        def __init__(self, g, other, slots, total, result):
            super().__init__(g, other, slots, None, 0, 0, g.shape[3])
            self.rows, self.sum, self.result = g.shape[2], total, result

        def end(self):
            self.zsum.end()

            def add(o):
                s = pl.ds(o, 16)
                self.sum[s] = self.zsum.total(self.g[zh, c, s].astype(f32), [self.slots[k, s] for k in range(4)])

            loop(self.rows, 16, add)

    class Carry:
        def __init__(self, own, sib, buf, later):
            self.own, self.sib, self.buf, self.later = own, sib, buf, later
            self.rc, self.rz = new(), new(RING * NL)
            self.out = []

        def order(self):
            return range(RING * NL) if self.later else reversed(range(RING * NL))

        def send_core(self):
            self.out.append(push(self.own, self.sib, to_core, self.rc))

        def send(self):
            arrived(self.sib, self.rc)
            own, sib = self.own[...], self.sib[...]
            near = (c == 0) if self.later else (c == 1)
            head, tail = jnp.where(near, own, sib), jnp.where(near, sib, own)
            self.buf[flat_z, 0:PLANE] = tail[0:PLANE] * head[0:PLANE]
            self.buf[flat_z, PLANE : 2 * PLANE] = (
                tail[0:PLANE] * head[PLANE : 2 * PLANE] + tail[PLANE : 2 * PLANE]
            )
            part = self.buf.at[flat_z]
            for at in self.order():
                pred = (flat_z < at) if self.later else (flat_z > at)
                self.out.append(push(part, part, {"zh": at // NL, "zl": at % NL}, self.rz + flat_z, pred))

        def fold(self, into):
            into[...] = jnp.zeros_like(into)

            def take(part):
                into[0:PLANE] = part[0:PLANE] * into[0:PLANE] + part[PLANE : 2 * PLANE]

            for at in self.order():
                pred = (flat_z > at) if self.later else (flat_z < at)

                def chip(at=at):
                    arrived(self.buf.at[at], self.rz + at)
                    take(self.buf[at])

                pl.when(pred)(chip)
            pl.when((c == 1) if self.later else (c == 0))(lambda: take(self.sib[...]))
            settle(*self.out)

    GL = PLANE * RD
    ring = zh * 2 + c

    def ring_place(at):
        return {"zh": at // 2, "c": at % 2}

    class Small:
        def __init__(self):
            self.rr, self.rk = new(), new()
            self.out = []

        def pack(self):
            for load in small_loads:
                local_wait(*load)
            lengths = r.lens[...]
            rows = [r.gain_a[...], r.gain_b[...], r.taps[...], r.bias_a[...], r.bias_b[...], r.bias_c[...]]
            rows += [lax.shift_right_logical(lengths, 8), lengths & 255]
            rows = [row.astype(f32) for row in rows]
            rows = [jnp.concatenate([row, jnp.zeros((row.shape[0], 128 - row.shape[1]), f32)], axis=1) for row in rows]
            r.pack[...] = jnp.concatenate([*rows, jnp.zeros((5, 128), f32)], axis=0).astype(bf16)

        def one(self):
            for at in range(2 * RING):
                self.out.append(push(r.pack, r.pr.at[ring], ring_place(at), self.rr, ring != at))
            keep_local(r.pack, r.pr.at[ring], self.rr)

        def two(self):
            arrived(r.pr, self.rr)
            lines = []
            for at in range(2 * RING):
                tile = r.pr[at].astype(f32)
                lines.append(jnp.concatenate([tile[row : row + 1, 0:32] for row in (0, 1, 9, 10)], axis=1))
            r.line[...] = jnp.concatenate([*lines, jnp.zeros((16 - 2 * RING, 128), f32)], axis=0).astype(bf16)
            for _, dev in plane_peers:
                self.out.append(push(r.line, r.pp.at[p], dev, self.rk))
            keep_local(r.line, r.pp.at[p], self.rk)

        def three(self):
            arrived(r.pp, self.rk)
            parts = [r.pp[k].astype(f32) for k in range(PLANE)]
            for row in (0, 1):
                lanes = slice(row * 32, row * 32 + RD)
                wide = jnp.concatenate([part[:, lanes] for part in parts], axis=1)
                for at in range(2 * RING):
                    r.gains[row : row + 1, at * GL : (at + 1) * GL] = wide[at : at + 1]
            whole = jnp.concatenate([r.pr[at, :, 0:RW].astype(f32) for at in range(2 * RING)], axis=1)
            r.chan[...] = whole[2:10]
            rates = r.rates[...].astype(f32)
            rates = jnp.concatenate([rates[k : k + 1] for k in range(W // 128)], axis=1)
            mine = jnp.zeros((1, CW), f32)
            for k in range(PLANE):
                at = [(g * PLANE + k) * RW for g in range(2 * RING)]
                mine = jnp.where(p == k, jnp.concatenate([rates[:, o : o + RW] for o in at], axis=1), mine)
            r.chan[7:8] = jnp.exp2(-mine)

        def four(self):
            where = lax.broadcasted_iota(jnp.int32, (T, 128), 0).astype(f32) + (pos * T).astype(f32)
            for k in range(PLANE):
                part = r.pp[k].astype(f32)
                starts, ends = [], []
                total = jnp.zeros((1, 1), f32)
                for j in range(dims.SEGS):
                    starts.append(total)
                    total = total + part[0:1, 64 + j : 65 + j] * 256.0 + part[0:1, 96 + j : 97 + j]
                    ends.append(total)

                def seg(shift):
                    at = where + float(shift)
                    value = jnp.zeros((T, 128), f32)
                    for end in ends:
                        value = value + jnp.where(at >= end, 1.0, 0.0)
                    return jnp.where((at < 0.0) | (at >= float(T * places)), -1.0, value)

                here = seg(0)
                rows = pl.ds(k * T, T)
                first = jnp.zeros((T, 128), f32)
                for start in starts:
                    first = jnp.where(where == start, 1.0, first)
                r.masks[0, rows] = first
                for j in (1, 2, 3):
                    r.masks[j, rows] = jnp.where(seg(-j) == here, 1.0, 0.0)
                    r.masks[3 + j, rows] = jnp.where(seg(j) == here, 1.0, 0.0)
            settle(*self.out)

    class SmallGrad:
        def __init__(self):
            self.rg = new()
            self.out = []

        def one(self):
            for at in range(2 * RING):
                own = jnp.concatenate([r.gchan[:, at * RW : (at + 1) * RW], jnp.zeros((8, 128 - RW), f32)], axis=1)
                r.gs[at] = own
            for at in range(2 * RING):
                self.out.append(push(r.gs.at[at], r.gg.at[ring], ring_place(at), self.rg, ring != at))
            keep_local(r.gs.at[ring], r.gg.at[ring], self.rg)

        def two(self):
            arrived(r.gg, self.rg)
            value = r.gg[0]
            for at in range(1, 2 * RING):
                value = value + r.gg[at]
            r.small_out[0:7] = value[0:7]
            gains = [r.gain_a[...].astype(f32), r.gain_b[...].astype(f32), jnp.zeros((1, 128 - 2 * RD), f32)]
            r.small_out[7:8] = jnp.concatenate(gains, axis=1)
            settle(*self.out)

    barrier = pltpu.get_barrier_semaphore()
    for _, dev in plane_peers:
        pl.semaphore_signal(barrier, 1, device_id=dev, device_id_type=MESH)
    for at in range(places):

        @pl.when(pos != at)
        def _(at=at):
            pl.semaphore_signal(barrier, 1, device_id=place(at), device_id_type=MESH)

    first_loads = [
        (src, dst, new())
        for src, dst in (
            (r.tokens, r.x_all.at[p]),
            (r.cotangent, r.cot_all.at[p]),
        )
    ]
    small_loads = [
        (src, dst, new())
        for src, dst in (
            (r.first_gain, r.gain_a),
            (r.second_gain, r.gain_b),
            (r.conv_taps, r.taps),
            (r.conv_bias, r.bias_a),
            (r.decay_bias, r.bias_b),
            (r.inject_bias, r.bias_c),
            (r.doc_lengths, r.lens),
            (r.decay_exponent, r.rates),
        )
    ]
    for load in small_loads + first_loads:
        keep_local(*load)

    w_i = Column(r.input_weight, r.raw_i, r.sort_i, r.w_ib, RD, CW, 0)
    w_b = Column(r.branch_weight, r.raw_b, r.sort_b, r.w_ib, RD, CW, CW)
    w_d = Column(r.decay_weight, r.raw_d, r.sort_d, r.w_di, RW, CW, 0)
    w_j = Column(r.inject_weight, r.raw_j, r.sort_j, r.w_di, RW, CW, CW)
    w_g = Column(r.mlp_gate, r.raw_g, r.sort_g, r.w_gu, RD, CF, 0)
    w_u = Column(r.mlp_up, r.raw_u, r.sort_u, r.w_gu, RD, CF, CF)
    w_g1, w_g2 = w_g.halves()
    w_o, w_dn = Row(r.output_weight, r.w_o), Row(r.mlp_down, r.w_dn)
    ag_x, ag_conv, ag_two = Gather(r.x_all), Gather(r.conv), Gather(r.n_two)
    ag_cot, ag_out = Gather(r.cot_all), Gather(r.d_out)
    small, small_grad = Small(), SmallGrad()
    after, before = flat_z + c, flat_z - (1 - c)
    to_next = {"zh": after // NL, "zl": after % NL, "c": 1 - c}
    to_prev = {"zh": before // NL, "zl": before % NL, "c": 1 - c}
    step = 256
    chunk = PLANE * RD * 2

    for w in (w_i, w_d, w_j, w_b, w_g, w_u):
        w.load()
    small.pack()
    w_i.prepare()
    w_d.prepare()
    pl.semaphore_wait(barrier, len(plane_peers) + places - 1)
    small.one()
    local_wait(*first_loads[0])
    halo_x = new()
    sent_x = push(r.x_all.at[p, pl.ds(T - 16, 16)], r.x_halo.at[p], to_next, halo_x, pos < places - 1)
    w_o.z_send((2,))
    w_i.spread()
    w_d.spread()
    ag_x.start()
    w_j.prepare()
    w_i.z_send()
    small.two()
    w_b.prepare()

    @pl.when(pos == 0)
    def _():
        r.x_halo[p] = jnp.zeros((16, D), bf16)

    arrived(r.x_halo.at[p], halo_x, pos > 0)
    halo_p = new(PLANE)
    sent_p = [push(r.x_halo.at[p], r.x_halo.at[p], dev, halo_p + p) for _, dev in plane_peers]
    ag_x.mid()
    w_i.z_forward()
    w_o.z_send((1,))
    w_g.prepare()
    local_wait(*first_loads[1])
    small.three()

    def norm_block(k):
        def norm_one(o):
            s = pl.ds(o, 32)
            v = r.x_all[k, s].astype(f32)
            r.n_one[k, s] = (v * inverse_rms(v) * r.gains[0:1]).astype(bf16)

        loop(T, 32, norm_one)

    norm_block(p)
    w_d.z_send()
    ag_x.wait_x()
    norm_block(px)
    ag_x.wait_y()
    norm_block(py)
    w_j.spread()
    small.four()
    for k, _ in plane_peers:
        arrived(r.x_halo.at[k], halo_p + k)
    v = r.x_halo[...].reshape(PLANE * 16, D).astype(f32)
    r.n_halo[...] = (v * inverse_rms(v) * r.gains[0:1]).astype(bf16).reshape(PLANE, 16, D)
    ag_x.wait_d()
    norm_block(pd)
    settle(*ag_x.out, sent_x, *sent_p)
    w_b.spread()
    w_g.spread()
    w_o.z_forward()
    w_i.z_wait()
    w_u.prepare()
    w_j.z_send()
    w_i.end()

    def weight_ib(lanes):
        return r.w_ib[:, :, :, lanes].reshape(D, CW)

    lanes_a, lanes_b = pl.ds(0, CW), pl.ds(CW, CW)
    halo = dot(r.n_halo[...].reshape(PLANE * 16, D), weight_ib(lanes_a)).astype(bf16).astype(f32)
    body = dot(r.n_one[...].reshape(M, D), weight_ib(lanes_a)).astype(bf16).astype(f32)
    for k in range(PLANE):
        r.u[k, 0:8] = halo[k * 16 + 8 : (k + 1) * 16]
        r.u[k, 8 : 8 + T] = body[k * T : (k + 1) * T]

    def wide(j, rows):
        return jnp.concatenate([r.masks[j, rows]] * (CW // 128), axis=1) > 0.5

    def convolve(o):
        for k in range(PLANE):
            ext = r.u[k, pl.ds(o, 24)]
            rows = ds(k * T + o, 16, 16)
            total = r.chan[4:5] + r.chan[0:1] * ext[8:24]
            for j in range(1, 4):
                total = total + jnp.where(wide(j, rows), r.chan[j : j + 1] * ext[8 - j : 24 - j], 0.0)
            r.conv[p, rows] = total.astype(bf16)

    loop(T, 16, convolve)
    ag_conv.start()
    w_d.z_forward()
    ag_conv.mid()
    w_j.z_forward()
    w_b.z_send()
    w_d.z_wait()
    w_d.end()

    def pre(q, lanes):
        return dot(r.conv[q], r.w_di[:, :, ds(q * RW, RW, 16), lanes].reshape(CW, CW))

    r.pair[:, 0:CW] = pre(p, lanes_a)
    ag_conv.wait_x()
    r.pair[:, 0:CW] += pre(px, lanes_a)
    ag_conv.wait_y()
    r.pair[:, 0:CW] += pre(py, lanes_a)
    w_b.z_forward()
    ag_conv.wait_d()
    r.pair[:, 0:CW] += pre(pd, lanes_a)
    settle(*ag_conv.out)
    w_g.spread_wait()
    w_g1.z_send(False)
    w_j.z_wait()
    w_u.spread()
    ag_cot.start()
    w_o.z_wait()
    w_j.end()
    r.pair[:, CW : 2 * CW] = (pre(0, lanes_b) + pre(1, lanes_b)) + (pre(2, lanes_b) + pre(3, lanes_b))

    def decay_terms(s, rg):
        log_a = -rate_scale * rg * r.chan[7:8]
        root = jnp.exp(log_a)
        gap = minus_expm1(2.0 * log_a, root)
        first = wide(0, s)
        return root, gap, jnp.where(first, 1.0, jnp.sqrt(jnp.maximum(gap, floor_gap))), first

    def gates_two(o):
        s = pl.ds(o, 16)
        rg = jax.nn.sigmoid(r.pair[s, 0:CW] + r.chan[5:6])
        ig = jax.nn.sigmoid(r.pair[s, CW : 2 * CW] + r.chan[6:7])
        root, _, mult, first = decay_terms(s, rg)
        r.rgate[s], r.igate[s] = rg, ig
        r.decay[s] = jnp.where(first, 0.0, root)
        r.work[s] = mult * ig * r.conv[p, s].astype(f32)

    loop(M, 16, gates_two)
    row = lax.broadcasted_iota(jnp.int32, (8, CW), 0)

    def scan_forward(j, carry):
        out = []
        for k in range(PLANE):
            s = ds(k * T + j * 8, 8, 8)
            a, b = r.decay[s], r.work[s]
            for n in (1, 2, 4):
                a_b = jnp.where(row >= n, pltpu.roll(a, n, 0), 1.0)
                b_b = jnp.where(row >= n, pltpu.roll(b, n, 0), 0.0)
                a, b = a * a_b, a * b_b + b
            total, prod = b + a * carry[2 * k], a * carry[2 * k + 1]
            r.state[k, ds(8 + j * 8, 8, 8)] = total
            r.cum[s] = prod
            out += [total[7:8], prod[7:8]]
        return tuple(out)

    zero, one = jnp.zeros((1, CW), f32), jnp.ones((1, CW), f32)
    ends = lax.fori_loop(0, T // 8, scan_forward, (zero, one) * PLANE)
    carry_f = Carry(r.own_f, r.sib_f, r.carry_f, True)
    for k in range(PLANE):
        r.own_f[k : k + 1] = ends[2 * k + 1]
        r.own_f[PLANE + k : PLANE + k + 1] = ends[2 * k]
    carry_f.send_core()
    w_b.z_wait()
    carry_f.send()
    w_g1.z_forward()
    w_g2.z_send(False)
    w_b.end()
    r.work[...] = dot(r.n_one[...].reshape(M, D), weight_ib(lanes_b))

    def gates_one(o):
        s = pl.ds(o, 16)
        r.gated[s], r.slope[s] = gelu_parts(r.work[s])

    loop(M, 16, gates_one)
    ag_cot.mid()
    carry_f.fold(r.into)
    for k in range(PLANE):
        r.state[k, 0:8] = jnp.broadcast_to(r.into[k : k + 1], (8, CW))

    def mix(o):
        for k in range(PLANE):
            s, t = ds(k * T + o, 16, 16), ds(8 + o, 16, 8)
            state = r.state[k, t] + r.cum[s] * r.into[k : k + 1]
            r.state[k, t] = state
            r.mixed[s] = (state * r.gated[s]).astype(bf16)

    loop(T, 16, mix)

    w_o.end()

    def out_part(o):
        q = pl.ds(o, step)
        r.part[:, :, q] = dot(r.mixed[...], r.w_o[:, :, :, q].reshape(CW, step)).astype(bf16).reshape(PLANE, T, step)

    loop(D, step, out_part)
    rs_one = Scatter(r.part, r.got_one)
    rs_one.start()
    w_g1.z_wait()
    w_g2.z_forward()
    w_u.z_send()
    ag_cot.end()
    rs_one.mid()
    rs_one.end()

    def norm_two(o, summed, _):
        s = pl.ds(o, 32)
        v = r.x_all[p, s].astype(f32) + summed
        r.x_one[s] = v
        r.n_two[p, s] = (v * inverse_rms(v) * r.gains[1:2]).astype(bf16)

    rs_one.each(32, norm_two)
    ag_two.start()
    w_u.z_forward()
    ag_two.mid()
    w_dn.z_send()
    w_g2.z_wait()
    w_g1.end()
    w_u.z_wait()
    w_g2.end()
    ag_two.end()

    def mlp_in(o):
        q = pl.ds(o, step)
        r.pair[:, q] = dot(r.n_two[...].reshape(M, D), r.w_gu[:, :, :, q].reshape(D, step))

    loop(CF, step, mlp_in)
    w_dn.z_forward()
    w_u.end()
    loop(CF, step, lambda o: mlp_in(pl.multiple_of(CF + o, step)))

    def gates_mlp(o):
        s = pl.ds(o, 16)
        value, slope = gelu_parts(r.pair[s, 0:CF])
        up = r.pair[s, CF : 2 * CF]
        r.hidden[s] = (value * up).astype(bf16)
        r.pair[s, 0:CF] = slope * up
        r.pair[s, CF : 2 * CF] = value

    loop(M, 16, gates_mlp)

    half = CF // 2
    for k in (0, 1):
        for o in range(0, D, D // 2):
            value = dot_tn(r.hidden[:, k * half : (k + 1) * half], r.cot_all[:, :, o : o + D // 2].reshape(M, D // 2))
            r.g_dn[k * RING // 2 : (k + 1) * RING // 2, :, :, o : o + D // 2] = value.astype(bf16).reshape(
                RING // 2, 2, RF, D // 2
            )
    g_dn = RowsGrad(r.g_dn, r.h_dn, r.z_dn, r.grad_mlp_down, r.grad_mlp_down)
    g_dn.core_send()
    g_dn.z_send()
    w_dn.z_wait()
    w_dn.end()

    for k in range(CF // step):
        back = dot_nt(r.cot_all[...].reshape(M, D), r.w_dn[...].reshape(CF, D)[k * step : (k + 1) * step])
        r.d_pair[:, k * step : (k + 1) * step] = (back * r.pair[:, k * step : (k + 1) * step]).astype(bf16)
        r.d_pair[:, CF + k * step : CF + (k + 1) * step] = (
            back * r.pair[:, CF + k * step : CF + (k + 1) * step]
        ).astype(bf16)

    def d_two_part(z, _):
        q = ds(z * chunk, chunk, chunk)
        r.part[:, :, q] = (
            dot_nt(r.d_pair[...], r.w_gu[z].reshape(chunk, 2 * CF)).astype(bf16).reshape(PLANE, T, chunk)
        )
        return 0

    lax.fori_loop(0, RING, d_two_part, 0)
    rs_two = Scatter(r.part, r.got_two)
    rs_two.start()

    def grad_gate_up(lane0):
        lanes = pl.ds(lane0, CF)

        def run(z, _):
            q = ds(z * chunk, chunk, chunk)
            value = dot_tn(r.n_two[:, :, q].reshape(M, chunk), r.d_pair[:, lanes])
            r.w_gu[z, :, :, lanes] = value.astype(bf16).reshape(2, chunk // 2, CF)
            return 0

        lax.fori_loop(0, RING, run, 0)

    grad_gate_up(0)
    g_g = ColumnsGrad(r.w_gu, r.h_gu, r.z_gu, r.l_gu, RD, 0, CF)
    g_g.core_send()
    rs_two.mid()
    g_dn.z_forward()
    g_g.z_send()
    grad_gate_up(CF)
    g_u, g_v = (
        ColumnsGrad(r.w_gu, r.h_gu, r.z_gu, r.l_gu, RD, lane0, CF // 2) for lane0 in (CF, CF + CF // 2)
    )
    g_u.core_send()
    g_v.core_send()

    def act_part(o):
        q = pl.ds(o, step)
        r.part_act[:, :, q] = dot(r.hidden[...], r.w_dn[:, :, :, q].reshape(CF, step)).astype(bf16).reshape(PLANE, T, step)

    loop(D, step, act_part)
    r.gchan[...] = jnp.zeros_like(r.gchan)
    rs_two.end()

    def norm_two_back(o, d_two, _):
        s = pl.ds(o, 32)
        v = r.x_one[s]
        rs = inverse_rms(v)
        z = v * rs
        dz = d_two * r.gains[1:2]
        d_one = r.cot_all[p, s].astype(f32) + rs * (dz - z * jnp.mean(dz * z, axis=-1, keepdims=True))
        r.d_one[s] = d_one
        r.d_out[p, s] = d_one.astype(bf16)

    rs_two.each(32, norm_two_back)
    ag_out.start()
    ag_out.mid()
    g_g.z_forward()
    g_u.z_send()
    ag_out.end()
    rs_act = Scatter(r.part_act, r.got_act)
    rs_act.start()

    r.work[...] = dot_nt(r.d_out[...].reshape(M, D), r.w_o[...].reshape(CW, D))

    def split(o):
        for k in range(PLANE):
            s = ds(k * T + o, 16, 16)
            d_mixed = r.work[s]
            r.d_gu[s, CW : 2 * CW] = (d_mixed * r.state[k, ds(8 + o, 16, 8)] * r.slope[s]).astype(bf16)
            r.work[s] = d_mixed * r.gated[s]

    loop(T, 16, split)

    def scan_backward(i, carry):
        j = T // 8 - 1 - i
        out = []
        for k in range(PLANE):
            s = ds(k * T + j * 8, 8, 8)
            decay, b = r.decay[s], r.work[s]
            a = jnp.where(row < 7, pltpu.roll(decay, 7, 0), carry[3 * k + 2])
            for n in (1, 2, 4):
                a_b = jnp.where(row < 8 - n, pltpu.roll(a, 8 - n, 0), 1.0)
                b_b = jnp.where(row < 8 - n, pltpu.roll(b, 8 - n, 0), 0.0)
                a, b = a * a_b, a * b_b + b
            total, prod = b + a * carry[3 * k], a * carry[3 * k + 1]
            r.work[s], r.cum[s] = total, prod
            out += [total[0:1], prod[0:1], decay[0:1]]
        return tuple(out)

    heads = lax.fori_loop(0, T // 8, scan_backward, (zero, one, one) * PLANE)
    carry_b = Carry(r.own_b, r.sib_b, r.carry_b, False)
    for k in range(PLANE):
        r.own_b[k : k + 1] = r.own_f[k : k + 1]
        r.own_b[PLANE + k : PLANE + k + 1] = heads[3 * k] * heads[3 * k + 2]
    carry_b.send_core()

    def grad_out(o):
        q = pl.ds(o, D // 2)
        value = dot_tn(r.mixed[...], r.d_out[:, :, q].reshape(M, D // 2))
        r.w_o[:, :, :, q] = value.astype(bf16).reshape(RING, 2, RW, D // 2)

    loop(D, D // 2, grad_out)
    g_o = RowsGrad(r.w_o, r.h_o, r.z_o, r.grad_output_weight, r.grad_output_weight)
    g_o.core_send()
    carry_b.send()
    g_u.z_forward()
    g_v.z_send()
    rs_act.mid()

    def d_branch_part(z, _):
        q = ds(z * chunk, chunk, chunk)
        r.part[:, :, q] = (
            dot_nt(r.d_gu[:, lanes_b], r.w_ib[z, :, :, lanes_b].reshape(chunk, CW))
            .astype(bf16)
            .reshape(PLANE, T, chunk)
        )
        value = dot_tn(r.n_one[:, :, q].reshape(M, chunk), r.d_gu[:, lanes_b])
        r.w_ib[z, :, :, lanes_b] = value.astype(bf16).reshape(2, chunk // 2, CW)
        return 0

    lax.fori_loop(0, RING, d_branch_part, 0)
    g_b = ColumnsGrad(r.w_ib, r.h_ib, r.z_ib, r.l_ib, RD, CW, CW)
    g_b.core_send()
    g_g.plane_send()
    carry_b.fold(r.into)
    g_o.z_send()

    def back(o):
        sums = [jnp.zeros((1, CW), f32)] * 2
        for k in range(PLANE):
            s = ds(k * T + o, 16, 16)
            adjoint = r.work[s] + r.cum[s] * r.into[k : k + 1]
            previous = r.state[k, pl.ds(o, 24)][7:23]
            rg, ig, decay, conv = r.rgate[s], r.igate[s], r.decay[s], r.conv[p, s].astype(f32)
            _, gap, mult, first = decay_terms(s, rg)
            d_mult = jnp.where(first, 0.0, adjoint * ig * conv)
            d_log = adjoint * previous * decay - jnp.where(gap > floor_gap, (1.0 - gap) * d_mult / mult, 0.0)
            d_decay = (-rate_scale * r.chan[7:8] * d_log * rg * (1.0 - rg)).astype(bf16)
            d_inject = (adjoint * mult * conv * ig * (1.0 - ig)).astype(bf16)
            r.d_pre[s, 0:CW] = d_decay
            r.d_pre[s, CW : 2 * CW] = d_inject
            sums[0] = sums[0] + jnp.sum(d_decay.astype(f32), axis=0, keepdims=True)
            sums[1] = sums[1] + jnp.sum(d_inject.astype(f32), axis=0, keepdims=True)
            r.d_conv[k, pl.ds(o, 16)] = adjoint * mult * ig
        r.gchan[5:6] += sums[0]
        r.gchan[6:7] += sums[1]

    loop(T, 16, back)

    def conv_part(q):
        r.part_conv[q] = dot_nt(r.d_pre[...], r.w_di[:, :, ds(q * RW, RW, 16), :].reshape(CW, 2 * CW)).astype(bf16)

    rs_conv = Scatter(r.part_conv, r.got_conv)
    conv_part(pd)
    rs_act.end()
    rs_conv.start_far()
    conv_part(px)
    conv_part(py)
    rs_conv.start_near()
    conv_part(p)
    g_v.z_forward()

    def finish_act(o, summed, _):
        s = pl.ds(o, 16)
        r.activations[s] = (r.x_one[s] + summed).astype(bf16)

    rs_act.each(16, finish_act)
    g_b.z_send()
    g_dn.end()

    def grad_dec_inj(lanes):
        def run(q, _):
            value = dot_tn(r.conv[q], r.d_pre[:, lanes])
            r.w_di[:, :, ds(q * RW, RW, 16), lanes] = value.astype(bf16).reshape(RING, 2, RW, CW)
            return 0

        lax.fori_loop(0, RING, run, 0)

    grad_dec_inj(lanes_a)
    g_d, g_j, g_k = (
        ColumnsGrad(r.w_di, r.h_di, r.z_di, r.l_di, RW, lane0, lanes)
        for lane0, lanes in ((0, 128), (128, CW - 128), (CW, CW))
    )
    g_d.core_send()
    g_j.core_send()
    rs_conv.mid()
    grad_dec_inj(lanes_b)
    g_k.core_send()
    g_o.z_forward()
    g_d.z_send()
    rs_conv.end()

    for half in (0, 1):

        def add_conv(o, half=half):
            for k in (2 * half, 2 * half + 1):
                at = (k - 2 * half) * T + o
                r.d_conv[k, pl.ds(o, 16)] += rs_conv.total(half, pl.multiple_of(at, 16), 16)

        loop(T, 16, add_conv)
    halo_b = new()
    for k in range(PLANE):
        r.halo_out[4 * k : 4 * k + 4] = r.d_conv[k, 0:4]
    sent_b = push(r.halo_out, r.halo_in, to_prev, halo_b, pos > 0)
    g_b.z_forward()
    g_j.z_send()

    def taps_back(o):
        sums = [jnp.zeros((1, CW), f32)] * 5
        for k in range(PLANE):
            ext = r.u[k, pl.ds(o, 24)]
            rows = ds(k * T + o, 16, 16)
            dc = r.d_conv[k, pl.ds(o, 16)]
            sums[4] = sums[4] + jnp.sum(dc, axis=0, keepdims=True)
            sums[0] = sums[0] + jnp.sum(dc * ext[8:24], axis=0, keepdims=True)
            for j in range(1, 4):
                term = jnp.where(wide(j, rows), dc * ext[8 - j : 24 - j], 0.0)
                sums[j] = sums[j] + jnp.sum(term, axis=0, keepdims=True)
        for j in range(5):
            r.gchan[j : j + 1] += sums[j]

    loop(T, 16, taps_back)
    small_grad.one()

    @pl.when(pos == places - 1)
    def _():
        r.halo_in[...] = jnp.zeros((16, CW), f32)

    g_d.z_forward()
    g_u.plane_send()
    g_v.plane_send()
    arrived(r.halo_in, halo_b, pos < places - 1)
    for k in range(PLANE):
        r.d_conv[k, T : T + 8] = jnp.concatenate([r.halo_in[4 * k : 4 * k + 4], jnp.zeros((4, CW), f32)], axis=0)

    def conv_back(o):
        for k in range(PLANE):
            ext = r.d_conv[k, pl.ds(o, 24)]
            rows = ds(k * T + o, 16, 16)
            total = r.chan[0:1] * ext[0:16]
            for j in range(1, 4):
                total = total + jnp.where(wide(3 + j, rows), r.chan[j : j + 1] * ext[j : 16 + j], 0.0)
            r.d_gu[rows, 0:CW] = total.astype(bf16)

    loop(T, 16, conv_back)

    def d_input_part(z, _):
        q = ds(z * chunk, chunk, chunk)
        value = dot_nt(r.d_gu[:, lanes_a], r.w_ib[z, :, :, lanes_a].reshape(chunk, CW)).reshape(PLANE, T, chunk)
        r.part[:, :, q] = (r.part[:, :, q].astype(f32) + value).astype(bf16)
        return 0

    lax.fori_loop(0, RING, d_input_part, 0)
    rs_three = Scatter(r.part, r.got_three)
    rs_three.start()

    def grad_input(z, _):
        q = ds(z * chunk, chunk, chunk)
        value = dot_tn(r.n_one[:, :, q].reshape(M, chunk), r.d_gu[:, lanes_a])
        r.w_ib[z, :, :, lanes_a] = value.astype(bf16).reshape(2, chunk // 2, CW)
        return 0

    lax.fori_loop(0, RING, grad_input, 0)
    g_i = LastGrad(r.w_ib, r.h_ib, r.st_i, r.z_i, RD, 0, CW, r.grad_input_weight, r.grad_input_weight)
    g_i.core_send()
    g_j.z_forward()
    g_k.z_send()
    g_i.plane_send()
    rs_three.mid()
    g_k.z_forward()
    rs_three.end()
    g_i.z_send()
    g_b.plane_send()
    g_d.plane_send()
    g_j.plane_send()

    def norm_one_back(o, d_n, _):
        s = pl.ds(o, 32)
        v = r.x_all[p, s].astype(f32)
        rs = inverse_rms(v)
        z = v * rs
        dz = d_n * r.gains[0:1]
        r.d_tokens[s] = r.d_one[s] + rs * (dz - z * jnp.mean(dz * z, axis=-1, keepdims=True))

    rs_three.each(32, norm_one_back)
    settle(sent_b)
    g_i.z_forward()
    g_k.plane_send()
    g_g.end()
    in_order(r.l_gu, 0, CF, r.grad_mlp_gate, r.grad_mlp_gate)
    g_u.end()
    g_v.end()
    in_order(r.l_gu, CF, CF, r.grad_mlp_up, r.grad_mlp_up)
    g_b.end()
    in_order(r.l_ib, CW, CW, r.grad_branch_weight, r.grad_branch_weight)
    g_o.end()
    small_grad.two()
    g_d.end()
    g_j.end()
    in_order(r.l_di, 0, CW, r.grad_decay_weight, r.grad_decay_weight)
    g_k.end()
    in_order(r.l_di, CW, CW, r.grad_inject_weight, r.grad_inject_weight)
    g_i.end()
    assert not sent


WEIGHTS = (
    "branch_weight",
    "input_weight",
    "decay_weight",
    "inject_weight",
    "output_weight",
    "mlp_gate",
    "mlp_up",
    "mlp_down",
)


def run_layer(NL, tokens, cotangent, small, weights):
    T, D = tokens.shape
    SEGS = small["doc_lengths"].shape[1]
    W, F = weights["branch_weight"].shape[1], weights["mlp_gate"].shape[1]
    CW, CF = W // PLANE, F // PLANE
    RD, RW, RF = D // SHARES, W // SHARES, F // SHARES
    GL, M, places = PLANE * RD, PLANE * T, RING * NL * 2
    hbm = pl.BlockSpec(memory_space=pl.ANY)
    ins = ["tokens", "cotangent", *small, *WEIGHTS]
    outs = dict(
        activations=((T, D), bf16),
        d_tokens=((T, D), f32),
        grad_input_weight=((RD, W), f32),
        grad_branch_weight=((RD, W), f32),
        grad_decay_weight=((RW, W), f32),
        grad_inject_weight=((RW, W), f32),
        grad_output_weight=((RW, D), f32),
        grad_mlp_gate=((RD, F), f32),
        grad_mlp_up=((RD, F), f32),
        grad_mlp_down=((RF, D), f32),
        small_out=((8, 128), f32),
    )
    columns = (("i", RD, CW), ("b", RD, CW), ("d", RW, CW), ("j", RW, CW), ("g", RD, CF), ("u", RD, CF))
    scratch = dict(
        w_ib=((RING, 2, PLANE * RD, 2 * CW), bf16),
        w_di=((RING, 2, PLANE * RW, 2 * CW), bf16),
        w_gu=((RING, 2, PLANE * RD, 2 * CF), bf16),
        w_o=((RING, 2, RW, D), bf16),
        w_dn=((RING, 2, RF, D), bf16),
        **{"raw_" + n: ((R, PLANE * C), bf16) for n, R, C in columns},
        **{"sort_" + n: ((PLANE, R, C), bf16) for n, R, C in columns},
        h_ib=((RING, PLANE * RD, 2 * CW), bf16),
        h_di=((RING, PLANE * RW, 2 * CW), bf16),
        h_gu=((RING, PLANE * RD, 2 * CF), bf16),
        h_o=((RING, RW, D), bf16),
        h_dn=((RING, RF, D), bf16),
        z_ib=((4, PLANE * RD, 2 * CW), bf16),
        z_di=((4, PLANE * RW, 2 * CW), bf16),
        z_gu=((4, PLANE * RD, 2 * CF), bf16),
        z_o=((4, RW, D), bf16),
        z_dn=((4, RF, D), bf16),
        l_ib=((PLANE, RD, 2 * CW), bf16),
        l_di=((PLANE, RW, 2 * CW), bf16),
        l_gu=((PLANE, RD, 2 * CF), bf16),
        n_one=((PLANE, T, D), bf16),
        n_two=((PLANE, T, D), bf16),
        cot_all=((PLANE, T, D), bf16),
        d_out=((PLANE, T, D), bf16),
        conv=((PLANE, M, CW), bf16),
        part=((PLANE, T, D), bf16),
        part_act=((PLANE, T, D), bf16),
        part_conv=((PLANE, M, CW), bf16),
        got_one=((6, T // 2, D), bf16),
        got_two=((6, T // 2, D), bf16),
        got_three=((6, T // 2, D), bf16),
        got_act=((6, T // 2, D), bf16),
        got_conv=((6, M // 2, CW), bf16),
        mixed=((M, CW), bf16),
        hidden=((M, CF), bf16),
        d_pair=((M, 2 * CF), bf16),
        d_gu=((M, 2 * CW), bf16),
        d_pre=((M, 2 * CW), bf16),
        pair=((M, 2 * CF), f32),
        u=((PLANE, T + 8, CW), f32),
        state=((PLANE, T + 8, CW), f32),
        d_conv=((PLANE, T + 8, CW), f32),
        **{name: ((M, CW), f32) for name in ("gated", "slope", "rgate", "igate", "decay", "work", "cum")},
        x_one=((T, D), f32),
        d_one=((T, D), f32),
        carry_f=((RING * NL, 2 * PLANE, CW), f32),
        carry_b=((RING * NL, 2 * PLANE, CW), f32),
        **{name: ((2 * PLANE, CW), f32) for name in ("own_f", "sib_f", "own_b", "sib_b")},
        halo_out=((16, CW), f32),
        halo_in=((16, CW), f32),
        into=((8, CW), f32),
        x_all=((PLANE, T, D), bf16),
        x_halo=((PLANE, 16, D), bf16),
        n_halo=((PLANE, 16, D), bf16),
        g_dn=((RING, 2, RF, D), bf16),
        masks=((7, M, 128), f32),
        pack=((16, 128), bf16),
        gain_a=((1, RD), bf16),
        gain_b=((1, RD), bf16),
        taps=((4, RW), bf16),
        bias_a=((1, RW), bf16),
        bias_b=((1, RW), bf16),
        bias_c=((1, RW), bf16),
        lens=((1, SEGS), jnp.int32),
        rates=((W // 128, 128), jnp.int32),
        pr=((2 * RING, 16, 128), bf16),
        line=((16, 128), bf16),
        pp=((PLANE, 16, 128), bf16),
        st_i=((PLANE, RING, RD, CW), bf16),
        z_i=((4, PLANE, RD, CW), bf16),
        gains=((8, D), f32),
        chan=((8, CW), f32),
        gchan=((8, CW), f32),
        gs=((2 * RING, 8, 128), f32),
        gg=((2 * RING, 8, 128), f32),
    )
    dims = SimpleNamespace(
        T=T, D=D, W=W, F=F, CW=CW, CF=CF, RD=RD, RW=RW, RF=RF, NL=NL, SEGS=SEGS, receives=RECEIVES + 2 * RING * NL, names=[*ins, *outs, *scratch, "ss", "rs"]
    )
    flops = 3 * 2 * M * (D * 2 * CW + W * 2 * CW + CW * D + 3 * D * CF)
    results = pl.pallas_call(
        partial(layer, dims),
        out_shape=[pltpu.VMEM(shape, kind) for shape, kind in outs.values()],
        in_specs=[hbm] * len(ins),
        out_specs=[pl.BlockSpec(memory_space=pltpu.VMEM)] * len(outs),
        scratch_shapes=[pltpu.VMEM(shape, kind) for shape, kind in scratch.values()]
        + [pltpu.SemaphoreType.DMA((SENDS,)), pltpu.SemaphoreType.DMA((dims.receives,))],
        compiler_params=pltpu.CompilerParams(
            collective_id=0, has_side_effects=True, vmem_limit_bytes=58 * 2**20
        ),
        cost_estimate=pl.CostEstimate(flops=flops, bytes_accessed=8 * 2**20, transcendentals=M * CW * 16),
        name="griffin_layer",
    )(tokens, cotangent, *small.values(), *[weights[name] for name in WEIGHTS])
    return finish({**small, **dict(zip(outs, results, strict=True))}, weights)


def finish(got, weights):
    hbm = pl.BlockSpec(memory_space=pl.ANY)
    behind = {"first_gain": ("input_weight", "branch_weight"), "second_gain": ("mlp_gate", "mlp_up")}
    RD, RW = got["grad_input_weight"].shape[0], got["grad_decay_weight"].shape[0]
    channels = {"conv_taps": (0, 4), "conv_bias": (4, 5), "decay_bias": (5, 6), "inject_bias": (6, 7)}
    shared = [name for names in behind.values() for name in names]
    rest = ["grad_" + name for name in WEIGHTS if name not in shared]
    plain = [*["grad_" + name for name in shared], *rest, "d_tokens", "activations"]
    source = {**got, **{name: weights[name] for name in shared}}
    names = ["small_out", *shared, *plain]
    shapes = {name: got[name] for name in plain}
    for name in behind:
        shapes["grad_" + name] = jax.ShapeDtypeStruct((1, RD), f32)
    for name, (low, high) in channels.items():
        shapes["grad_" + name] = jax.ShapeDtypeStruct((high - low, RW), f32)
    fetched = shared
    scratch = {name: (source[name].shape, source[name].dtype) for name in fetched}
    scratch.update({name: (like.shape, f32) for name, like in shapes.items() if name not in plain})

    def body(*refs):
        ins = dict(zip(names, refs[: len(names)], strict=True))
        outs = dict(zip(shapes, refs[len(names) : len(names) + len(shapes)], strict=True))
        held, sems = dict(zip(scratch, refs[len(names) + len(shapes) : -1], strict=True)), refs[-1]
        copies = []

        def copy(src, dst):
            copies.append(pltpu.make_async_copy(src, dst, sems.at[len(copies)]))
            copies[-1].start()
            return copies[-1]

        loads = {name: copy(ins[name], held[name]) for name in fetched}
        held.update({name: ins[name] for name in names if name not in fetched})
        stores = []

        def store(name):
            stores.append(copy(held[name], outs[name]))

        for name, (low, high) in channels.items():
            held["grad_" + name][...] = held["small_out"][low:high, 0:RW]
            store("grad_" + name)
        for name in plain:
            store(name)
        for i, (gain, pair) in enumerate(behind.items()):
            sums = jnp.zeros((RD, 128), f32)
            for name in pair:
                loads[name].wait()
                product = held["grad_" + name][...] * held[name][...].astype(f32)
                sums = sums + sum(product[:, k * 128 : (k + 1) * 128] for k in range(product.shape[1] // 128))
            total = lax.dot_general(
                jnp.ones((8, 128), f32),
                sums,
                (((1,), (1,)), ((), ())),
                precision=lax.Precision.HIGHEST,
                preferred_element_type=f32,
            )
            held["grad_" + gain][...] = total[0:1] / held["small_out"][7:8, i * RD : (i + 1) * RD]
            store("grad_" + gain)
        for each in stores:
            each.wait()

    results = pl.pallas_call(
        body,
        out_shape=[jax.ShapeDtypeStruct(like.shape, like.dtype) for like in shapes.values()],
        in_specs=[hbm if name in fetched else pl.BlockSpec(memory_space=pltpu.VMEM) for name in names],
        out_specs=[hbm] * len(shapes),
        scratch_shapes=[
            *[pltpu.VMEM(shape, kind) for shape, kind in scratch.values()],
            pltpu.SemaphoreType.DMA((len(names) + len(shapes),)),
        ],
        compiler_params=pltpu.CompilerParams(vmem_limit_bytes=24 * 2**20),
        name="finish",
    )(*[source[name] for name in names])
    return {**got, **dict(zip(shapes, results, strict=True))}


def local(
    sizes,
    tokens,
    cotangent,
    doc_lengths,
    decay_exponent,
    branch_weight,
    input_weight,
    decay_weight,
    inject_weight,
    output_weight,
    mlp_gate,
    mlp_up,
    mlp_down,
    first_gain,
    second_gain,
    conv_taps,
    conv_bias,
    decay_bias,
    inject_bias,
):
    devices = math.prod(sizes.values())
    at = {name: lax.axis_index(name) for name in AXES}
    mine = at["yl"] * 2 + at["xl"]
    ring = at["zh"] * 2 + at["c"]
    share = ring * PLANE + mine
    groups = devices // SHARES

    def pooled(value, axis=0):
        if groups == 1:
            return value
        whole = lax.all_gather(value, AXES, axis=axis, tiled=True)
        size = whole.shape[axis] // SHARES
        return lax.dynamic_slice_in_dim(whole, share * size, size, axis)

    small = dict(
        first_gain=pooled(first_gain[None], 1),
        second_gain=pooled(second_gain[None], 1),
        conv_taps=pooled(conv_taps.T, 1),
        conv_bias=pooled(conv_bias[None], 1),
        decay_bias=pooled(decay_bias[None], 1),
        inject_bias=pooled(inject_bias[None], 1),
        doc_lengths=doc_lengths,
        decay_exponent=decay_exponent.reshape(-1, 128),
    )
    weights = dict(
        zip(
            WEIGHTS,
            (branch_weight, input_weight, decay_weight, inject_weight, output_weight, mlp_gate, mlp_up, mlp_down),
            strict=True,
        )
    )
    weights = {name: pooled(value) for name, value in weights.items()}
    got = run_layer(sizes["zl"], tokens[0], cotangent[0], small, weights)

    def returned(value, axis=0):
        if groups == 1:
            return value
        shape = list(value.shape)
        size = shape[axis]
        shape[axis] = size * SHARES
        whole = lax.dynamic_update_slice_in_dim(jnp.zeros(shape, bf16), value.astype(bf16), share * size, axis)
        return lax.psum_scatter(whole, AXES, scatter_dimension=axis, tiled=True).astype(f32)

    grads = [returned(got["grad_" + name]) for name in WEIGHTS]
    first, second, taps, *biases = (
        returned(got["grad_" + name], 1)
        for name in ("first_gain", "second_gain", "conv_taps", "conv_bias", "decay_bias", "inject_bias")
    )
    return (
        got["activations"][None],
        got["d_tokens"][None],
        *grads,
        first[0],
        second[0],
        taps.T,
        *[bias[0] for bias in biases],
    )


def solution(mesh):
    seq, dp = mesh.shape["seq"], mesh.shape["dp"]
    across = 1 << ((dp.bit_length() - 1) // 2)
    sizes = dict(zip(AXES, (RING, seq // (2 * RING), 2, dp // across // 2, 2, across // 2, 2), strict=True))
    split = Mesh(mesh.devices.reshape(tuple(sizes.values())), AXES)
    along_seq, along_dp = AXES[:3], AXES[3:]
    rows = P(along_dp, along_seq, None)
    in_specs = (rows, rows, P(along_dp, None), P(), *[P(AXES, None)] * 8, P(AXES), P(AXES), P(AXES, None), *[P(AXES)] * 3)
    out_specs = (rows, rows, *[P(AXES, None)] * 8, P(AXES), P(AXES), P(AXES, None), *[P(AXES)] * 3)
    return jax.shard_map(partial(local, sizes), mesh=split, in_specs=in_specs, out_specs=out_specs, check_vma=False)
```

```python
import itertools
import math
from functools import cached_property, partial
from types import SimpleNamespace

import jax
import jax.numpy as jnp
from jax import lax
from jax.experimental import pallas as pl
from jax.experimental.pallas import tpu as pltpu
from jax.sharding import Mesh, PartitionSpec as P

f32, bf16 = jnp.float32, jnp.bfloat16
MESH = pl.DeviceIdType.MESH
AXES = ("zh", "zl", "c", "yh", "yl", "xh", "xl")
RING = 4
PLANE = 4
SHARES = RING * 2 * PLANE
SENDS = 53
RECEIVES = 180

eps_norm = 1e-06
floor_gap = 1e-05
rate_scale = 8.0
gelu_root = math.sqrt(2.0 / math.pi)
gelu_cube = 0.044715


def dot(left, right):
    return jnp.dot(left, right, preferred_element_type=f32)


def dot_nt(left, right):
    return lax.dot_general(left, right, (((1,), (1,)), ((), ())), preferred_element_type=f32)


def dot_tn(left, right):
    return lax.dot_general(left, right, (((0,), (0,)), ((), ())), preferred_element_type=f32)


def gelu_parts(v):
    t = jnp.tanh(gelu_root * (v + gelu_cube * v * v * v))
    half = 0.5 * (1.0 + t)
    slope = half + 0.5 * v * (1.0 - t * t) * gelu_root * (1.0 + 3.0 * gelu_cube * v * v)
    return v * half, slope


def minus_expm1(y, root):
    poly = 1.0 + y * (1.0 / 7.0)
    for k in (6, 5, 4, 3, 2):
        poly = 1.0 + y * poly * (1.0 / k)
    return jnp.where(y > -0.35, -y * poly, 1.0 - root * root)


def inverse_rms(v):
    return lax.rsqrt(jnp.mean(v * v, axis=-1, keepdims=True) + eps_norm)


def unsorted(parts):
    size = parts[0].shape[1] // (2 * RING)
    return jnp.concatenate([part[:, g * size : (g + 1) * size] for g in range(2 * RING) for part in parts], axis=1)


def loop(total, step, body):
    def run(j, _):
        body(pl.multiple_of(j * step, step))
        return 0

    lax.fori_loop(0, total // step, run, 0)


def layer(dims, *refs):
    T, D, W, F, CW, CF = dims.T, dims.D, dims.W, dims.F, dims.CW, dims.CF
    RD, RW, RF, NL = dims.RD, dims.RW, dims.RF, dims.NL
    M = PLANE * T
    r = SimpleNamespace(**dict(zip(dims.names, refs, strict=True)))

    zh, zl, c = lax.axis_index("zh"), lax.axis_index("zl"), lax.axis_index("c")
    yl, xl = lax.axis_index("yl"), lax.axis_index("xl")
    p = yl * 2 + xl
    px, py, pd = yl * 2 + (1 - xl), (1 - yl) * 2 + xl, (1 - yl) * 2 + (1 - xl)
    to_x, to_y, to_d = {"xl": 1 - xl}, {"yl": 1 - yl}, {"yl": 1 - yl, "xl": 1 - xl}
    plane_peers = ((px, to_x), (py, to_y), (pd, to_d))
    to_core = {"c": 1 - c}
    flat_z = zh * NL + zl
    places = RING * NL * 2
    pos = flat_z * 2 + c

    def place(at):
        return {"zh": at // (2 * NL), "zl": (at // 2) % NL, "c": at % 2}

    count = itertools.count()

    def new(n=1):
        first = next(count)
        for _ in range(n - 1):
            next(count)
        assert first + n <= dims.receives
        return first

    spare = list(range(SENDS))
    sent = []

    def push(src, dst, dev, rsem, pred=None, instead=None):
        i = spare.pop(0) if instead is None else instead[2]

        def make():
            return pltpu.make_async_remote_copy(
                src, dst, r.ss.at[i], r.rs.at[rsem], device_id=dev, device_id_type=MESH
            )

        if pred is None:
            make().start()
        else:
            pl.when(pred)(lambda: make().start())
        entry = (make, pred, i, instead is None)
        sent.append(entry)
        return entry

    def settle(*entries):
        for entry in entries:
            make, pred, i, owner = entry
            if pred is None:
                make().wait_send()
            else:
                pl.when(pred)(lambda make=make: make().wait_send())
            sent.remove(entry)
            if owner:
                spare.append(i)

    def arrived(dst, rsem, pred=None):
        def wait():
            pltpu.make_async_remote_copy(
                dst, dst, r.ss.at[0], r.rs.at[rsem], device_id=to_core, device_id_type=MESH
            ).wait_recv()

        if pred is None:
            wait()
        else:
            pl.when(pred)(wait)

    def keep_local(src, dst, rsem):
        pltpu.make_async_copy(src, dst, r.rs.at[rsem]).start()

    def local_wait(src, dst, rsem):
        pltpu.make_async_copy(src, dst, r.rs.at[rsem]).wait()

    def ds(start, size, unit):
        return pl.ds(pl.multiple_of(start, unit), size)

    class Gather:
        def __init__(self, buf):
            self.buf, half = buf, buf.shape[1] // 2
            self.h0, self.h1 = pl.ds(0, half), pl.ds(half, half)
            self.rx0, self.rx1, self.ry0, self.ry1, self.rd = (new() for _ in range(5))
            self.out = []

        def start(self):
            b = self.buf
            own0, own1 = b.at[p, self.h0], b.at[p, self.h1]
            self.out.append(push(own0, own0, to_x, self.rx0))
            self.out.append(push(own1, own1, to_y, self.ry1))
            self.out.append(push(own1, own1, to_x, self.rx1))
            self.out.append(push(own0, own0, to_y, self.ry0))

        def mid(self):
            b = self.buf
            got0, got1 = b.at[px, self.h0], b.at[py, self.h1]
            arrived(got0, self.rx0)
            self.out.append(push(got0, got0, to_y, self.rd))
            arrived(got1, self.ry1)
            self.out.append(push(got1, got1, to_x, self.rd))

        def wait_x(self):
            arrived(self.buf.at[px, self.h1], self.rx1)

        def wait_y(self):
            arrived(self.buf.at[py, self.h0], self.ry0)

        def wait_d(self):
            arrived(self.buf.at[pd], self.rd)

        def end(self):
            self.wait_x()
            self.wait_y()
            self.wait_d()
            settle(*self.out)

    class Scatter:
        def __init__(self, buf, recv):
            self.buf, self.recv = buf, recv
            self.half = buf.shape[1] // 2
            self.h0, self.h1 = pl.ds(0, self.half), pl.ds(self.half, self.half)
            self.sems = [new(), new(), *[new()] * 4]
            self.out = []

        def start(self):
            self.start_far()
            self.start_near()

        def start_far(self):
            b, v, s = self.buf, self.recv, self.sems
            self.out.append(push(b.at[pd, self.h0], v.at[0], to_x, s[0]))
            self.out.append(push(b.at[pd, self.h1], v.at[1], to_y, s[1]))

        def start_near(self):
            b, v, s = self.buf, self.recv, self.sems
            self.out.append(push(b.at[px, self.h0], v.at[2], to_x, s[2]))
            self.out.append(push(b.at[py, self.h1], v.at[3], to_y, s[3]))

        def mid(self):
            b, v, s = self.buf, self.recv, self.sems
            arrived(v.at[0], s[0])
            step = 16

            def add0(o):
                b[py, pl.ds(o, step)] = (b[py, pl.ds(o, step)].astype(f32) + v[0, pl.ds(o, step)].astype(f32)).astype(bf16)

            loop(self.half, step, add0)
            self.out.append(push(b.at[py, self.h0], v.at[4], to_y, s[4]))
            arrived(v.at[1], s[1])

            def add1(o):
                q = pl.ds(pl.multiple_of(self.half + o, step), step)
                b[px, q] = (b[px, q].astype(f32) + v[1, pl.ds(o, step)].astype(f32)).astype(bf16)

            loop(self.half, step, add1)
            self.out.append(push(b.at[px, self.h1], v.at[5], to_x, s[5]))

        def end(self):
            arrived(self.recv.at[pl.ds(2, 4)], self.sems[2])
            settle(*self.out)

        def total(self, half, o, step):
            b, v = self.buf, self.recv
            own = b[p, pl.ds(pl.multiple_of(half * self.half + o, step), step)].astype(f32)
            q = pl.ds(o, step)
            return own + v[2 + half, q].astype(f32) + v[4 + half, q].astype(f32)

        def each(self, step, body, init=None):
            for half in (0, 1):

                def run(j, carry, half=half):
                    o = pl.multiple_of(j * step, step)
                    return body(pl.multiple_of(half * self.half + o, step), self.total(half, o, step), carry)

                init = lax.fori_loop(0, self.half // step, run, init)
            return init

    def z_send(src, block, rz, away=(2, 1)):
        out = []
        if 2 in away:
            out.append(push(src, block(zh), {"zh": zh + 2}, rz + zh, zh + 2 < RING))
            out.append(push(src, block(zh), {"zh": zh - 2}, rz + zh, zh - 2 >= 0, out[-1]))
        if 1 in away:
            out.append(push(src, block(zh), {"zh": zh + 1}, rz + zh, zh + 1 < RING))
            out.append(push(src, block(zh), {"zh": zh - 1}, rz + zh, zh - 1 >= 0))
        return out

    def z_forward(block, rz):
        last = RING - 1
        arrived(block(0), rz, zh == last - 1)
        one = push(block(0), block(0), {"zh": zh + 1}, rz, zh == last - 1)
        arrived(block(last), rz + last, zh == 1)
        two = push(block(last), block(last), {"zh": zh - 1}, rz + last, zh == 1, one)
        return [one, two]

    def z_wait(block, rz, use):
        last = RING - 1

        def take(k, pred, waited=None, instead=None):
            arrived(block(k), rz + k, pred if waited is None else pred & ~waited)
            return use(block(k), pred, instead)

        out = [take(zh - 1, zh >= 1), take(zh + 1, zh < last)]
        out.append(take(zh - 2, zh >= 2, zh == last - 1))
        out.append(take(zh + 2, zh <= 1, zh == 1, out[-1]))
        out.append(take(0, zh == last))
        out.append(take(last, zh == 0, None, out[-1]))
        return out

    class ZSum:
        def __init__(self, block, slot, add, direct):
            self.block, self.slot, self.add, self.direct = block, slot, add, direct
            self.valid = (direct | (zh >= 1), zh >= 2, direct | (zh <= 2), zh <= 1)
            self.sems = new(4)
            self.out = []

        def send(self):
            b, v, s = self.block, self.slot, self.sems
            last = RING - 1
            o = self.out
            if self.direct:
                o.append(push(b(last), v(2), {"zh": zh + last}, s + 2, zh == 0))
                o.append(push(b(0), v(0), {"zh": zh - last}, s + 0, zh == last, o[-1]))
                o.append(push(b(zh + 2), v(1), {"zh": zh + 2}, s + 1, zh <= 1))
                o.append(push(b(zh - 2), v(3), {"zh": zh - 2}, s + 3, zh >= 2, o[-1]))
            else:
                o.append(push(b(last), v(1), {"zh": zh + 1}, s + 1, zh == 0))
                o.append(push(b(0), v(3), {"zh": zh - 1}, s + 3, zh == last, o[-1]))
                o.append(push(b(zh + 2), v(1), {"zh": zh + 2}, s + 1, zh == 0))
                o.append(push(b(zh - 2), v(3), {"zh": zh - 2}, s + 3, zh == last, o[-1]))
            o.append(push(b(zh + 1), v(0), {"zh": zh + 1}, s + 0, zh < last))
            o.append(push(b(zh - 1), v(2), {"zh": zh - 1}, s + 2, zh > 0))

        def forward(self):
            b, v, s = self.block, self.slot, self.sems
            last = RING - 1

            def up():
                arrived(v(1), s + 1)
                self.add(last, 1)

            def down():
                arrived(v(3), s + 3)
                self.add(0, 3)

            pl.when(zh == 1)(up)
            self.out.append(push(b(last), v(1), {"zh": zh + 2}, s + 1, zh == 1))
            pl.when(zh == last - 1)(down)
            self.out.append(push(b(0), v(3), {"zh": zh - 2}, s + 3, zh == last - 1, self.out[-1]))

        def end(self):
            for k, valid in enumerate(self.valid):
                arrived(self.slot(k), self.sems + k, valid)
            settle(*self.out)

        def total(self, own, parts):
            for part, pred in zip(parts, self.valid, strict=True):
                own = own + jnp.where(pred, part.astype(f32), 0.0)
            return own

    class Column:
        def __init__(self, src, raw, sorted_, w, R, C, lane0):
            self.src, self.raw, self.sorted = src, raw, sorted_
            self.w, self.R, self.C, self.lanes = w, R, C, pl.ds(lane0, C)
            self.out = []

        rl = cached_property(lambda self: new())
        ra = cached_property(lambda self: new())
        rz = cached_property(lambda self: new(4))
        rc = cached_property(lambda self: new())

        def halves(self):
            out = []
            for k in (0, 1):
                part = Column(self.src, self.raw, self.sorted, self.w, self.R, self.C, 0)
                part.lanes = pl.ds(self.lanes.start + k * self.C // 2, self.C // 2)
                out.append(part)
            return out

        def spread_wait(self):
            arrived(self.block(zh), self.ra)
            settle(*self.out)
            self.out = []

        def load(self):
            keep_local(self.src, self.raw, self.rl)

        def prepare(self):
            local_wait(self.src, self.raw, self.rl)
            value, part = self.raw[...], self.C // (2 * RING)
            for k in range(PLANE):
                first = [(g * PLANE + k) * part for g in range(2 * RING)]
                self.sorted[k] = jnp.concatenate([value[:, at : at + part] for at in first], axis=1)

        def spread(self):
            dst = self.w.at[zh, c, ds(p * self.R, self.R, 16), self.lanes]
            for k, dev in plane_peers:
                self.out.append(push(self.sorted.at[k], dst, dev, self.ra))
            keep_local(self.sorted.at[p], dst, self.ra)

        def block(self, z):
            return self.w.at[z, c, :, self.lanes]

        def z_send(self, spread=True):
            if spread:
                arrived(self.block(zh), self.ra)
            self.out += z_send(self.block(zh), self.block, self.rz)
            self.out.append(self.core_push(self.block(zh)))

        def z_forward(self):
            self.out += z_forward(self.block, self.rz)

        def core_push(self, block, pred=None, instead=None):
            return push(block, block, to_core, self.rc, pred, instead)

        def z_wait(self):
            self.out += z_wait(self.block, self.rz, self.core_push)

        def end(self):
            arrived(self.w.at[:, 1 - c, :, self.lanes], self.rc)
            settle(*self.out)

    class Row(Column):
        def __init__(self, src, w):
            self.src, self.w, self.lanes = src, w, pl.ds(0, w.shape[3])
            self.out = []

        def z_send(self, away=(2, 1)):
            if 2 in away:
                keep_local(self.src, self.block(zh), self.ra)
            self.out += z_send(self.src, self.block, self.rz, away)

        def z_wait(self):
            pltpu.make_async_copy(self.src, self.block(zh), r.rs.at[self.ra]).wait()
            self.out.append(self.core_push(self.block(zh)))
            super().z_wait()

    class ColumnsGrad:
        def __init__(self, g, other, slots, land, R, lane0, lanes, direct=False):
            self.g, self.other, self.slots, self.land = g, other, slots, land
            self.R, self.lanes = R, pl.ds(lane0, lanes)
            self.rows = PLANE * R
            self.rc, self.rl = new(), new()
            self.zsum = ZSum(
                lambda z: g.at[z, c, :, self.lanes], lambda k: slots.at[k, :, self.lanes], self.add_slot, direct
            )

        def add_slot(self, z, k):
            g, q = self.g, self.lanes

            def add(o):
                s = pl.ds(o, 16)
                g[z, c, s, q] = (g[z, c, s, q].astype(f32) + self.slots[k, s, q].astype(f32)).astype(bf16)

            loop(self.rows, 16, add)

        def core_send(self):
            self.pushed = push(
                self.g.at[:, 1 - c, :, self.lanes], self.other.at[:, :, self.lanes], to_core, self.rc
            )

        def core_sum(self):
            g, q = self.g, self.lanes
            arrived(self.other.at[:, :, q], self.rc)
            settle(self.pushed)
            for z in range(RING):

                def add(o):
                    s = pl.ds(o, 16)
                    g[z, c, s, q] = (g[z, c, s, q].astype(f32) + self.other[z, s, q].astype(f32)).astype(bf16)

                loop(self.rows, 16, add)

        def z_send(self):
            self.core_sum()
            self.zsum.send()

        def z_forward(self):
            self.zsum.forward()

        def plane_send(self):
            g, q, R = self.g, self.lanes, self.R
            self.zsum.end()

            def add(o):
                s = pl.ds(o, 16)
                parts = [self.slots[k, s, q] for k in range(4)]
                g[zh, c, s, q] = self.zsum.total(g[zh, c, s, q].astype(f32), parts).astype(bf16)

            loop(PLANE * R, 16, add)
            dst = self.land.at[p, :, q]
            self.out = []
            for k, dev in plane_peers:
                self.out.append(push(g.at[zh, c, ds(k * R, R, 16), q], dst, dev, self.rl))
            keep_local(g.at[zh, c, ds(p * R, R, 16), q], dst, self.rl)

        def end(self):
            arrived(self.land.at[:, :, self.lanes], self.rl)
            settle(*self.out)

    def in_order(land, lane0, C, held, result):
        held[...] = unsorted([land[k, :, lane0 : lane0 + C].astype(f32) for k in range(PLANE)])

    class LastGrad(ColumnsGrad):
        def __init__(self, g, other, stage, slots, R, lane0, lanes, total, result):
            super().__init__(g, other, slots, None, R, lane0, lanes)
            self.stage, self.sum, self.result = stage, total, result
            self.zsum.block, self.zsum.slot = (lambda z: stage.at[:, z]), (lambda k: slots.at[k])

        def add_slot(self, z, k):
            for q in range(PLANE):
                self.stage[q, z] = (self.stage[q, z].astype(f32) + self.slots[k, q].astype(f32)).astype(bf16)

        def plane_send(self):
            R, dst = self.R, self.stage.at[p]
            self.core_sum()
            self.out = []
            for k, dev in plane_peers:
                self.out.append(push(self.g.at[:, c, ds(k * R, R, 16), self.lanes], dst, dev, self.rl))
            keep_local(self.g.at[:, c, ds(p * R, R, 16), self.lanes], dst, self.rl)

        def z_send(self):
            arrived(self.stage, self.rl)
            self.zsum.send()

        def end(self):
            self.zsum.end()
            settle(*self.out)
            values = [
                self.zsum.total(self.stage[q, zh].astype(f32), [self.slots[k, q] for k in range(4)]) for q in range(PLANE)
            ]
            self.sum[...] = unsorted(values)

    def gain_grad(gain, *pairs):
        sums = jnp.zeros((RD, 128), f32)
        for grad, weight in pairs:
            product = grad[...] * weight[...].astype(f32)
            sums = sums + sum(product[:, k * 128 : (k + 1) * 128] for k in range(product.shape[1] // 128))
        total = lax.dot_general(
            jnp.ones((8, 128), f32),
            sums,
            (((1,), (1,)), ((), ())),
            precision=lax.Precision.HIGHEST,
            preferred_element_type=f32,
        )
        return total[0:1] / gain[...].astype(f32)

    class RowsGrad(ColumnsGrad):
        def __init__(self, g, other, slots, total, result):
            super().__init__(g, other, slots, None, 0, 0, g.shape[3])
            self.rows, self.sum, self.result = g.shape[2], total, result

        def end(self):
            self.zsum.end()

            def add(o):
                s = pl.ds(o, 16)
                self.sum[s] = self.zsum.total(self.g[zh, c, s].astype(f32), [self.slots[k, s] for k in range(4)])

            loop(self.rows, 16, add)

    class Carry:
        def __init__(self, own, sib, buf, later):
            self.own, self.sib, self.buf, self.later = own, sib, buf, later
            self.rc, self.rz = new(), new(RING * NL)
            self.out = []

        def order(self):
            return range(RING * NL) if self.later else reversed(range(RING * NL))

        def send_core(self):
            self.out.append(push(self.own, self.sib, to_core, self.rc))

        def send(self):
            arrived(self.sib, self.rc)
            own, sib = self.own[...], self.sib[...]
            near = (c == 0) if self.later else (c == 1)
            head, tail = jnp.where(near, own, sib), jnp.where(near, sib, own)
            self.buf[flat_z, 0:PLANE] = tail[0:PLANE] * head[0:PLANE]
            self.buf[flat_z, PLANE : 2 * PLANE] = (
                tail[0:PLANE] * head[PLANE : 2 * PLANE] + tail[PLANE : 2 * PLANE]
            )
            part = self.buf.at[flat_z]
            for at in self.order():
                pred = (flat_z < at) if self.later else (flat_z > at)
                self.out.append(push(part, part, {"zh": at // NL, "zl": at % NL}, self.rz + flat_z, pred))

        def fold(self, into):
            into[...] = jnp.zeros_like(into)

            def take(part):
                into[0:PLANE] = part[0:PLANE] * into[0:PLANE] + part[PLANE : 2 * PLANE]

            for at in self.order():
                pred = (flat_z > at) if self.later else (flat_z < at)

                def chip(at=at):
                    arrived(self.buf.at[at], self.rz + at)
                    take(self.buf[at])

                pl.when(pred)(chip)
            pl.when((c == 1) if self.later else (c == 0))(lambda: take(self.sib[...]))
            settle(*self.out)

    GL = PLANE * RD
    ring = zh * 2 + c

    def ring_place(at):
        return {"zh": at // 2, "c": at % 2}

    class Small:
        def __init__(self):
            self.rr, self.rk = new(), new()
            self.out = []

        def pack(self):
            for load in small_loads:
                local_wait(*load)
            lengths = r.lens[...]
            rows = [r.gain_a[...], r.gain_b[...], r.taps[...], r.bias_a[...], r.bias_b[...], r.bias_c[...]]
            rows += [lax.shift_right_logical(lengths, 8), lengths & 255]
            rows = [row.astype(f32) for row in rows]
            rows = [jnp.concatenate([row, jnp.zeros((row.shape[0], 128 - row.shape[1]), f32)], axis=1) for row in rows]
            r.pack[...] = jnp.concatenate([*rows, jnp.zeros((5, 128), f32)], axis=0).astype(bf16)

        def one(self):
            for at in range(2 * RING):
                self.out.append(push(r.pack, r.pr.at[ring], ring_place(at), self.rr, ring != at))
            keep_local(r.pack, r.pr.at[ring], self.rr)

        def two(self):
            arrived(r.pr, self.rr)
            lines = []
            for at in range(2 * RING):
                tile = r.pr[at].astype(f32)
                lines.append(jnp.concatenate([tile[row : row + 1, 0:32] for row in (0, 1, 9, 10)], axis=1))
            r.line[...] = jnp.concatenate([*lines, jnp.zeros((16 - 2 * RING, 128), f32)], axis=0).astype(bf16)
            for _, dev in plane_peers:
                self.out.append(push(r.line, r.pp.at[p], dev, self.rk))
            keep_local(r.line, r.pp.at[p], self.rk)

        def three(self):
            arrived(r.pp, self.rk)
            parts = [r.pp[k].astype(f32) for k in range(PLANE)]
            for row in (0, 1):
                lanes = slice(row * 32, row * 32 + RD)
                wide = jnp.concatenate([part[:, lanes] for part in parts], axis=1)
                for at in range(2 * RING):
                    r.gains[row : row + 1, at * GL : (at + 1) * GL] = wide[at : at + 1]
            whole = jnp.concatenate([r.pr[at, :, 0:RW].astype(f32) for at in range(2 * RING)], axis=1)
            r.chan[...] = whole[2:10]
            rates = r.rates[...].astype(f32)
            rates = jnp.concatenate([rates[k : k + 1] for k in range(W // 128)], axis=1)
            mine = jnp.zeros((1, CW), f32)
            for k in range(PLANE):
                at = [(g * PLANE + k) * RW for g in range(2 * RING)]
                mine = jnp.where(p == k, jnp.concatenate([rates[:, o : o + RW] for o in at], axis=1), mine)
            r.chan[7:8] = jnp.exp2(-mine)

        def four(self):
            where = lax.broadcasted_iota(jnp.int32, (T, 128), 0).astype(f32) + (pos * T).astype(f32)
            for k in range(PLANE):
                part = r.pp[k].astype(f32)
                starts, ends = [], []
                total = jnp.zeros((1, 1), f32)
                for j in range(dims.SEGS):
                    starts.append(total)
                    total = total + part[0:1, 64 + j : 65 + j] * 256.0 + part[0:1, 96 + j : 97 + j]
                    ends.append(total)

                def seg(shift):
                    at = where + float(shift)
                    value = jnp.zeros((T, 128), f32)
                    for end in ends:
                        value = value + jnp.where(at >= end, 1.0, 0.0)
                    return jnp.where((at < 0.0) | (at >= float(T * places)), -1.0, value)

                here = seg(0)
                rows = pl.ds(k * T, T)
                first = jnp.zeros((T, 128), f32)
                for start in starts:
                    first = jnp.where(where == start, 1.0, first)
                r.masks[0, rows] = first
                for j in (1, 2, 3):
                    r.masks[j, rows] = jnp.where(seg(-j) == here, 1.0, 0.0)
                    r.masks[3 + j, rows] = jnp.where(seg(j) == here, 1.0, 0.0)
            settle(*self.out)

    class SmallGrad:
        def __init__(self):
            self.rg = new()
            self.out = []

        def one(self):
            for at in range(2 * RING):
                own = jnp.concatenate([r.gchan[:, at * RW : (at + 1) * RW], jnp.zeros((8, 128 - RW), f32)], axis=1)
                r.gs[at] = own
            for at in range(2 * RING):
                self.out.append(push(r.gs.at[at], r.gg.at[ring], ring_place(at), self.rg, ring != at))
            keep_local(r.gs.at[ring], r.gg.at[ring], self.rg)

        def two(self):
            arrived(r.gg, self.rg)
            value = r.gg[0]
            for at in range(1, 2 * RING):
                value = value + r.gg[at]
            r.small_out[0:7] = value[0:7]
            settle(*self.out)

    barrier = pltpu.get_barrier_semaphore()
    for _, dev in plane_peers:
        pl.semaphore_signal(barrier, 1, device_id=dev, device_id_type=MESH)
    for at in range(places):

        @pl.when(pos != at)
        def _(at=at):
            pl.semaphore_signal(barrier, 1, device_id=place(at), device_id_type=MESH)

    first_loads = [
        (src, dst, new())
        for src, dst in (
            (r.tokens, r.x_all.at[p]),
            (r.cotangent, r.cot_all.at[p]),
        )
    ]
    small_loads = [
        (src, dst, new())
        for src, dst in (
            (r.first_gain, r.gain_a),
            (r.second_gain, r.gain_b),
            (r.conv_taps, r.taps),
            (r.conv_bias, r.bias_a),
            (r.decay_bias, r.bias_b),
            (r.inject_bias, r.bias_c),
            (r.doc_lengths, r.lens),
            (r.decay_exponent, r.rates),
        )
    ]
    for load in small_loads + first_loads:
        keep_local(*load)

    w_i = Column(r.input_weight, r.raw_i, r.sort_i, r.w_ib, RD, CW, 0)
    w_b = Column(r.branch_weight, r.raw_b, r.sort_b, r.w_ib, RD, CW, CW)
    w_d = Column(r.decay_weight, r.raw_d, r.sort_d, r.w_di, RW, CW, 0)
    w_j = Column(r.inject_weight, r.raw_j, r.sort_j, r.w_di, RW, CW, CW)
    w_g = Column(r.mlp_gate, r.raw_g, r.sort_g, r.w_gu, RD, CF, 0)
    w_u = Column(r.mlp_up, r.raw_u, r.sort_u, r.w_gu, RD, CF, CF)
    w_g1, w_g2 = w_g.halves()
    w_o, w_dn = Row(r.output_weight, r.w_o), Row(r.mlp_down, r.w_dn)
    ag_x, ag_conv, ag_two = Gather(r.x_all), Gather(r.conv), Gather(r.n_two)
    ag_cot, ag_out = Gather(r.cot_all), Gather(r.d_out)
    small, small_grad = Small(), SmallGrad()
    after, before = flat_z + c, flat_z - (1 - c)
    to_next = {"zh": after // NL, "zl": after % NL, "c": 1 - c}
    to_prev = {"zh": before // NL, "zl": before % NL, "c": 1 - c}
    step = 256
    chunk = PLANE * RD * 2

    for w in (w_i, w_d, w_j, w_b, w_g, w_u):
        w.load()
    small.pack()
    w_i.prepare()
    w_d.prepare()
    pl.semaphore_wait(barrier, len(plane_peers) + places - 1)
    small.one()
    local_wait(*first_loads[0])
    halo_x = new()
    sent_x = push(r.x_all.at[p, pl.ds(T - 16, 16)], r.x_halo.at[p], to_next, halo_x, pos < places - 1)
    w_o.z_send((2,))
    w_i.spread()
    w_d.spread()
    ag_x.start()
    w_j.prepare()
    w_i.z_send()
    small.two()
    w_b.prepare()

    @pl.when(pos == 0)
    def _():
        r.x_halo[p] = jnp.zeros((16, D), bf16)

    arrived(r.x_halo.at[p], halo_x, pos > 0)
    halo_p = new(PLANE)
    sent_p = [push(r.x_halo.at[p], r.x_halo.at[p], dev, halo_p + p) for _, dev in plane_peers]
    ag_x.mid()
    w_i.z_forward()
    w_o.z_send((1,))
    w_g.prepare()
    local_wait(*first_loads[1])
    small.three()

    def norm_block(k):
        def norm_one(o):
            s = pl.ds(o, 32)
            v = r.x_all[k, s].astype(f32)
            r.n_one[k, s] = (v * inverse_rms(v) * r.gains[0:1]).astype(bf16)

        loop(T, 32, norm_one)

    norm_block(p)
    w_d.z_send()
    ag_x.wait_x()
    norm_block(px)
    ag_x.wait_y()
    norm_block(py)
    w_j.spread()
    small.four()
    for k, _ in plane_peers:
        arrived(r.x_halo.at[k], halo_p + k)
    v = r.x_halo[...].reshape(PLANE * 16, D).astype(f32)
    r.n_halo[...] = (v * inverse_rms(v) * r.gains[0:1]).astype(bf16).reshape(PLANE, 16, D)
    ag_x.wait_d()
    norm_block(pd)
    settle(*ag_x.out, sent_x, *sent_p)
    w_b.spread()
    w_g.spread()
    w_o.z_forward()
    w_i.z_wait()
    w_u.prepare()
    w_j.z_send()
    w_i.end()

    def weight_ib(lanes):
        return r.w_ib[:, :, :, lanes].reshape(D, CW)

    lanes_a, lanes_b = pl.ds(0, CW), pl.ds(CW, CW)
    halo = dot(r.n_halo[...].reshape(PLANE * 16, D), weight_ib(lanes_a)).astype(bf16).astype(f32)
    body = dot(r.n_one[...].reshape(M, D), weight_ib(lanes_a)).astype(bf16).astype(f32)
    for k in range(PLANE):
        r.u[k, 0:8] = halo[k * 16 + 8 : (k + 1) * 16]
        r.u[k, 8 : 8 + T] = body[k * T : (k + 1) * T]

    def wide(j, rows):
        return jnp.concatenate([r.masks[j, rows]] * (CW // 128), axis=1) > 0.5

    def convolve(o):
        for k in range(PLANE):
            ext = r.u[k, pl.ds(o, 24)]
            rows = ds(k * T + o, 16, 16)
            total = r.chan[4:5] + r.chan[0:1] * ext[8:24]
            for j in range(1, 4):
                total = total + jnp.where(wide(j, rows), r.chan[j : j + 1] * ext[8 - j : 24 - j], 0.0)
            r.conv[p, rows] = total.astype(bf16)

    loop(T, 16, convolve)
    ag_conv.start()
    w_d.z_forward()
    ag_conv.mid()
    w_j.z_forward()
    w_b.z_send()
    w_d.z_wait()
    w_d.end()

    def pre(q, lanes):
        return dot(r.conv[q], r.w_di[:, :, ds(q * RW, RW, 16), lanes].reshape(CW, CW))

    r.pair[:, 0:CW] = pre(p, lanes_a)
    ag_conv.wait_x()
    r.pair[:, 0:CW] += pre(px, lanes_a)
    ag_conv.wait_y()
    r.pair[:, 0:CW] += pre(py, lanes_a)
    w_b.z_forward()
    ag_conv.wait_d()
    r.pair[:, 0:CW] += pre(pd, lanes_a)
    settle(*ag_conv.out)
    w_g.spread_wait()
    w_g1.z_send(False)
    w_j.z_wait()
    w_u.spread()
    ag_cot.start()
    w_o.z_wait()
    w_j.end()
    r.pair[:, CW : 2 * CW] = (pre(0, lanes_b) + pre(1, lanes_b)) + (pre(2, lanes_b) + pre(3, lanes_b))

    def decay_terms(s, rg):
        log_a = -rate_scale * rg * r.chan[7:8]
        root = jnp.exp(log_a)
        gap = minus_expm1(2.0 * log_a, root)
        first = wide(0, s)
        return root, gap, jnp.where(first, 1.0, jnp.sqrt(jnp.maximum(gap, floor_gap))), first

    def gates_two(o):
        s = pl.ds(o, 16)
        rg = jax.nn.sigmoid(r.pair[s, 0:CW] + r.chan[5:6])
        ig = jax.nn.sigmoid(r.pair[s, CW : 2 * CW] + r.chan[6:7])
        root, _, mult, first = decay_terms(s, rg)
        r.rgate[s], r.igate[s] = rg, ig
        r.decay[s] = jnp.where(first, 0.0, root)
        r.work[s] = mult * ig * r.conv[p, s].astype(f32)

    loop(M, 16, gates_two)
    row = lax.broadcasted_iota(jnp.int32, (8, CW), 0)

    def scan_forward(j, carry):
        out = []
        for k in range(PLANE):
            s = ds(k * T + j * 8, 8, 8)
            a, b = r.decay[s], r.work[s]
            for n in (1, 2, 4):
                a_b = jnp.where(row >= n, pltpu.roll(a, n, 0), 1.0)
                b_b = jnp.where(row >= n, pltpu.roll(b, n, 0), 0.0)
                a, b = a * a_b, a * b_b + b
            total, prod = b + a * carry[2 * k], a * carry[2 * k + 1]
            r.state[k, ds(8 + j * 8, 8, 8)] = total
            r.cum[s] = prod
            out += [total[7:8], prod[7:8]]
        return tuple(out)

    zero, one = jnp.zeros((1, CW), f32), jnp.ones((1, CW), f32)
    ends = lax.fori_loop(0, T // 8, scan_forward, (zero, one) * PLANE)
    carry_f = Carry(r.own_f, r.sib_f, r.carry_f, True)
    for k in range(PLANE):
        r.own_f[k : k + 1] = ends[2 * k + 1]
        r.own_f[PLANE + k : PLANE + k + 1] = ends[2 * k]
    carry_f.send_core()
    w_b.z_wait()
    carry_f.send()
    w_g1.z_forward()
    w_g2.z_send(False)
    w_b.end()
    r.work[...] = dot(r.n_one[...].reshape(M, D), weight_ib(lanes_b))

    def gates_one(o):
        s = pl.ds(o, 16)
        r.gated[s], r.slope[s] = gelu_parts(r.work[s])

    loop(M, 16, gates_one)
    ag_cot.mid()
    carry_f.fold(r.into)
    for k in range(PLANE):
        r.state[k, 0:8] = jnp.broadcast_to(r.into[k : k + 1], (8, CW))

    def mix(o):
        for k in range(PLANE):
            s, t = ds(k * T + o, 16, 16), ds(8 + o, 16, 8)
            state = r.state[k, t] + r.cum[s] * r.into[k : k + 1]
            r.state[k, t] = state
            r.mixed[s] = (state * r.gated[s]).astype(bf16)

    loop(T, 16, mix)

    w_o.end()

    def out_part(o):
        q = pl.ds(o, step)
        r.part[:, :, q] = dot(r.mixed[...], r.w_o[:, :, :, q].reshape(CW, step)).astype(bf16).reshape(PLANE, T, step)

    loop(D, step, out_part)
    rs_one = Scatter(r.part, r.got_one)
    rs_one.start()
    w_g1.z_wait()
    w_g2.z_forward()
    w_u.z_send()
    ag_cot.end()
    rs_one.mid()
    rs_one.end()

    def norm_two(o, summed, _):
        s = pl.ds(o, 32)
        v = r.x_all[p, s].astype(f32) + summed
        r.x_one[s] = v
        r.n_two[p, s] = (v * inverse_rms(v) * r.gains[1:2]).astype(bf16)

    rs_one.each(32, norm_two)
    ag_two.start()
    w_u.z_forward()
    ag_two.mid()
    w_dn.z_send()
    w_g2.z_wait()
    w_g1.end()
    w_u.z_wait()
    w_g2.end()
    ag_two.end()

    def mlp_in(o):
        q = pl.ds(o, step)
        r.pair[:, q] = dot(r.n_two[...].reshape(M, D), r.w_gu[:, :, :, q].reshape(D, step))

    loop(CF, step, mlp_in)
    w_dn.z_forward()
    w_u.end()
    loop(CF, step, lambda o: mlp_in(pl.multiple_of(CF + o, step)))

    def gates_mlp(o):
        s = pl.ds(o, 16)
        value, slope = gelu_parts(r.pair[s, 0:CF])
        up = r.pair[s, CF : 2 * CF]
        r.hidden[s] = (value * up).astype(bf16)
        r.pair[s, 0:CF] = slope * up
        r.pair[s, CF : 2 * CF] = value

    loop(M, 16, gates_mlp)

    half = CF // 2
    for k in (0, 1):
        for o in range(0, D, D // 2):
            value = dot_tn(r.hidden[:, k * half : (k + 1) * half], r.cot_all[:, :, o : o + D // 2].reshape(M, D // 2))
            r.g_dn[k * RING // 2 : (k + 1) * RING // 2, :, :, o : o + D // 2] = value.astype(bf16).reshape(
                RING // 2, 2, RF, D // 2
            )
    g_dn = RowsGrad(r.g_dn, r.h_dn, r.z_dn, r.grad_mlp_down, r.grad_mlp_down)
    g_dn.core_send()
    g_dn.z_send()
    w_dn.z_wait()
    w_dn.end()

    for k in range(CF // step):
        back = dot_nt(r.cot_all[...].reshape(M, D), r.w_dn[...].reshape(CF, D)[k * step : (k + 1) * step])
        r.d_pair[:, k * step : (k + 1) * step] = (back * r.pair[:, k * step : (k + 1) * step]).astype(bf16)
        r.d_pair[:, CF + k * step : CF + (k + 1) * step] = (
            back * r.pair[:, CF + k * step : CF + (k + 1) * step]
        ).astype(bf16)

    def d_two_part(z, _):
        q = ds(z * chunk, chunk, chunk)
        r.part[:, :, q] = (
            dot_nt(r.d_pair[...], r.w_gu[z].reshape(chunk, 2 * CF)).astype(bf16).reshape(PLANE, T, chunk)
        )
        return 0

    lax.fori_loop(0, RING, d_two_part, 0)
    rs_two = Scatter(r.part, r.got_two)
    rs_two.start()

    def grad_gate_up(lane0):
        lanes = pl.ds(lane0, CF)

        def run(z, _):
            q = ds(z * chunk, chunk, chunk)
            value = dot_tn(r.n_two[:, :, q].reshape(M, chunk), r.d_pair[:, lanes])
            r.w_gu[z, :, :, lanes] = value.astype(bf16).reshape(2, chunk // 2, CF)
            return 0

        lax.fori_loop(0, RING, run, 0)

    grad_gate_up(0)
    g_g = ColumnsGrad(r.w_gu, r.h_gu, r.z_gu, r.l_gu, RD, 0, CF)
    g_g.core_send()
    rs_two.mid()
    g_dn.z_forward()
    g_g.z_send()
    grad_gate_up(CF)
    g_u, g_v = (
        ColumnsGrad(r.w_gu, r.h_gu, r.z_gu, r.l_gu, RD, lane0, CF // 2) for lane0 in (CF, CF + CF // 2)
    )
    g_u.core_send()
    g_v.core_send()

    def act_part(o):
        q = pl.ds(o, step)
        r.part_act[:, :, q] = dot(r.hidden[...], r.w_dn[:, :, :, q].reshape(CF, step)).astype(bf16).reshape(PLANE, T, step)

    loop(D, step, act_part)
    r.gchan[...] = jnp.zeros_like(r.gchan)
    rs_two.end()

    def norm_two_back(o, d_two, _):
        s = pl.ds(o, 32)
        v = r.x_one[s]
        rs = inverse_rms(v)
        z = v * rs
        dz = d_two * r.gains[1:2]
        d_one = r.cot_all[p, s].astype(f32) + rs * (dz - z * jnp.mean(dz * z, axis=-1, keepdims=True))
        r.d_one[s] = d_one
        r.d_out[p, s] = d_one.astype(bf16)

    rs_two.each(32, norm_two_back)
    ag_out.start()
    ag_out.mid()
    g_g.z_forward()
    g_u.z_send()
    ag_out.end()
    rs_act = Scatter(r.part_act, r.got_act)
    rs_act.start()

    r.work[...] = dot_nt(r.d_out[...].reshape(M, D), r.w_o[...].reshape(CW, D))

    def split(o):
        for k in range(PLANE):
            s = ds(k * T + o, 16, 16)
            d_mixed = r.work[s]
            r.d_gu[s, CW : 2 * CW] = (d_mixed * r.state[k, ds(8 + o, 16, 8)] * r.slope[s]).astype(bf16)
            r.work[s] = d_mixed * r.gated[s]

    loop(T, 16, split)

    def scan_backward(i, carry):
        j = T // 8 - 1 - i
        out = []
        for k in range(PLANE):
            s = ds(k * T + j * 8, 8, 8)
            decay, b = r.decay[s], r.work[s]
            a = jnp.where(row < 7, pltpu.roll(decay, 7, 0), carry[3 * k + 2])
            for n in (1, 2, 4):
                a_b = jnp.where(row < 8 - n, pltpu.roll(a, 8 - n, 0), 1.0)
                b_b = jnp.where(row < 8 - n, pltpu.roll(b, 8 - n, 0), 0.0)
                a, b = a * a_b, a * b_b + b
            total, prod = b + a * carry[3 * k], a * carry[3 * k + 1]
            r.work[s], r.cum[s] = total, prod
            out += [total[0:1], prod[0:1], decay[0:1]]
        return tuple(out)

    heads = lax.fori_loop(0, T // 8, scan_backward, (zero, one, one) * PLANE)
    carry_b = Carry(r.own_b, r.sib_b, r.carry_b, False)
    for k in range(PLANE):
        r.own_b[k : k + 1] = r.own_f[k : k + 1]
        r.own_b[PLANE + k : PLANE + k + 1] = heads[3 * k] * heads[3 * k + 2]
    carry_b.send_core()

    def grad_out(o):
        q = pl.ds(o, D // 2)
        value = dot_tn(r.mixed[...], r.d_out[:, :, q].reshape(M, D // 2))
        r.w_o[:, :, :, q] = value.astype(bf16).reshape(RING, 2, RW, D // 2)

    loop(D, D // 2, grad_out)
    g_o = RowsGrad(r.w_o, r.h_o, r.z_o, r.grad_output_weight, r.grad_output_weight)
    g_o.core_send()
    carry_b.send()
    g_u.z_forward()
    g_v.z_send()
    rs_act.mid()

    def d_branch_part(z, _):
        q = ds(z * chunk, chunk, chunk)
        r.part[:, :, q] = (
            dot_nt(r.d_gu[:, lanes_b], r.w_ib[z, :, :, lanes_b].reshape(chunk, CW))
            .astype(bf16)
            .reshape(PLANE, T, chunk)
        )
        value = dot_tn(r.n_one[:, :, q].reshape(M, chunk), r.d_gu[:, lanes_b])
        r.w_ib[z, :, :, lanes_b] = value.astype(bf16).reshape(2, chunk // 2, CW)
        return 0

    lax.fori_loop(0, RING, d_branch_part, 0)
    g_b = ColumnsGrad(r.w_ib, r.h_ib, r.z_ib, r.l_ib, RD, CW, CW)
    g_b.core_send()
    g_g.plane_send()
    carry_b.fold(r.into)
    g_o.z_send()

    def back(o):
        sums = [jnp.zeros((1, CW), f32)] * 2
        for k in range(PLANE):
            s = ds(k * T + o, 16, 16)
            adjoint = r.work[s] + r.cum[s] * r.into[k : k + 1]
            previous = r.state[k, pl.ds(o, 24)][7:23]
            rg, ig, decay, conv = r.rgate[s], r.igate[s], r.decay[s], r.conv[p, s].astype(f32)
            _, gap, mult, first = decay_terms(s, rg)
            d_mult = jnp.where(first, 0.0, adjoint * ig * conv)
            d_log = adjoint * previous * decay - jnp.where(gap > floor_gap, (1.0 - gap) * d_mult / mult, 0.0)
            d_decay = (-rate_scale * r.chan[7:8] * d_log * rg * (1.0 - rg)).astype(bf16)
            d_inject = (adjoint * mult * conv * ig * (1.0 - ig)).astype(bf16)
            r.d_pre[s, 0:CW] = d_decay
            r.d_pre[s, CW : 2 * CW] = d_inject
            sums[0] = sums[0] + jnp.sum(d_decay.astype(f32), axis=0, keepdims=True)
            sums[1] = sums[1] + jnp.sum(d_inject.astype(f32), axis=0, keepdims=True)
            r.d_conv[k, pl.ds(o, 16)] = adjoint * mult * ig
        r.gchan[5:6] += sums[0]
        r.gchan[6:7] += sums[1]

    loop(T, 16, back)

    def conv_part(q):
        r.part_conv[q] = dot_nt(r.d_pre[...], r.w_di[:, :, ds(q * RW, RW, 16), :].reshape(CW, 2 * CW)).astype(bf16)

    rs_conv = Scatter(r.part_conv, r.got_conv)
    conv_part(pd)
    rs_act.end()
    rs_conv.start_far()
    conv_part(px)
    conv_part(py)
    rs_conv.start_near()
    conv_part(p)
    g_v.z_forward()

    def finish_act(o, summed, _):
        s = pl.ds(o, 16)
        r.activations[s] = (r.x_one[s] + summed).astype(bf16)

    rs_act.each(16, finish_act)
    g_b.z_send()
    g_dn.end()

    def grad_dec_inj(lanes):
        def run(q, _):
            value = dot_tn(r.conv[q], r.d_pre[:, lanes])
            r.w_di[:, :, ds(q * RW, RW, 16), lanes] = value.astype(bf16).reshape(RING, 2, RW, CW)
            return 0

        lax.fori_loop(0, RING, run, 0)

    grad_dec_inj(lanes_a)
    g_d, g_j, g_k = (
        ColumnsGrad(r.w_di, r.h_di, r.z_di, r.l_di, RW, lane0, lanes)
        for lane0, lanes in ((0, 128), (128, CW - 128), (CW, CW))
    )
    g_d.core_send()
    g_j.core_send()
    rs_conv.mid()
    grad_dec_inj(lanes_b)
    g_k.core_send()
    g_o.z_forward()
    g_d.z_send()
    rs_conv.end()

    for half in (0, 1):

        def add_conv(o, half=half):
            for k in (2 * half, 2 * half + 1):
                at = (k - 2 * half) * T + o
                r.d_conv[k, pl.ds(o, 16)] += rs_conv.total(half, pl.multiple_of(at, 16), 16)

        loop(T, 16, add_conv)
    halo_b = new()
    for k in range(PLANE):
        r.halo_out[4 * k : 4 * k + 4] = r.d_conv[k, 0:4]
    sent_b = push(r.halo_out, r.halo_in, to_prev, halo_b, pos > 0)
    g_b.z_forward()
    g_j.z_send()

    def taps_back(o):
        sums = [jnp.zeros((1, CW), f32)] * 5
        for k in range(PLANE):
            ext = r.u[k, pl.ds(o, 24)]
            rows = ds(k * T + o, 16, 16)
            dc = r.d_conv[k, pl.ds(o, 16)]
            sums[4] = sums[4] + jnp.sum(dc, axis=0, keepdims=True)
            sums[0] = sums[0] + jnp.sum(dc * ext[8:24], axis=0, keepdims=True)
            for j in range(1, 4):
                term = jnp.where(wide(j, rows), dc * ext[8 - j : 24 - j], 0.0)
                sums[j] = sums[j] + jnp.sum(term, axis=0, keepdims=True)
        for j in range(5):
            r.gchan[j : j + 1] += sums[j]

    loop(T, 16, taps_back)
    small_grad.one()

    @pl.when(pos == places - 1)
    def _():
        r.halo_in[...] = jnp.zeros((16, CW), f32)

    g_d.z_forward()
    g_u.plane_send()
    g_v.plane_send()
    arrived(r.halo_in, halo_b, pos < places - 1)
    for k in range(PLANE):
        r.d_conv[k, T : T + 8] = jnp.concatenate([r.halo_in[4 * k : 4 * k + 4], jnp.zeros((4, CW), f32)], axis=0)

    def conv_back(o):
        for k in range(PLANE):
            ext = r.d_conv[k, pl.ds(o, 24)]
            rows = ds(k * T + o, 16, 16)
            total = r.chan[0:1] * ext[0:16]
            for j in range(1, 4):
                total = total + jnp.where(wide(3 + j, rows), r.chan[j : j + 1] * ext[j : 16 + j], 0.0)
            r.d_gu[rows, 0:CW] = total.astype(bf16)

    loop(T, 16, conv_back)

    def d_input_part(z, _):
        q = ds(z * chunk, chunk, chunk)
        value = dot_nt(r.d_gu[:, lanes_a], r.w_ib[z, :, :, lanes_a].reshape(chunk, CW)).reshape(PLANE, T, chunk)
        r.part[:, :, q] = (r.part[:, :, q].astype(f32) + value).astype(bf16)
        return 0

    lax.fori_loop(0, RING, d_input_part, 0)
    rs_three = Scatter(r.part, r.got_three)
    rs_three.start()

    def grad_input(z, _):
        q = ds(z * chunk, chunk, chunk)
        value = dot_tn(r.n_one[:, :, q].reshape(M, chunk), r.d_gu[:, lanes_a])
        r.w_ib[z, :, :, lanes_a] = value.astype(bf16).reshape(2, chunk // 2, CW)
        return 0

    lax.fori_loop(0, RING, grad_input, 0)
    g_i = LastGrad(r.w_ib, r.h_ib, r.st_i, r.z_i, RD, 0, CW, r.grad_input_weight, r.grad_input_weight)
    g_i.core_send()
    g_j.z_forward()
    g_k.z_send()
    g_i.plane_send()
    rs_three.mid()
    g_k.z_forward()
    rs_three.end()
    g_i.z_send()
    g_b.plane_send()
    g_d.plane_send()
    g_j.plane_send()

    def norm_one_back(o, d_n, _):
        s = pl.ds(o, 32)
        v = r.x_all[p, s].astype(f32)
        rs = inverse_rms(v)
        z = v * rs
        dz = d_n * r.gains[0:1]
        r.d_tokens[s] = r.d_one[s] + rs * (dz - z * jnp.mean(dz * z, axis=-1, keepdims=True))

    rs_three.each(32, norm_one_back)
    settle(sent_b)
    g_i.z_forward()
    g_k.plane_send()
    g_g.end()
    in_order(r.l_gu, 0, CF, r.grad_mlp_gate, r.grad_mlp_gate)
    g_u.end()
    g_v.end()
    in_order(r.l_gu, CF, CF, r.grad_mlp_up, r.grad_mlp_up)
    g_b.end()
    in_order(r.l_ib, CW, CW, r.grad_branch_weight, r.grad_branch_weight)
    g_o.end()
    small_grad.two()
    g_d.end()
    g_j.end()
    in_order(r.l_di, 0, CW, r.grad_decay_weight, r.grad_decay_weight)
    g_k.end()
    in_order(r.l_di, CW, CW, r.grad_inject_weight, r.grad_inject_weight)
    second = gain_grad(r.gain_b, (r.grad_mlp_gate, r.raw_g), (r.grad_mlp_up, r.raw_u))
    g_i.end()
    first = gain_grad(r.gain_a, (r.grad_input_weight, r.raw_i), (r.grad_branch_weight, r.raw_b))
    r.small_out[7:8] = jnp.concatenate([first, second, jnp.zeros((1, 128 - 2 * RD), f32)], axis=1)
    assert not sent


WEIGHTS = (
    "branch_weight",
    "input_weight",
    "decay_weight",
    "inject_weight",
    "output_weight",
    "mlp_gate",
    "mlp_up",
    "mlp_down",
)


def run_layer(NL, tokens, cotangent, small, weights):
    T, D = tokens.shape
    SEGS = small["doc_lengths"].shape[1]
    W, F = weights["branch_weight"].shape[1], weights["mlp_gate"].shape[1]
    CW, CF = W // PLANE, F // PLANE
    RD, RW, RF = D // SHARES, W // SHARES, F // SHARES
    GL, M, places = PLANE * RD, PLANE * T, RING * NL * 2
    hbm = pl.BlockSpec(memory_space=pl.ANY)
    ins = ["tokens", "cotangent", *small, *WEIGHTS]
    outs = dict(
        activations=((T, D), bf16),
        d_tokens=((T, D), f32),
        grad_input_weight=((RD, W), f32),
        grad_branch_weight=((RD, W), f32),
        grad_decay_weight=((RW, W), f32),
        grad_inject_weight=((RW, W), f32),
        grad_output_weight=((RW, D), f32),
        grad_mlp_gate=((RD, F), f32),
        grad_mlp_up=((RD, F), f32),
        grad_mlp_down=((RF, D), f32),
        small_out=((8, 128), f32),
    )
    columns = (("i", RD, CW), ("b", RD, CW), ("d", RW, CW), ("j", RW, CW), ("g", RD, CF), ("u", RD, CF))
    scratch = dict(
        w_ib=((RING, 2, PLANE * RD, 2 * CW), bf16),
        w_di=((RING, 2, PLANE * RW, 2 * CW), bf16),
        w_gu=((RING, 2, PLANE * RD, 2 * CF), bf16),
        w_o=((RING, 2, RW, D), bf16),
        w_dn=((RING, 2, RF, D), bf16),
        **{"raw_" + n: ((R, PLANE * C), bf16) for n, R, C in columns},
        **{"sort_" + n: ((PLANE, R, C), bf16) for n, R, C in columns},
        h_ib=((RING, PLANE * RD, 2 * CW), bf16),
        h_di=((RING, PLANE * RW, 2 * CW), bf16),
        h_gu=((RING, PLANE * RD, 2 * CF), bf16),
        h_o=((RING, RW, D), bf16),
        h_dn=((RING, RF, D), bf16),
        z_ib=((4, PLANE * RD, 2 * CW), bf16),
        z_di=((4, PLANE * RW, 2 * CW), bf16),
        z_gu=((4, PLANE * RD, 2 * CF), bf16),
        z_o=((4, RW, D), bf16),
        z_dn=((4, RF, D), bf16),
        l_ib=((PLANE, RD, 2 * CW), bf16),
        l_di=((PLANE, RW, 2 * CW), bf16),
        l_gu=((PLANE, RD, 2 * CF), bf16),
        n_one=((PLANE, T, D), bf16),
        n_two=((PLANE, T, D), bf16),
        cot_all=((PLANE, T, D), bf16),
        d_out=((PLANE, T, D), bf16),
        conv=((PLANE, M, CW), bf16),
        part=((PLANE, T, D), bf16),
        part_act=((PLANE, T, D), bf16),
        part_conv=((PLANE, M, CW), bf16),
        got_one=((6, T // 2, D), bf16),
        got_two=((6, T // 2, D), bf16),
        got_three=((6, T // 2, D), bf16),
        got_act=((6, T // 2, D), bf16),
        got_conv=((6, M // 2, CW), bf16),
        mixed=((M, CW), bf16),
        hidden=((M, CF), bf16),
        d_pair=((M, 2 * CF), bf16),
        d_gu=((M, 2 * CW), bf16),
        d_pre=((M, 2 * CW), bf16),
        pair=((M, 2 * CF), f32),
        u=((PLANE, T + 8, CW), f32),
        state=((PLANE, T + 8, CW), f32),
        d_conv=((PLANE, T + 8, CW), f32),
        **{name: ((M, CW), f32) for name in ("gated", "slope", "rgate", "igate", "decay", "work", "cum")},
        x_one=((T, D), f32),
        d_one=((T, D), f32),
        carry_f=((RING * NL, 2 * PLANE, CW), f32),
        carry_b=((RING * NL, 2 * PLANE, CW), f32),
        **{name: ((2 * PLANE, CW), f32) for name in ("own_f", "sib_f", "own_b", "sib_b")},
        halo_out=((16, CW), f32),
        halo_in=((16, CW), f32),
        into=((8, CW), f32),
        x_all=((PLANE, T, D), bf16),
        x_halo=((PLANE, 16, D), bf16),
        n_halo=((PLANE, 16, D), bf16),
        g_dn=((RING, 2, RF, D), bf16),
        masks=((7, M, 128), f32),
        pack=((16, 128), bf16),
        gain_a=((1, RD), bf16),
        gain_b=((1, RD), bf16),
        taps=((4, RW), bf16),
        bias_a=((1, RW), bf16),
        bias_b=((1, RW), bf16),
        bias_c=((1, RW), bf16),
        lens=((1, SEGS), jnp.int32),
        rates=((W // 128, 128), jnp.int32),
        pr=((2 * RING, 16, 128), bf16),
        line=((16, 128), bf16),
        pp=((PLANE, 16, 128), bf16),
        st_i=((PLANE, RING, RD, CW), bf16),
        z_i=((4, PLANE, RD, CW), bf16),
        gains=((8, D), f32),
        chan=((8, CW), f32),
        gchan=((8, CW), f32),
        gs=((2 * RING, 8, 128), f32),
        gg=((2 * RING, 8, 128), f32),
    )
    dims = SimpleNamespace(
        T=T, D=D, W=W, F=F, CW=CW, CF=CF, RD=RD, RW=RW, RF=RF, NL=NL, SEGS=SEGS, receives=RECEIVES + 2 * RING * NL, names=[*ins, *outs, *scratch, "ss", "rs"]
    )
    flops = 3 * 2 * M * (D * 2 * CW + W * 2 * CW + CW * D + 3 * D * CF)
    results = pl.pallas_call(
        partial(layer, dims),
        out_shape=[pltpu.VMEM(shape, kind) for shape, kind in outs.values()],
        in_specs=[hbm] * len(ins),
        out_specs=[pl.BlockSpec(memory_space=pltpu.VMEM)] * len(outs),
        scratch_shapes=[pltpu.VMEM(shape, kind) for shape, kind in scratch.values()]
        + [pltpu.SemaphoreType.DMA((SENDS,)), pltpu.SemaphoreType.DMA((dims.receives,))],
        compiler_params=pltpu.CompilerParams(
            collective_id=0, has_side_effects=True, vmem_limit_bytes=58 * 2**20
        ),
        cost_estimate=pl.CostEstimate(flops=flops, bytes_accessed=8 * 2**20, transcendentals=M * CW * 16),
        name="griffin_layer",
    )(tokens, cotangent, *small.values(), *[weights[name] for name in WEIGHTS])
    return finish({**small, **dict(zip(outs, results, strict=True))}, weights)


def finish(got, weights):
    hbm = pl.BlockSpec(memory_space=pl.ANY)
    behind = {"first_gain": ("input_weight", "branch_weight"), "second_gain": ("mlp_gate", "mlp_up")}
    RD, RW = got["grad_input_weight"].shape[0], got["grad_decay_weight"].shape[0]
    channels = {"conv_taps": (0, 4), "conv_bias": (4, 5), "decay_bias": (5, 6), "inject_bias": (6, 7)}
    shared = [name for names in behind.values() for name in names]
    rest = ["grad_" + name for name in WEIGHTS if name not in shared]
    plain = [*["grad_" + name for name in shared], *rest, "d_tokens", "activations"]
    names = ["small_out", *plain]
    shapes = {name: got[name] for name in plain}
    for name in behind:
        shapes["grad_" + name] = jax.ShapeDtypeStruct((1, RD), f32)
    for name, (low, high) in channels.items():
        shapes["grad_" + name] = jax.ShapeDtypeStruct((high - low, RW), f32)
    scratch = {name: (like.shape, f32) for name, like in shapes.items() if name not in plain}

    def body(*refs):
        ins = dict(zip(names, refs[: len(names)], strict=True))
        outs = dict(zip(shapes, refs[len(names) : len(names) + len(shapes)], strict=True))
        held, sems = dict(zip(scratch, refs[len(names) + len(shapes) : -1], strict=True)), refs[-1]
        copies = []

        def copy(src, dst):
            copies.append(pltpu.make_async_copy(src, dst, sems.at[len(copies)]))
            copies[-1].start()
            return copies[-1]

        held.update(ins)
        stores = []

        def store(name):
            stores.append(copy(held[name], outs[name]))

        for name, (low, high) in channels.items():
            held["grad_" + name][...] = held["small_out"][low:high, 0:RW]
            store("grad_" + name)
        for name in plain:
            store(name)
        for i, gain in enumerate(behind):
            held["grad_" + gain][...] = held["small_out"][7:8, i * RD : (i + 1) * RD]
            store("grad_" + gain)
        for each in stores:
            each.wait()

    results = pl.pallas_call(
        body,
        out_shape=[jax.ShapeDtypeStruct(like.shape, like.dtype) for like in shapes.values()],
        in_specs=[pl.BlockSpec(memory_space=pltpu.VMEM)] * len(names),
        out_specs=[hbm] * len(shapes),
        scratch_shapes=[
            *[pltpu.VMEM(shape, kind) for shape, kind in scratch.values()],
            pltpu.SemaphoreType.DMA((len(names) + len(shapes),)),
        ],
        compiler_params=pltpu.CompilerParams(vmem_limit_bytes=24 * 2**20),
        name="finish",
    )(*[got[name] for name in names])
    return {**got, **dict(zip(shapes, results, strict=True))}


def local(
    sizes,
    tokens,
    cotangent,
    doc_lengths,
    decay_exponent,
    branch_weight,
    input_weight,
    decay_weight,
    inject_weight,
    output_weight,
    mlp_gate,
    mlp_up,
    mlp_down,
    first_gain,
    second_gain,
    conv_taps,
    conv_bias,
    decay_bias,
    inject_bias,
):
    devices = math.prod(sizes.values())
    at = {name: lax.axis_index(name) for name in AXES}
    mine = at["yl"] * 2 + at["xl"]
    ring = at["zh"] * 2 + at["c"]
    share = ring * PLANE + mine
    groups = devices // SHARES

    def pooled(value, axis=0):
        if groups == 1:
            return value
        whole = lax.all_gather(value, AXES, axis=axis, tiled=True)
        size = whole.shape[axis] // SHARES
        return lax.dynamic_slice_in_dim(whole, share * size, size, axis)

    small = dict(
        first_gain=pooled(first_gain[None], 1),
        second_gain=pooled(second_gain[None], 1),
        conv_taps=pooled(conv_taps.T, 1),
        conv_bias=pooled(conv_bias[None], 1),
        decay_bias=pooled(decay_bias[None], 1),
        inject_bias=pooled(inject_bias[None], 1),
        doc_lengths=doc_lengths,
        decay_exponent=decay_exponent.reshape(-1, 128),
    )
    weights = dict(
        zip(
            WEIGHTS,
            (branch_weight, input_weight, decay_weight, inject_weight, output_weight, mlp_gate, mlp_up, mlp_down),
            strict=True,
        )
    )
    weights = {name: pooled(value) for name, value in weights.items()}
    got = run_layer(sizes["zl"], tokens[0], cotangent[0], small, weights)

    def returned(value, axis=0):
        if groups == 1:
            return value
        shape = list(value.shape)
        size = shape[axis]
        shape[axis] = size * SHARES
        whole = lax.dynamic_update_slice_in_dim(jnp.zeros(shape, bf16), value.astype(bf16), share * size, axis)
        return lax.psum_scatter(whole, AXES, scatter_dimension=axis, tiled=True).astype(f32)

    grads = [returned(got["grad_" + name]) for name in WEIGHTS]
    first, second, taps, *biases = (
        returned(got["grad_" + name], 1)
        for name in ("first_gain", "second_gain", "conv_taps", "conv_bias", "decay_bias", "inject_bias")
    )
    return (
        got["activations"][None],
        got["d_tokens"][None],
        *grads,
        first[0],
        second[0],
        taps.T,
        *[bias[0] for bias in biases],
    )


def solution(mesh):
    seq, dp = mesh.shape["seq"], mesh.shape["dp"]
    across = 1 << ((dp.bit_length() - 1) // 2)
    sizes = dict(zip(AXES, (RING, seq // (2 * RING), 2, dp // across // 2, 2, across // 2, 2), strict=True))
    split = Mesh(mesh.devices.reshape(tuple(sizes.values())), AXES)
    along_seq, along_dp = AXES[:3], AXES[3:]
    rows = P(along_dp, along_seq, None)
    in_specs = (rows, rows, P(along_dp, None), P(), *[P(AXES, None)] * 8, P(AXES), P(AXES), P(AXES, None), *[P(AXES)] * 3)
    out_specs = (rows, rows, *[P(AXES, None)] * 8, P(AXES), P(AXES), P(AXES, None), *[P(AXES)] * 3)
    return jax.shard_map(partial(local, sizes), mesh=split, in_specs=in_specs, out_specs=out_specs, check_vma=False)
```
